32 devices in a mesh: gx: 8 (over z, y), gz: 4 (over x, core).
Axes of the slice: x: 2, y: 2, z: 4, core: 2. Of those that a mesh axis runs over, the one named last changes fastest.
Arguments:
- solid_state: float32 [9, 20, 8192], P(None, None, ('gx', 'gz')), may hold values from -6 to 6
- jacobians: float32 [3, 9, 9, 8192], P(None, None, None, ('gx', 'gz')), may hold values from -2 to 2
- flux_solvers: float32 [4, 9, 9, 8192], P(None, None, None, ('gx', 'gz')), may hold values from -2 to 2
- stiffness: float32 [3, 20, 20], replicated, may hold values from -1.25 to 1.25
- trace_matrix: float32 [4, 10, 20], replicated, may hold values from -1.25 to 1.25
- lift_matrix: float32 [4, 20, 10], replicated, may hold values from -2 to 2
- neighbours: int32 [4, 8192], P(None, ('gx', 'gz')), may hold values from 0 to 1575, as said below
- send_faces: int32 [4, 4096], P(None, ('gx', 'gz')), may hold values from 0 to 1023, as said below
- surface_map: int32 [3, 5, 256], P(None, None, ('gx', 'gz')), may hold values from 0 to 16383, as said below
- surface_normals: float32 [3, 5, 256], P(None, None, ('gx', 'gz')), may hold values from -1 to 1
- air_state: float32 [4, 64, 64, 128], P(None, 'gx', 'gz'), may hold values from -6 to 6
- wind_field: float32 [3, 64, 64, 128], P(None, 'gx', 'gz'), may hold values from -0.3 to 0.3
- air_medium: float32 [2, 64, 64, 128], P(None, 'gx', 'gz'), may hold values from 0.05 to 0.25
Outputs:
- solid_next: float32 [9, 20, 8192], P(None, None, ('gx', 'gz'))
- air_next: float32 [4, 64, 64, 128], P(None, 'gx', 'gz')
The draws below stay inside these ranges and needn't reach their ends.
Inputs may be any that keep to these rules, and one draw needn't show every extreme that they name: `neighbours`: entry [f, e] of a partition names what lies across face f of its tetrahedron e: below 1024 a face slot of the same partition (such slots name each other in pairs), from 1024 the slot 1024 + d * 128 + k of the k-th face shared in direction d, from 1536 the surface slot r * 8 + k. `send_faces`: the entries of a partition are distinct face slots; the face slot in [d, k] has neighbour entry 1024 + d * 128 + k. `surface_map`: row 0 holds distinct face slots, none of them in send_faces, whose neighbour entry is their surface slot; row 1 a cell index below 16384; row 2 is 1 for coupled slots and 0 otherwise. The coupled slots of one r are the lowest k; slots whose target strip lies outside 0 to 7 are uncoupled; the slots with r = 2 are all coupled.
All inputs are finite; a program needn't handle non-finite values.
Results may differ from the reference program's by a relative error of at most 0.0003.
Values sent between devices are 32-bit elements; how exact they have to be, the bound alone decides.
No kernel may reach another device: no remote copies, remote signals or barrier semaphores. Data moves between devices by JAX's collectives and lax.ppermute only.
A program may use at most 128 MiB of HBM per device.

```python
import jax
import jax.numpy as jnp
from jax import lax

QUANT = 9
BASIS = 20
FACE_BASIS = 10
ORDERS = 4
RADIUS = 4
SUBSTEPS = 3
REACH = 5
TET_DEV = 256
BF = 128
CAP = 8
CX = 8
CZ = 16
CY = 128
STRIPS = 8
BANDS = 4
TETS = 8192
NX = 64
NZ = 64
DEVICES = 32


def layout(key):
    slots = 4 * TET_DEV

    def single(partition):
        device_key = jax.random.fold_in(key, partition)
        shuffle_key, count_key, cell_key = jax.random.split(device_key, 3)
        shuffled = jax.random.permutation(shuffle_key, slots).astype(jnp.int32)
        top_where = jnp.argmax((shuffled == slots - 1).astype(jnp.int32)).astype(jnp.int32)
        shuffled = shuffled.at[top_where].set(shuffled[0])
        shuffled = shuffled.at[0].set(slots - 1)
        low_where = jnp.argmax((shuffled == 0).astype(jnp.int32)).astype(jnp.int32)
        shuffled = shuffled.at[low_where].set(shuffled[1])
        shuffled = shuffled.at[1].set(0)
        shared_slots = shuffled[:4 * BF]
        surface_slots = shuffled[4 * BF:4 * BF + REACH * CAP]
        remaining = shuffled[4 * BF + REACH * CAP:]
        first_half = remaining[0::2]
        second_half = remaining[1::2]
        partner_slots = jnp.zeros((slots,), jnp.int32)
        partner_slots = partner_slots.at[shared_slots].set(slots + jnp.arange(4 * BF, dtype=jnp.int32))
        partner_slots = partner_slots.at[surface_slots].set(slots + 4 * BF + jnp.arange(REACH * CAP, dtype=jnp.int32))
        partner_slots = partner_slots.at[first_half].set(second_half)
        partner_slots = partner_slots.at[second_half].set(first_half)
        strip_id = partition // BANDS
        limits = jnp.array([CAP // 2 + 1, CAP + 1, CAP + 1, CAP + 1, CAP // 2 + 1], jnp.int32)
        counts = jax.random.randint(count_key, (REACH,), 0, limits).astype(jnp.int32)
        counts = counts.at[REACH // 2].set(CAP)
        targets = strip_id + jnp.arange(REACH, dtype=jnp.int32) - REACH // 2
        inside = (targets >= 0) & (targets < STRIPS)
        coupled = ((jnp.arange(CAP, dtype=jnp.int32)[None, :] < counts[:, None]) & inside[:, None]).astype(jnp.int32)
        target_cells = jax.random.randint(cell_key, (REACH, CAP), 0, CX * CZ * CY).astype(jnp.int32)
        target_cells = target_cells.at[REACH // 2, 0].set(CX * CZ * CY - 1)
        surface_rows = jnp.stack([surface_slots.reshape(REACH, CAP), target_cells, coupled])
        return (partner_slots.reshape(4, TET_DEV), shared_slots.reshape(4, BF), surface_rows)
    partner_all, shared_all, surface_all = jax.vmap(single)(jnp.arange(STRIPS * BANDS, dtype=jnp.int32))
    neighbour_whole = jnp.moveaxis(partner_all, 0, 1).reshape(4, STRIPS * BANDS * TET_DEV)
    shared_whole = jnp.moveaxis(shared_all, 0, 1).reshape(4, STRIPS * BANDS * BF)
    surface_whole = jnp.moveaxis(surface_all, 0, 2).reshape(3, REACH, STRIPS * BANDS * CAP)
    return (neighbour_whole, shared_whole, surface_whole)


def draw_neighbours(key, part):
    pieces = layout(key)
    return pieces[0]


def draw_send_faces(key, part):
    pieces = layout(key)
    return pieces[1]


def draw_surface_map(key, part):
    pieces = layout(key)
    return pieces[2]


def levels(own_key, dims, cuts, low, high):
    def one(dim, parts):
        steps = jax.random.uniform(jax.random.fold_in(jax.random.fold_in(own_key, 6), dim), (parts,), jnp.float32, low / len(cuts), high / len(cuts))
        return jnp.repeat(jnp.exp(steps), dims[dim] // parts).reshape((-1,) + (1,) * (len(dims) - dim - 1))

    loudness = one(*cuts[0])
    for cut in cuts[1:]:
        loudness = loudness * one(*cut)
    return loudness


def normal_values(key, dims, width, most, cuts=(), held_as=jnp.bfloat16):
    result = jax.random.normal(key, dims, jnp.float32) * width
    if len(cuts) > 0:
        result = levels(key, dims, cuts, -0.22, 0.18) * result
    return jnp.clip(result, min=-most, max=most).astype(held_as)


def setup_inputs(seed: int = 0) -> dict:
    arg_keys = jax.random.split(jax.random.key(seed), 14)
    solid_state = normal_values(arg_keys[0], (QUANT, BASIS, TETS), 1.0, 6.0, ((2, 32),), jnp.float32)
    jacobians = normal_values(arg_keys[1], (3, QUANT, QUANT, TETS), QUANT ** -0.5, 2.0, ((3, 32),), jnp.float32)
    flux_solvers = normal_values(arg_keys[2], (4, QUANT, QUANT, TETS), QUANT ** -0.5, 2.0, ((3, 32),), jnp.float32)
    stiffness = normal_values(arg_keys[3], (3, BASIS, BASIS), BASIS ** -0.5, 1.25, (), jnp.float32)
    trace_matrix = normal_values(arg_keys[4], (4, FACE_BASIS, BASIS), BASIS ** -0.5, 1.25, (), jnp.float32)
    lift_matrix = normal_values(arg_keys[5], (4, BASIS, FACE_BASIS), FACE_BASIS ** -0.5, 2.0, (), jnp.float32)
    neighbours = draw_neighbours(jax.random.fold_in(arg_keys[13], 71), 0)
    send_faces = draw_send_faces(jax.random.fold_in(arg_keys[13], 71), 0)
    surface_map = draw_surface_map(jax.random.fold_in(arg_keys[13], 71), 0)
    surface_normals = jnp.clip(jax.random.uniform(arg_keys[9], (3, REACH, CAP * DEVICES), jnp.float32, -1.0, 1.0) * levels(arg_keys[9], (3, REACH, CAP * DEVICES), ((2, 32),), -0.4, 0.0), -1.0, 1.0)
    air_state = normal_values(arg_keys[10], (4, NX, NZ, CY), 1.0, 6.0, ((1, 8), (2, 4)), jnp.float32)
    wind_field = jnp.clip(jax.random.uniform(arg_keys[11], (3, NX, NZ, CY), jnp.float32, -0.3, 0.3) * levels(arg_keys[11], (3, NX, NZ, CY), ((1, 8), (2, 4)), -0.4, 0.0), -0.3, 0.3)
    air_medium = jnp.clip(0.05 + 0.2 * jax.random.uniform(arg_keys[12], (2, NX, NZ, CY), jnp.float32) ** levels(arg_keys[12], (2, NX, NZ, CY), ((1, 8), (2, 4)), -0.2, 0.2), 0.05, 0.25)
    return {"solid_state": solid_state, "jacobians": jacobians, "flux_solvers": flux_solvers, "stiffness": stiffness, "trace_matrix": trace_matrix, "lift_matrix": lift_matrix, "neighbours": neighbours, "send_faces": send_faces, "surface_map": surface_map, "surface_normals": surface_normals, "air_state": air_state, "wind_field": wind_field, "air_medium": air_medium}


PRECISE = lax.Precision.HIGHEST
TIME_STEP = 0.5
COUPLING_GAIN = 1.0
STENCIL_WEIGHTS = (0.8, -0.2, 4.0 / 105.0, -1.0 / 280.0)


def centered(values, dimension, begin_at, length_out):
    accumulated = jnp.zeros_like(lax.slice_in_dim(values, begin_at, begin_at + length_out, axis=dimension))
    for offset, weight in enumerate(STENCIL_WEIGHTS, 1):
        ahead = lax.slice_in_dim(values, begin_at + offset, begin_at + offset + length_out, axis=dimension)
        behind = lax.slice_in_dim(values, begin_at - offset, begin_at - offset + length_out, axis=dimension)
        accumulated = accumulated + weight * (ahead - behind)
    return accumulated


def derivative(values, margin, rim_out, dimension):
    shift_in = margin - rim_out
    first_len = values.shape[0] - 2 * shift_in
    second_len = values.shape[1] - 2 * shift_in
    if dimension == 0:
        return centered(values[:, shift_in:shift_in + second_len], 0, shift_in, first_len)
    if dimension == 1:
        return centered(values[shift_in:shift_in + first_len], 1, shift_in, second_len)
    cropped = values[shift_in:shift_in + first_len, shift_in:shift_in + second_len]
    padded = jnp.pad(cropped, ((0, 0), (0, 0), (RADIUS, RADIUS)))
    return centered(padded, 2, RADIUS, values.shape[2])


def pressure_update(widened, margin, rim_out, wind_part, bulk_part):
    pressure = widened[0]
    shift_in = margin - rim_out
    first_len = pressure.shape[0] - 2 * shift_in
    second_len = pressure.shape[1] - 2 * shift_in
    divergence = derivative(widened[1], margin, rim_out, 0) + derivative(widened[2], margin, rim_out, 1) + derivative(widened[3], margin, rim_out, 2)
    advection = wind_part[0] * derivative(pressure, margin, rim_out, 0) + wind_part[1] * derivative(pressure, margin, rim_out, 1) + wind_part[2] * derivative(pressure, margin, rim_out, 2)
    return pressure[shift_in:shift_in + first_len, shift_in:shift_in + second_len] - bulk_part * divergence - advection


def velocity_update(widened, margin, new_pressure, pressure_margin, wind_part, buoyancy):
    results = []
    for component in range(3):
        velocity = widened[1 + component]
        interior = velocity[margin:velocity.shape[0] - margin, margin:velocity.shape[1] - margin]
        advection = wind_part[0] * derivative(velocity, margin, 0, 0) + wind_part[1] * derivative(velocity, margin, 0, 1) + wind_part[2] * derivative(velocity, margin, 0, 2)
        results.append(interior - buoyancy * derivative(new_pressure, pressure_margin, 0, component) - advection)
    return jnp.stack(results)


def predict(state, jacobians, stiffness):
    current = state
    integral = TIME_STEP * state
    weight_now = TIME_STEP
    for degree in range(1, ORDERS):
        rotated = jnp.einsum("dbc,qce->dqbe", stiffness, current, precision=PRECISE)
        current = -jnp.einsum("dpqe,dqbe->pbe", jacobians, rotated, precision=PRECISE)
        weight_now = weight_now * TIME_STEP / (degree + 1)
        integral = integral + weight_now * current
    return integral


def correct(state, integral, jacobians, flux_solvers, stiffness, lift_matrix, own_traces, outer_traces):
    rotated = jnp.einsum("dcb,qce->dqbe", stiffness, integral, precision=PRECISE)
    volume_term = jnp.einsum("dpqe,dqbe->pbe", jacobians, rotated, precision=PRECISE)
    fluxed = jnp.einsum("fpqe,qjfe->pjfe", flux_solvers, outer_traces - own_traces, precision=PRECISE)
    surface_term = jnp.einsum("fbj,pjfe->pbe", lift_matrix, fluxed, precision=PRECISE)
    return state + volume_term + surface_term


def from_lower(values, dimension):
    empty_rim = jnp.zeros_like(lax.slice_in_dim(values, 0, 1, axis=dimension))
    return jnp.concatenate([empty_rim, lax.slice_in_dim(values, 0, values.shape[dimension] - 1, axis=dimension)], axis=dimension)


def from_upper(values, dimension):
    empty_rim = jnp.zeros_like(lax.slice_in_dim(values, 0, 1, axis=dimension))
    return jnp.concatenate([lax.slice_in_dim(values, 1, values.shape[dimension], axis=dimension), empty_rim], axis=dimension)


def reference(solid_state, jacobians, flux_solvers, stiffness, trace_matrix, lift_matrix, neighbours, send_faces, surface_map, surface_normals, air_state, wind_field, air_medium):
    partitions = STRIPS * BANDS

    def by_partition(values):
        values = values.reshape(values.shape[:-1] + (partitions, values.shape[-1] // partitions))
        return jnp.moveaxis(values, -2, 0)

    state_parts = by_partition(solid_state)
    jacobian_parts = by_partition(jacobians)
    solver_parts = by_partition(flux_solvers)
    neighbour_parts = by_partition(neighbours)
    send_parts = by_partition(send_faces)
    surface_parts = by_partition(surface_map)
    normal_parts = by_partition(surface_normals)

    def predict_part(packed):
        state_one, jacobian_one = packed
        integral = predict(state_one, jacobian_one, stiffness)
        own_traces = jnp.einsum("fjb,qbe->qjfe", trace_matrix, integral, precision=PRECISE)
        return integral, own_traces.reshape(QUANT, FACE_BASIS, 4 * TET_DEV)

    integral_parts, trace_parts = lax.map(predict_part, (state_parts, jacobian_parts))

    def pick_outgoing(traces_one, sends_one):
        return jnp.take(traces_one, sends_one.reshape(-1), axis=2).reshape(QUANT, FACE_BASIS, 4, BF)

    outgoing = jax.vmap(pick_outgoing)(trace_parts, send_parts)
    partition_grid = outgoing.reshape(STRIPS, BANDS, QUANT, FACE_BASIS, 4, BF)
    received = jnp.stack([
        from_lower(partition_grid[:, :, :, :, 1], 0),
        from_upper(partition_grid[:, :, :, :, 0], 0),
        from_lower(partition_grid[:, :, :, :, 3], 1),
        from_upper(partition_grid[:, :, :, :, 2], 1)], axis=4).reshape(partitions, QUANT, FACE_BASIS, 4 * BF)

    face_slots = surface_parts[:, 0]
    target_cells = surface_parts[:, 1]
    coupled = surface_parts[:, 2].astype(jnp.float32)
    mean_speed = jnp.mean(trace_parts[:, 6:9], axis=2)

    def pick_speed(speed_one, slots_one):
        return jnp.take(speed_one, slots_one.reshape(-1), axis=1).reshape(3, REACH, CAP)

    at_faces = jax.vmap(pick_speed)(mean_speed, face_slots)
    normal_speed = coupled * jnp.sum(normal_parts * at_faces, axis=1)

    part_ids = jnp.arange(partitions, dtype=jnp.int32)
    strip_ids = part_ids // BANDS
    band_ids = part_ids % BANDS
    targets = jnp.clip(strip_ids[:, None] + jnp.arange(REACH, dtype=jnp.int32)[None, :] - 2, 0, STRIPS - 1)
    first_idx = targets[:, :, None] * CX + target_cells // (CZ * CY)
    vertical_idx = band_ids[:, None, None] * CZ + (target_cells // CY) % CZ
    third_idx = target_cells % CY
    flat_index = ((first_idx * NZ + vertical_idx) * CY + third_idx).astype(jnp.int32)
    pressure_flat = air_state[0].reshape(-1)
    replies = coupled * pressure_flat[flat_index]
    injected = pressure_flat.at[flat_index.reshape(-1)].add(COUPLING_GAIN * normal_speed.reshape(-1))

    air_now = jnp.concatenate([injected.reshape((1,) + air_state.shape[1:]), air_state[1:]], axis=0)
    for substep in range(SUBSTEPS):
        padded = jnp.pad(air_now, ((0, 0), (RADIUS, RADIUS), (RADIUS, RADIUS), (0, 0)))
        new_pressure = pressure_update(padded, RADIUS, 0, wind_field, air_medium[0])
        padded_pressure = jnp.pad(new_pressure, ((RADIUS, RADIUS), (RADIUS, RADIUS), (0, 0)))
        velocities = velocity_update(padded, RADIUS, padded_pressure, RADIUS, wind_field, air_medium[1])
        air_now = jnp.concatenate([new_pressure[None], velocities], axis=0)

    def correct_part(packed):
        state_one, integral_one, jacobian_one, solver_one, traces_one, received_one, slots_one, replies_one, neighbour_one = packed
        own_at = jnp.take(traces_one, slots_one.reshape(-1), axis=2)
        mirrored = jnp.concatenate([-2.0 * replies_one.reshape(-1) - own_at[0:3], own_at[3:]], axis=0)
        extended = jnp.concatenate([traces_one, received_one, mirrored], axis=2)
        outer_traces = jnp.take(extended, neighbour_one.reshape(-1), axis=2).reshape(QUANT, FACE_BASIS, 4, TET_DEV)
        return correct(state_one, integral_one, jacobian_one, solver_one, stiffness, lift_matrix, traces_one.reshape(QUANT, FACE_BASIS, 4, TET_DEV), outer_traces)

    next_parts = lax.map(correct_part, (state_parts, integral_parts, jacobian_parts, solver_parts, trace_parts, received, face_slots, replies, neighbour_parts))
    solid_next = jnp.moveaxis(next_parts, 0, 2).reshape(QUANT, BASIS, TETS)
    return solid_next, air_now
```

```python
import functools

import jax
import jax.numpy as jnp
from jax import lax
from jax.experimental import pallas as pl
from jax.experimental.pallas import tpu as pltpu
from jax.sharding import PartitionSpec as P

ORDERS = 4
RADIUS = 4
SUBSTEPS = 3
ZRIM = 8
LANES = 128
TIME_STEP = 0.5
STENCIL_WEIGHTS = (0.8, -0.2, 4.0 / 105.0, -1.0 / 280.0)
F32 = jnp.float32
BF16 = jnp.bfloat16


def call(kernel, name, outs, ins, scratch=(), flops=1_000_000):
    nbytes = 4 * sum(x.size for x in ins) + 4 * sum(functools.reduce(lambda m, n: m * n, s, 1) for s in outs)
    return pl.pallas_call(
        kernel,
        out_shape=[jax.ShapeDtypeStruct(s, F32) for s in outs],
        in_specs=[pl.BlockSpec(memory_space=pltpu.VMEM) for _ in ins],
        out_specs=[pl.BlockSpec(memory_space=pltpu.VMEM) for _ in outs],
        scratch_shapes=[pltpu.VMEM(s, F32) for s in scratch],
        compiler_params=pltpu.CompilerParams(vmem_limit_bytes=24 * 1024 * 1024),
        cost_estimate=pl.CostEstimate(flops=flops, bytes_accessed=nbytes, transcendentals=0),
        name=name,
    )(*ins)


def swap(values, axis, odd):
    count = lax.axis_size(axis)
    pairs = []
    for i in range(odd, count - 1, 2):
        pairs += [(i, i + 1), (i + 1, i)]
    return lax.ppermute(values, axis, pairs)


def exchange(xa, xb, za, zb):
    return (swap(za, "gz", 0), swap(zb, "gz", 1), swap(xa, "gx", 0), swap(xb, "gx", 1))


def sides(axis):
    parity = lax.axis_index(axis) & 1
    return 1 - parity, parity


def halves(values):
    high = values.astype(BF16)
    return high, (values - high.astype(F32)).astype(BF16)


def dot3(left, right, dims=(((1,), (0,)), ((), ()))):
    lh, ll = halves(left)
    rh, rl = halves(right)
    mul = functools.partial(lax.dot_general, dimension_numbers=dims, preferred_element_type=F32)
    return mul(lh, rh) + (mul(lh, rl) + mul(ll, rh))


def dot_exact(left, right, dims=(((1,), (0,)), ((), ()))):
    return lax.dot_general(
        left, right, dims, precision=lax.Precision.HIGHEST, preferred_element_type=F32
    )


def flat_slots(values):
    rows, slots = values.shape
    lane = lax.broadcasted_iota(jnp.int32, (slots, LANES), 1)
    place = lax.broadcasted_iota(jnp.int32, (slots, LANES), 0)
    spread = dot_exact(values, jnp.where(lane % slots == place, 1.0, 0.0).astype(F32))
    lane = lax.broadcasted_iota(jnp.int32, (rows, LANES), 1)
    place = lax.broadcasted_iota(jnp.int32, (rows, LANES), 0)
    return jnp.sum(jnp.where(lane // slots == place, spread, 0.0), axis=0, keepdims=True)


def pack_x(out, at, source, side):
    start = side * (source.shape[1] - RADIUS)
    out[pl.ds(at, source.shape[0])] = source[:, pl.ds(start, RADIUS)]


def pack_z(out, at, source, side):
    start = pl.multiple_of(side * (source.shape[2] - ZRIM), ZRIM)
    out[pl.ds(at, source.shape[0])] = source[:, :, pl.ds(start, ZRIM), :]


def widen(ext, center, za, zb, xa, xb, first, rims=None):
    fields, nx, nz = center.shape[0], center.shape[1], center.shape[2]
    ext[:, RADIUS:RADIUS + nx, ZRIM:ZRIM + nz] = center[...]
    for got, side in zip((xa, xb), sides("gx")):
        ext[:, pl.ds(side * (nx + RADIUS), RADIUS), ZRIM:ZRIM + nz] = got[first:first + fields]
    for got, side in zip((za, zb), sides("gz")):
        start = pl.multiple_of(side * (nz + ZRIM), ZRIM)
        ext[:, RADIUS:RADIUS + nx, pl.ds(start, ZRIM)] = got[first:first + fields]


def d1(load, x, lo, hi):
    total = None
    for m, w in enumerate(STENCIL_WEIGHTS, 1):
        term = w * (load(x + m, lo, hi) - load(x - m, lo, hi))
        total = term if total is None else total + term
    return total


def d2(load, x, lo, hi):
    total = None
    for m, w in enumerate(STENCIL_WEIGHTS, 1):
        term = w * (load(x, lo + m, hi + m) - load(x, lo - m, hi - m))
        total = term if total is None else total + term
    return total


def d3(values):
    width = values.shape[1]
    lane = lax.broadcasted_iota(jnp.int32, (1, width), 1)
    total = None
    for m, w in enumerate(STENCIL_WEIGHTS, 1):
        ahead = jnp.where(lane < width - m, w, 0.0) * pltpu.roll(values, width - m, 1)
        behind = jnp.where(lane >= m, w, 0.0) * pltpu.roll(values, m, 1)
        term = ahead - behind
        total = term if total is None else total + term
    return total


def field(ref, c):
    return lambda x, lo, hi: ref[c, x, lo:hi, :]


def plane(ref):
    return lambda x, lo, hi: ref[x, lo:hi, :]


def arrived(table, strip, band, n_gx, n_gz, reach, slots):
    lane = lax.broadcasted_iota(jnp.int32, (1, LANES), 1)
    got = jnp.zeros((1, LANES), F32)
    inside = (strip >= 0) & (strip < n_gx) & (band >= 0) & (band < n_gz)
    for r in range(reach):
        source = strip - (r - reach // 2)
        valid = inside & (source >= 0) & (source < n_gx)
        at = jnp.where(valid, source * n_gz + band, 0)
        row = table[pl.ds(at, 1), :]
        scale = jnp.where(valid, 1.0, 0.0)
        got = jnp.where(lane // slots == r, row * scale, got)
    return got


def cell_masks(cells, rows):
    cells = cells.astype(jnp.int32)
    place = lax.broadcasted_iota(jnp.int32, (rows, LANES), 0)
    third = lax.broadcasted_iota(jnp.int32, (LANES, LANES), 0)
    return cells // LANES == place, cells % LANES == third


def raw_rims_kernel(air, wind, smap, xa, xb, za, zb, row):
    fields = air.shape[0]
    for out, side in zip((xa, xb), sides("gx")):
        pack_x(out, 0, air, side)
        pack_x(out, fields, wind, side)
    for out, side in zip((za, zb), sides("gz")):
        pack_z(out, 0, air, side)
        pack_z(out, fields, wind, side)
    row[...] = flat_slots(smap[1].astype(F32))


def jacobian_step(jac, rot, emit):
    dims, quants = jac.shape[0], jac.shape[1]
    width = jac.shape[3]
    rows = rot.shape[0] // dims
    for h in range(width // LANES):
        at = h * LANES

        def body(d, acc):
            acc = list(acc)
            for q in range(quants):
                start = pl.multiple_of(d * rows, 8)
                turned = rot[pl.ds(start, rows), q * width + at:q * width + at + LANES]
                for p in range(quants):
                    acc[p] = acc[p] + jac[d, p, q:q + 1, at:at + LANES] * turned
            return tuple(acc)

        zeros = tuple(jnp.zeros((rows, LANES), F32) for _ in range(quants))
        acc = lax.fori_loop(0, dims, body, zeros)
        for p in range(quants):
            emit(p, at, acc[p])


def rotate(rot, matrix, source, quants, width):
    for q in range(quants):
        cut = slice(q * width, (q + 1) * width)
        rot[:, cut] = dot3(matrix[...], source[:, cut])


def take_slots(tiles, index):
    low = index % LANES
    high = index // LANES
    got = None
    for s, tile in enumerate(tiles):
        picked = jnp.take_along_axis(tile, low, axis=1, mode="promise_in_bounds")
        got = picked if got is None else jnp.where(high == s, picked, got)
    return got


def predict_kernel(
    state, jac, stiff, trace, sends, smap, normals,
    integral, traces, own, xa, xb, za, zb, row,
    cur, rot, sp, tp, picked,
):
    quants, basis, width = state.shape
    pad = integral.shape[0]
    faces, face_basis = trace.shape[0], trace.shape[1]
    dims = stiff.shape[0]
    sp[...] = jnp.zeros_like(sp)
    tp[...] = jnp.zeros_like(tp)
    cur[...] = jnp.zeros_like(cur)
    for d in range(dims):
        sp[d * pad:d * pad + basis, 0:basis] = stiff[d]
    for f in range(faces):
        tp[f * 16:f * 16 + face_basis, 0:basis] = trace[f]
    for q in range(quants):
        cur[0:basis, q * width:(q + 1) * width] = state[q]
    integral[...] = TIME_STEP * cur[0:pad, :]

    def degree(k, weight):
        weight = jnp.where(k == 1, TIME_STEP**2 / 2, jnp.where(k == 2, TIME_STEP**3 / 6, TIME_STEP**4 / 24))
        rotate(rot, sp, cur, quants, width)

        def emit(p, at, value):
            cut = slice(p * width + at, p * width + at + LANES)
            cur[0:pad, cut] = -value
            integral[:, cut] = integral[:, cut] - weight * value

        jacobian_step(jac, rot, emit)
        return weight

    lax.fori_loop(1, ORDERS, degree, F32(0))
    for q in range(quants):
        cut = slice(q * width, (q + 1) * width)
        done = dot3(tp[:, 0:pad], integral[:, cut])
        for f in range(faces):
            traces[q, :, f * width:(f + 1) * width] = done[f * 16:(f + 1) * 16]
    slots = flat_slots(smap[0].astype(F32)).astype(jnp.int32)
    wanted = [jnp.broadcast_to(sends[d:d + 1, :], (16, LANES)) for d in range(4)]
    wanted.append(jnp.broadcast_to(slots, (16, LANES)))
    tiles_in = faces * width // LANES

    def gather(q, carry):
        tiles = [traces[q, :, s * LANES:(s + 1) * LANES] for s in range(tiles_in)]
        for d in range(4):
            picked[d, q] = take_slots(tiles, wanted[d])
        own[q] = take_slots(tiles, wanted[4])
        return carry

    lax.fori_loop(0, quants, gather, 0)
    for axis, base, outs in (("gx", 0, (xa, xb)), ("gz", 2, (za, zb))):
        for out, side in zip(outs, sides(axis)):
            for q in range(quants):
                out[q * 8:q * 8 + 8, :] = picked[base + side, q, 0:8, :]
                out[quants * 8 + q * 2:quants * 8 + q * 2 + 2, :] = picked[base + side, q, 8:face_basis, :]
            out[quants * face_basis:, :] = jnp.zeros((out.shape[0] - quants * face_basis, LANES), F32)
    coupled = flat_slots(smap[2].astype(F32))
    speed = jnp.zeros((1, LANES), F32)
    for c in range(3):
        mean = jnp.sum(own[6 + c, 0:face_basis, :], axis=0, keepdims=True) * (1.0 / face_basis)
        speed = speed + flat_slots(normals[c]) * mean
    row[...] = coupled * speed


def pressure_rows(ext, wind, medium, x, nz):
    lo, hi = ZRIM, ZRIM + nz
    xe = x + RADIUS
    pressure = field(ext, 0)
    here = pressure(xe, lo, hi)
    divergence = d1(field(ext, 1), xe, lo, hi) + d2(field(ext, 2), xe, lo, hi) + d3(ext[3, xe, lo:hi, :])
    moved = (
        wind[0, x] * d1(pressure, xe, lo, hi)
        + wind[1, x] * d2(pressure, xe, lo, hi)
        + wind[2, x] * d3(here)
    )
    return here - medium[0, x] * divergence - moved


def pack_pressure(center, xa, xb, za, zb):
    nx, nz, ny = center.shape[1:]
    for out, side in zip((xa, xb), sides("gx")):
        start = side * (nx - RADIUS)
        out[0:RADIUS * nz, :] = center[0, pl.ds(start, RADIUS)].reshape(RADIUS * nz, ny)
    for out, side in zip((za, zb), sides("gz")):
        start = pl.multiple_of(side * (nz - ZRIM), ZRIM)
        out[0:nx * ZRIM, :] = center[0, :, pl.ds(start, ZRIM), :].reshape(nx * ZRIM, ny)


def widen_pressure(ext, center, za, zb, xa, xb):
    nx, nz, ny = center.shape
    ext[RADIUS:RADIUS + nx, ZRIM:ZRIM + nz] = center[...]
    for got, side in zip((xa, xb), sides("gx")):
        ext[pl.ds(side * (nx + RADIUS), RADIUS), ZRIM:ZRIM + nz] = got[0:RADIUS * nz, :].reshape(RADIUS, nz, ny)
    for got, side in zip((za, zb), sides("gz")):
        start = pl.multiple_of(side * (nz + ZRIM), ZRIM)
        ext[RADIUS:RADIUS + nx, pl.ds(start, ZRIM)] = got[0:nx * ZRIM, :].reshape(nx, ZRIM, ny)


def raw_pressure_kernel(
    n_gx, n_gz, air, wind, medium, za, zb, xa, xb, txa, txb, tza, tzb, cells, smap,
    pressure, oxa, oxb, oza, ozb, answers, ext, fresh,
):
    nx, nz, ny = air.shape[1:]
    widen(ext, air, za, zb, xa, xb, 0)
    for x in range(nx):
        fresh[0, x] = pressure_rows(ext, wind, medium, x, nz)
    pressure[...] = fresh[0]
    pack_pressure(fresh, oxa, oxb, oza, ozb)
    for out, sent in zip((oxa, oxb, oza, ozb), (txa, txb, tza, tzb)):
        out[out.shape[0] - sent.shape[0]:, :] = sent[...]
    reach, slots = smap.shape[1:]
    mine = arrived(cells, lax.axis_index("gx"), lax.axis_index("gz"), n_gx, n_gz, reach, slots)
    row_mask, third_mask = cell_masks(mine, nx * nz)
    looked_high, looked_low = halves(air[0].reshape(nx * nz, ny))
    columns = jnp.where(third_mask, 1.0, 0.0).astype(BF16)
    looked = jnp.dot(looked_high, columns, preferred_element_type=F32) + jnp.dot(
        looked_low, columns, preferred_element_type=F32
    )
    answers[...] = jnp.sum(jnp.where(row_mask, looked, 0.0), axis=0, keepdims=True)


def advection_kernel(air, wind, za, zb, xa, xb, moved, ext):
    nx, nz, ny = air.shape[1:]
    widen(ext, air, za, zb, xa, xb, 0)
    lo, hi = ZRIM, ZRIM + nz
    for x in range(nx):
        xe = x + RADIUS
        for c in range(3):
            load = field(ext, 1 + c)
            moved[c, x] = (
                wind[0, x] * d1(load, xe, lo, hi)
                + wind[1, x] * d2(load, xe, lo, hi)
                + wind[2, x] * d3(load(xe, lo, hi))
            )


def velocities(out, center, moved, medium, wide, nx, nz):
    lo, hi = ZRIM, ZRIM + nz
    load = plane(wide)
    for x in range(nx):
        xe = x + RADIUS
        slopes = (d1(load, xe, lo, hi), d2(load, xe, lo, hi), d3(load(xe, lo, hi)))
        out[0, x] = load(xe, lo, hi)
        for c in range(3):
            out[1 + c, x] = center[1 + c, x] - medium[1, x] * slopes[c] - moved[c, x]


def pack_air(out, xa, xb, za, zb):
    for rim, side in zip((xa, xb), sides("gx")):
        pack_x(rim, 0, out, side)
    for rim, side in zip((za, zb), sides("gz")):
        pack_z(rim, 0, out, side)


def injected_kernel(
    n_gx, n_gz, air, wind, medium, raw, moved, wza, wzb, wxa, wxb, pza, pzb, pxa, pxb, cells, speeds, smap,
    out, oxa, oxb, oza, ozb, spread, wide, wide_wind,
):
    nx, nz, ny = air.shape[1:]
    reach, slots = smap.shape[1:]
    strip, band = lax.axis_index("gx"), lax.axis_index("gz")
    for da in range(3):
        for db in range(3):
            where = (strip + da - 1, band + db - 1, n_gx, n_gz, reach, slots)
            row_mask, third_mask = cell_masks(arrived(cells, *where), nx * nz)
            speed = arrived(speeds, *where)
            high, low = halves(jnp.where(row_mask, speed, 0.0))
            columns = jnp.where(third_mask, 1.0, 0.0).astype(BF16)
            mul = functools.partial(
                lax.dot_general, dimension_numbers=(((1,), (1,)), ((), ())), preferred_element_type=F32
            )
            block = mul(high, columns) + mul(low, columns)
            spread[da * nx:(da + 1) * nx, db * nz:(db + 1) * nz] = block.reshape(nx, nz, ny)
    widen(wide_wind, wind, wza, wzb, wxa, wxb, air.shape[0])
    widen_pressure(wide, raw, pza, pzb, pxa, pxb)
    load = plane(spread)
    for x in range(nx + 2 * RADIUS):
        xs = x + nx - RADIUS
        if RADIUS <= x < RADIUS + nx:
            lo, hi = 0, nz + 2 * ZRIM
        else:
            lo, hi = ZRIM, ZRIM + nz
        slo, shi = lo + nz - ZRIM, hi + nz - ZRIM
        here = load(xs, slo, shi)
        turned = (
            wide_wind[0, x, lo:hi, :] * d1(load, xs, slo, shi)
            + wide_wind[1, x, lo:hi, :] * d2(load, xs, slo, shi)
            + wide_wind[2, x, lo:hi, :] * d3(here)
        )
        wide[x, lo:hi, :] = wide[x, lo:hi, :] + (here - turned)
    velocities(out, air, moved, medium, wide, nx, nz)
    pack_air(out, oxa, oxb, oza, ozb)


def pressure_kernel(air, wind, medium, za, zb, xa, xb, pressure, oxa, oxb, oza, ozb, ext, fresh):
    nx, nz, ny = air.shape[1:]
    widen(ext, air, za, zb, xa, xb, 0)
    for x in range(nx):
        fresh[0, x] = pressure_rows(ext, wind, medium, x, nz)
    pressure[...] = fresh[0]
    pack_pressure(fresh, oxa, oxb, oza, ozb)


def velocity_kernel(air, pressure, medium, moved, za, zb, xa, xb, out, *rest):
    nx, nz, ny = air.shape[1:]
    wide = rest[-1]
    widen_pressure(wide, pressure, za, zb, xa, xb)
    velocities(out, air, moved, medium, wide, nx, nz)
    if len(rest) > 1:
        pack_air(out, *rest[:-1])


def volume_kernel(state, integral, jac, stiff, out, rot, sp):
    quants, basis, width = state.shape
    pad = integral.shape[0]
    dims = stiff.shape[0]
    sp[...] = jnp.zeros_like(sp)
    place = lax.broadcasted_iota(jnp.int32, (basis, basis), 0)
    other = lax.broadcasted_iota(jnp.int32, (basis, basis), 1)
    unit = jnp.where(place == other, 1.0, 0.0).astype(F32)
    for d in range(dims):
        sp[d * pad:d * pad + basis, 0:basis] = dot_exact(unit, stiff[d], (((1,), (1,)), ((), ())))
    for q in range(quants):
        cut = slice(q * width, (q + 1) * width)
        rot[:, cut] = dot3(sp[:, 0:pad], integral[:, cut])

    def emit(p, at, value):
        out[p, :, at:at + LANES] = state[p, :, at:at + LANES] + value[0:basis]

    jacobian_step(jac, rot, emit)


def flux_kernel(
    n_gx, n_gz, base, traces, own, solvers, lift, neighbours, smap, za, zb, xa, xb, answers,
    out, tiles, flux, lp,
):
    quants, basis, width = base.shape
    faces, face_basis = lift.shape[0], lift.shape[2]
    reach, slots = smap.shape[1:]
    strip, band = lax.axis_index("gx"), lax.axis_index("gz")
    lane = lax.broadcasted_iota(jnp.int32, (1, LANES), 1)
    replies = jnp.zeros((1, LANES), F32)
    for r in range(reach):
        target = strip + r - reach // 2
        valid = (target >= 0) & (target < n_gx)
        row = answers[pl.ds(jnp.where(valid, target * n_gz + band, 0), 1), :]
        replies = jnp.where(lane // slots == r, row * jnp.where(valid, 1.0, 0.0), replies)
    replies = replies * flat_slots(smap[2].astype(F32))
    skip = xa.shape[0] - 96
    for axis, base_tile, gots in (("gx", 0, (xa, xb)), ("gz", 2, (za, zb))):
        for got, side in zip(gots, sides(axis)):
            for q in range(quants):
                tiles[q, base_tile + side, 0:8, :] = got[skip + q * 8:skip + q * 8 + 8, :]
                at = skip + quants * 8 + q * 2
                tiles[q, base_tile + side, 8:face_basis, :] = got[at:at + 2, :]
                tiles[q, base_tile + side, face_basis:, :] = jnp.zeros((16 - face_basis, LANES), F32)
    for q in range(quants):
        tiles[q, 4] = -2.0 * replies - own[q] if q < 3 else own[q]
    lp[...] = jnp.zeros_like(lp)
    for f in range(faces):
        lp[f, 0:basis, 0:face_basis] = lift[f]
    local = faces * width // LANES
    halves_in = width // LANES

    def one(t, carry):
        f = t // halves_in
        at = pl.multiple_of((t % halves_in) * LANES, LANES)
        index = neighbours[:, pl.ds(at, LANES)]
        face = lax.broadcasted_iota(jnp.int32, index.shape, 0)
        index = jnp.sum(jnp.where(face == f, index, 0), axis=0, keepdims=True)
        index = jnp.broadcast_to(index, (16, LANES))
        acc = [jnp.zeros((16, LANES), F32) for _ in range(quants)]
        for q in range(quants):
            pool = [traces[q, :, s * LANES:(s + 1) * LANES] for s in range(local)]
            pool += [tiles[q, s] for s in range(5)]
            mine = traces[q, :, pl.ds(pl.multiple_of(t * LANES, LANES), LANES)]
            jump = take_slots(pool, index) - mine
            for p in range(quants):
                acc[p] = acc[p] + solvers[f, p, q:q + 1, pl.ds(at, LANES)] * jump
        for p in range(quants):
            flux[f, :, pl.ds(pl.multiple_of(p * width + at, LANES), LANES)] = acc[p]
        return carry

    lax.fori_loop(0, local, one, 0)
    for p in range(quants):
        cut = slice(p * width, (p + 1) * width)
        total = base[p]
        for f in range(faces):
            total = total + dot3(lp[f, :, 0:16], flux[f, :, cut])[0:basis]
        out[p] = total


def shards(
    solid_state, jacobians, flux_solvers, stiffness, trace_matrix, lift_matrix,
    neighbours, send_faces, surface_map, surface_normals, air_state, wind_field, air_medium,
):
    quants, basis, width = solid_state.shape
    faces, face_basis = trace_matrix.shape[0], trace_matrix.shape[1]
    dims = stiffness.shape[0]
    nx, nz, ny = air_state.shape[1:]
    n_gx, n_gz = lax.axis_size("gx"), lax.axis_size("gz")
    everyone = ("gx", "gz")
    pad = -(-basis // 8) * 8
    pad_k = -(-basis // 16) * 16
    rim_x = (7, RADIUS, nz, ny)
    rim_z = (7, nx, ZRIM, ny)
    sent_rows = -(-quants * face_basis // 8) * 8
    ext = (4, nx + 2 * RADIUS, nz + 2 * ZRIM, ny)
    wide = ext[1:]

    xa, xb, za, zb, row = call(
        raw_rims_kernel, "raw_rims", [rim_x, rim_x, rim_z, rim_z, (1, LANES)],
        [air_state, wind_field, surface_map],
    )
    cells = lax.all_gather(row, everyone, axis=0, tiled=True)
    rims = exchange(xa, xb, za, zb)

    sent = (sent_rows, LANES)
    integral, traces, own, txa, txb, tza, tzb, speed = call(
        predict_kernel, "predict",
        [(pad, quants * width), (quants, 16, faces * width), (quants, 16, LANES), sent, sent, sent, sent, (1, LANES)],
        [solid_state, jacobians, stiffness, trace_matrix, send_faces, surface_map, surface_normals],
        [(pad_k, quants * width), (dims * pad, quants * width), (dims * pad, pad_k), (faces * 16, pad_k),
         (4, quants, 16, LANES)],
        flops=40_000_000,
    )
    speeds = lax.all_gather(speed, everyone, axis=0, tiled=True)

    both_x = (RADIUS * nz + sent_rows, LANES)
    both_z = (nx * ZRIM + sent_rows, LANES)
    raw, xa, xb, za, zb, answer = call(
        functools.partial(raw_pressure_kernel, n_gx, n_gz), "raw_pressure",
        [(nx, nz, ny), both_x, both_x, both_z, both_z, (1, LANES)],
        [air_state, wind_field, air_medium, *rims, txa, txb, tza, tzb, cells, surface_map],
        [ext, (1, nx, nz, ny)],
    )
    both = exchange(xa, xb, za, zb)
    answers = lax.all_gather(answer, everyone, axis=0, tiled=True)
    (moved,) = call(
        advection_kernel, "advection", [(3, nx, nz, ny)], [air_state, wind_field, *rims], [ext],
        flops=10_000_000,
    )
    (volume,) = call(
        volume_kernel, "volume", [solid_state.shape], [solid_state, integral, jacobians, stiffness],
        [(dims * pad, quants * width), (dims * pad, pad_k)], flops=10_000_000,
    )

    rim_x = (4, RADIUS, nz, ny)
    rim_z = (4, nx, ZRIM, ny)
    air, xa, xb, za, zb = call(
        functools.partial(injected_kernel, n_gx, n_gz), "injected",
        [air_state.shape, rim_x, rim_x, rim_z, rim_z],
        [air_state, wind_field, air_medium, raw, moved, *rims, *both, cells, speeds, surface_map],
        [(3 * nx, 3 * nz, ny), wide, (3,) + wide],
    )
    for substep in range(1, SUBSTEPS):
        rims = exchange(xa, xb, za, zb)
        if substep == 1:
            (solid_next,) = call(
                functools.partial(flux_kernel, n_gx, n_gz), "flux", [solid_state.shape],
                [volume, traces, own, flux_solvers, lift_matrix, neighbours, surface_map, *both, answers],
                [(quants, 5, 16, LANES), (faces, 16, quants * width), (faces, pad, 16)], flops=20_000_000,
            )
        pressure, xa, xb, za, zb = call(
            pressure_kernel, "pressure",
            [(nx, nz, ny), (RADIUS * nz, ny), (RADIUS * nz, ny), (nx * ZRIM, ny), (nx * ZRIM, ny)],
            [air, wind_field, air_medium, *rims], [ext, (1, nx, nz, ny)],
        )
        rises = exchange(xa, xb, za, zb)
        (moved,) = call(
            advection_kernel, "advection", [(3, nx, nz, ny)], [air, wind_field, *rims], [ext], flops=10_000_000
        )
        last = substep == SUBSTEPS - 1
        outs = [air_state.shape] + ([] if last else [rim_x, rim_x, rim_z, rim_z])
        done = call(
            velocity_kernel, "velocity", outs, [air, pressure, air_medium, moved, *rises], [wide]
        )
        air = done[0]
        if not last:
            xa, xb, za, zb = done[1:]
    return (solid_next, air)


def solution(mesh):
    in_specs = (
        P(None, None, ("gx", "gz")),
        P(None, None, None, ("gx", "gz")),
        P(None, None, None, ("gx", "gz")),
        P(),
        P(),
        P(),
        P(None, ("gx", "gz")),
        P(None, ("gx", "gz")),
        P(None, None, ("gx", "gz")),
        P(None, None, ("gx", "gz")),
        P(None, "gx", "gz", None),
        P(None, "gx", "gz", None),
        P(None, "gx", "gz", None),
    )
    out_specs = (P(None, None, ("gx", "gz")), P(None, "gx", "gz", None))
    return jax.shard_map(shards, mesh=mesh, in_specs=in_specs, out_specs=out_specs, check_vma=False)
```

```python
import functools

import jax
import jax.numpy as jnp
from jax import lax
from jax.experimental import pallas as pl
from jax.experimental.pallas import tpu as pltpu
from jax.sharding import PartitionSpec as P

ORDERS = 4
RADIUS = 4
SUBSTEPS = 3
ZRIM = 8
LANES = 128
TIME_STEP = 0.5
STENCIL_WEIGHTS = (0.8, -0.2, 4.0 / 105.0, -1.0 / 280.0)
F32 = jnp.float32
BF16 = jnp.bfloat16


def call(kernel, name, outs, ins, scratch=(), flops=1_000_000):
    nbytes = 4 * sum(x.size for x in ins) + 4 * sum(functools.reduce(lambda m, n: m * n, s, 1) for s in outs)
    return pl.pallas_call(
        kernel,
        out_shape=[jax.ShapeDtypeStruct(s, F32) for s in outs],
        in_specs=[pl.BlockSpec(memory_space=pltpu.VMEM) for _ in ins],
        out_specs=[pl.BlockSpec(memory_space=pltpu.VMEM) for _ in outs],
        scratch_shapes=[pltpu.VMEM(s, F32) for s in scratch],
        compiler_params=pltpu.CompilerParams(vmem_limit_bytes=24 * 1024 * 1024),
        cost_estimate=pl.CostEstimate(flops=flops, bytes_accessed=nbytes, transcendentals=0),
        name=name,
    )(*ins)


def swap(values, axis, odd):
    count = lax.axis_size(axis)
    pairs = []
    for i in range(odd, count - 1, 2):
        pairs += [(i, i + 1), (i + 1, i)]
    return lax.ppermute(values, axis, pairs)


def swap_pairs(values, odd):
    count = lax.axis_size("gx")
    pairs = []
    for i in range(count - 2):
        if i // 2 % 2 == odd:
            pairs += [(i, i + 2), (i + 2, i)]
    return lax.ppermute(values, "gx", pairs)


def exchange(xa, xb, za, zb):
    xb = swap(xb, "gx", 1)
    xa = swap(xa, "gx", 0)
    zb = swap(zb, "gz", 1)
    za = swap(za, "gz", 0)
    return za, zb, xa, xb


def sides(axis):
    parity = lax.axis_index(axis) & 1
    return 1 - parity, parity


def halves(values):
    high = values.astype(BF16)
    return high, (values - high.astype(F32)).astype(BF16)


def dot3(left, right, dims=(((1,), (0,)), ((), ()))):
    lh, ll = halves(left)
    rh, rl = halves(right)
    mul = functools.partial(lax.dot_general, dimension_numbers=dims, preferred_element_type=F32)
    return mul(lh, rh) + (mul(lh, rl) + mul(ll, rh))


def dot_exact(left, right, dims=(((1,), (0,)), ((), ()))):
    return lax.dot_general(
        left, right, dims, precision=lax.Precision.HIGHEST, preferred_element_type=F32
    )


def flat_slots(values):
    rows, slots = values.shape
    lane = lax.broadcasted_iota(jnp.int32, (slots, LANES), 1)
    place = lax.broadcasted_iota(jnp.int32, (slots, LANES), 0)
    spread = dot_exact(values, jnp.where(lane % slots == place, 1.0, 0.0).astype(F32))
    lane = lax.broadcasted_iota(jnp.int32, (rows, LANES), 1)
    place = lax.broadcasted_iota(jnp.int32, (rows, LANES), 0)
    return jnp.sum(jnp.where(lane // slots == place, spread, 0.0), axis=0, keepdims=True)


def pack_x(out, at, source, side):
    start = side * (source.shape[1] - RADIUS)
    out[pl.ds(at, source.shape[0])] = source[:, pl.ds(start, RADIUS)]


def pack_z(out, at, source, side):
    start = pl.multiple_of(side * (source.shape[2] - ZRIM), ZRIM)
    out[pl.ds(at, source.shape[0])] = source[:, :, pl.ds(start, ZRIM), :]


def widen(ext, center, za, zb, xa, xb, first=0, block=0):
    fields, nx, nz = center.shape[0], center.shape[1], center.shape[2]
    ext[:, RADIUS:RADIUS + nx, ZRIM:ZRIM + nz] = center[...]
    for got, side in zip((xa, xb), sides("gx")):
        place = pl.ds(side * (nx + RADIUS), RADIUS)
        if block:
            ext[0, place, ZRIM:ZRIM + nz] = got[(block - 1) * (1 - side)]
            ext[1:, place, ZRIM:ZRIM + nz] = got[block:block + fields - 1]
        else:
            skip = xa.shape[0] - za.shape[0] if first else 0
            ext[:, place, ZRIM:ZRIM + nz] = got[first + skip:first + skip + fields]
    for got, side in zip((za, zb), sides("gz")):
        start = pl.multiple_of(side * (nz + ZRIM), ZRIM)
        ext[:, RADIUS:RADIUS + nx, pl.ds(start, ZRIM)] = got[first:first + fields]


def d1(load, x, lo, hi):
    total = None
    for m, w in enumerate(STENCIL_WEIGHTS, 1):
        term = w * (load(x + m, lo, hi) - load(x - m, lo, hi))
        total = term if total is None else total + term
    return total


def d2(load, x, lo, hi):
    total = None
    for m, w in enumerate(STENCIL_WEIGHTS, 1):
        term = w * (load(x, lo + m, hi + m) - load(x, lo - m, hi - m))
        total = term if total is None else total + term
    return total


def d3(values):
    width = values.shape[1]
    lane = lax.broadcasted_iota(jnp.int32, (1, width), 1)
    total = None
    for m, w in enumerate(STENCIL_WEIGHTS, 1):
        ahead = jnp.where(lane < width - m, w, 0.0) * pltpu.roll(values, width - m, 1)
        behind = jnp.where(lane >= m, w, 0.0) * pltpu.roll(values, m, 1)
        term = ahead - behind
        total = term if total is None else total + term
    return total


def field(ref, c):
    return lambda x, lo, hi: ref[c, x, lo:hi, :]


def plane(ref):
    return lambda x, lo, hi: ref[x, lo:hi, :]


def arrived(table, strip, band, n_gx, n_gz, reach, slots):
    lane = lax.broadcasted_iota(jnp.int32, (1, LANES), 1)
    got = jnp.zeros((1, LANES), F32)
    inside = (strip >= 0) & (strip < n_gx) & (band >= 0) & (band < n_gz)
    for r in range(reach):
        source = strip - (r - reach // 2)
        valid = inside & (source >= 0) & (source < n_gx)
        at = jnp.where(valid, source * n_gz + band, 0)
        row = table[pl.ds(at, 1), :]
        scale = jnp.where(valid, 1.0, 0.0)
        got = jnp.where((lane & (LANES // 2 - 1)) // slots == r, row * scale, got)
    return got, pltpu.roll(got, LANES // 2, 1)


def cell_masks(cells, rows):
    cells = cells.astype(jnp.int32)
    place = lax.broadcasted_iota(jnp.int32, (rows, LANES), 0)
    third = lax.broadcasted_iota(jnp.int32, (LANES, LANES), 0)
    return cells // LANES == place, cells % LANES == third


def raw_rims_kernel(air, wind, xa, xb, za, zb, block):
    fields, nx = air.shape[:2]
    parts = nx // RADIUS
    block[...] = air[0]
    for out, side in zip((xa, xb), sides("gx")):
        start = side * (nx - RADIUS)
        for part in range(parts):
            out[part] = air[0, part * RADIUS:(part + 1) * RADIUS]
        out[parts:parts + fields - 1] = air[1:, pl.ds(start, RADIUS)]
        pack_x(out, parts + fields - 1, wind, side)
    for out, side in zip((za, zb), sides("gz")):
        pack_z(out, 0, air, side)
        pack_z(out, fields, wind, side)


def jacobian_step(jac, rot, emit):
    dims, quants = jac.shape[0], jac.shape[1]
    width = jac.shape[3]
    rows = rot.shape[0] // dims
    for h in range(width // LANES):
        at = h * LANES

        def body(d, acc):
            acc = list(acc)
            for q in range(quants):
                start = pl.multiple_of(d * rows, 8)
                turned = rot[pl.ds(start, rows), q * width + at:q * width + at + LANES]
                for p in range(quants):
                    acc[p] = acc[p] + jac[d, p, q:q + 1, at:at + LANES] * turned
            return tuple(acc)

        zeros = tuple(jnp.zeros((rows, LANES), F32) for _ in range(quants))
        acc = lax.fori_loop(0, dims, body, zeros)
        for p in range(quants):
            emit(p, at, acc[p])


def rotate(rot, matrix, source, quants, width):
    for q in range(quants):
        cut = slice(q * width, (q + 1) * width)
        rot[:, cut] = dot3(matrix[...], source[:, cut])


def take_slots(tiles, index):
    low = index % LANES
    high = index // LANES
    got = None
    for s, tile in enumerate(tiles):
        picked = jnp.take_along_axis(tile, low, axis=1, mode="promise_in_bounds")
        got = picked if got is None else jnp.where(high == s, picked, got)
    return got


def predict_kernel(
    state, jac, stiff, trace, sends, smap, normals,
    integral, traces, own, xa, xb, za, zb, rows,
    cur, rot, sp, tp, picked,
):
    quants, basis, width = state.shape
    pad = integral.shape[0]
    faces, face_basis = trace.shape[0], trace.shape[1]
    dims = stiff.shape[0]
    sp[...] = jnp.zeros_like(sp)
    tp[...] = jnp.zeros_like(tp)
    cur[...] = jnp.zeros_like(cur)
    for d in range(dims):
        sp[d * pad:d * pad + basis, 0:basis] = stiff[d]
    for f in range(faces):
        tp[f * 16:f * 16 + face_basis, 0:basis] = trace[f]
    for q in range(quants):
        cur[0:basis, q * width:(q + 1) * width] = state[q]
    integral[...] = TIME_STEP * cur[0:pad, :]

    def degree(k, weight):
        weight = jnp.where(k == 1, TIME_STEP**2 / 2, jnp.where(k == 2, TIME_STEP**3 / 6, TIME_STEP**4 / 24))
        rotate(rot, sp, cur, quants, width)

        def emit(p, at, value):
            cut = slice(p * width + at, p * width + at + LANES)
            cur[0:pad, cut] = -value
            integral[:, cut] = integral[:, cut] - weight * value

        jacobian_step(jac, rot, emit)
        return weight

    lax.fori_loop(1, ORDERS, degree, F32(0))
    for q in range(quants):
        cut = slice(q * width, (q + 1) * width)
        done = dot3(tp[:, 0:pad], integral[:, cut])
        for f in range(faces):
            traces[q, :, f * width:(f + 1) * width] = done[f * 16:(f + 1) * 16]
    slots = flat_slots(smap[0].astype(F32)).astype(jnp.int32)
    wanted = [jnp.broadcast_to(sends[d:d + 1, :], (16, LANES)) for d in range(4)]
    wanted.append(jnp.broadcast_to(slots, (16, LANES)))
    tiles_in = faces * width // LANES

    def gather(q, carry):
        tiles = [traces[q, :, s * LANES:(s + 1) * LANES] for s in range(tiles_in)]
        for d in range(4):
            picked[d, q] = take_slots(tiles, wanted[d])
        own[q] = take_slots(tiles, wanted[4])
        return carry

    lax.fori_loop(0, quants, gather, 0)
    for axis, base, outs in (("gx", 0, (xa, xb)), ("gz", 2, (za, zb))):
        for out, side in zip(outs, sides(axis)):
            for q in range(quants):
                out[q * 8:q * 8 + 8, :] = picked[base + side, q, 0:8, :]
                out[quants * 8 + q * 2:quants * 8 + q * 2 + 2, :] = picked[base + side, q, 8:face_basis, :]
            out[quants * face_basis:, :] = jnp.zeros((out.shape[0] - quants * face_basis, LANES), F32)
    coupled = flat_slots(smap[2].astype(F32))
    speed = jnp.zeros((1, LANES), F32)
    for c in range(3):
        mean = jnp.sum(own[6 + c, 0:face_basis, :], axis=0, keepdims=True) * (1.0 / face_basis)
        speed = speed + flat_slots(normals[c]) * mean
    lane = lax.broadcasted_iota(jnp.int32, (1, LANES), 1)
    cells = pltpu.roll(flat_slots(smap[1].astype(F32)), LANES // 2, 1)
    row = jnp.where(lane < LANES // 2, coupled * speed, cells)
    rows[...] = jnp.broadcast_to(row, rows.shape)


def pressure_rows(ext, wind, medium, x, nz):
    lo, hi = ZRIM, ZRIM + nz
    xe = x + RADIUS
    pressure = field(ext, 0)
    here = pressure(xe, lo, hi)
    divergence = d1(field(ext, 1), xe, lo, hi) + d2(field(ext, 2), xe, lo, hi) + d3(ext[3, xe, lo:hi, :])
    moved = (
        wind[0, x] * d1(pressure, xe, lo, hi)
        + wind[1, x] * d2(pressure, xe, lo, hi)
        + wind[2, x] * d3(here)
    )
    return here - medium[0, x] * divergence - moved


def pack_pressure(center, xa, xb, za, zb):
    nx, nz, ny = center.shape[1:]
    for out, side in zip((xa, xb), sides("gx")):
        start = side * (nx - RADIUS)
        out[0:RADIUS * nz, :] = center[0, pl.ds(start, RADIUS)].reshape(RADIUS * nz, ny)
    for out, side in zip((za, zb), sides("gz")):
        start = pl.multiple_of(side * (nz - ZRIM), ZRIM)
        out[0:nx * ZRIM, :] = center[0, :, pl.ds(start, ZRIM), :].reshape(nx * ZRIM, ny)


def widen_pressure(ext, center, za, zb, xa, xb):
    nx, nz, ny = center.shape
    ext[RADIUS:RADIUS + nx, ZRIM:ZRIM + nz] = center[...]
    for got, side in zip((xa, xb), sides("gx")):
        ext[pl.ds(side * (nx + RADIUS), RADIUS), ZRIM:ZRIM + nz] = got[0:RADIUS * nz, :].reshape(RADIUS, nz, ny)
    for got, side in zip((za, zb), sides("gz")):
        start = pl.multiple_of(side * (nz + ZRIM), ZRIM)
        ext[RADIUS:RADIUS + nx, pl.ds(start, ZRIM)] = got[0:nx * ZRIM, :].reshape(nx, ZRIM, ny)


def raw_pressure_kernel(
    air, wind, medium, za, zb, xa, xb, txa, txb, tza, tzb,
    pressure, oxa, oxb, oza, ozb, ext, fresh,
):
    nx, nz, ny = air.shape[1:]
    widen(ext, air, za, zb, xa, xb, block=nx // RADIUS)
    for x in range(nx):
        fresh[0, x] = pressure_rows(ext, wind, medium, x, nz)
    pressure[...] = fresh[0]
    pack_pressure(fresh, oxa, oxb, oza, ozb)
    for out, sent in zip((oxa, oxb, oza, ozb), (txa, txb, tza, tzb)):
        out[out.shape[0] - sent.shape[0]:, :] = sent[...]


def advection_kernel(block, air, wind, za, zb, xa, xb, moved, ext):
    nx, nz, ny = air.shape[1:]
    widen(ext, air, za, zb, xa, xb, block=block)
    lo, hi = ZRIM, ZRIM + nz
    for x in range(nx):
        xe = x + RADIUS
        for c in range(3):
            load = field(ext, 1 + c)
            moved[c, x] = (
                wind[0, x] * d1(load, xe, lo, hi)
                + wind[1, x] * d2(load, xe, lo, hi)
                + wind[2, x] * d3(load(xe, lo, hi))
            )


def velocities(out, center, moved, medium, wide, nx, nz):
    lo, hi = ZRIM, ZRIM + nz
    load = plane(wide)
    for x in range(nx):
        xe = x + RADIUS
        slopes = (d1(load, xe, lo, hi), d2(load, xe, lo, hi), d3(load(xe, lo, hi)))
        out[0, x] = load(xe, lo, hi)
        for c in range(3):
            out[1 + c, x] = center[1 + c, x] - medium[1, x] * slopes[c] - moved[c, x]


def pack_air(out, xa, xb, za, zb):
    for rim, side in zip((xa, xb), sides("gx")):
        pack_x(rim, 0, out, side)
    for rim, side in zip((za, zb), sides("gz")):
        pack_z(rim, 0, out, side)


def injected_kernel(
    n_gx, n_gz, air, wind, medium, raw, moved, wza, wzb, wxa, wxb, pza, pzb, pxa, pxb, lists, smap,
    out, oxa, oxb, oza, ozb, spread, wide, wide_wind,
):
    nx, nz, ny = air.shape[1:]
    reach, slots = smap.shape[1:]
    strip, band = lax.axis_index("gx"), lax.axis_index("gz")
    used = lax.broadcasted_iota(jnp.int32, (nx * nz, LANES), 1) < reach * slots
    for da in range(3):
        for db in range(3):
            where = (strip + da - 1, band + db - 1, n_gx, n_gz, reach, slots)
            speed, cells = arrived(lists, *where)
            row_mask, third_mask = cell_masks(cells, nx * nz)
            high, low = halves(jnp.where(row_mask & used, speed, 0.0))
            columns = jnp.where(third_mask, 1.0, 0.0).astype(BF16)
            mul = functools.partial(
                lax.dot_general, dimension_numbers=(((1,), (1,)), ((), ())), preferred_element_type=F32
            )
            block = mul(high, columns) + mul(low, columns)
            spread[da * nx:(da + 1) * nx, db * nz:(db + 1) * nz] = block.reshape(nx, nz, ny)
    widen(wide_wind, wind, wza, wzb, wxa, wxb, first=air.shape[0])
    widen_pressure(wide, raw, pza, pzb, pxa, pxb)
    load = plane(spread)
    for x in range(nx + 2 * RADIUS):
        xs = x + nx - RADIUS
        if RADIUS <= x < RADIUS + nx:
            lo, hi = 0, nz + 2 * ZRIM
        else:
            lo, hi = ZRIM, ZRIM + nz
        slo, shi = lo + nz - ZRIM, hi + nz - ZRIM
        here = load(xs, slo, shi)
        turned = (
            wide_wind[0, x, lo:hi, :] * d1(load, xs, slo, shi)
            + wide_wind[1, x, lo:hi, :] * d2(load, xs, slo, shi)
            + wide_wind[2, x, lo:hi, :] * d3(here)
        )
        wide[x, lo:hi, :] = wide[x, lo:hi, :] + (here - turned)
    velocities(out, air, moved, medium, wide, nx, nz)
    pack_air(out, oxa, oxb, oza, ozb)


def pressure_kernel(air, wind, medium, za, zb, xa, xb, pressure, oxa, oxb, oza, ozb, ext, fresh):
    nx, nz, ny = air.shape[1:]
    widen(ext, air, za, zb, xa, xb)
    for x in range(nx):
        fresh[0, x] = pressure_rows(ext, wind, medium, x, nz)
    pressure[...] = fresh[0]
    pack_pressure(fresh, oxa, oxb, oza, ozb)


def velocity_kernel(air, pressure, medium, moved, za, zb, xa, xb, out, *rest):
    nx, nz, ny = air.shape[1:]
    wide = rest[-1]
    widen_pressure(wide, pressure, za, zb, xa, xb)
    velocities(out, air, moved, medium, wide, nx, nz)
    if len(rest) > 1:
        pack_air(out, *rest[:-1])


def volume_kernel(state, integral, jac, stiff, out, rot, sp):
    quants, basis, width = state.shape
    pad = integral.shape[0]
    dims = stiff.shape[0]
    sp[...] = jnp.zeros_like(sp)
    place = lax.broadcasted_iota(jnp.int32, (basis, basis), 0)
    other = lax.broadcasted_iota(jnp.int32, (basis, basis), 1)
    unit = jnp.where(place == other, 1.0, 0.0).astype(F32)
    for d in range(dims):
        sp[d * pad:d * pad + basis, 0:basis] = dot_exact(unit, stiff[d], (((1,), (1,)), ((), ())))
    for q in range(quants):
        cut = slice(q * width, (q + 1) * width)
        rot[:, cut] = dot3(sp[:, 0:pad], integral[:, cut])

    def emit(p, at, value):
        out[p, :, at:at + LANES] = state[p, :, at:at + LANES] + value[0:basis]

    jacobian_step(jac, rot, emit)


def flux_kernel(
    n_gx, base, traces, own, solvers, lift, neighbours, smap, za, zb, xa, xb, air, nxa, nxb, fxa, fxb,
    out, tiles, flux, lp,
):
    quants, basis, width = base.shape
    faces, face_basis = lift.shape[0], lift.shape[2]
    reach, slots = smap.shape[1:]
    strip = lax.axis_index("gx")
    nx, nz, ny = air.shape[1:]
    rows = nx * nz
    lane = lax.broadcasted_iota(jnp.int32, (1, LANES), 1)
    cells = flat_slots(smap[1].astype(F32))
    row_mask, third_mask = cell_masks(cells, rows)
    columns = jnp.where(third_mask, 1.0, 0.0).astype(BF16)
    near, far = sides("gx")[0], 1 - (strip // 2) % 2
    near_blocks = [got[0:nx // RADIUS].reshape(rows, ny) for got in (nxa, nxb)]
    far_blocks = [got[...].reshape(rows, ny) for got in (fxa, fxb)]
    blocks = [
        jnp.where(far == 0, far_blocks[0], far_blocks[1]),
        jnp.where(near == 0, near_blocks[0], near_blocks[1]),
        air[0].reshape(rows, ny),
        jnp.where(near == 1, near_blocks[0], near_blocks[1]),
        jnp.where(far == 1, far_blocks[0], far_blocks[1]),
    ]
    replies = jnp.zeros((1, LANES), F32)
    for r in range(reach):
        high, low = halves(blocks[r])
        looked = jnp.dot(high, columns, preferred_element_type=F32)
        looked = looked + jnp.dot(low, columns, preferred_element_type=F32)
        found = jnp.sum(jnp.where(row_mask, looked, 0.0), axis=0, keepdims=True)
        replies = jnp.where(lane // slots == r, found, replies)
    replies = replies * flat_slots(smap[2].astype(F32))
    skip = xa.shape[0] - 96
    for axis, base_tile, gots in (("gx", 0, (xa, xb)), ("gz", 2, (za, zb))):
        for got, side in zip(gots, sides(axis)):
            for q in range(quants):
                tiles[q, base_tile + side, 0:8, :] = got[skip + q * 8:skip + q * 8 + 8, :]
                at = skip + quants * 8 + q * 2
                tiles[q, base_tile + side, 8:face_basis, :] = got[at:at + 2, :]
                tiles[q, base_tile + side, face_basis:, :] = jnp.zeros((16 - face_basis, LANES), F32)
    for q in range(quants):
        tiles[q, 4] = -2.0 * replies - own[q] if q < 3 else own[q]
    lp[...] = jnp.zeros_like(lp)
    for f in range(faces):
        lp[f, 0:basis, 0:face_basis] = lift[f]
    local = faces * width // LANES
    halves_in = width // LANES

    def one(t, carry):
        f = t // halves_in
        at = pl.multiple_of((t % halves_in) * LANES, LANES)
        index = neighbours[:, pl.ds(at, LANES)]
        face = lax.broadcasted_iota(jnp.int32, index.shape, 0)
        index = jnp.sum(jnp.where(face == f, index, 0), axis=0, keepdims=True)
        index = jnp.broadcast_to(index, (16, LANES))
        acc = [jnp.zeros((16, LANES), F32) for _ in range(quants)]
        for q in range(quants):
            pool = [traces[q, :, s * LANES:(s + 1) * LANES] for s in range(local)]
            pool += [tiles[q, s] for s in range(5)]
            mine = traces[q, :, pl.ds(pl.multiple_of(t * LANES, LANES), LANES)]
            jump = take_slots(pool, index) - mine
            for p in range(quants):
                acc[p] = acc[p] + solvers[f, p, q:q + 1, pl.ds(at, LANES)] * jump
        for p in range(quants):
            flux[f, :, pl.ds(pl.multiple_of(p * width + at, LANES), LANES)] = acc[p]
        return carry

    lax.fori_loop(0, local, one, 0)
    for p in range(quants):
        cut = slice(p * width, (p + 1) * width)
        total = base[p]
        for f in range(faces):
            total = total + dot3(lp[f, :, 0:16], flux[f, :, cut])[0:basis]
        out[p] = total


def shards(
    solid_state, jacobians, flux_solvers, stiffness, trace_matrix, lift_matrix,
    neighbours, send_faces, surface_map, surface_normals, air_state, wind_field, air_medium,
):
    quants, basis, width = solid_state.shape
    faces, face_basis = trace_matrix.shape[0], trace_matrix.shape[1]
    dims = stiffness.shape[0]
    nx, nz, ny = air_state.shape[1:]
    n_gx, n_gz = lax.axis_size("gx"), lax.axis_size("gz")
    devices = n_gx * n_gz
    pad = -(-basis // 8) * 8
    pad_k = -(-basis // 16) * 16
    parts = nx // RADIUS
    rim_x = (parts + 6, RADIUS, nz, ny)
    rim_z = (7, nx, ZRIM, ny)
    sent_rows = -(-quants * face_basis // 8) * 8
    ext = (4, nx + 2 * RADIUS, nz + 2 * ZRIM, ny)
    wide = ext[1:]

    xa, xb, za, zb, block = call(
        raw_rims_kernel, "raw_rims", [rim_x, rim_x, rim_z, rim_z, (nx, nz, ny)], [air_state, wind_field]
    )
    rims = exchange(xa, xb, za, zb)
    far = (swap_pairs(block, 0), swap_pairs(block, 1))

    sent = (sent_rows, LANES)
    integral, traces, own, txa, txb, tza, tzb, lists = call(
        predict_kernel, "predict",
        [(pad, quants * width), (quants, 16, faces * width), (quants, 16, LANES), sent, sent, sent, sent,
         (devices, LANES)],
        [solid_state, jacobians, stiffness, trace_matrix, send_faces, surface_map, surface_normals],
        [(pad_k, quants * width), (dims * pad, quants * width), (dims * pad, pad_k), (faces * 16, pad_k),
         (4, quants, 16, LANES)],
        flops=40_000_000,
    )
    both_x = (RADIUS * nz + sent_rows, LANES)
    both_z = (nx * ZRIM + sent_rows, LANES)
    raw, xa, xb, za, zb = call(
        raw_pressure_kernel, "raw_pressure",
        [(nx, nz, ny), both_x, both_x, both_z, both_z],
        [air_state, wind_field, air_medium, *rims, txa, txb, tza, tzb],
        [ext, (1, nx, nz, ny)],
    )
    both = exchange(xa, xb, za, zb)
    lists = lax.all_to_all(lists, ("gx", "gz"), split_axis=0, concat_axis=0, tiled=True)
    (moved,) = call(
        functools.partial(advection_kernel, parts), "advection", [(3, nx, nz, ny)],
        [air_state, wind_field, *rims], [ext], flops=10_000_000,
    )
    (volume,) = call(
        volume_kernel, "volume", [solid_state.shape], [solid_state, integral, jacobians, stiffness],
        [(dims * pad, quants * width), (dims * pad, pad_k)], flops=10_000_000,
    )

    raw_xa, raw_xb = rims[2:]
    rim_x = (4, RADIUS, nz, ny)
    rim_z = (4, nx, ZRIM, ny)
    air, xa, xb, za, zb = call(
        functools.partial(injected_kernel, n_gx, n_gz), "injected",
        [air_state.shape, rim_x, rim_x, rim_z, rim_z],
        [air_state, wind_field, air_medium, raw, moved, *rims, *both, lists, surface_map],
        [(3 * nx, 3 * nz, ny), wide, (3,) + wide],
    )
    for substep in range(1, SUBSTEPS):
        rims = exchange(xa, xb, za, zb)
        if substep == 1:
            (solid_next,) = call(
                functools.partial(flux_kernel, n_gx), "flux", [solid_state.shape],
                [volume, traces, own, flux_solvers, lift_matrix, neighbours, surface_map, *both,
                 air_state, raw_xa, raw_xb, *far],
                [(quants, 5, 16, LANES), (faces, 16, quants * width), (faces, pad, 16)], flops=20_000_000,
            )
        pressure, xa, xb, za, zb = call(
            pressure_kernel, "pressure",
            [(nx, nz, ny), (RADIUS * nz, ny), (RADIUS * nz, ny), (nx * ZRIM, ny), (nx * ZRIM, ny)],
            [air, wind_field, air_medium, *rims], [ext, (1, nx, nz, ny)],
        )
        rises = exchange(xa, xb, za, zb)
        (moved,) = call(
            functools.partial(advection_kernel, 0), "advection", [(3, nx, nz, ny)],
            [air, wind_field, *rims], [ext], flops=10_000_000,
        )
        last = substep == SUBSTEPS - 1
        outs = [air_state.shape] + ([] if last else [rim_x, rim_x, rim_z, rim_z])
        done = call(
            velocity_kernel, "velocity", outs, [air, pressure, air_medium, moved, *rises], [wide]
        )
        air = done[0]
        if not last:
            xa, xb, za, zb = done[1:]
    return (solid_next, air)


def solution(mesh):
    in_specs = (
        P(None, None, ("gx", "gz")),
        P(None, None, None, ("gx", "gz")),
        P(None, None, None, ("gx", "gz")),
        P(),
        P(),
        P(),
        P(None, ("gx", "gz")),
        P(None, ("gx", "gz")),
        P(None, None, ("gx", "gz")),
        P(None, None, ("gx", "gz")),
        P(None, "gx", "gz", None),
        P(None, "gx", "gz", None),
        P(None, "gx", "gz", None),
    )
    out_specs = (P(None, None, ("gx", "gz")), P(None, "gx", "gz", None))
    return jax.shard_map(shards, mesh=mesh, in_specs=in_specs, out_specs=out_specs, check_vma=False)
```

```python
import functools

import jax
import jax.numpy as jnp
from jax import lax
from jax.experimental import pallas as pl
from jax.experimental.pallas import tpu as pltpu
from jax.sharding import PartitionSpec as P

ORDERS = 4
RADIUS = 4
SUBSTEPS = 3
ZRIM = 8
LANES = 128
HEAD = 8
TIME_STEP = 0.5
STENCIL_WEIGHTS = (0.8, -0.2, 4.0 / 105.0, -1.0 / 280.0)
F32 = jnp.float32
BF16 = jnp.bfloat16


def call(kernel, name, outs, ins, scratch=(), flops=1_000_000, after=()):
    count, skip = len(ins), len(after)
    nbytes = 4 * sum(x.size for x in ins) + 4 * sum(functools.reduce(lambda m, n: m * n, s, 1) for s in outs)

    def body(*refs):
        kernel(*refs[:count], *refs[count + skip:])

    return pl.pallas_call(
        body,
        out_shape=[jax.ShapeDtypeStruct(s, F32) for s in outs],
        in_specs=[pl.BlockSpec(memory_space=pltpu.VMEM) for _ in ins]
        + [pl.BlockSpec(memory_space=pl.ANY) for _ in after],
        out_specs=[pl.BlockSpec(memory_space=pltpu.VMEM) for _ in outs],
        scratch_shapes=[pltpu.VMEM(s, F32) for s in scratch],
        compiler_params=pltpu.CompilerParams(vmem_limit_bytes=8 * 1024 * 1024),
        cost_estimate=pl.CostEstimate(flops=flops, bytes_accessed=nbytes, transcendentals=0),
        name=name,
    )(*ins, *after)


def swap(values, axis, odd, by=1):
    count = lax.axis_size(axis)
    pairs = []
    for i in range(count - by):
        if i // by % 2 == odd:
            pairs += [(i, i + by), (i + by, i)]
    return lax.ppermute(values, axis, pairs)


def exchange(xa, xb, za, zb):
    xb = swap(xb, "gx", 1)
    xa = swap(xa, "gx", 0)
    zb = swap(zb, "gz", 1)
    za = swap(za, "gz", 0)
    return za, zb, xa, xb


def sides(axis, by=1):
    parity = (lax.axis_index(axis) // by) & 1
    return 1 - parity, parity


def by_side(pair, axis, by=1):
    first = sides(axis, by)[0]
    return jnp.where(first == 0, pair[0], pair[1]), jnp.where(first == 1, pair[0], pair[1])


def halves(values):
    high = values.astype(BF16)
    return high, (values - high.astype(F32)).astype(BF16)


def dot3(left, right, dims=(((1,), (0,)), ((), ()))):
    lh, ll = halves(left)
    rh, rl = halves(right)
    mul = functools.partial(lax.dot_general, dimension_numbers=dims, preferred_element_type=F32)
    return mul(lh, rh) + (mul(lh, rl) + mul(ll, rh))


def dot_exact(left, right, dims=(((1,), (0,)), ((), ()))):
    return lax.dot_general(
        left, right, dims, precision=lax.Precision.HIGHEST, preferred_element_type=F32
    )


def flat_slots(table):
    rows, fields, slots = table.shape
    lane = lax.broadcasted_iota(jnp.int32, (slots, LANES), 1)
    place = lax.broadcasted_iota(jnp.int32, (slots, LANES), 0)
    spread = jnp.where(lane % slots == place, 1.0, 0.0).astype(F32)
    lane = lax.broadcasted_iota(jnp.int32, (fields, LANES), 1)
    flat = jnp.zeros((fields, LANES), F32)
    for r in range(rows):
        flat = jnp.where(lane // slots == r, dot_exact(table[r].astype(F32), spread), flat)
    return flat


def pack_x(out, at, source, side):
    start = side * (source.shape[1] - RADIUS)
    out[pl.ds(at, source.shape[0])] = source[:, pl.ds(start, RADIUS)]


def pack_z(out, at, source, side):
    start = pl.multiple_of(side * (source.shape[2] - ZRIM), ZRIM)
    out[pl.ds(at, source.shape[0])] = source[:, :, pl.ds(start, ZRIM), :]


def widen(ext, center, za, zb, xa, xb, first=0, block=0):
    fields, nx, nz = center.shape[0], center.shape[1], center.shape[2]
    ext[:, RADIUS:RADIUS + nx, ZRIM:ZRIM + nz] = center[...]
    for got, side in zip((xa, xb), sides("gx")):
        place = pl.ds(side * (nx + RADIUS), RADIUS)
        if block:
            ext[0, place, ZRIM:ZRIM + nz] = got[(block - 1) * (1 - side)]
            ext[1:, place, ZRIM:ZRIM + nz] = got[block:block + fields - 1]
        else:
            skip = xa.shape[0] - za.shape[0] if first else 0
            ext[:, place, ZRIM:ZRIM + nz] = got[first + skip:first + skip + fields]
    for got, side in zip((za, zb), sides("gz")):
        start = pl.multiple_of(side * (nz + ZRIM), ZRIM)
        ext[:, RADIUS:RADIUS + nx, pl.ds(start, ZRIM)] = got[first:first + fields]


def d1(load, x, lo, hi):
    total = None
    for m, w in enumerate(STENCIL_WEIGHTS, 1):
        term = w * (load(x + m, lo, hi) - load(x - m, lo, hi))
        total = term if total is None else total + term
    return total


def d2(load, x, lo, hi):
    total = None
    for m, w in enumerate(STENCIL_WEIGHTS, 1):
        term = w * (load(x, lo + m, hi + m) - load(x, lo - m, hi - m))
        total = term if total is None else total + term
    return total


def d3(values):
    width = values.shape[1]
    lane = lax.broadcasted_iota(jnp.int32, (1, width), 1)
    total = None
    for m, w in enumerate(STENCIL_WEIGHTS, 1):
        ahead = jnp.where(lane < width - m, w, 0.0) * pltpu.roll(values, width - m, 1)
        behind = jnp.where(lane >= m, w, 0.0) * pltpu.roll(values, m, 1)
        term = ahead - behind
        total = term if total is None else total + term
    return total


def field(ref, c):
    return lambda x, lo, hi: ref[c, x, lo:hi, :]


def plane(ref):
    return lambda x, lo, hi: ref[x, lo:hi, :]


def arrived(lists, da, band, reach, slots):
    lane = lax.broadcasted_iota(jnp.int32, (1, LANES), 1)
    got = jnp.zeros((1, LANES), F32)
    for r in range(reach):
        row = lists[da - (r - reach // 2) + 3][band:band + 1]
        got = jnp.where((lane & (LANES // 2 - 1)) // slots == r, row, got)
    return got, pltpu.roll(got, LANES // 2, 1)


def cell_masks(cells, rows):
    cells = cells.astype(jnp.int32)
    place = lax.broadcasted_iota(jnp.int32, (rows, LANES), 0)
    third = lax.broadcasted_iota(jnp.int32, (LANES, LANES), 0)
    return cells // LANES == place, cells % LANES == third


def raw_rims_kernel(air, wind, xa, xb, za, zb):
    fields, nx = air.shape[:2]
    parts = nx // RADIUS
    for out, side in zip((xa, xb), sides("gx")):
        start = side * (nx - RADIUS)
        for part in range(parts):
            out[part] = air[0, part * RADIUS:(part + 1) * RADIUS]
        out[parts:parts + fields - 1] = air[1:, pl.ds(start, RADIUS)]
        pack_x(out, parts + fields - 1, wind, side)
    for out, side in zip((za, zb), sides("gz")):
        pack_z(out, 0, air, side)
        pack_z(out, fields, wind, side)


def lanes(at):
    return pl.ds(at if isinstance(at, int) else pl.multiple_of(at, LANES), LANES)


def jacobian_step(jac, rot, emit):
    quants, dims, width = jac.shape[1:]
    rows = rot.shape[0] // dims

    def half(h, carry):
        at = h * LANES
        acc = [None] * quants
        for d in range(dims):
            for q in range(quants):
                turned = rot[d * rows:(d + 1) * rows, lanes(q * width + at)]
                for p in range(quants):
                    term = jac[p, q, d:d + 1, lanes(at)] * turned
                    acc[p] = term if acc[p] is None else acc[p] + term
        for p in range(quants):
            emit(p, at, acc[p])
        return carry

    lax.fori_loop(0, width // LANES, half, 0)


def rotate(rot, matrix, source, quants, width):
    for q in range(quants):
        cut = slice(q * width, (q + 1) * width)
        rot[:, cut] = dot3(matrix[...], source[:, cut])


def take_slots(tiles, index):
    low = index % LANES
    high = index // LANES
    got = None
    for s, tile in enumerate(tiles):
        picked = jnp.take_along_axis(tile, low, axis=1, mode="promise_in_bounds")
        got = picked if got is None else jnp.where(high == s, picked, got)
    return got


def predict_kernel(
    state, jac, stiff, trace, sends, smap, normals,
    integral, traces, own, xa, xb, za, zb, row,
    cur, rot, sp, tp, picked,
):
    quants, basis, width = state.shape
    pad = integral.shape[0]
    face_basis, faces = trace.shape[:2]
    dims = stiff.shape[0]
    sp[...] = jnp.zeros_like(sp)
    tp[...] = jnp.zeros_like(tp)
    cur[...] = jnp.zeros_like(cur)
    for d in range(dims):
        sp[d * pad:d * pad + basis, 0:basis] = stiff[d]
    for f in range(faces):
        for j in range(face_basis):
            tp[f * 16 + j:f * 16 + j + 1, 0:basis] = trace[j, f:f + 1, :]
    for q in range(quants):
        cur[0:basis, q * width:(q + 1) * width] = state[q]
    integral[...] = TIME_STEP * cur[0:pad, :]

    def degree(k, weight):
        weight = jnp.where(k == 1, TIME_STEP**2 / 2, jnp.where(k == 2, TIME_STEP**3 / 6, TIME_STEP**4 / 24))
        rotate(rot, sp, cur, quants, width)

        def emit(p, at, value):
            cut = lanes(p * width + at)
            cur[0:pad, cut] = -value
            integral[:, cut] = integral[:, cut] - weight * value

        jacobian_step(jac, rot, emit)
        return weight

    lax.fori_loop(1, ORDERS, degree, F32(0))
    for q in range(quants):
        cut = slice(q * width, (q + 1) * width)
        done = dot3(tp[:, 0:pad], integral[:, cut])
        for f in range(faces):
            traces[q, :, f * width:(f + 1) * width] = done[f * 16:(f + 1) * 16]
    slots = flat_slots(smap)
    wanted = [jnp.broadcast_to(sends[d:d + 1, :], (16, LANES)) for d in range(4)]
    wanted.append(jnp.broadcast_to(slots[0:1].astype(jnp.int32), (16, LANES)))
    tiles_in = faces * width // LANES

    def gather(q, carry):
        tiles = [traces[q, :, s * LANES:(s + 1) * LANES] for s in range(tiles_in)]
        for d in range(4):
            picked[d, q] = take_slots(tiles, wanted[d])
        own[q] = take_slots(tiles, wanted[4])
        return carry

    lax.fori_loop(0, quants, gather, 0)
    for axis, base, outs in (("gx", 0, (xa, xb)), ("gz", 2, (za, zb))):
        for out, side in zip(outs, sides(axis)):
            for q in range(quants):
                out[q * 8:q * 8 + 8, :] = picked[base + side, q, 0:8, :]
                out[quants * 8 + q * 2:quants * 8 + q * 2 + 2, :] = picked[base + side, q, 8:face_basis, :]
            out[quants * face_basis:, :] = jnp.zeros((out.shape[0] - quants * face_basis, LANES), F32)
    normal = flat_slots(normals)
    speed = jnp.zeros((1, LANES), F32)
    for c in range(3):
        mean = jnp.sum(own[6 + c, 0:face_basis, :], axis=0, keepdims=True) * (1.0 / face_basis)
        speed = speed + normal[c:c + 1] * mean
    lane = lax.broadcasted_iota(jnp.int32, (1, LANES), 1)
    cells = pltpu.roll(slots[1:2], LANES // 2, 1)
    row[...] = jnp.where(lane < LANES // 2, slots[2:3] * speed, cells)


def pressure_rows(ext, wind, medium, x, nz):
    lo, hi = ZRIM, ZRIM + nz
    xe = x + RADIUS
    pressure = field(ext, 0)
    here = pressure(xe, lo, hi)
    divergence = d1(field(ext, 1), xe, lo, hi) + d2(field(ext, 2), xe, lo, hi) + d3(ext[3, xe, lo:hi, :])
    moved = (
        wind[0, x] * d1(pressure, xe, lo, hi)
        + wind[1, x] * d2(pressure, xe, lo, hi)
        + wind[2, x] * d3(here)
    )
    return here - medium[0, x] * divergence - moved


def pack_pressure(center, xs, zs, at=0):
    nx, nz, ny = center.shape[1:]
    for out, side in zip(xs, sides("gx")):
        start = side * (nx - RADIUS)
        out[at:at + RADIUS * nz, :] = center[0, pl.ds(start, RADIUS)].reshape(RADIUS * nz, ny)
    for out, side in zip(zs, sides("gz")):
        start = pl.multiple_of(side * (nz - ZRIM), ZRIM)
        out[at:at + nx * ZRIM, :] = center[0, :, pl.ds(start, ZRIM), :].reshape(nx * ZRIM, ny)


def widen_pressure(ext, center, za, zb, xa, xb, at=0):
    nx, nz, ny = center.shape
    ext[RADIUS:RADIUS + nx, ZRIM:ZRIM + nz] = center[...]
    for got, side in zip((xa, xb), sides("gx")):
        ext[pl.ds(side * (nx + RADIUS), RADIUS), ZRIM:ZRIM + nz] = got[at:at + RADIUS * nz, :].reshape(RADIUS, nz, ny)
    for got, side in zip((za, zb), sides("gz")):
        start = pl.multiple_of(side * (nz + ZRIM), ZRIM)
        ext[RADIUS:RADIUS + nx, pl.ds(start, ZRIM)] = got[at:at + nx * ZRIM, :].reshape(nx, ZRIM, ny)


def raw_pressure_kernel(air, wind, medium, za, zb, xa, xb, tza, tzb, row, pressure, oza, ozb, ext):
    nx, nz, ny = air.shape[1:]
    widen(ext, air, za, zb, xa, xb, block=nx // RADIUS)
    for x in range(nx):
        pressure[0, x] = pressure_rows(ext, wind, medium, x, nz)
    pack_pressure(pressure, (), (oza, ozb), HEAD)
    for out, sent in zip((oza, ozb), (tza, tzb)):
        out[0:HEAD, :] = jnp.broadcast_to(row[...], (HEAD, LANES))
        out[out.shape[0] - sent.shape[0]:, :] = sent[...]


def merge_kernel(air, raw, txa, txb, za, zb, row, oxa, oxb, far, farther):
    nx, nz, ny = air.shape[1:]
    low, high = by_side((za[0:1, :], zb[0:1, :]), "gz")
    place = lax.broadcasted_iota(jnp.int32, (HEAD, LANES), 0)
    lists = jnp.where(place == 0, row[...], jnp.where(place == 1, low, jnp.where(place == 2, high, 0.0)))
    pack_pressure(raw, (oxa, oxb), (), HEAD)
    for out, sent in zip((oxa, oxb), (txa, txb)):
        out[0:HEAD, :] = lists
        out[out.shape[0] - sent.shape[0]:, :] = sent[...]
    far[0:HEAD, :] = lists
    far[HEAD:, :] = air[0].reshape(nx * nz, ny)
    farther[...] = lists


def advection_kernel(block, air, wind, za, zb, xa, xb, moved, ext):
    nx, nz, ny = air.shape[1:]
    widen(ext, air, za, zb, xa, xb, block=block)
    lo, hi = ZRIM, ZRIM + nz
    for x in range(nx):
        xe = x + RADIUS
        for c in range(3):
            load = field(ext, 1 + c)
            moved[c, x] = (
                wind[0, x] * d1(load, xe, lo, hi)
                + wind[1, x] * d2(load, xe, lo, hi)
                + wind[2, x] * d3(load(xe, lo, hi))
            )


def velocities(out, center, moved, medium, wide, nx, nz):
    lo, hi = ZRIM, ZRIM + nz
    load = plane(wide)
    for x in range(nx):
        xe = x + RADIUS
        slopes = (d1(load, xe, lo, hi), d2(load, xe, lo, hi), d3(load(xe, lo, hi)))
        out[0, x] = load(xe, lo, hi)
        for c in range(3):
            out[1 + c, x] = center[1 + c, x] - medium[1, x] * slopes[c] - moved[c, x]


def pack_air(out, xa, xb, za, zb):
    for rim, side in zip((xa, xb), sides("gx")):
        pack_x(rim, 0, out, side)
    for rim, side in zip((za, zb), sides("gz")):
        pack_z(rim, 0, out, side)


def injected_kernel(
    air, wind, medium, raw, moved, wza, wzb, wxa, wxb, pza, pzb, pxa, pxb, farther, f2a, f2b, f3a, f3b, smap,
    out, oxa, oxb, oza, ozb, spread, wide, wide_wind,
):
    nx, nz, ny = air.shape[1:]
    reach, _, slots = smap.shape
    used = lax.broadcasted_iota(jnp.int32, (nx * nz, LANES), 1) < reach * slots
    lists = [None, None, None, farther[...], None, None, None]
    for by, pair in ((1, (pxa, pxb)), (2, (f2a, f2b)), (3, (f3a, f3b))):
        lists[3 - by], lists[3 + by] = by_side([got[0:HEAD, :] for got in pair], "gx", by)
    for da in range(3):
        for db in range(3):
            speed, cells = arrived(lists, da - 1, (1, 0, 2)[db], reach, slots)
            row_mask, third_mask = cell_masks(cells, nx * nz)
            high, low = halves(jnp.where(row_mask & used, speed, 0.0))
            columns = jnp.where(third_mask, 1.0, 0.0).astype(BF16)
            mul = functools.partial(
                lax.dot_general, dimension_numbers=(((1,), (1,)), ((), ())), preferred_element_type=F32
            )
            block = mul(high, columns) + mul(low, columns)
            spread[da * nx:(da + 1) * nx, db * nz:(db + 1) * nz] = block.reshape(nx, nz, ny)
    widen(wide_wind, wind, wza, wzb, wxa, wxb, first=air.shape[0])
    widen_pressure(wide, raw.at[0], pza, pzb, pxa, pxb, HEAD)
    load = plane(spread)
    for x in range(nx + 2 * RADIUS):
        xs = x + nx - RADIUS
        if RADIUS <= x < RADIUS + nx:
            lo, hi = 0, nz + 2 * ZRIM
        else:
            lo, hi = ZRIM, ZRIM + nz
        slo, shi = lo + nz - ZRIM, hi + nz - ZRIM
        here = load(xs, slo, shi)
        turned = (
            wide_wind[0, x, lo:hi, :] * d1(load, xs, slo, shi)
            + wide_wind[1, x, lo:hi, :] * d2(load, xs, slo, shi)
            + wide_wind[2, x, lo:hi, :] * d3(here)
        )
        wide[x, lo:hi, :] = wide[x, lo:hi, :] + (here - turned)
    velocities(out, air, moved, medium, wide, nx, nz)
    pack_air(out, oxa, oxb, oza, ozb)


def pressure_kernel(air, wind, medium, za, zb, xa, xb, pressure, oxa, oxb, oza, ozb, ext):
    nx, nz, ny = air.shape[1:]
    widen(ext, air, za, zb, xa, xb)
    for x in range(nx):
        pressure[0, x] = pressure_rows(ext, wind, medium, x, nz)
    pack_pressure(pressure, (oxa, oxb), (oza, ozb))


def velocity_kernel(air, pressure, medium, moved, za, zb, xa, xb, out, *rest):
    nx, nz, ny = air.shape[1:]
    wide = rest[-1]
    widen_pressure(wide, pressure.at[0], za, zb, xa, xb)
    velocities(out, air, moved, medium, wide, nx, nz)
    if len(rest) > 1:
        pack_air(out, *rest[:-1])


def volume_kernel(state, integral, jac, stiff, out, rot, sp):
    quants, basis, width = state.shape
    pad = integral.shape[0]
    dims = stiff.shape[0]
    sp[...] = jnp.zeros_like(sp)
    place = lax.broadcasted_iota(jnp.int32, (basis, basis), 0)
    other = lax.broadcasted_iota(jnp.int32, (basis, basis), 1)
    unit = jnp.where(place == other, 1.0, 0.0).astype(F32)
    for d in range(dims):
        sp[d * pad:d * pad + basis, 0:basis] = dot_exact(unit, stiff[d], (((1,), (1,)), ((), ())))
    for q in range(quants):
        cut = slice(q * width, (q + 1) * width)
        rot[:, cut] = dot3(sp[:, 0:pad], integral[:, cut])

    def emit(p, at, value):
        out[p, :, lanes(at)] = state[p, :, lanes(at)] + value[0:basis]

    jacobian_step(jac, rot, emit)


def flux_kernel(
    first, faces, base, traces, own, solvers, lift, neighbours, smap, za, zb, xa, xb, air, nxa, nxb, fxa, fxb,
    out, tiles, flux, lp,
):
    quants, basis, width = base.shape
    face_basis = lift.shape[0]
    reach, _, slots = smap.shape
    nx, nz, ny = air.shape[1:]
    rows = nx * nz
    lane = lax.broadcasted_iota(jnp.int32, (1, LANES), 1)
    flat = flat_slots(smap)
    row_mask, third_mask = cell_masks(flat[1:2], rows)
    columns = jnp.where(third_mask, 1.0, 0.0).astype(BF16)
    near = by_side([got[0:nx // RADIUS].reshape(rows, ny) for got in (nxa, nxb)], "gx")
    far = by_side([got[HEAD:, :] for got in (fxa, fxb)], "gx", 2)
    blocks = [far[0], near[0], air[0].reshape(rows, ny), near[1], far[1]]
    replies = jnp.zeros((1, LANES), F32)
    for r in range(reach):
        high, low = halves(blocks[r])
        looked = jnp.dot(high, columns, preferred_element_type=F32)
        looked = looked + jnp.dot(low, columns, preferred_element_type=F32)
        found = jnp.sum(jnp.where(row_mask, looked, 0.0), axis=0, keepdims=True)
        replies = jnp.where(lane // slots == r, found, replies)
    replies = replies * flat[2:3]
    skip = xa.shape[0] - sent_rows(quants, face_basis)
    for axis, base_tile, gots in (("gx", 0, (xa, xb)), ("gz", 2, (za, zb))):
        for got, side in zip(gots, sides(axis)):
            for q in range(quants):
                tiles[q, base_tile + side, 0:8, :] = got[skip + q * 8:skip + q * 8 + 8, :]
                at = skip + quants * 8 + q * 2
                tiles[q, base_tile + side, 8:face_basis, :] = got[at:at + 2, :]
                tiles[q, base_tile + side, face_basis:, :] = jnp.zeros((16 - face_basis, LANES), F32)
    for q in range(quants):
        tiles[q, 4] = -2.0 * replies - own[q] if q < 3 else own[q]
    lp[...] = jnp.zeros_like(lp)
    for f in range(faces):
        for j in range(face_basis):
            lp[f * 16 + j:f * 16 + j + 1, 0:basis] = lift[j, first + f:first + f + 1, :]
    unit = lax.broadcasted_iota(jnp.int32, (lp.shape[1], lp.shape[1]), 0) == lax.broadcasted_iota(
        jnp.int32, (lp.shape[1], lp.shape[1]), 1
    )
    lifted = dot_exact(jnp.where(unit, 1.0, 0.0).astype(F32), lp[...], (((1,), (1,)), ((), ())))
    local = traces.shape[2] // LANES
    halves_in = width // LANES

    def one(h, carry):
        at = h * LANES
        for f in range(faces):
            index = jnp.broadcast_to(neighbours[first + f:first + f + 1, lanes(at)], (16, LANES))
            acc = [None] * quants
            for q in range(quants):
                pool = [traces[q, :, s * LANES:(s + 1) * LANES] for s in range(local)]
                pool += [tiles[q, s] for s in range(5)]
                mine = traces[q, :, lanes((first + f) * width + at)]
                jump = take_slots(pool, index) - mine
                for p in range(quants):
                    term = solvers[p, q, first + f:first + f + 1, lanes(at)] * jump
                    acc[p] = term if acc[p] is None else acc[p] + term
            for p in range(quants):
                flux[f * 16:(f + 1) * 16, lanes(p * width + at)] = acc[p]
        return carry

    lax.fori_loop(0, halves_in, one, 0)
    for p in range(quants):
        cut = slice(p * width, (p + 1) * width)
        out[p] = base[p] + dot3(lifted, flux[:, cut])[0:basis]


def sent_rows(quants, face_basis):
    return -(-quants * face_basis // 8) * 8


def shards(
    solid_state, jacobians, flux_solvers, stiffness, trace_matrix, lift_matrix,
    neighbours, send_faces, surface_map, surface_normals, air_state, wind_field, air_medium,
):
    quants, basis, width = solid_state.shape
    faces, face_basis = trace_matrix.shape[0], trace_matrix.shape[1]
    dims = stiffness.shape[0]
    nx, nz, ny = air_state.shape[1:]
    jacobians = jnp.transpose(jacobians, (1, 2, 0, 3))
    flux_solvers = jnp.transpose(flux_solvers, (1, 2, 0, 3))
    trace_matrix = jnp.transpose(trace_matrix, (1, 0, 2))
    lift_matrix = jnp.transpose(lift_matrix, (2, 0, 1))
    surface_map = jnp.transpose(surface_map, (1, 0, 2))
    surface_normals = jnp.transpose(surface_normals, (1, 0, 2))
    pad = -(-basis // 8) * 8
    pad_k = -(-basis // 16) * 16
    parts = nx // RADIUS
    rim_x = (parts + 6, RADIUS, nz, ny)
    rim_z = (7, nx, ZRIM, ny)
    ext = (4, nx + 2 * RADIUS, nz + 2 * ZRIM, ny)
    wide = ext[1:]
    block = (1, nx, nz, ny)

    xa, xb, za, zb = call(raw_rims_kernel, "raw_rims", [rim_x, rim_x, rim_z, rim_z], [air_state, wind_field])
    rims = exchange(xa, xb, za, zb)

    sent = (sent_rows(quants, face_basis), LANES)
    integral, traces, own, txa, txb, tza, tzb, row = call(
        predict_kernel, "predict",
        [(pad, quants * width), (quants, 16, faces * width), (quants, 16, LANES), sent, sent, sent, sent,
         (1, LANES)],
        [solid_state, jacobians, stiffness, trace_matrix, send_faces, surface_map, surface_normals],
        [(pad_k, quants * width), (dims * pad, quants * width), (dims * pad, pad_k), (faces * 16, pad_k),
         (4, quants, 16, LANES)],
        flops=40_000_000,
    )
    both_x = (HEAD + RADIUS * nz + sent[0], LANES)
    both_z = (HEAD + nx * ZRIM + sent[0], LANES)
    raw, za, zb = call(
        raw_pressure_kernel, "raw_pressure", [block, both_z, both_z],
        [air_state, wind_field, air_medium, *rims, tza, tzb, row], [ext],
    )
    both_za, both_zb = swap(za, "gz", 0), swap(zb, "gz", 1)
    (moved,) = call(
        functools.partial(advection_kernel, parts), "advection", [(3, nx, nz, ny)],
        [air_state, wind_field, *rims], [ext], flops=10_000_000, after=[za],
    )
    (volume,) = call(
        volume_kernel, "volume", [solid_state.shape], [solid_state, integral, jacobians, stiffness],
        [(dims * pad, quants * width), (dims * pad, pad_k)], flops=10_000_000, after=[za],
    )
    xa, xb, far, farther = call(
        merge_kernel, "merge", [both_x, both_x, (HEAD + nx * nz, LANES), (HEAD, LANES)],
        [air_state, raw, txa, txb, both_za, both_zb, row],
    )
    both = (both_za, both_zb, swap(xa, "gx", 0), swap(xb, "gx", 1))
    far2 = swap(far, "gx", 0, 2), swap(far, "gx", 1, 2)
    far3 = swap(farther, "gx", 0, 3), swap(farther, "gx", 1, 3)

    raw_xa, raw_xb = rims[2:]
    rim_x = (4, RADIUS, nz, ny)
    rim_z = (4, nx, ZRIM, ny)
    air, xa, xb, za, zb = call(
        injected_kernel, "injected",
        [air_state.shape, rim_x, rim_x, rim_z, rim_z],
        [air_state, wind_field, air_medium, raw, moved, *rims, *both, farther, *far2, *far3, surface_map],
        [(3 * nx, 3 * nz, ny), wide, (3,) + wide], after=[volume],
    )
    half = faces // 2
    solid = volume
    for substep in range(1, SUBSTEPS):
        rims = exchange(xa, xb, za, zb)
        (solid,) = call(
            functools.partial(flux_kernel, (substep - 1) * half, half), "flux", [solid_state.shape],
            [solid, traces, own, flux_solvers, lift_matrix, neighbours, surface_map, *both,
             air_state, raw_xa, raw_xb, *far2],
            [(quants, 5, 16, LANES), (half * 16, quants * width), (half * 16, pad)], flops=20_000_000,
            after=[xa],
        )
        pressure, xa, xb, za, zb = call(
            pressure_kernel, "pressure",
            [block, (RADIUS * nz, ny), (RADIUS * nz, ny), (nx * ZRIM, ny), (nx * ZRIM, ny)],
            [air, wind_field, air_medium, *rims], [ext], after=[solid],
        )
        rises = exchange(xa, xb, za, zb)
        (moved,) = call(
            functools.partial(advection_kernel, 0), "advection", [(3, nx, nz, ny)],
            [air, wind_field, *rims], [ext], flops=10_000_000, after=[xa],
        )
        last = substep == SUBSTEPS - 1
        outs = [air_state.shape] + ([] if last else [rim_x, rim_x, rim_z, rim_z])
        done = call(
            velocity_kernel, "velocity", outs, [air, pressure, air_medium, moved, *rises], [wide]
        )
        air = done[0]
        if not last:
            xa, xb, za, zb = done[1:]
    return (solid, air)


def solution(mesh):
    in_specs = (
        P(None, None, ("gx", "gz")),
        P(None, None, None, ("gx", "gz")),
        P(None, None, None, ("gx", "gz")),
        P(),
        P(),
        P(),
        P(None, ("gx", "gz")),
        P(None, ("gx", "gz")),
        P(None, None, ("gx", "gz")),
        P(None, None, ("gx", "gz")),
        P(None, "gx", "gz", None),
        P(None, "gx", "gz", None),
        P(None, "gx", "gz", None),
    )
    out_specs = (P(None, None, ("gx", "gz")), P(None, "gx", "gz", None))
    return jax.shard_map(shards, mesh=mesh, in_specs=in_specs, out_specs=out_specs, check_vma=False)
```

```python
import functools

import jax
import jax.numpy as jnp
from jax import lax
from jax.experimental import pallas as pl
from jax.experimental.pallas import tpu as pltpu
from jax.sharding import PartitionSpec as P

ORDERS = 4
RADIUS = 4
SUBSTEPS = 3
ZRIM = 8
LANES = 128
HEAD = 8
TIME_STEP = 0.5
STENCIL_WEIGHTS = (0.8, -0.2, 4.0 / 105.0, -1.0 / 280.0)
F32 = jnp.float32
BF16 = jnp.bfloat16


def call(kernel, name, outs, ins, scratch=(), flops=1_000_000, after=()):
    count, skip = len(ins), len(after)
    nbytes = 4 * sum(x.size for x in ins) + 4 * sum(functools.reduce(lambda m, n: m * n, s, 1) for s in outs)

    def body(*refs):
        kernel(*refs[:count], *refs[count + skip:])

    return pl.pallas_call(
        body,
        out_shape=[jax.ShapeDtypeStruct(s, F32) for s in outs],
        in_specs=[pl.BlockSpec(memory_space=pltpu.VMEM) for _ in ins]
        + [pl.BlockSpec(memory_space=pl.ANY) for _ in after],
        out_specs=[pl.BlockSpec(memory_space=pltpu.VMEM) for _ in outs],
        scratch_shapes=[pltpu.VMEM(s, F32) for s in scratch],
        compiler_params=pltpu.CompilerParams(vmem_limit_bytes=8 * 1024 * 1024),
        cost_estimate=pl.CostEstimate(flops=flops, bytes_accessed=nbytes, transcendentals=0),
        name=name,
    )(*ins, *after)


def swap(values, axis, odd, by=1):
    count = lax.axis_size(axis)
    pairs = []
    for i in range(count - by):
        if i // by % 2 == odd:
            pairs += [(i, i + by), (i + by, i)]
    return lax.ppermute(values, axis, pairs)


def exchange(xb, xa, zb, za):
    return swap(xb, "gx", 1), swap(xa, "gx", 0), swap(zb, "gz", 1), swap(za, "gz", 0)


def sides(axis, by=1):
    parity = (lax.axis_index(axis) // by) & 1
    return 1 - parity, parity


def by_side(pair, axis, by=1):
    first = sides(axis, by)[0]
    return jnp.where(first == 0, pair[0], pair[1]), jnp.where(first == 1, pair[0], pair[1])


def halves(values):
    high = values.astype(BF16)
    return high, (values - high.astype(F32)).astype(BF16)


def dot3(left, right, dims=(((1,), (0,)), ((), ()))):
    lh, ll = halves(left)
    rh, rl = halves(right)
    mul = functools.partial(lax.dot_general, dimension_numbers=dims, preferred_element_type=F32)
    return mul(lh, rh) + (mul(lh, rl) + mul(ll, rh))


def dot_exact(left, right, dims=(((1,), (0,)), ((), ()))):
    return lax.dot_general(
        left, right, dims, precision=lax.Precision.HIGHEST, preferred_element_type=F32
    )


def flat_slots(table):
    rows, fields, slots = table.shape
    lane = lax.broadcasted_iota(jnp.int32, (slots, LANES), 1)
    place = lax.broadcasted_iota(jnp.int32, (slots, LANES), 0)
    spread = jnp.where(lane % slots == place, 1.0, 0.0).astype(F32)
    lane = lax.broadcasted_iota(jnp.int32, (fields, LANES), 1)
    flat = jnp.zeros((fields, LANES), F32)
    for r in range(rows):
        flat = jnp.where(lane // slots == r, dot_exact(table[r].astype(F32), spread), flat)
    return flat


def pack_x(out, at, source, side):
    fields, nx, nz, ny = source.shape
    start = side * (nx - RADIUS)
    rows = fields * RADIUS * nz
    at = HEAD + at * RADIUS * nz
    out[at:at + rows, :] = source[:, pl.ds(start, RADIUS)].reshape(rows, ny)


def pack_z(out, at, source, side):
    start = pl.multiple_of(side * (source.shape[2] - ZRIM), ZRIM)
    out[pl.ds(at, source.shape[0])] = source[:, :, pl.ds(start, ZRIM), :]


def widen(ext, center, xb, xa, zb, za, first=0):
    fields, nx, nz, ny = center.shape
    ext[:, RADIUS:RADIUS + nx, ZRIM:ZRIM + nz] = center[...]
    for got, side in zip((xa, xb), sides("gx")):
        place = pl.ds(side * (nx + RADIUS), RADIUS)
        rows = got[HEAD + first * RADIUS * nz:HEAD + (first + fields) * RADIUS * nz, :]
        ext[:, place, ZRIM:ZRIM + nz] = rows.reshape(fields, RADIUS, nz, ny)
    for got, side in zip((za, zb), sides("gz")):
        start = pl.multiple_of(side * (nz + ZRIM), ZRIM)
        ext[:, RADIUS:RADIUS + nx, pl.ds(start, ZRIM)] = got[first:first + fields]


def d1(load, x, lo, hi):
    total = None
    for m, w in enumerate(STENCIL_WEIGHTS, 1):
        term = w * (load(x + m, lo, hi) - load(x - m, lo, hi))
        total = term if total is None else total + term
    return total


def d2(load, x, lo, hi):
    total = None
    for m, w in enumerate(STENCIL_WEIGHTS, 1):
        term = w * (load(x, lo + m, hi + m) - load(x, lo - m, hi - m))
        total = term if total is None else total + term
    return total


def d3(values):
    width = values.shape[1]
    lane = lax.broadcasted_iota(jnp.int32, (1, width), 1)
    total = None
    for m, w in enumerate(STENCIL_WEIGHTS, 1):
        ahead = jnp.where(lane < width - m, w, 0.0) * pltpu.roll(values, width - m, 1)
        behind = jnp.where(lane >= m, w, 0.0) * pltpu.roll(values, m, 1)
        term = ahead - behind
        total = term if total is None else total + term
    return total


def field(ref, c):
    return lambda x, lo, hi: ref[c, x, lo:hi, :]


def plane(ref):
    return lambda x, lo, hi: ref[x, lo:hi, :]


def arrived(lists, da, band, reach, slots):
    lane = lax.broadcasted_iota(jnp.int32, (1, LANES), 1)
    got = jnp.zeros((1, LANES), F32)
    for r in range(reach):
        row = lists[da - (r - reach // 2) + 3][band:band + 1]
        got = jnp.where((lane & (LANES // 2 - 1)) // slots == r, row, got)
    return got, pltpu.roll(got, LANES // 2, 1)


def cell_masks(cells, rows):
    cells = cells.astype(jnp.int32)
    place = lax.broadcasted_iota(jnp.int32, (rows, LANES), 0)
    third = lax.broadcasted_iota(jnp.int32, (LANES, LANES), 0)
    return cells // LANES == place, cells % LANES == third


def raw_rims_kernel(air, wind, xb, xa, zb, za):
    fields = air.shape[0]
    for out, side in zip((xa, xb), sides("gx")):
        out[0:HEAD, :] = jnp.zeros((HEAD, LANES), F32)
        pack_x(out, 0, air, side)
        pack_x(out, fields, wind, side)
    for out, side in zip((za, zb), sides("gz")):
        pack_z(out, 0, air, side)
        pack_z(out, fields, wind, side)


def lanes(at):
    return pl.ds(at if isinstance(at, int) else pl.multiple_of(at, LANES), LANES)


def jacobian_step(jac, rot, emit):
    quants, dims, width = jac.shape[1:]
    rows = rot.shape[0] // dims

    def half(h, carry):
        at = h * LANES
        acc = [None] * quants
        for d in range(dims):
            for q in range(quants):
                turned = rot[d * rows:(d + 1) * rows, lanes(q * width + at)]
                for p in range(quants):
                    term = jac[p, q, d:d + 1, lanes(at)] * turned
                    acc[p] = term if acc[p] is None else acc[p] + term
        for p in range(quants):
            emit(p, at, acc[p])
        return carry

    lax.fori_loop(0, width // LANES, half, 0)


def rotate(rot, matrix, source, quants, width):
    for q in range(quants):
        cut = slice(q * width, (q + 1) * width)
        rot[:, cut] = dot3(matrix[...], source[:, cut])


def take_slots(tiles, index):
    low = index % LANES
    high = index // LANES
    got = None
    for s, tile in enumerate(tiles):
        picked = jnp.take_along_axis(tile, low, axis=1, mode="promise_in_bounds")
        got = picked if got is None else jnp.where(high == s, picked, got)
    return got


def predict_kernel(
    state, jac, stiff, trace, sends, smap, normals,
    integral, traces, own, xa, xb, za, zb, row,
    cur, rot, sp, tp, picked,
):
    quants, basis, width = state.shape
    pad = integral.shape[0]
    face_basis, faces = trace.shape[:2]
    dims = stiff.shape[0]
    sp[...] = jnp.zeros_like(sp)
    tp[...] = jnp.zeros_like(tp)
    cur[...] = jnp.zeros_like(cur)
    for d in range(dims):
        sp[d * pad:d * pad + basis, 0:basis] = stiff[d]
    for f in range(faces):
        for j in range(face_basis):
            tp[f * 16 + j:f * 16 + j + 1, 0:basis] = trace[j, f:f + 1, :]
    for q in range(quants):
        cur[0:basis, q * width:(q + 1) * width] = state[q]
    integral[...] = TIME_STEP * cur[0:pad, :]

    def degree(k, weight):
        weight = jnp.where(k == 1, TIME_STEP**2 / 2, jnp.where(k == 2, TIME_STEP**3 / 6, TIME_STEP**4 / 24))
        rotate(rot, sp, cur, quants, width)

        def emit(p, at, value):
            cut = lanes(p * width + at)
            cur[0:pad, cut] = -value
            integral[:, cut] = integral[:, cut] - weight * value

        jacobian_step(jac, rot, emit)
        return weight

    lax.fori_loop(1, ORDERS, degree, F32(0))
    for q in range(quants):
        cut = slice(q * width, (q + 1) * width)
        done = dot3(tp[:, 0:pad], integral[:, cut])
        for f in range(faces):
            traces[q, :, f * width:(f + 1) * width] = done[f * 16:(f + 1) * 16]
    slots = flat_slots(smap)
    wanted = [jnp.broadcast_to(sends[d:d + 1, :], (16, LANES)) for d in range(4)]
    wanted.append(jnp.broadcast_to(slots[0:1].astype(jnp.int32), (16, LANES)))
    tiles_in = faces * width // LANES

    def gather(q, carry):
        tiles = [traces[q, :, s * LANES:(s + 1) * LANES] for s in range(tiles_in)]
        for d in range(4):
            picked[d, q] = take_slots(tiles, wanted[d])
        own[q] = take_slots(tiles, wanted[4])
        return carry

    lax.fori_loop(0, quants, gather, 0)
    for axis, base, outs in (("gx", 0, (xa, xb)), ("gz", 2, (za, zb))):
        for out, side in zip(outs, sides(axis)):
            for q in range(quants):
                out[q * 8:q * 8 + 8, :] = picked[base + side, q, 0:8, :]
                out[quants * 8 + q * 2:quants * 8 + q * 2 + 2, :] = picked[base + side, q, 8:face_basis, :]
            out[quants * face_basis:, :] = jnp.zeros((out.shape[0] - quants * face_basis, LANES), F32)
    normal = flat_slots(normals)
    speed = jnp.zeros((1, LANES), F32)
    for c in range(3):
        mean = jnp.sum(own[6 + c, 0:face_basis, :], axis=0, keepdims=True) * (1.0 / face_basis)
        speed = speed + normal[c:c + 1] * mean
    lane = lax.broadcasted_iota(jnp.int32, (1, LANES), 1)
    cells = pltpu.roll(slots[1:2], LANES // 2, 1)
    row[...] = jnp.where(lane < LANES // 2, slots[2:3] * speed, cells)


def pressure_rows(ext, wind, medium, x, nz):
    lo, hi = ZRIM, ZRIM + nz
    xe = x + RADIUS
    pressure = field(ext, 0)
    here = pressure(xe, lo, hi)
    divergence = d1(field(ext, 1), xe, lo, hi) + d2(field(ext, 2), xe, lo, hi) + d3(ext[3, xe, lo:hi, :])
    moved = (
        wind[0, x] * d1(pressure, xe, lo, hi)
        + wind[1, x] * d2(pressure, xe, lo, hi)
        + wind[2, x] * d3(here)
    )
    return here - medium[0, x] * divergence - moved


def pack_pressure(center, xs, zs):
    nx, nz, ny = center.shape[1:]
    for out, side in zip(xs, sides("gx")):
        start = side * (nx - RADIUS)
        out[HEAD:HEAD + RADIUS * nz, :] = center[0, pl.ds(start, RADIUS)].reshape(RADIUS * nz, ny)
    for out, side in zip(zs, sides("gz")):
        start = pl.multiple_of(side * (nz - ZRIM), ZRIM)
        out[HEAD:HEAD + nx * ZRIM, :] = center[0, :, pl.ds(start, ZRIM), :].reshape(nx * ZRIM, ny)


def widen_pressure(ext, center, xb, xa, zb, za):
    nx, nz, ny = center.shape
    ext[RADIUS:RADIUS + nx, ZRIM:ZRIM + nz] = center[...]
    for got, side in zip((xa, xb), sides("gx")):
        ext[pl.ds(side * (nx + RADIUS), RADIUS), ZRIM:ZRIM + nz] = got[HEAD:HEAD + RADIUS * nz, :].reshape(RADIUS, nz, ny)
    for got, side in zip((za, zb), sides("gz")):
        start = pl.multiple_of(side * (nz + ZRIM), ZRIM)
        ext[RADIUS:RADIUS + nx, pl.ds(start, ZRIM)] = got[HEAD:HEAD + nx * ZRIM, :].reshape(nx, ZRIM, ny)


def raw_pressure_kernel(air, wind, medium, xb, xa, zb, za, tza, tzb, row, pressure, ozb, oza, ext):
    nx, nz, ny = air.shape[1:]
    widen(ext, air, xb, xa, zb, za)
    for x in range(nx):
        pressure[0, x] = pressure_rows(ext, wind, medium, x, nz)
    pack_pressure(pressure, (), (oza, ozb))
    for out, sent in zip((oza, ozb), (tza, tzb)):
        out[0:HEAD, :] = jnp.broadcast_to(row[...], (HEAD, LANES))
        out[out.shape[0] - sent.shape[0]:, :] = sent[...]


def put_rows(rows):
    place = lax.broadcasted_iota(jnp.int32, (HEAD, LANES), 0)
    out = jnp.zeros((HEAD, LANES), F32)
    for at, row in enumerate(rows):
        out = jnp.where(place == at, row, out)
    return out


def merge_kernel(raw, txa, txb, zb, za, row, oxb, oxa, lists):
    low, high = by_side((za[0:1, :], zb[0:1, :]), "gz")
    lists[...] = put_rows((row[...], low, high))
    pack_pressure(raw, (oxa, oxb), ())
    for out, sent in zip((oxa, oxb), (txa, txb)):
        out[0:HEAD, :] = lists[...]
        out[out.shape[0] - sent.shape[0]:, :] = sent[...]


def merge_far_kernel(lists, xb, xa, out):
    low, high = by_side((xa[0:HEAD, :], xb[0:HEAD, :]), "gx")
    out[0:HEAD, :] = low
    out[HEAD:2 * HEAD, :] = lists[...]
    out[2 * HEAD:, :] = high


def advection_kernel(air, wind, xb, xa, zb, za, moved, ext):
    nx, nz, ny = air.shape[1:]
    widen(ext, air, xb, xa, zb, za)
    lo, hi = ZRIM, ZRIM + nz
    for x in range(nx):
        xe = x + RADIUS
        for c in range(3):
            load = field(ext, 1 + c)
            moved[c, x] = (
                wind[0, x] * d1(load, xe, lo, hi)
                + wind[1, x] * d2(load, xe, lo, hi)
                + wind[2, x] * d3(load(xe, lo, hi))
            )


def velocities(out, center, moved, medium, wide, nx, nz):
    lo, hi = ZRIM, ZRIM + nz
    load = plane(wide)
    for x in range(nx):
        xe = x + RADIUS
        slopes = (d1(load, xe, lo, hi), d2(load, xe, lo, hi), d3(load(xe, lo, hi)))
        out[0, x] = load(xe, lo, hi)
        for c in range(3):
            out[1 + c, x] = center[1 + c, x] - medium[1, x] * slopes[c] - moved[c, x]


def pack_air(out, xb, xa, zb, za):
    for rim, side in zip((xa, xb), sides("gx")):
        pack_x(rim, 0, out, side)
    for rim, side in zip((za, zb), sides("gz")):
        pack_z(rim, 0, out, side)


def injected_kernel(
    air, wind, medium, raw, moved, wxb, wxa, wzb, wza, pxb, pxa, pzb, pza, near, f2a, f2b, smap,
    out, oxb, oxa, ozb, oza, answer, spread, wide, wide_wind,
):
    nx, nz, ny = air.shape[1:]
    reach, _, slots = smap.shape
    used = lax.broadcasted_iota(jnp.int32, (nx * nz, LANES), 1) < reach * slots
    low, high = by_side((f2a[...], f2b[...]), "gx", 2)
    lists = [low[0:HEAD], low[HEAD:2 * HEAD]]
    lists += [near[HEAD * s:HEAD * (s + 1), :] for s in range(3)]
    lists += [high[HEAD:2 * HEAD], high[2 * HEAD:]]
    mul = functools.partial(
        lax.dot_general, dimension_numbers=(((1,), (1,)), ((), ())), preferred_element_type=F32
    )
    for da in range(3):
        for db in range(3):
            speed, cells = arrived(lists, da - 1, (1, 0, 2)[db], reach, slots)
            row_mask, third_mask = cell_masks(cells, nx * nz)
            high, low = halves(jnp.where(row_mask & used, speed, 0.0))
            columns = jnp.where(third_mask, 1.0, 0.0).astype(BF16)
            if da == 1 and db == 1:
                seen, rest = halves(air[0].reshape(nx * nz, ny))
                looked = jnp.dot(seen, columns, preferred_element_type=F32)
                looked = looked + jnp.dot(rest, columns, preferred_element_type=F32)
                answer[...] = jnp.sum(jnp.where(row_mask, looked, 0.0), axis=0, keepdims=True)
            block = mul(high, columns) + mul(low, columns)
            spread[da * nx:(da + 1) * nx, db * nz:(db + 1) * nz] = block.reshape(nx, nz, ny)
    widen(wide_wind, wind, wxb, wxa, wzb, wza, first=air.shape[0])
    widen_pressure(wide, raw.at[0], pxb, pxa, pzb, pza)
    load = plane(spread)
    for x in range(nx + 2 * RADIUS):
        xs = x + nx - RADIUS
        if RADIUS <= x < RADIUS + nx:
            lo, hi = 0, nz + 2 * ZRIM
        else:
            lo, hi = ZRIM, ZRIM + nz
        slo, shi = lo + nz - ZRIM, hi + nz - ZRIM
        here = load(xs, slo, shi)
        turned = (
            wide_wind[0, x, lo:hi, :] * d1(load, xs, slo, shi)
            + wide_wind[1, x, lo:hi, :] * d2(load, xs, slo, shi)
            + wide_wind[2, x, lo:hi, :] * d3(here)
        )
        wide[x, lo:hi, :] = wide[x, lo:hi, :] + (here - turned)
    velocities(out, air, moved, medium, wide, nx, nz)
    pack_air(out, oxb, oxa, ozb, oza)
    for rim in (oxa, oxb):
        rim[0:HEAD, :] = put_rows((answer[...],))


def pressure_kernel(air, wind, medium, xb, xa, zb, za, answer, pressure, oxb, oxa, ozb, oza, ext):
    nx, nz, ny = air.shape[1:]
    widen(ext, air, xb, xa, zb, za)
    for x in range(nx):
        pressure[0, x] = pressure_rows(ext, wind, medium, x, nz)
    pack_pressure(pressure, (oxa, oxb), (oza, ozb))
    low, high = by_side((xa[0:1, :], xb[0:1, :]), "gx")
    for rim in (oxa, oxb):
        rim[0:HEAD, :] = put_rows((answer[...], low, high))
    for rim in (oza, ozb):
        rim[0:HEAD, :] = jnp.zeros((HEAD, LANES), F32)


def velocity_kernel(air, pressure, medium, moved, xb, xa, zb, za, out, *rest):
    nx, nz, ny = air.shape[1:]
    wide = rest[-1]
    widen_pressure(wide, pressure.at[0], xb, xa, zb, za)
    velocities(out, air, moved, medium, wide, nx, nz)
    if len(rest) > 1:
        pack_air(out, *rest[:-1])
        for rim in rest[:2]:
            rim[0:HEAD, :] = jnp.zeros((HEAD, LANES), F32)


def volume_kernel(state, integral, jac, stiff, out, rot, sp):
    quants, basis, width = state.shape
    pad = integral.shape[0]
    dims = stiff.shape[0]
    sp[...] = jnp.zeros_like(sp)
    place = lax.broadcasted_iota(jnp.int32, (basis, basis), 0)
    other = lax.broadcasted_iota(jnp.int32, (basis, basis), 1)
    unit = jnp.where(place == other, 1.0, 0.0).astype(F32)
    for d in range(dims):
        sp[d * pad:d * pad + basis, 0:basis] = dot_exact(unit, stiff[d], (((1,), (1,)), ((), ())))
    for q in range(quants):
        cut = slice(q * width, (q + 1) * width)
        rot[:, cut] = dot3(sp[:, 0:pad], integral[:, cut])

    def emit(p, at, value):
        out[p, :, lanes(at)] = state[p, :, lanes(at)] + value[0:basis]

    jacobian_step(jac, rot, emit)


def flux_kernel(
    first, faces, base, traces, own, solvers, lift, neighbours, smap, xb, xa, zb, za, *rest
):
    answer, rxb, rxa = rest[:3] if len(rest) > 4 else (None,) * 3
    out, tiles, flux, lp = rest[-4:]
    quants, basis, width = base.shape
    face_basis, all_faces = lift.shape[:2]
    reach, _, slots = smap.shape
    skip = xa.shape[0] - sent_rows(quants, face_basis)
    for axis, base_tile, gots in (("gx", 0, (xa, xb)), ("gz", 2, (za, zb))):
        for got, side in zip(gots, sides(axis)):
            for q in range(quants):
                tiles[q, base_tile + side, 0:8, :] = got[skip + q * 8:skip + q * 8 + 8, :]
                at = skip + quants * 8 + q * 2
                tiles[q, base_tile + side, 8:face_basis, :] = got[at:at + 2, :]
                tiles[q, base_tile + side, face_basis:, :] = jnp.zeros((16 - face_basis, LANES), F32)
    for q in range(quants):
        tiles[q, 4] = -own[q] if q < 3 else own[q]
    lp[...] = jnp.zeros_like(lp)
    for f in range(faces):
        for j in range(face_basis):
            lp[f * 16 + j:f * 16 + j + 1, 0:basis] = lift[j, first + f:first + f + 1, :]
    unit = lax.broadcasted_iota(jnp.int32, (lp.shape[1], lp.shape[1]), 0) == lax.broadcasted_iota(
        jnp.int32, (lp.shape[1], lp.shape[1]), 1
    )
    lifted = dot_exact(jnp.where(unit, 1.0, 0.0).astype(F32), lp[...], (((1,), (1,)), ((), ())))
    local = traces.shape[2] // LANES
    halves_in = width // LANES

    def one(h, carry):
        at = h * LANES
        for f in range(faces):
            index = jnp.broadcast_to(neighbours[first + f:first + f + 1, lanes(at)], (16, LANES))
            acc = [None] * quants
            for q in range(quants):
                pool = [traces[q, :, s * LANES:(s + 1) * LANES] for s in range(local)]
                pool += [tiles[q, s] for s in range(5)]
                mine = traces[q, :, lanes((first + f) * width + at)]
                jump = take_slots(pool, index) - mine
                for p in range(quants):
                    term = solvers[p, q, first + f:first + f + 1, lanes(at)] * jump
                    acc[p] = term if acc[p] is None else acc[p] + term
            for p in range(quants):
                flux[f * 16:(f + 1) * 16, lanes(p * width + at)] = acc[p]
        return carry

    lax.fori_loop(0, halves_in, one, 0)
    for p in range(quants):
        cut = slice(p * width, (p + 1) * width)
        out[p] = base[p] + dot3(lifted, flux[:, cut])[0:basis]
    if answer is None:
        return
    low, high = by_side((rxa[0:HEAD, :], rxb[0:HEAD, :]), "gx")
    lane = lax.broadcasted_iota(jnp.int32, (1, LANES), 1)
    replies = jnp.zeros((1, LANES), F32)
    for r, row in enumerate((low[1:2], low[0:1], answer[...], high[0:1], high[2:3])):
        replies = jnp.where(lane // slots == r, row, replies)
    replies = jnp.broadcast_to(-2.0 * replies * flat_slots(smap)[2:3], (8, LANES))
    begin = (local + 4) * LANES
    for f in range(all_faces):
        column = lift[0, f:f + 1, :]
        for j in range(1, face_basis):
            column = column + lift[j, f:f + 1, :]
        square = lax.broadcasted_iota(jnp.int32, (basis, basis), 0) == lax.broadcasted_iota(
            jnp.int32, (basis, basis), 1
        )
        column = jnp.sum(jnp.where(square, column, 0.0), axis=1, keepdims=True)
        for h in range(halves_in):
            at = h * LANES
            index = jnp.broadcast_to(neighbours[f:f + 1, at:at + LANES], (8, LANES))
            found = jnp.take_along_axis(replies, index % LANES, axis=1, mode="promise_in_bounds")
            found = jnp.where(index >= begin, found, 0.0)[0:1]
            spread = column * found
            for p in range(quants):
                both = solvers[p, 0, f:f + 1, at:at + LANES]
                for q in range(1, 3):
                    both = both + solvers[p, q, f:f + 1, at:at + LANES]
                out[p, :, at:at + LANES] = out[p, :, at:at + LANES] + both * spread


def sent_rows(quants, face_basis):
    return -(-quants * face_basis // 8) * 8


def shards(
    solid_state, jacobians, flux_solvers, stiffness, trace_matrix, lift_matrix,
    neighbours, send_faces, surface_map, surface_normals, air_state, wind_field, air_medium,
):
    quants, basis, width = solid_state.shape
    faces, face_basis = trace_matrix.shape[0], trace_matrix.shape[1]
    dims = stiffness.shape[0]
    nx, nz, ny = air_state.shape[1:]
    jacobians = jnp.transpose(jacobians, (1, 2, 0, 3))
    flux_solvers = jnp.transpose(flux_solvers, (1, 2, 0, 3))
    trace_matrix = jnp.transpose(trace_matrix, (1, 0, 2))
    lift_matrix = jnp.transpose(lift_matrix, (2, 0, 1))
    surface_map = jnp.transpose(surface_map, (1, 0, 2))
    surface_normals = jnp.transpose(surface_normals, (1, 0, 2))
    pad = -(-basis // 8) * 8
    pad_k = -(-basis // 16) * 16
    rim_z = (7, nx, ZRIM, ny)
    rim_x = (HEAD + 7 * RADIUS * nz, ny)
    ext = (4, nx + 2 * RADIUS, nz + 2 * ZRIM, ny)
    wide = ext[1:]
    block = (1, nx, nz, ny)

    rims = exchange(
        *call(raw_rims_kernel, "raw_rims", [rim_x, rim_x, rim_z, rim_z], [air_state, wind_field])
    )

    sent = (sent_rows(quants, face_basis), LANES)
    integral, traces, own, txa, txb, tza, tzb, row = call(
        predict_kernel, "predict",
        [(pad, quants * width), (quants, 16, faces * width), (quants, 16, LANES), sent, sent, sent, sent,
         (1, LANES)],
        [solid_state, jacobians, stiffness, trace_matrix, send_faces, surface_map, surface_normals],
        [(pad_k, quants * width), (dims * pad, quants * width), (dims * pad, pad_k), (faces * 16, pad_k),
         (4, quants, 16, LANES)],
        flops=40_000_000,
    )
    pressure_x = (HEAD + RADIUS * nz, ny)
    pressure_z = (HEAD + nx * ZRIM, ny)
    both_x = (pressure_x[0] + sent[0], LANES)
    both_z = (pressure_z[0] + sent[0], LANES)
    raw, zb, za = call(
        raw_pressure_kernel, "raw_pressure", [block, both_z, both_z],
        [air_state, wind_field, air_medium, *rims, tza, tzb, row], [ext],
    )
    both_zb, both_za = swap(zb, "gz", 1), swap(za, "gz", 0)
    xb, xa, lists = call(
        merge_kernel, "merge", [both_x, both_x, (HEAD, LANES)], [raw, txa, txb, both_zb, both_za, row]
    )
    both = (swap(xb, "gx", 1), swap(xa, "gx", 0), both_zb, both_za)
    (volume,) = call(
        volume_kernel, "volume", [solid_state.shape], [solid_state, integral, jacobians, stiffness],
        [(dims * pad, quants * width), (dims * pad, pad_k)], flops=10_000_000, after=[xa],
    )
    (near,) = call(merge_far_kernel, "merge_far", [(3 * HEAD, LANES)], [lists, *both[:2]], after=[volume])
    far = swap(near, "gx", 0, 2), swap(near, "gx", 1, 2)
    (moved,) = call(
        advection_kernel, "advection", [(3, nx, nz, ny)],
        [air_state, wind_field, *rims], [ext], flops=10_000_000, after=[near],
    )

    rim_x = (HEAD + 4 * RADIUS * nz, ny)
    rim_z = (4, nx, ZRIM, ny)
    air, xb, xa, zb, za, answer = call(
        injected_kernel, "injected",
        [air_state.shape, rim_x, rim_x, rim_z, rim_z, (1, LANES)],
        [air_state, wind_field, air_medium, raw, moved, *rims, *both, near, *far, surface_map],
        [(3 * nx, 3 * nz, ny), wide, (3,) + wide],
    )
    half = faces // 2
    solid = volume
    replies = []
    for substep in range(1, SUBSTEPS):
        rims = exchange(xb, xa, zb, za)
        (solid,) = call(
            functools.partial(flux_kernel, (substep - 1) * half, half), "flux", [solid_state.shape],
            [solid, traces, own, flux_solvers, lift_matrix, neighbours, surface_map, *both, *replies],
            [(quants, 5, 16, LANES), (half * 16, quants * width), (half * 16, pad)], flops=20_000_000,
            after=[xa],
        )
        pressure, xb, xa, zb, za = call(
            pressure_kernel, "pressure", [block, pressure_x, pressure_x, pressure_z, pressure_z],
            [air, wind_field, air_medium, *rims, answer], [ext], after=[solid],
        )
        rises = exchange(xb, xa, zb, za)
        if substep == 1:
            replies = [answer, *rises[:2]]
        (moved,) = call(
            advection_kernel, "advection", [(3, nx, nz, ny)],
            [air, wind_field, *rims], [ext], flops=10_000_000, after=[xa],
        )
        last = substep == SUBSTEPS - 1
        outs = [air_state.shape] + ([] if last else [rim_x, rim_x, rim_z, rim_z])
        done = call(
            velocity_kernel, "velocity", outs, [air, pressure, air_medium, moved, *rises], [wide]
        )
        air = done[0]
        if not last:
            xb, xa, zb, za = done[1:]
    return (solid, air)


def solution(mesh):
    in_specs = (
        P(None, None, ("gx", "gz")),
        P(None, None, None, ("gx", "gz")),
        P(None, None, None, ("gx", "gz")),
        P(),
        P(),
        P(),
        P(None, ("gx", "gz")),
        P(None, ("gx", "gz")),
        P(None, None, ("gx", "gz")),
        P(None, None, ("gx", "gz")),
        P(None, "gx", "gz", None),
        P(None, "gx", "gz", None),
        P(None, "gx", "gz", None),
    )
    out_specs = (P(None, None, ("gx", "gz")), P(None, "gx", "gz", None))
    return jax.shard_map(shards, mesh=mesh, in_specs=in_specs, out_specs=out_specs, check_vma=False)
```

```python
import functools

import jax
import jax.numpy as jnp
from jax import lax
from jax.experimental import pallas as pl
from jax.experimental.pallas import tpu as pltpu
from jax.sharding import PartitionSpec as P

ORDERS = 4
RADIUS = 4
SUBSTEPS = 3
ZRIM = 8
LANES = 128
HEAD = 16
TIME_STEP = 0.5
STENCIL_WEIGHTS = (0.8, -0.2, 4.0 / 105.0, -1.0 / 280.0)
F32 = jnp.float32
BF16 = jnp.bfloat16


def call(kernel, name, outs, ins, scratch=(), flops=1_000_000, after=(), raw=False):
    count, skip = len(ins), len(after)
    nbytes = 4 * sum(x.size for x in ins) + 4 * sum(functools.reduce(lambda m, n: m * n, s, 1) for s in outs)

    def body(*refs):
        kernel(*refs[:count], *refs[count + skip:])

    return pl.pallas_call(
        body,
        out_shape=[jax.ShapeDtypeStruct(s, F32) for s in outs],
        in_specs=[pl.BlockSpec(memory_space=pltpu.HBM if raw else pltpu.VMEM) for _ in ins]
        + [pl.BlockSpec(memory_space=pl.ANY) for _ in after],
        out_specs=[pl.BlockSpec(memory_space=pltpu.HBM if raw else pltpu.VMEM) for _ in outs],
        scratch_shapes=[s if raw else pltpu.VMEM(s, F32) for s in scratch],
        compiler_params=pltpu.CompilerParams(vmem_limit_bytes=(60 if raw else 8) * 1024 * 1024),
        cost_estimate=pl.CostEstimate(flops=flops, bytes_accessed=nbytes, transcendentals=0),
        name=name,
    )(*ins, *after)


def swap(values, axis, odd, by=1):
    count = lax.axis_size(axis)
    pairs = []
    for i in range(count - by):
        if i // by % 2 == odd:
            pairs += [(i, i + by), (i + by, i)]
    return lax.ppermute(values, axis, pairs)


def exchange(xb, zb, xa, za):
    return swap(xb, "gx", 1), swap(zb, "gz", 1), swap(xa, "gx", 0), swap(za, "gz", 0)


def sides(axis, by=1):
    parity = (lax.axis_index(axis) // by) & 1
    return 1 - parity, parity


def by_side(pair, axis, by=1):
    first = sides(axis, by)[0]
    return jnp.where(first == 0, pair[0], pair[1]), jnp.where(first == 1, pair[0], pair[1])


def halves(values):
    high = values.astype(BF16)
    return high, (values - high.astype(F32)).astype(BF16)


def stacked_left(matrix):
    k = matrix.shape[1]
    lane = lax.broadcasted_iota(jnp.int32, (k, 3 * k), 1)
    place = lax.broadcasted_iota(jnp.int32, (k, 3 * k), 0)
    spread = dot_exact(matrix, jnp.where(lane % k == place, 1.0, 0.0).astype(F32))
    high = spread.astype(BF16).astype(F32)
    lane = lax.broadcasted_iota(jnp.int32, spread.shape, 1)
    return jnp.where(lane < 2 * k, high, spread - high).astype(BF16)


def dot3(left, right):
    high, low = halves(right)
    return jnp.dot(left, jnp.concatenate([high, low, high], axis=0), preferred_element_type=F32)


def dot_exact(left, right, dims=(((1,), (0,)), ((), ()))):
    return lax.dot_general(
        left, right, dims, precision=lax.Precision.HIGHEST, preferred_element_type=F32
    )


def flat_slots(table):
    rows, fields, slots = table.shape
    lane = lax.broadcasted_iota(jnp.int32, (slots, LANES), 1)
    place = lax.broadcasted_iota(jnp.int32, (slots, LANES), 0)
    spread = jnp.where(lane % slots == place, 1.0, 0.0).astype(F32)
    lane = lax.broadcasted_iota(jnp.int32, (fields, LANES), 1)
    flat = jnp.zeros((fields, LANES), F32)
    for r in range(rows):
        flat = jnp.where(lane // slots == r, dot_exact(table[r].astype(F32), spread), flat)
    return flat


def pack_x(out, at, source, side):
    fields, nx, nz, ny = source.shape
    start = side * (nx - RADIUS)
    rows = fields * RADIUS * nz
    at = HEAD + at * RADIUS * nz
    out[at:at + rows, :] = source[:, pl.ds(start, RADIUS)].reshape(rows, ny)


def pack_z(out, at, source, side):
    start = pl.multiple_of(side * (source.shape[2] - ZRIM), ZRIM)
    out[pl.ds(at, source.shape[0])] = source[:, :, pl.ds(start, ZRIM), :]


def widen(ext, center, xb, zb, xa, za, first=0):
    fields, nx, nz, ny = center.shape
    ext[:, RADIUS:RADIUS + nx, ZRIM:ZRIM + nz] = center[...]
    for got, side in zip((xa, xb), sides("gx")):
        place = pl.ds(side * (nx + RADIUS), RADIUS)
        if len(got.shape) == 4:
            rows = got[first:first + fields]
        else:
            rows = got[HEAD:HEAD + fields * RADIUS * nz, :].reshape(fields, RADIUS, nz, ny)
        ext[:, place, ZRIM:ZRIM + nz] = rows
    for got, side in zip((za, zb), sides("gz")):
        start = pl.multiple_of(side * (nz + ZRIM), ZRIM)
        ext[:, RADIUS:RADIUS + nx, pl.ds(start, ZRIM)] = got[first:first + fields]


def d1(load, x, lo, hi):
    total = None
    for m, w in enumerate(STENCIL_WEIGHTS, 1):
        term = w * (load(x + m, lo, hi) - load(x - m, lo, hi))
        total = term if total is None else total + term
    return total


def d2(load, x, lo, hi):
    total = None
    for m, w in enumerate(STENCIL_WEIGHTS, 1):
        term = w * (load(x, lo + m, hi + m) - load(x, lo - m, hi - m))
        total = term if total is None else total + term
    return total


def d3(values):
    width = values.shape[1]
    lane = lax.broadcasted_iota(jnp.int32, (1, width), 1)
    total = None
    for m, w in enumerate(STENCIL_WEIGHTS, 1):
        ahead = jnp.where(lane < width - m, w, 0.0) * pltpu.roll(values, width - m, 1)
        behind = jnp.where(lane >= m, w, 0.0) * pltpu.roll(values, m, 1)
        term = ahead - behind
        total = term if total is None else total + term
    return total


def field(ref, c):
    return lambda x, lo, hi: ref[c, x, lo:hi, :]


def plane(ref):
    return lambda x, lo, hi: ref[x, lo:hi, :]


def arrived(lists, da, band, reach, slots):
    lane = lax.broadcasted_iota(jnp.int32, (1, LANES), 1)
    got = jnp.zeros((1, LANES), F32)
    for r in range(reach):
        row = lists[da - (r - reach // 2) + 3][band]
        got = jnp.where((lane & (LANES // 2 - 1)) // slots == r, row, got)
    return got, pltpu.roll(got, LANES // 2, 1)


def cell_masks(cells, rows):
    cells = cells.astype(jnp.int32)
    place = lax.broadcasted_iota(jnp.int32, (rows, LANES), 0)
    third = lax.broadcasted_iota(jnp.int32, (LANES, LANES), 0)
    return cells // LANES == place, cells % LANES == third


def raw_rims_kernel(air, wind, xb, zb, xa, za, sems):
    fields, nx, nz = air.shape[:3]
    copies = []
    for out, side in zip((xb, xa), sides("gx")[::-1]):
        rows = pl.ds(side * (nx - RADIUS), RADIUS)
        copies.append((air.at[:, rows], out.at[0:fields]))
        copies.append((wind.at[:, rows], out.at[fields:]))
    for out, side in zip((zb, za), sides("gz")[::-1]):
        rows = pl.ds(pl.multiple_of(side * (nz - ZRIM), ZRIM), ZRIM)
        copies.append((air.at[:, :, rows], out.at[0:fields]))
        copies.append((wind.at[:, :, rows], out.at[fields:]))
    copies = [pltpu.make_async_copy(a, b, sems.at[i]) for i, (a, b) in enumerate(copies)]
    for copy in copies:
        copy.start()
    for copy in copies:
        copy.wait()


def lanes(at):
    return pl.ds(at if isinstance(at, int) else pl.multiple_of(at, LANES), LANES)


def jacobian_step(jac, rot, emit):
    quants, dims, width = jac.shape[1:]
    rows = rot.shape[0] // dims

    def half(h, carry):
        at = h * LANES
        acc = [None] * quants
        for d in range(dims):
            for q in range(quants):
                turned = rot[d * rows:(d + 1) * rows, lanes(q * width + at)]
                for p in range(quants):
                    term = jac[p, q, d:d + 1, lanes(at)] * turned
                    acc[p] = term if acc[p] is None else acc[p] + term
        for p in range(quants):
            emit(p, at, acc[p])
        return carry

    lax.fori_loop(0, width // LANES, half, 0)


def rotate(rot, left, source, quants, width):
    for q in range(quants):
        cut = slice(q * width, (q + 1) * width)
        rot[:, cut] = dot3(left, source[:, cut])


def take_slots(tiles, index):
    low = index % LANES
    high = index // LANES
    got = None
    for s, tile in enumerate(tiles):
        picked = jnp.take_along_axis(tile, low, axis=1, mode="promise_in_bounds")
        got = picked if got is None else jnp.where(high == s, picked, got)
    return got


def predict_kernel(
    state, jac, stiff, trace, sends, smap, normals,
    integral, traces, own, xa, xb, za, zb, row,
    cur, rot, sp, tp, picked,
):
    quants, basis, width = state.shape
    pad = sp.shape[0] // stiff.shape[0]
    face_basis, faces = trace.shape[:2]
    dims = stiff.shape[0]
    sp[...] = jnp.zeros_like(sp)
    tp[...] = jnp.zeros_like(tp)
    cur[...] = jnp.zeros_like(cur)
    for d in range(dims):
        sp[d * pad:d * pad + basis, 0:basis] = stiff[d]
    for f in range(faces):
        for j in range(face_basis):
            tp[f * 16 + j:f * 16 + j + 1, 0:basis] = trace[j, f:f + 1, :]
    for q in range(quants):
        cur[0:basis, q * width:(q + 1) * width] = state[q]
    integral[...] = TIME_STEP * cur[...]
    left = stacked_left(sp[...])

    def degree(k, weight):
        weight = jnp.where(k == 1, TIME_STEP**2 / 2, jnp.where(k == 2, TIME_STEP**3 / 6, TIME_STEP**4 / 24))
        rotate(rot, left, cur, quants, width)

        def emit(p, at, value):
            cut = lanes(p * width + at)
            cur[0:pad, cut] = -value
            integral[0:pad, cut] = integral[0:pad, cut] - weight * value

        jacobian_step(jac, rot, emit)
        return weight

    lax.fori_loop(1, ORDERS, degree, F32(0))
    restrict = stacked_left(tp[...])
    for q in range(quants):
        cut = slice(q * width, (q + 1) * width)
        done = dot3(restrict, integral[:, cut])
        for f in range(faces):
            traces[q, :, f * width:(f + 1) * width] = done[f * 16:(f + 1) * 16]
    slots = flat_slots(smap)
    wanted = [jnp.broadcast_to(sends[d:d + 1, :], (16, LANES)) for d in range(4)]
    wanted.append(jnp.broadcast_to(slots[0:1].astype(jnp.int32), (16, LANES)))
    tiles_in = faces * width // LANES

    def gather(q, carry):
        tiles = [traces[q, :, s * LANES:(s + 1) * LANES] for s in range(tiles_in)]
        for d in range(4):
            picked[d, q] = take_slots(tiles, wanted[d])
        own[q] = take_slots(tiles, wanted[4])
        return carry

    lax.fori_loop(0, quants, gather, 0)
    for axis, base, outs in (("gx", 0, (xa, xb)), ("gz", 2, (za, zb))):
        for out, side in zip(outs, sides(axis)):
            for q in range(quants):
                out[q * 8:q * 8 + 8, :] = picked[base + side, q, 0:8, :]
                out[quants * 8 + q * 2:quants * 8 + q * 2 + 2, :] = picked[base + side, q, 8:face_basis, :]
            out[quants * face_basis:, :] = jnp.zeros((out.shape[0] - quants * face_basis, LANES), F32)
    normal = flat_slots(normals)
    speed = jnp.zeros((1, LANES), F32)
    for c in range(3):
        mean = jnp.sum(own[6 + c, 0:face_basis, :], axis=0, keepdims=True) * (1.0 / face_basis)
        speed = speed + normal[c:c + 1] * mean
    lane = lax.broadcasted_iota(jnp.int32, (1, LANES), 1)
    cells = pltpu.roll(slots[1:2], LANES // 2, 1)
    row[...] = jnp.broadcast_to(jnp.where(lane < LANES // 2, slots[2:3] * speed, cells), row.shape)


def pressure_rows(ext, wind, medium, x, nz):
    lo, hi = ZRIM, ZRIM + nz
    xe = x + RADIUS
    pressure = field(ext, 0)
    here = pressure(xe, lo, hi)
    divergence = d1(field(ext, 1), xe, lo, hi) + d2(field(ext, 2), xe, lo, hi) + d3(ext[3, xe, lo:hi, :])
    moved = (
        wind[0, x] * d1(pressure, xe, lo, hi)
        + wind[1, x] * d2(pressure, xe, lo, hi)
        + wind[2, x] * d3(here)
    )
    return here - medium[0, x] * divergence - moved


def pack_pressure(center, xs, zs):
    nx, nz, ny = center.shape[1:]
    for out, side in zip(xs, sides("gx")):
        start = side * (nx - RADIUS)
        out[HEAD:HEAD + RADIUS * nz, :] = center[0, pl.ds(start, RADIUS)].reshape(RADIUS * nz, ny)
    for out, side in zip(zs, sides("gz")):
        start = pl.multiple_of(side * (nz - ZRIM), ZRIM)
        out[HEAD:HEAD + nx * ZRIM, :] = center[0, :, pl.ds(start, ZRIM), :].reshape(nx * ZRIM, ny)


def widen_pressure(ext, center, xb, zb, xa, za):
    nx, nz, ny = center.shape
    ext[RADIUS:RADIUS + nx, ZRIM:ZRIM + nz] = center[...]
    for got, side in zip((xa, xb), sides("gx")):
        ext[pl.ds(side * (nx + RADIUS), RADIUS), ZRIM:ZRIM + nz] = got[HEAD:HEAD + RADIUS * nz, :].reshape(RADIUS, nz, ny)
    for got, side in zip((za, zb), sides("gz")):
        start = pl.multiple_of(side * (nz + ZRIM), ZRIM)
        ext[RADIUS:RADIUS + nx, pl.ds(start, ZRIM)] = got[HEAD:HEAD + nx * ZRIM, :].reshape(nx, ZRIM, ny)


def same_kernel(values, out):
    out[...] = values[...]


def raw_pressure_kernel(air, wind, medium, xb, zb, xa, za, tza, tzb, row, fa, fb, pressure, ozb, oza, ext):
    nx, nz, ny = air.shape[1:]
    widen(ext, air, xb, zb, xa, za)
    for x in range(nx):
        pressure[0, x] = pressure_rows(ext, wind, medium, x, nz)
    pack_pressure(pressure, (), (oza, ozb))
    lists = put_rows((row[0:1, :], *by_side((fa[0:1, :], fb[0:1, :]), "gx", 2)))
    for out, sent in zip((oza, ozb), (tza, tzb)):
        out[0:HEAD, :] = lists
        out[out.shape[0] - sent.shape[0]:, :] = sent[...]


def put_rows(rows):
    place = lax.broadcasted_iota(jnp.int32, (HEAD, LANES), 0)
    out = jnp.zeros((HEAD, LANES), F32)
    for at, row in enumerate(rows):
        out = jnp.where(place == at, row, out)
    return out


def merge_kernel(raw, txa, txb, zb, za, row, fa, fb, oxb, oxa, lists):
    far = by_side((fa[0:1, :], fb[0:1, :]), "gx", 2)
    low, high = by_side((za[0:HEAD, :], zb[0:HEAD, :]), "gz")
    rows = [row[0:1, :], *far]
    for band in (low, high):
        rows += [band[s:s + 1] for s in range(3)]
    lists[...] = put_rows(rows)
    pack_pressure(raw, (oxa, oxb), ())
    for out, sent in zip((oxa, oxb), (txa, txb)):
        out[0:HEAD, :] = lists[...]
        out[out.shape[0] - sent.shape[0]:, :] = sent[...]


def advection_kernel(air, wind, xb, zb, xa, za, moved, ext):
    nx, nz, ny = air.shape[1:]
    widen(ext, air, xb, zb, xa, za)
    lo, hi = ZRIM, ZRIM + nz
    for x in range(nx):
        xe = x + RADIUS
        for c in range(3):
            load = field(ext, 1 + c)
            moved[c, x] = (
                wind[0, x] * d1(load, xe, lo, hi)
                + wind[1, x] * d2(load, xe, lo, hi)
                + wind[2, x] * d3(load(xe, lo, hi))
            )


def velocities(out, center, moved, medium, wide, nx, nz):
    lo, hi = ZRIM, ZRIM + nz
    load = plane(wide)
    for x in range(nx):
        xe = x + RADIUS
        slopes = (d1(load, xe, lo, hi), d2(load, xe, lo, hi), d3(load(xe, lo, hi)))
        out[0, x] = load(xe, lo, hi)
        for c in range(3):
            out[1 + c, x] = center[1 + c, x] - medium[1, x] * slopes[c] - moved[c, x]


def pack_air(out, xb, zb, xa, za):
    for rim, side in zip((xa, xb), sides("gx")):
        pack_x(rim, 0, out, side)
    for rim, side in zip((za, zb), sides("gz")):
        pack_z(rim, 0, out, side)


def injected_kernel(
    air, wind, medium, raw, moved, wxb, wzb, wxa, wza, pxb, pzb, pxa, pza, near, smap,
    out, oxb, ozb, oxa, oza, answer, spread, wide, wide_wind,
):
    nx, nz, ny = air.shape[1:]
    reach, _, slots = smap.shape
    used = lax.broadcasted_iota(jnp.int32, (nx * nz, LANES), 1) < reach * slots
    low, high = by_side((pxa[0:HEAD, :], pxb[0:HEAD, :]), "gx")
    own = near[...]
    lists = [
        [table[3 * t + s:3 * t + s + 1] for t in range(3)]
        for table, s in ((low, 1), (own, 1), (low, 0), (own, 0), (high, 0), (own, 2), (high, 2))
    ]
    mul = functools.partial(
        lax.dot_general, dimension_numbers=(((1,), (1,)), ((), ())), preferred_element_type=F32
    )
    for da in range(3):
        for db in range(3):
            speed, cells = arrived(lists, da - 1, (1, 0, 2)[db], reach, slots)
            row_mask, third_mask = cell_masks(cells, nx * nz)
            high, low = halves(jnp.where(row_mask & used, speed, 0.0))
            columns = jnp.where(third_mask, 1.0, 0.0).astype(BF16)
            if da == 1 and db == 1:
                seen, rest = halves(air[0].reshape(nx * nz, ny))
                looked = jnp.dot(seen, columns, preferred_element_type=F32)
                looked = looked + jnp.dot(rest, columns, preferred_element_type=F32)
                answer[...] = jnp.sum(jnp.where(row_mask, looked, 0.0), axis=0, keepdims=True)
            block = mul(high, columns) + mul(low, columns)
            spread[da * nx:(da + 1) * nx, db * nz:(db + 1) * nz] = block.reshape(nx, nz, ny)
    widen(wide_wind, wind, wxb, wzb, wxa, wza, first=air.shape[0])
    widen_pressure(wide, raw.at[0], pxb, pzb, pxa, pza)
    load = plane(spread)
    for x in range(nx + 2 * RADIUS):
        xs = x + nx - RADIUS
        if RADIUS <= x < RADIUS + nx:
            lo, hi = 0, nz + 2 * ZRIM
        else:
            lo, hi = ZRIM, ZRIM + nz
        slo, shi = lo + nz - ZRIM, hi + nz - ZRIM
        here = load(xs, slo, shi)
        turned = (
            wide_wind[0, x, lo:hi, :] * d1(load, xs, slo, shi)
            + wide_wind[1, x, lo:hi, :] * d2(load, xs, slo, shi)
            + wide_wind[2, x, lo:hi, :] * d3(here)
        )
        wide[x, lo:hi, :] = wide[x, lo:hi, :] + (here - turned)
    velocities(out, air, moved, medium, wide, nx, nz)
    pack_air(out, oxb, ozb, oxa, oza)
    for rim in (oxa, oxb):
        rim[0:HEAD, :] = put_rows((answer[...],))


def pressure_kernel(air, wind, medium, xb, zb, xa, za, answer, pressure, oxb, ozb, oxa, oza, ext):
    nx, nz, ny = air.shape[1:]
    widen(ext, air, xb, zb, xa, za)
    for x in range(nx):
        pressure[0, x] = pressure_rows(ext, wind, medium, x, nz)
    pack_pressure(pressure, (oxa, oxb), (oza, ozb))
    low, high = by_side((xa[0:1, :], xb[0:1, :]), "gx")
    for rim in (oxa, oxb):
        rim[0:HEAD, :] = put_rows((answer[...], low, high))
    for rim in (oza, ozb):
        rim[0:HEAD, :] = jnp.zeros((HEAD, LANES), F32)


def velocity_kernel(air, pressure, medium, moved, xb, zb, xa, za, out, *rest):
    nx, nz, ny = air.shape[1:]
    wide = rest[-1]
    widen_pressure(wide, pressure.at[0], xb, zb, xa, za)
    velocities(out, air, moved, medium, wide, nx, nz)
    if len(rest) > 1:
        pack_air(out, *rest[:-1])
        for rim in (rest[0], rest[2]):
            rim[0:HEAD, :] = jnp.zeros((HEAD, LANES), F32)


def volume_kernel(state, integral, jac, stiff, out, token, rot, sp):
    quants, basis, width = state.shape
    dims = stiff.shape[0]
    pad = sp.shape[0] // dims
    token[...] = jnp.zeros_like(token)
    sp[...] = jnp.zeros_like(sp)
    place = lax.broadcasted_iota(jnp.int32, (basis, basis), 0)
    other = lax.broadcasted_iota(jnp.int32, (basis, basis), 1)
    unit = jnp.where(place == other, 1.0, 0.0).astype(F32)
    for d in range(dims):
        sp[d * pad:d * pad + basis, 0:basis] = dot_exact(unit, stiff[d], (((1,), (1,)), ((), ())))
    rotate(rot, stacked_left(sp[...]), integral, quants, width)

    def emit(p, at, value):
        out[p, :, lanes(at)] = state[p, :, lanes(at)] + value[0:basis]

    jacobian_step(jac, rot, emit)


def flux_kernel(
    first, faces, base, traces, own, solvers, lift, neighbours, smap, xb, zb, xa, za, *rest
):
    answer, rxb, rxa = rest[:3] if len(rest) > 5 else (None,) * 3
    out, token, tiles, flux, lp = rest[-5:]
    token[...] = jnp.zeros_like(token)
    quants, basis, width = base.shape
    face_basis, all_faces = lift.shape[:2]
    reach, _, slots = smap.shape
    skip = xa.shape[0] - sent_rows(quants, face_basis)
    for axis, base_tile, gots in (("gx", 0, (xa, xb)), ("gz", 2, (za, zb))):
        for got, side in zip(gots, sides(axis)):
            for q in range(quants):
                tiles[q, base_tile + side, 0:8, :] = got[skip + q * 8:skip + q * 8 + 8, :]
                at = skip + quants * 8 + q * 2
                tiles[q, base_tile + side, 8:face_basis, :] = got[at:at + 2, :]
                tiles[q, base_tile + side, face_basis:, :] = jnp.zeros((16 - face_basis, LANES), F32)
    for q in range(quants):
        tiles[q, 4] = -own[q] if q < 3 else own[q]
    lp[...] = jnp.zeros_like(lp)
    for f in range(faces):
        for j in range(face_basis):
            lp[f * 16 + j:f * 16 + j + 1, 0:basis] = lift[j, first + f:first + f + 1, :]
    unit = lax.broadcasted_iota(jnp.int32, (lp.shape[1], lp.shape[1]), 0) == lax.broadcasted_iota(
        jnp.int32, (lp.shape[1], lp.shape[1]), 1
    )
    lifted = dot_exact(jnp.where(unit, 1.0, 0.0).astype(F32), lp[...], (((1,), (1,)), ((), ())))
    lifted = stacked_left(lifted)
    local = traces.shape[2] // LANES
    halves_in = width // LANES

    def one(h, carry):
        at = h * LANES
        for f in range(faces):
            index = jnp.broadcast_to(neighbours[first + f:first + f + 1, lanes(at)], (16, LANES))
            acc = [None] * quants
            for q in range(quants):
                pool = [traces[q, :, s * LANES:(s + 1) * LANES] for s in range(local)]
                pool += [tiles[q, s] for s in range(5)]
                mine = traces[q, :, lanes((first + f) * width + at)]
                jump = take_slots(pool, index) - mine
                for p in range(quants):
                    term = solvers[p, q, first + f:first + f + 1, lanes(at)] * jump
                    acc[p] = term if acc[p] is None else acc[p] + term
            for p in range(quants):
                flux[f * 16:(f + 1) * 16, lanes(p * width + at)] = acc[p]
        return carry

    lax.fori_loop(0, halves_in, one, 0)
    for p in range(quants):
        cut = slice(p * width, (p + 1) * width)
        out[p] = base[p] + dot3(lifted, flux[:, cut])[0:basis]
    if answer is None:
        return
    low, high = by_side((rxa[0:HEAD, :], rxb[0:HEAD, :]), "gx")
    lane = lax.broadcasted_iota(jnp.int32, (1, LANES), 1)
    replies = jnp.zeros((1, LANES), F32)
    for r, row in enumerate((low[1:2], low[0:1], answer[...], high[0:1], high[2:3])):
        replies = jnp.where(lane // slots == r, row, replies)
    replies = jnp.broadcast_to(-2.0 * replies * flat_slots(smap)[2:3], (8, LANES))
    begin = (local + 4) * LANES
    for f in range(all_faces):
        column = lift[0, f:f + 1, :]
        for j in range(1, face_basis):
            column = column + lift[j, f:f + 1, :]
        square = lax.broadcasted_iota(jnp.int32, (basis, basis), 0) == lax.broadcasted_iota(
            jnp.int32, (basis, basis), 1
        )
        column = jnp.sum(jnp.where(square, column, 0.0), axis=1, keepdims=True)
        for h in range(halves_in):
            at = h * LANES
            index = jnp.broadcast_to(neighbours[f:f + 1, at:at + LANES], (8, LANES))
            found = jnp.take_along_axis(replies, index % LANES, axis=1, mode="promise_in_bounds")
            found = jnp.where(index >= begin, found, 0.0)[0:1]
            spread = column * found
            for p in range(quants):
                both = solvers[p, 0, f:f + 1, at:at + LANES]
                for q in range(1, 3):
                    both = both + solvers[p, q, f:f + 1, at:at + LANES]
                out[p, :, at:at + LANES] = out[p, :, at:at + LANES] + both * spread


def sent_rows(quants, face_basis):
    return -(-quants * face_basis // 8) * 8


def shards(
    solid_state, jacobians, flux_solvers, stiffness, trace_matrix, lift_matrix,
    neighbours, send_faces, surface_map, surface_normals, air_state, wind_field, air_medium,
):
    quants, basis, width = solid_state.shape
    faces, face_basis = trace_matrix.shape[0], trace_matrix.shape[1]
    dims = stiffness.shape[0]
    nx, nz, ny = air_state.shape[1:]
    jacobians = jnp.transpose(jacobians, (1, 2, 0, 3))
    flux_solvers = jnp.transpose(flux_solvers, (1, 2, 0, 3))
    trace_matrix = jnp.transpose(trace_matrix, (1, 0, 2))
    lift_matrix = jnp.transpose(lift_matrix, (2, 0, 1))
    surface_map = jnp.transpose(surface_map, (1, 0, 2))
    surface_normals = jnp.transpose(surface_normals, (1, 0, 2))
    pad = -(-basis // 8) * 8
    pad_k = -(-basis // 16) * 16
    rim_z = (7, nx, ZRIM, ny)
    rim_x = (7, RADIUS, nz, ny)
    ext = (4, nx + 2 * RADIUS, nz + 2 * ZRIM, ny)
    wide = ext[1:]
    block = (1, nx, nz, ny)
    tile = (8, LANES)

    rims = exchange(
        *call(
            raw_rims_kernel, "raw_rims", [rim_x, rim_z, rim_x, rim_z], [air_state, wind_field],
            [pltpu.SemaphoreType.DMA((8,))], raw=True,
        )
    )

    sent = (sent_rows(quants, face_basis), LANES)
    integral, traces, own, txa, txb, tza, tzb, row = call(
        predict_kernel, "predict",
        [(pad_k, quants * width), (quants, 16, faces * width), (quants, 16, LANES), sent, sent, sent, sent,
         tile],
        [solid_state, jacobians, stiffness, trace_matrix, send_faces, surface_map, surface_normals],
        [(pad_k, quants * width), (dims * pad, quants * width), (dims * pad, pad_k), (faces * 16, pad_k),
         (4, quants, 16, LANES)],
        flops=40_000_000,
    )
    (own_list,) = call(same_kernel, "own_list", [tile], [row], after=[rims[1], rims[3]])
    far = swap(own_list, "gx", 0, 2), swap(own_list, "gx", 1, 2)
    pressure_x = (HEAD + RADIUS * nz, ny)
    pressure_z = (HEAD + nx * ZRIM, ny)
    both_x = (pressure_x[0] + sent[0], LANES)
    both_z = (pressure_z[0] + sent[0], LANES)
    raw, zb, za = call(
        raw_pressure_kernel, "raw_pressure", [block, both_z, both_z],
        [air_state, wind_field, air_medium, *rims, tza, tzb, row, *far], [ext],
    )
    both_zb, both_za = swap(zb, "gz", 1), swap(za, "gz", 0)
    (moved,) = call(
        advection_kernel, "advection", [(3, nx, nz, ny)],
        [air_state, wind_field, *rims], [ext], flops=10_000_000, after=[za],
    )
    xb, xa, lists = call(
        merge_kernel, "merge", [both_x, both_x, (HEAD, LANES)], [raw, txa, txb, both_zb, both_za, row, *far]
    )
    both_xb, both_xa = swap(xb, "gx", 1), swap(xa, "gx", 0)
    both = both_xb, both_zb, both_xa, both_za
    volume, token = call(
        volume_kernel, "volume", [solid_state.shape, tile], [solid_state, integral, jacobians, stiffness],
        [(dims * pad, quants * width), (dims * pad, pad_k)], flops=10_000_000, after=[lists],
    )

    rim_x = (HEAD + 4 * RADIUS * nz, ny)
    rim_z = (4, nx, ZRIM, ny)
    air, xb, zb, xa, za, answer = call(
        injected_kernel, "injected",
        [air_state.shape, rim_x, rim_z, rim_x, rim_z, (1, LANES)],
        [air_state, wind_field, air_medium, raw, moved, *rims, *both, lists, surface_map],
        [(3 * nx, 3 * nz, ny), wide, (3,) + wide], after=[token],
    )
    half = faces // 2
    solid = volume
    replies = []
    for substep in range(1, SUBSTEPS):
        rims = exchange(xb, zb, xa, za)
        solid, token = call(
            functools.partial(flux_kernel, (substep - 1) * half, half), "flux", [solid_state.shape, tile],
            [solid, traces, own, flux_solvers, lift_matrix, neighbours, surface_map, *both, *replies],
            [(quants, 5, 16, LANES), (half * 16, quants * width), (half * 16, pad)], flops=20_000_000,
            after=[xa],
        )
        pressure, xb, zb, xa, za = call(
            pressure_kernel, "pressure", [block, pressure_x, pressure_z, pressure_x, pressure_z],
            [air, wind_field, air_medium, *rims, answer], [ext], after=[token],
        )
        rises = exchange(xb, zb, xa, za)
        if substep == 1:
            replies = [answer, rises[0], rises[2]]
        (moved,) = call(
            advection_kernel, "advection", [(3, nx, nz, ny)],
            [air, wind_field, *rims], [ext], flops=10_000_000, after=[xa],
        )
        last = substep == SUBSTEPS - 1
        outs = [air_state.shape] + ([] if last else [rim_x, rim_z, rim_x, rim_z])
        done = call(
            velocity_kernel, "velocity", outs, [air, pressure, air_medium, moved, *rises], [wide]
        )
        air = done[0]
        if not last:
            xb, zb, xa, za = done[1:]
    return (solid, air)


def solution(mesh):
    in_specs = (
        P(None, None, ("gx", "gz")),
        P(None, None, None, ("gx", "gz")),
        P(None, None, None, ("gx", "gz")),
        P(),
        P(),
        P(),
        P(None, ("gx", "gz")),
        P(None, ("gx", "gz")),
        P(None, None, ("gx", "gz")),
        P(None, None, ("gx", "gz")),
        P(None, "gx", "gz", None),
        P(None, "gx", "gz", None),
        P(None, "gx", "gz", None),
    )
    out_specs = (P(None, None, ("gx", "gz")), P(None, "gx", "gz", None))
    return jax.shard_map(shards, mesh=mesh, in_specs=in_specs, out_specs=out_specs, check_vma=False)
```

```python
import functools

import jax
import jax.numpy as jnp
from jax import lax
from jax.experimental import pallas as pl
from jax.experimental.pallas import tpu as pltpu
from jax.sharding import PartitionSpec as P

ORDERS = 4
RADIUS = 4
SUBSTEPS = 3
ZRIM = 8
LANES = 128
HEAD = 16
TIME_STEP = 0.5
STENCIL_WEIGHTS = (0.8, -0.2, 4.0 / 105.0, -1.0 / 280.0)
F32 = jnp.float32
BF16 = jnp.bfloat16


def call(kernel, name, outs, ins, scratch=(), flops=1_000_000, after=()):
    count, skip = len(ins), len(after)
    nbytes = 4 * sum(x.size for x in ins) + 4 * sum(functools.reduce(lambda m, n: m * n, s, 1) for s in outs)

    def body(*refs):
        kernel(*refs[:count], *refs[count + skip:])

    return pl.pallas_call(
        body,
        out_shape=[jax.ShapeDtypeStruct(s, F32) for s in outs],
        in_specs=[pl.BlockSpec(memory_space=pltpu.VMEM) for _ in ins]
        + [pl.BlockSpec(memory_space=pl.ANY) for _ in after],
        out_specs=[pl.BlockSpec(memory_space=pltpu.VMEM) for _ in outs],
        scratch_shapes=[pltpu.VMEM(s, F32) for s in scratch],
        compiler_params=pltpu.CompilerParams(vmem_limit_bytes=8 * 1024 * 1024),
        cost_estimate=pl.CostEstimate(flops=flops, bytes_accessed=nbytes, transcendentals=0),
        name=name,
    )(*ins, *after)


def swap(values, axis, odd, by=1):
    count = lax.axis_size(axis)
    pairs = []
    for i in range(count - by):
        if i // by % 2 == odd:
            pairs += [(i, i + by), (i + by, i)]
    return lax.ppermute(values, axis, pairs)


def exchange(xb, zb, xa, za):
    return swap(xb, "gx", 1), swap(zb, "gz", 1), swap(xa, "gx", 0), swap(za, "gz", 0)


def sides(axis, by=1):
    parity = (lax.axis_index(axis) // by) & 1
    return 1 - parity, parity


def by_side(pair, axis, by=1):
    first = sides(axis, by)[0]
    return jnp.where(first == 0, pair[0], pair[1]), jnp.where(first == 1, pair[0], pair[1])


def halves(values):
    high = values.astype(BF16)
    return high, (values - high.astype(F32)).astype(BF16)


def stacked_left(matrix):
    k = matrix.shape[1]
    lane = lax.broadcasted_iota(jnp.int32, (k, 3 * k), 1)
    place = lax.broadcasted_iota(jnp.int32, (k, 3 * k), 0)
    spread = dot_exact(matrix, jnp.where(lane % k == place, 1.0, 0.0).astype(F32))
    high = spread.astype(BF16).astype(F32)
    lane = lax.broadcasted_iota(jnp.int32, spread.shape, 1)
    return jnp.where(lane < 2 * k, high, spread - high).astype(BF16)


def dot3(left, right):
    high, low = halves(right)
    return jnp.dot(left, jnp.concatenate([high, low, high], axis=0), preferred_element_type=F32)


def dot_exact(left, right, dims=(((1,), (0,)), ((), ()))):
    return lax.dot_general(
        left, right, dims, precision=lax.Precision.HIGHEST, preferred_element_type=F32
    )


def flat_slots(table):
    rows, fields, slots = table.shape
    lane = lax.broadcasted_iota(jnp.int32, (slots, LANES), 1)
    place = lax.broadcasted_iota(jnp.int32, (slots, LANES), 0)
    spread = jnp.where(lane % slots == place, 1.0, 0.0).astype(F32)
    lane = lax.broadcasted_iota(jnp.int32, (fields, LANES), 1)
    flat = jnp.zeros((fields, LANES), F32)
    for r in range(rows):
        flat = jnp.where(lane // slots == r, dot_exact(table[r].astype(F32), spread), flat)
    return flat


def pack_x(out, at, source, side):
    fields, nx, nz, ny = source.shape
    start = side * (nx - RADIUS)
    rows = fields * RADIUS * nz
    at = HEAD + at * RADIUS * nz
    out[at:at + rows, :] = source[:, pl.ds(start, RADIUS)].reshape(rows, ny)


def pack_z(out, at, source, side):
    start = pl.multiple_of(side * (source.shape[2] - ZRIM), ZRIM)
    out[pl.ds(at, source.shape[0])] = source[:, :, pl.ds(start, ZRIM), :]


def widen(ext, center, xb, zb, xa, za, first=0):
    fields, nx, nz, ny = center.shape
    ext[:, RADIUS:RADIUS + nx, ZRIM:ZRIM + nz] = center[...]
    for got, side in zip((xa, xb), sides("gx")):
        place = pl.ds(side * (nx + RADIUS), RADIUS)
        if len(got.shape) == 4:
            rows = got[first:first + fields]
        else:
            rows = got[HEAD:HEAD + fields * RADIUS * nz, :].reshape(fields, RADIUS, nz, ny)
        ext[:, place, ZRIM:ZRIM + nz] = rows
    for got, side in zip((za, zb), sides("gz")):
        start = pl.multiple_of(side * (nz + ZRIM), ZRIM)
        ext[:, RADIUS:RADIUS + nx, pl.ds(start, ZRIM)] = got[first:first + fields]


def d1(load, x, lo, hi):
    total = None
    for m, w in enumerate(STENCIL_WEIGHTS, 1):
        term = w * (load(x + m, lo, hi) - load(x - m, lo, hi))
        total = term if total is None else total + term
    return total


def d2(load, x, lo, hi):
    total = None
    for m, w in enumerate(STENCIL_WEIGHTS, 1):
        term = w * (load(x, lo + m, hi + m) - load(x, lo - m, hi - m))
        total = term if total is None else total + term
    return total


def d3(values):
    width = values.shape[1]
    lane = lax.broadcasted_iota(jnp.int32, (1, width), 1)
    total = None
    for m, w in enumerate(STENCIL_WEIGHTS, 1):
        ahead = jnp.where(lane < width - m, w, 0.0) * pltpu.roll(values, width - m, 1)
        behind = jnp.where(lane >= m, w, 0.0) * pltpu.roll(values, m, 1)
        term = ahead - behind
        total = term if total is None else total + term
    return total


def field(ref, c):
    return lambda x, lo, hi: ref[c, x, lo:hi, :]


def plane(ref):
    return lambda x, lo, hi: ref[x, lo:hi, :]


def arrived(lists, da, band, reach, slots):
    lane = lax.broadcasted_iota(jnp.int32, (1, LANES), 1)
    got = jnp.zeros((1, LANES), F32)
    for r in range(reach):
        row = lists[da - (r - reach // 2) + 3][band]
        got = jnp.where((lane & (LANES // 2 - 1)) // slots == r, row, got)
    return got, pltpu.roll(got, LANES // 2, 1)


def cell_masks(cells, rows):
    cells = cells.astype(jnp.int32)
    place = lax.broadcasted_iota(jnp.int32, (rows, LANES), 0)
    third = lax.broadcasted_iota(jnp.int32, (LANES, LANES), 0)
    return cells // LANES == place, cells % LANES == third


def raw_rims_kernel(air, wind, xb, zb, xa, za):
    fields, nx = air.shape[:2]
    for out, side in zip((xa, xb), sides("gx")):
        rows = pl.ds(side * (nx - RADIUS), RADIUS)
        out[0:fields] = air[:, rows]
        out[fields:] = wind[:, rows]
    for out, side in zip((za, zb), sides("gz")):
        pack_z(out, 0, air, side)
        pack_z(out, fields, wind, side)


def lanes(at):
    return pl.ds(at if isinstance(at, int) else pl.multiple_of(at, LANES), LANES)


def jacobian_step(load, rot, emit, quants, dims, width):
    rows = rot.shape[0] // dims

    def half(h, carry):
        at = h * LANES
        acc = [None] * quants
        for d in range(dims):
            for q in range(quants):
                turned = rot[d * rows:(d + 1) * rows, lanes(q * width + at)].reshape(rows // 8, 8, LANES)
                for p in range(quants):
                    term = load(p, q, d, lanes(at)) * turned
                    acc[p] = term if acc[p] is None else acc[p] + term
        for p in range(quants):
            emit(p, at, acc[p].reshape(rows, LANES))
        return carry

    lax.fori_loop(0, width // LANES, half, 0)


def rotate(rot, left, source, quants, width):
    for q in range(quants):
        cut = slice(q * width, (q + 1) * width)
        rot[:, cut] = dot3(left, source[:, cut])


def take_slots(tiles, index):
    low = index % LANES
    high = index // LANES
    got = None
    for s, tile in enumerate(tiles):
        picked = jnp.take_along_axis(tile, low, axis=1, mode="promise_in_bounds")
        got = picked if got is None else jnp.where(high == s, picked, got)
    return got


def predict_kernel(
    state, jac, stiff, trace, sends, smap, normals,
    integral, traces, own, xa, xb, za, zb, row,
    cur, rot, sp, tp, picked, full,
):
    quants, basis, width = state.shape
    pad = sp.shape[0] // stiff.shape[0]
    face_basis, faces = trace.shape[:2]
    dims = stiff.shape[0]
    for d in range(dims):

        def spread(p, carry):
            for q in range(quants):
                full[p, q, d] = jnp.broadcast_to(jac[p, q, d:d + 1, :], (8, width))
            return carry

        lax.fori_loop(0, quants, spread, 0)
    sp[...] = jnp.zeros_like(sp)
    tp[...] = jnp.zeros_like(tp)
    cur[...] = jnp.zeros_like(cur)
    for d in range(dims):
        sp[d * pad:d * pad + basis, 0:basis] = stiff[d]
    for f in range(faces):
        for j in range(face_basis):
            tp[f * 16 + j:f * 16 + j + 1, 0:basis] = trace[j, f:f + 1, :]
    for q in range(quants):
        cur[0:basis, q * width:(q + 1) * width] = state[q]
    integral[...] = TIME_STEP * cur[...]
    left = stacked_left(sp[...])

    def degree(k, weight):
        weight = jnp.where(k == 1, TIME_STEP**2 / 2, jnp.where(k == 2, TIME_STEP**3 / 6, TIME_STEP**4 / 24))
        rotate(rot, left, cur, quants, width)

        def emit(p, at, value):
            cut = lanes(p * width + at)
            cur[0:pad, cut] = -value
            integral[0:pad, cut] = integral[0:pad, cut] - weight * value

        jacobian_step(lambda p, q, d, cut: full[p, q, d, :, cut], rot, emit, quants, dims, width)
        return weight

    lax.fori_loop(1, ORDERS, degree, F32(0))
    restrict = stacked_left(tp[...])
    for q in range(quants):
        cut = slice(q * width, (q + 1) * width)
        done = dot3(restrict, integral[:, cut])
        for f in range(faces):
            traces[q, :, f * width:(f + 1) * width] = done[f * 16:(f + 1) * 16]
    slots = flat_slots(smap)
    wanted = [jnp.broadcast_to(sends[d:d + 1, :], (16, LANES)) for d in range(4)]
    wanted.append(jnp.broadcast_to(slots[0:1].astype(jnp.int32), (16, LANES)))
    tiles_in = faces * width // LANES

    def gather(q, carry):
        tiles = [traces[q, :, s * LANES:(s + 1) * LANES] for s in range(tiles_in)]
        for d in range(4):
            picked[d, q] = take_slots(tiles, wanted[d])
        own[q] = take_slots(tiles, wanted[4])
        return carry

    lax.fori_loop(0, quants, gather, 0)
    for axis, base, outs in (("gx", 0, (xa, xb)), ("gz", 2, (za, zb))):
        for out, side in zip(outs, sides(axis)):
            for q in range(quants):
                out[q * 8:q * 8 + 8, :] = picked[base + side, q, 0:8, :]
                out[quants * 8 + q * 2:quants * 8 + q * 2 + 2, :] = picked[base + side, q, 8:face_basis, :]
            out[quants * face_basis:, :] = jnp.zeros((out.shape[0] - quants * face_basis, LANES), F32)
    normal = flat_slots(normals)
    speed = jnp.zeros((1, LANES), F32)
    for c in range(3):
        mean = jnp.sum(own[6 + c, 0:face_basis, :], axis=0, keepdims=True) * (1.0 / face_basis)
        speed = speed + normal[c:c + 1] * mean
    lane = lax.broadcasted_iota(jnp.int32, (1, LANES), 1)
    cells = pltpu.roll(slots[1:2], LANES // 2, 1)
    row[...] = jnp.broadcast_to(jnp.where(lane < LANES // 2, slots[2:3] * speed, cells), row.shape)


def pressure_rows(ext, wind, medium, x, nz):
    lo, hi = ZRIM, ZRIM + nz
    xe = x + RADIUS
    pressure = field(ext, 0)
    here = pressure(xe, lo, hi)
    divergence = d1(field(ext, 1), xe, lo, hi) + d2(field(ext, 2), xe, lo, hi) + d3(ext[3, xe, lo:hi, :])
    moved = (
        wind[0, x] * d1(pressure, xe, lo, hi)
        + wind[1, x] * d2(pressure, xe, lo, hi)
        + wind[2, x] * d3(here)
    )
    return here - medium[0, x] * divergence - moved


def pack_pressure(center, xs, zs):
    nx, nz, ny = center.shape[1:]
    for out, side in zip(xs, sides("gx")):
        start = side * (nx - RADIUS)
        out[HEAD:HEAD + RADIUS * nz, :] = center[0, pl.ds(start, RADIUS)].reshape(RADIUS * nz, ny)
    for out, side in zip(zs, sides("gz")):
        start = pl.multiple_of(side * (nz - ZRIM), ZRIM)
        out[HEAD:HEAD + nx * ZRIM, :] = center[0, :, pl.ds(start, ZRIM), :].reshape(nx * ZRIM, ny)


def widen_pressure(ext, center, xb, zb, xa, za):
    nx, nz, ny = center.shape
    ext[RADIUS:RADIUS + nx, ZRIM:ZRIM + nz] = center[...]
    for got, side in zip((xa, xb), sides("gx")):
        ext[pl.ds(side * (nx + RADIUS), RADIUS), ZRIM:ZRIM + nz] = got[HEAD:HEAD + RADIUS * nz, :].reshape(RADIUS, nz, ny)
    for got, side in zip((za, zb), sides("gz")):
        start = pl.multiple_of(side * (nz + ZRIM), ZRIM)
        ext[RADIUS:RADIUS + nx, pl.ds(start, ZRIM)] = got[HEAD:HEAD + nx * ZRIM, :].reshape(nx, ZRIM, ny)


def same_kernel(values, out):
    out[...] = values[...]


def raw_pressure_kernel(air, wind, medium, xb, zb, xa, za, tza, tzb, row, fa, fb, pressure, ozb, oza, ext):
    nx, nz, ny = air.shape[1:]
    widen(ext, air, xb, zb, xa, za)
    for x in range(nx):
        pressure[0, x] = pressure_rows(ext, wind, medium, x, nz)
    pack_pressure(pressure, (), (oza, ozb))
    lists = put_rows((row[0:1, :], *by_side((fa[0:1, :], fb[0:1, :]), "gx", 2)))
    for out, sent in zip((oza, ozb), (tza, tzb)):
        out[0:HEAD, :] = lists
        out[out.shape[0] - sent.shape[0]:, :] = sent[...]


def put_rows(rows):
    place = lax.broadcasted_iota(jnp.int32, (HEAD, LANES), 0)
    out = jnp.zeros((HEAD, LANES), F32)
    for at, row in enumerate(rows):
        out = jnp.where(place == at, row, out)
    return out


def merge_kernel(raw, txa, txb, zb, za, row, fa, fb, oxb, oxa, lists):
    far = by_side((fa[0:1, :], fb[0:1, :]), "gx", 2)
    low, high = by_side((za[0:HEAD, :], zb[0:HEAD, :]), "gz")
    rows = [row[0:1, :], *far]
    for band in (low, high):
        rows += [band[s:s + 1] for s in range(3)]
    lists[...] = put_rows(rows)
    pack_pressure(raw, (oxa, oxb), ())
    for out, sent in zip((oxa, oxb), (txa, txb)):
        out[0:HEAD, :] = lists[...]
        out[out.shape[0] - sent.shape[0]:, :] = sent[...]


def advection_kernel(air, wind, xb, zb, xa, za, moved, ext):
    nx, nz, ny = air.shape[1:]
    widen(ext, air, xb, zb, xa, za)
    lo, hi = ZRIM, ZRIM + nz
    for x in range(nx):
        xe = x + RADIUS
        for c in range(3):
            load = field(ext, 1 + c)
            moved[c, x] = (
                wind[0, x] * d1(load, xe, lo, hi)
                + wind[1, x] * d2(load, xe, lo, hi)
                + wind[2, x] * d3(load(xe, lo, hi))
            )


def velocities(out, center, moved, medium, wide, nx, nz):
    lo, hi = ZRIM, ZRIM + nz
    load = plane(wide)
    for x in range(nx):
        xe = x + RADIUS
        slopes = (d1(load, xe, lo, hi), d2(load, xe, lo, hi), d3(load(xe, lo, hi)))
        out[0, x] = load(xe, lo, hi)
        for c in range(3):
            out[1 + c, x] = center[1 + c, x] - medium[1, x] * slopes[c] - moved[c, x]


def pack_air(out, xb, zb, xa, za):
    for rim, side in zip((xa, xb), sides("gx")):
        pack_x(rim, 0, out, side)
    for rim, side in zip((za, zb), sides("gz")):
        pack_z(rim, 0, out, side)


def injected_kernel(
    air, wind, medium, raw, moved, wxb, wzb, wxa, wza, pxb, pzb, pxa, pza, near, smap,
    out, oxb, ozb, oxa, oza, answer, spread, wide, wide_wind,
):
    nx, nz, ny = air.shape[1:]
    reach, _, slots = smap.shape
    used = lax.broadcasted_iota(jnp.int32, (nx * nz, LANES), 1) < reach * slots
    low, high = by_side((pxa[0:HEAD, :], pxb[0:HEAD, :]), "gx")
    own = near[...]
    lists = [
        [table[3 * t + s:3 * t + s + 1] for t in range(3)]
        for table, s in ((low, 1), (own, 1), (low, 0), (own, 0), (high, 0), (own, 2), (high, 2))
    ]
    mul = functools.partial(
        lax.dot_general, dimension_numbers=(((1,), (1,)), ((), ())), preferred_element_type=F32
    )
    for da in range(3):
        for db in range(3):
            speed, cells = arrived(lists, da - 1, (1, 0, 2)[db], reach, slots)
            row_mask, third_mask = cell_masks(cells, nx * nz)
            high, low = halves(jnp.where(row_mask & used, speed, 0.0))
            columns = jnp.where(third_mask, 1.0, 0.0).astype(BF16)
            if da == 1 and db == 1:
                seen, rest = halves(air[0].reshape(nx * nz, ny))
                looked = jnp.dot(seen, columns, preferred_element_type=F32)
                looked = looked + jnp.dot(rest, columns, preferred_element_type=F32)
                answer[...] = jnp.sum(jnp.where(row_mask, looked, 0.0), axis=0, keepdims=True)
            block = mul(high, columns) + mul(low, columns)
            spread[da * nx:(da + 1) * nx, db * nz:(db + 1) * nz] = block.reshape(nx, nz, ny)
    widen(wide_wind, wind, wxb, wzb, wxa, wza, first=air.shape[0])
    widen_pressure(wide, raw.at[0], pxb, pzb, pxa, pza)
    load = plane(spread)
    for x in range(nx + 2 * RADIUS):
        xs = x + nx - RADIUS
        if RADIUS <= x < RADIUS + nx:
            lo, hi = 0, nz + 2 * ZRIM
        else:
            lo, hi = ZRIM, ZRIM + nz
        slo, shi = lo + nz - ZRIM, hi + nz - ZRIM
        here = load(xs, slo, shi)
        turned = (
            wide_wind[0, x, lo:hi, :] * d1(load, xs, slo, shi)
            + wide_wind[1, x, lo:hi, :] * d2(load, xs, slo, shi)
            + wide_wind[2, x, lo:hi, :] * d3(here)
        )
        wide[x, lo:hi, :] = wide[x, lo:hi, :] + (here - turned)
    velocities(out, air, moved, medium, wide, nx, nz)
    pack_air(out, oxb, ozb, oxa, oza)
    for rim in (oxa, oxb):
        rim[0:HEAD, :] = put_rows((answer[...],))


def pressure_kernel(air, wind, medium, xb, zb, xa, za, answer, pressure, oxb, ozb, oxa, oza, ext):
    nx, nz, ny = air.shape[1:]
    widen(ext, air, xb, zb, xa, za)
    for x in range(nx):
        pressure[0, x] = pressure_rows(ext, wind, medium, x, nz)
    pack_pressure(pressure, (oxa, oxb), (oza, ozb))
    low, high = by_side((xa[0:1, :], xb[0:1, :]), "gx")
    for rim in (oxa, oxb):
        rim[0:HEAD, :] = put_rows((answer[...], low, high))
    for rim in (oza, ozb):
        rim[0:HEAD, :] = jnp.zeros((HEAD, LANES), F32)


def velocity_kernel(air, pressure, medium, moved, xb, zb, xa, za, out, *rest):
    nx, nz, ny = air.shape[1:]
    wide = rest[-1]
    widen_pressure(wide, pressure.at[0], xb, zb, xa, za)
    velocities(out, air, moved, medium, wide, nx, nz)
    if len(rest) > 1:
        pack_air(out, *rest[:-1])
        for rim in (rest[0], rest[2]):
            rim[0:HEAD, :] = jnp.zeros((HEAD, LANES), F32)


def volume_kernel(state, integral, jac, stiff, out, token, rot, sp):
    quants, basis, width = state.shape
    dims = stiff.shape[0]
    pad = sp.shape[0] // dims
    token[...] = jnp.zeros_like(token)
    sp[...] = jnp.zeros_like(sp)
    place = lax.broadcasted_iota(jnp.int32, (basis, basis), 0)
    other = lax.broadcasted_iota(jnp.int32, (basis, basis), 1)
    unit = jnp.where(place == other, 1.0, 0.0).astype(F32)
    for d in range(dims):
        sp[d * pad:d * pad + basis, 0:basis] = dot_exact(unit, stiff[d], (((1,), (1,)), ((), ())))
    rotate(rot, stacked_left(sp[...]), integral, quants, width)

    def emit(p, at, value):
        out[p, :, lanes(at)] = state[p, :, lanes(at)] + value[0:basis]

    jacobian_step(lambda p, q, d, cut: jac[p, q, d:d + 1, cut], rot, emit, quants, dims, width)


def flux_kernel(
    first, faces, base, traces, own, solvers, lift, neighbours, xb, zb, xa, za,
    out, token, tiles, flux, lp,
):
    token[...] = jnp.zeros_like(token)
    quants, basis, width = base.shape
    face_basis = lift.shape[0]
    skip = xa.shape[0] - sent_rows(quants, face_basis)
    for axis, base_tile, gots in (("gx", 0, (xa, xb)), ("gz", 2, (za, zb))):
        for got, side in zip(gots, sides(axis)):
            for q in range(quants):
                tiles[q, base_tile + side, 0:8, :] = got[skip + q * 8:skip + q * 8 + 8, :]
                at = skip + quants * 8 + q * 2
                tiles[q, base_tile + side, 8:face_basis, :] = got[at:at + 2, :]
                tiles[q, base_tile + side, face_basis:, :] = jnp.zeros((16 - face_basis, LANES), F32)
    for q in range(quants):
        tiles[q, 4] = -own[q] if q < 3 else own[q]
    lp[...] = jnp.zeros_like(lp)
    for f in range(faces):
        for j in range(face_basis):
            lp[f * 16 + j:f * 16 + j + 1, 0:basis] = lift[j, first + f:first + f + 1, :]
    unit = lax.broadcasted_iota(jnp.int32, (lp.shape[1], lp.shape[1]), 0) == lax.broadcasted_iota(
        jnp.int32, (lp.shape[1], lp.shape[1]), 1
    )
    lifted = dot_exact(jnp.where(unit, 1.0, 0.0).astype(F32), lp[...], (((1,), (1,)), ((), ())))
    lifted = stacked_left(lifted)
    local = traces.shape[2] // LANES
    halves_in = width // LANES

    def one(h, carry):
        at = h * LANES
        for f in range(faces):
            index = jnp.broadcast_to(neighbours[first + f:first + f + 1, lanes(at)], (16, LANES))
            acc = [None] * quants
            for q in range(quants):
                pool = [traces[q, :, s * LANES:(s + 1) * LANES] for s in range(local)]
                pool += [tiles[q, s] for s in range(5)]
                mine = traces[q, :, lanes((first + f) * width + at)]
                jump = take_slots(pool, index) - mine
                for p in range(quants):
                    term = solvers[p, q, first + f:first + f + 1, lanes(at)] * jump
                    acc[p] = term if acc[p] is None else acc[p] + term
            for p in range(quants):
                flux[f * 16:(f + 1) * 16, lanes(p * width + at)] = acc[p]
        return carry

    lax.fori_loop(0, halves_in, one, 0)
    for p in range(quants):
        cut = slice(p * width, (p + 1) * width)
        out[p] = base[p] + dot3(lifted, flux[:, cut])[0:basis]


def replies_kernel(base, solvers, lift, neighbours, smap, answer, rxb, rxa, out):
    quants, basis, width = base.shape
    face_basis, faces = lift.shape[:2]
    slots = smap.shape[2]
    low, high = by_side((rxa[0:HEAD, :], rxb[0:HEAD, :]), "gx")
    lane = lax.broadcasted_iota(jnp.int32, (1, LANES), 1)
    replies = jnp.zeros((1, LANES), F32)
    for r, row in enumerate((low[1:2], low[0:1], answer[...], high[0:1], high[2:3])):
        replies = jnp.where(lane // slots == r, row, replies)
    replies = jnp.broadcast_to(-2.0 * replies * flat_slots(smap)[2:3], (8, LANES))
    begin = faces * width + 4 * LANES
    square = lax.broadcasted_iota(jnp.int32, (basis, basis), 0) == lax.broadcasted_iota(
        jnp.int32, (basis, basis), 1
    )
    columns = []
    for f in range(faces):
        column = lift[0, f:f + 1, :]
        for j in range(1, face_basis):
            column = column + lift[j, f:f + 1, :]
        columns.append(jnp.sum(jnp.where(square, column, 0.0), axis=1, keepdims=True))
    for h in range(width // LANES):
        cut = slice(h * LANES, (h + 1) * LANES)
        spread = []
        for f in range(faces):
            index = jnp.broadcast_to(neighbours[f:f + 1, cut], (8, LANES))
            found = jnp.take_along_axis(replies, index % LANES, axis=1, mode="promise_in_bounds")
            spread.append(columns[f] * jnp.where(index >= begin, found, 0.0)[0:1])
        for p in range(quants):
            stress = solvers[p, 0, :, cut] + solvers[p, 1, :, cut] + solvers[p, 2, :, cut]
            total = base[p, :, cut]
            for f in range(faces):
                total = total + stress[f:f + 1] * spread[f]
            out[p, :, cut] = total


def sent_rows(quants, face_basis):
    return -(-quants * face_basis // 8) * 8


def shards(
    solid_state, jacobians, flux_solvers, stiffness, trace_matrix, lift_matrix,
    neighbours, send_faces, surface_map, surface_normals, air_state, wind_field, air_medium,
):
    quants, basis, width = solid_state.shape
    faces, face_basis = trace_matrix.shape[0], trace_matrix.shape[1]
    dims = stiffness.shape[0]
    nx, nz, ny = air_state.shape[1:]
    jacobians = jnp.transpose(jacobians, (1, 2, 0, 3))
    flux_solvers = jnp.transpose(flux_solvers, (1, 2, 0, 3))
    trace_matrix = jnp.transpose(trace_matrix, (1, 0, 2))
    lift_matrix = jnp.transpose(lift_matrix, (2, 0, 1))
    surface_map = jnp.transpose(surface_map, (1, 0, 2))
    surface_normals = jnp.transpose(surface_normals, (1, 0, 2))
    pad = -(-basis // 8) * 8
    pad_k = -(-basis // 16) * 16
    rim_z = (7, nx, ZRIM, ny)
    rim_x = (7, RADIUS, nz, ny)
    ext = (4, nx + 2 * RADIUS, nz + 2 * ZRIM, ny)
    wide = ext[1:]
    block = (1, nx, nz, ny)
    tile = (8, LANES)

    rims = exchange(
        *call(
            raw_rims_kernel, "raw_rims", [rim_x, rim_z, rim_x, rim_z], [air_state, wind_field],
        )
    )

    sent = (sent_rows(quants, face_basis), LANES)
    integral, traces, own, txa, txb, tza, tzb, row = call(
        predict_kernel, "predict",
        [(pad_k, quants * width), (quants, 16, faces * width), (quants, 16, LANES), sent, sent, sent, sent,
         tile],
        [solid_state, jacobians, stiffness, trace_matrix, send_faces, surface_map, surface_normals],
        [(pad_k, quants * width), (dims * pad, quants * width), (dims * pad, pad_k), (faces * 16, pad_k),
         (4, quants, 16, LANES), (quants, quants, dims, 8, width)],
        flops=40_000_000,
    )
    (own_list,) = call(same_kernel, "own_list", [tile], [row], after=[rims[3]])
    far = swap(own_list, "gx", 0, 2), swap(own_list, "gx", 1, 2)
    pressure_x = (HEAD + RADIUS * nz, ny)
    pressure_z = (HEAD + nx * ZRIM, ny)
    both_x = (pressure_x[0] + sent[0], LANES)
    both_z = (pressure_z[0] + sent[0], LANES)
    raw, zb, za = call(
        raw_pressure_kernel, "raw_pressure", [block, both_z, both_z],
        [air_state, wind_field, air_medium, *rims, tza, tzb, row, *far], [ext],
    )
    both_zb, both_za = swap(zb, "gz", 1), swap(za, "gz", 0)
    (moved,) = call(
        advection_kernel, "advection", [(3, nx, nz, ny)],
        [air_state, wind_field, *rims], [ext], flops=10_000_000, after=[za],
    )
    xb, xa, lists = call(
        merge_kernel, "merge", [both_x, both_x, (HEAD, LANES)], [raw, txa, txb, both_zb, both_za, row, *far]
    )
    both_xb, both_xa = swap(xb, "gx", 1), swap(xa, "gx", 0)
    both = both_xb, both_zb, both_xa, both_za
    volume, token = call(
        volume_kernel, "volume", [solid_state.shape, tile], [solid_state, integral, jacobians, stiffness],
        [(dims * pad, quants * width), (dims * pad, pad_k)], flops=10_000_000, after=[lists],
    )

    rim_x = (HEAD + 4 * RADIUS * nz, ny)
    rim_z = (4, nx, ZRIM, ny)
    air, xb, zb, xa, za, answer = call(
        injected_kernel, "injected",
        [air_state.shape, rim_x, rim_z, rim_x, rim_z, (1, LANES)],
        [air_state, wind_field, air_medium, raw, moved, *rims, *both, lists, surface_map],
        [(3 * nx, 3 * nz, ny), wide, (3,) + wide], after=[token],
    )
    half = faces // 2
    solid = volume
    for substep in range(1, SUBSTEPS):
        rims = exchange(xb, zb, xa, za)
        solid, token = call(
            functools.partial(flux_kernel, (substep - 1) * half, half), "flux", [solid_state.shape, tile],
            [solid, traces, own, flux_solvers, lift_matrix, neighbours, *both],
            [(quants, 5, 16, LANES), (half * 16, quants * width), (half * 16, pad)], flops=20_000_000,
            after=[xa],
        )
        pressure, xb, zb, xa, za = call(
            pressure_kernel, "pressure", [block, pressure_x, pressure_z, pressure_x, pressure_z],
            [air, wind_field, air_medium, *rims, answer], [ext], after=[token],
        )
        rises = exchange(xb, zb, xa, za)
        if substep == 1:
            replies = [answer, rises[0], rises[2]]
        (moved,) = call(
            advection_kernel, "advection", [(3, nx, nz, ny)],
            [air, wind_field, *rims], [ext], flops=10_000_000, after=[xa],
        )
        last = substep == SUBSTEPS - 1
        if last:
            (solid,) = call(
                replies_kernel, "replies", [solid_state.shape],
                [solid, flux_solvers, lift_matrix, neighbours, surface_map, *replies], after=[moved],
            )
        outs = [air_state.shape] + ([] if last else [rim_x, rim_z, rim_x, rim_z])
        done = call(
            velocity_kernel, "velocity", outs, [air, pressure, air_medium, moved, *rises], [wide]
        )
        air = done[0]
        if not last:
            xb, zb, xa, za = done[1:]
    return (solid, air)


def solution(mesh):
    in_specs = (
        P(None, None, ("gx", "gz")),
        P(None, None, None, ("gx", "gz")),
        P(None, None, None, ("gx", "gz")),
        P(),
        P(),
        P(),
        P(None, ("gx", "gz")),
        P(None, ("gx", "gz")),
        P(None, None, ("gx", "gz")),
        P(None, None, ("gx", "gz")),
        P(None, "gx", "gz", None),
        P(None, "gx", "gz", None),
        P(None, "gx", "gz", None),
    )
    out_specs = (P(None, None, ("gx", "gz")), P(None, "gx", "gz", None))
    return jax.shard_map(shards, mesh=mesh, in_specs=in_specs, out_specs=out_specs, check_vma=False)
```

```python
import functools

import jax
import jax.numpy as jnp
from jax import lax
from jax.experimental import pallas as pl
from jax.experimental.pallas import tpu as pltpu
from jax.sharding import PartitionSpec as P

ORDERS = 4
RADIUS = 4
SUBSTEPS = 3
ZRIM = 8
LANES = 128
HEAD = 16
FACE_ROWS = 10
TIME_STEP = 0.5
STENCIL_WEIGHTS = (0.8, -0.2, 4.0 / 105.0, -1.0 / 280.0)
F32 = jnp.float32
BF16 = jnp.bfloat16


def call(kernel, name, outs, ins, scratch=(), flops=1_000_000, after=()):
    count, skip = len(ins), len(after)
    nbytes = 4 * sum(x.size for x in ins) + 4 * sum(functools.reduce(lambda m, n: m * n, s, 1) for s in outs)

    def body(*refs):
        kernel(*refs[:count], *refs[count + skip:])

    return pl.pallas_call(
        body,
        out_shape=[jax.ShapeDtypeStruct(s, F32) for s in outs],
        in_specs=[pl.BlockSpec(memory_space=pltpu.VMEM) for _ in ins]
        + [pl.BlockSpec(memory_space=pl.ANY) for _ in after],
        out_specs=[pl.BlockSpec(memory_space=pltpu.VMEM) for _ in outs],
        scratch_shapes=[pltpu.VMEM(s, F32) for s in scratch],
        compiler_params=pltpu.CompilerParams(vmem_limit_bytes=8 * 1024 * 1024),
        cost_estimate=pl.CostEstimate(flops=flops, bytes_accessed=nbytes, transcendentals=0),
        name=name,
    )(*ins, *after)


def swap(values, axis, odd, by=1):
    count = lax.axis_size(axis)
    pairs = []
    for i in range(count - by):
        if i // by % 2 == odd:
            pairs += [(i, i + by), (i + by, i)]
    return lax.ppermute(values, axis, pairs)


def exchange(xb, zb, xa, za):
    return swap(xb, "gx", 1), swap(zb, "gz", 1), swap(xa, "gx", 0), swap(za, "gz", 0)


def sides(axis, by=1):
    parity = (lax.axis_index(axis) // by) & 1
    return 1 - parity, parity


def by_side(pair, axis, by=1):
    first = sides(axis, by)[0]
    return jnp.where(first == 0, pair[0], pair[1]), jnp.where(first == 1, pair[0], pair[1])


def halves(values):
    high = values.astype(BF16)
    return high, (values - high.astype(F32)).astype(BF16)


def stacked_left(matrix):
    k = matrix.shape[1]
    lane = lax.broadcasted_iota(jnp.int32, (k, 3 * k), 1)
    place = lax.broadcasted_iota(jnp.int32, (k, 3 * k), 0)
    spread = dot_exact(matrix, jnp.where(lane % k == place, 1.0, 0.0).astype(F32))
    high = spread.astype(BF16).astype(F32)
    lane = lax.broadcasted_iota(jnp.int32, spread.shape, 1)
    return jnp.where(lane < 2 * k, high, spread - high).astype(BF16)


def dot3(left, right):
    high, low = halves(right)
    return jnp.dot(left, jnp.concatenate([high, low, high], axis=0), preferred_element_type=F32)


def dot_exact(left, right, dims=(((1,), (0,)), ((), ()))):
    return lax.dot_general(
        left, right, dims, precision=lax.Precision.HIGHEST, preferred_element_type=F32
    )


def flat_slots(table):
    rows, fields, slots = table.shape
    lane = lax.broadcasted_iota(jnp.int32, (slots, LANES), 1)
    place = lax.broadcasted_iota(jnp.int32, (slots, LANES), 0)
    spread = jnp.where(lane % slots == place, 1.0, 0.0).astype(F32)
    lane = lax.broadcasted_iota(jnp.int32, (fields, LANES), 1)
    flat = jnp.zeros((fields, LANES), F32)
    for r in range(rows):
        flat = jnp.where(lane // slots == r, dot_exact(table[r].astype(F32), spread), flat)
    return flat


def pack_x(out, at, source, side):
    fields, nx, nz, ny = source.shape
    start = side * (nx - RADIUS)
    rows = fields * RADIUS * nz
    at = HEAD + at * RADIUS * nz
    out[at:at + rows, :] = source[:, pl.ds(start, RADIUS)].reshape(rows, ny)


def pack_z(out, at, source, side):
    fields, nz = source.shape[0], source.shape[2]
    out[at:at + fields] = jnp.where(side == 1, source[:, :, nz - RADIUS:, :], source[:, :, 0:RADIUS, :])


def widen(ext, center, xb, zb, xa, za, first=0):
    fields, nx, nz, ny = center.shape
    ext[:, RADIUS:RADIUS + nx, ZRIM:ZRIM + nz] = center[...]
    for got, side in zip((xa, xb), sides("gx")):
        place = pl.ds(side * (nx + RADIUS), RADIUS)
        if len(got.shape) == 4:
            rows = got[first:first + fields]
        else:
            rows = got[HEAD:HEAD + fields * RADIUS * nz, :].reshape(fields, RADIUS, nz, ny)
        ext[:, place, ZRIM:ZRIM + nz] = rows
    low, high = by_side([got[first:first + fields] for got in (za, zb)], "gz")
    ext[:, RADIUS:RADIUS + nx, ZRIM - RADIUS:ZRIM] = low
    ext[:, RADIUS:RADIUS + nx, ZRIM + nz:ZRIM + nz + RADIUS] = high


def d1(load, x, lo, hi):
    total = None
    for m, w in enumerate(STENCIL_WEIGHTS, 1):
        term = w * (load(x + m, lo, hi) - load(x - m, lo, hi))
        total = term if total is None else total + term
    return total


def d2(load, x, lo, hi):
    total = None
    for m, w in enumerate(STENCIL_WEIGHTS, 1):
        term = w * (load(x, lo + m, hi + m) - load(x, lo - m, hi - m))
        total = term if total is None else total + term
    return total


def d3(values):
    width = values.shape[1]
    lane = lax.broadcasted_iota(jnp.int32, (1, width), 1)
    total = None
    for m, w in enumerate(STENCIL_WEIGHTS, 1):
        ahead = jnp.where(lane < width - m, w, 0.0) * pltpu.roll(values, width - m, 1)
        behind = jnp.where(lane >= m, w, 0.0) * pltpu.roll(values, m, 1)
        term = ahead - behind
        total = term if total is None else total + term
    return total


def field(ref, c):
    return lambda x, lo, hi: ref[c, x, lo:hi, :]


def plane(ref):
    return lambda x, lo, hi: ref[x, lo:hi, :]


def arrived(lists, da, band, reach, slots):
    lane = lax.broadcasted_iota(jnp.int32, (1, LANES), 1)
    got = jnp.zeros((1, LANES), F32)
    for r in range(reach):
        row = lists[da - (r - reach // 2) + 3][band]
        got = jnp.where((lane & (LANES // 2 - 1)) // slots == r, row, got)
    turned = pltpu.roll(got, LANES // 2, 1)
    speed = jnp.where(lane < LANES // 2, got, turned)
    high = speed.astype(BF16).astype(F32)
    return jnp.where(lane < LANES // 2, high, speed - high), jnp.where(lane < LANES // 2, turned, got)


def cell_masks(cells, rows):
    cells = cells.astype(jnp.int32)
    place = lax.broadcasted_iota(jnp.int32, (rows, LANES), 0)
    third = lax.broadcasted_iota(jnp.int32, (LANES, LANES), 0)
    return cells // LANES == place, cells % LANES == third


def raw_rims_kernel(air, wind, xb, zb, xa, za):
    fields, nx = air.shape[:2]
    for out, side in zip((xa, xb), sides("gx")):
        rows = pl.ds(side * (nx - RADIUS), RADIUS)
        out[0:fields] = air[:, rows]
        out[fields:] = wind[:, rows]
    for out, side in zip((za, zb), sides("gz")):
        pack_z(out, 0, air, side)
        pack_z(out, fields, wind, side)


def lanes(at):
    return pl.ds(at if isinstance(at, int) else pl.multiple_of(at, LANES), LANES)


def jacobian_step(load, rot, emit, quants, dims, width):
    rows = rot.shape[0] // dims

    def half(h, carry):
        at = h * LANES
        acc = [None] * quants
        for d in range(dims):
            for q in range(quants):
                turned = rot[d * rows:(d + 1) * rows, lanes(q * width + at)].reshape(rows // 8, 8, LANES)
                for p in range(quants):
                    term = load(p, q, d, lanes(at)) * turned
                    acc[p] = term if acc[p] is None else acc[p] + term
        for p in range(quants):
            emit(p, at, acc[p].reshape(rows, LANES))
        return carry

    lax.fori_loop(0, width // LANES, half, 0)


def rotate(rot, left, source, quants, width):
    for q in range(quants):
        cut = slice(q * width, (q + 1) * width)
        rot[:, cut] = dot3(left, source[:, cut])


def take_slots(tiles, index):
    low = index % LANES
    high = index // LANES
    got = None
    for s, tile in enumerate(tiles):
        picked = jnp.take_along_axis(tile, low, axis=1, mode="promise_in_bounds")
        got = picked if got is None else jnp.where(high == s, picked, got)
    return got


def predict_kernel(
    state, jac, stiff, trace,
    integral, traces, kept,
    cur, rot, sp, tp,
):
    quants, basis, width = state.shape
    pad = sp.shape[0] // stiff.shape[0]
    face_basis, faces = trace.shape[:2]
    dims = stiff.shape[0]
    sp[...] = jnp.zeros_like(sp)
    tp[...] = jnp.zeros_like(tp)
    cur[...] = jnp.zeros_like(cur)
    for d in range(dims):
        sp[d * pad:d * pad + basis, 0:basis] = stiff[d]
    for f in range(faces):
        for j in range(face_basis):
            tp[f * 16 + j:f * 16 + j + 1, 0:basis] = trace[j, f:f + 1, :]
    for q in range(quants):
        cur[0:basis, q * width:(q + 1) * width] = state[q]
    kept[...] = state[...]
    integral[...] = TIME_STEP * cur[...]
    left = stacked_left(sp[...])

    def degree(k, weight):
        weight = jnp.where(k == 1, TIME_STEP**2 / 2, jnp.where(k == 2, TIME_STEP**3 / 6, TIME_STEP**4 / 24))
        rotate(rot, left, cur, quants, width)

        def emit(p, at, value):
            cut = lanes(p * width + at)
            cur[0:pad, cut] = -value
            integral[0:pad, cut] = integral[0:pad, cut] - weight * value

        jacobian_step(lambda p, q, d, cut: jac[p, q, d:d + 1, cut], rot, emit, quants, dims, width)
        return weight

    lax.fori_loop(1, ORDERS, degree, F32(0))
    restrict = stacked_left(tp[...])
    for q in range(quants):
        cut = slice(q * width, (q + 1) * width)
        done = dot3(restrict, integral[:, cut])
        for f in range(faces):
            traces[q, :, f * width:(f + 1) * width] = done[f * 16:(f + 1) * 16]


def own_list_kernel(traces, smap, normals, own, row):
    quants, _, all_slots = traces.shape
    slots = flat_slots(smap)
    wanted = jnp.broadcast_to(slots[0:1].astype(jnp.int32), (16, LANES))

    def gather(q, carry):
        own[q] = take_slots([traces[q, :, s * LANES:(s + 1) * LANES] for s in range(all_slots // LANES)], wanted)
        return carry

    lax.fori_loop(0, quants, gather, 0)
    normal = flat_slots(normals)
    speed = jnp.zeros((1, LANES), F32)
    for c in range(3):
        mean = jnp.sum(own[6 + c, 0:FACE_ROWS, :], axis=0, keepdims=True) * (1.0 / FACE_ROWS)
        speed = speed + normal[c:c + 1] * mean
    lane = lax.broadcasted_iota(jnp.int32, (1, LANES), 1)
    cells = pltpu.roll(slots[1:2], LANES // 2, 1)
    row[...] = jnp.broadcast_to(jnp.where(lane < LANES // 2, slots[2:3] * speed, cells), row.shape)


def outgoing_kernel(traces, sends, xa, xb, za, zb, picked):
    quants, _, slots = traces.shape
    rows = sent_rows(quants, FACE_ROWS)
    wanted = [jnp.broadcast_to(sends[d:d + 1, :], (16, LANES)) for d in range(4)]

    def gather(q, carry):
        tiles = [traces[q, :, s * LANES:(s + 1) * LANES] for s in range(slots // LANES)]
        for d in range(4):
            picked[d, q] = take_slots(tiles, wanted[d])
        return carry

    lax.fori_loop(0, quants, gather, 0)
    rest = FACE_ROWS - 8
    for axis, base, outs in (("gx", 0, (xa, xb)), ("gz", 2, (za, zb))):
        for out, side in zip(outs, sides(axis)):
            for q in range(quants):
                out[q * 8:q * 8 + 8, :] = picked[base + side, q, 0:8, :]
                at = quants * 8 + q * rest
                out[at:at + rest, :] = picked[base + side, q, 8:FACE_ROWS, :]
            out[quants * FACE_ROWS:, :] = jnp.zeros((rows - quants * FACE_ROWS, LANES), F32)


def pressure_rows(ext, wind, medium, x, nz):
    lo, hi = ZRIM, ZRIM + nz
    xe = x + RADIUS
    pressure = field(ext, 0)
    here = pressure(xe, lo, hi)
    divergence = d1(field(ext, 1), xe, lo, hi) + d2(field(ext, 2), xe, lo, hi) + d3(ext[3, xe, lo:hi, :])
    moved = (
        wind[0, x] * d1(pressure, xe, lo, hi)
        + wind[1, x] * d2(pressure, xe, lo, hi)
        + wind[2, x] * d3(here)
    )
    return here - medium[0, x] * divergence - moved


def pack_pressure(center, xs, zs):
    nx, nz, ny = center.shape[1:]
    for out, side in zip(xs, sides("gx")):
        start = side * (nx - RADIUS)
        out[HEAD:HEAD + RADIUS * nz, :] = center[0, pl.ds(start, RADIUS)].reshape(RADIUS * nz, ny)
    for out, side in zip(zs, sides("gz")):
        start = pl.multiple_of(side * (nz - ZRIM), ZRIM)
        out[HEAD:HEAD + nx * ZRIM, :] = center[0, :, pl.ds(start, ZRIM), :].reshape(nx * ZRIM, ny)


def widen_pressure(ext, center, xb, zb, xa, za):
    nx, nz, ny = center.shape
    ext[RADIUS:RADIUS + nx, ZRIM:ZRIM + nz] = center[...]
    for got, side in zip((xa, xb), sides("gx")):
        ext[pl.ds(side * (nx + RADIUS), RADIUS), ZRIM:ZRIM + nz] = got[HEAD:HEAD + RADIUS * nz, :].reshape(RADIUS, nz, ny)
    for got, side in zip((za, zb), sides("gz")):
        start = pl.multiple_of(side * (nz + ZRIM), ZRIM)
        ext[RADIUS:RADIUS + nx, pl.ds(start, ZRIM)] = got[HEAD:HEAD + nx * ZRIM, :].reshape(nx, ZRIM, ny)


def raw_pressure_kernel(air, wind, medium, xb, zb, xa, za, tza, tzb, row, fa, fb, pressure, ozb, oza, ext):
    nx, nz, ny = air.shape[1:]
    widen(ext, air, xb, zb, xa, za)
    for x in range(nx):
        pressure[0, x] = pressure_rows(ext, wind, medium, x, nz)
    pack_pressure(pressure, (), (oza, ozb))
    lists = put_rows((row[0:1, :], *by_side((fa[0:1, :], fb[0:1, :]), "gx", 2)))
    for out, sent in zip((oza, ozb), (tza, tzb)):
        out[0:HEAD, :] = lists
        out[out.shape[0] - sent.shape[0]:, :] = sent[...]


def put_rows(rows):
    place = lax.broadcasted_iota(jnp.int32, (HEAD, LANES), 0)
    out = jnp.zeros((HEAD, LANES), F32)
    for at, row in enumerate(rows):
        out = jnp.where(place == at, row, out)
    return out


def merge_kernel(raw, txa, txb, zb, za, row, fa, fb, oxb, oxa, lists):
    far = by_side((fa[0:1, :], fb[0:1, :]), "gx", 2)
    low, high = by_side((za[0:HEAD, :], zb[0:HEAD, :]), "gz")
    rows = [row[0:1, :], *far]
    for band in (low, high):
        rows += [band[s:s + 1] for s in range(3)]
    lists[...] = put_rows(rows)
    pack_pressure(raw, (oxa, oxb), ())
    for out, sent in zip((oxa, oxb), (txa, txb)):
        out[0:HEAD, :] = lists[...]
        out[out.shape[0] - sent.shape[0]:, :] = sent[...]


def advection_kernel(air, wind, xb, zb, xa, za, moved, ext):
    nx, nz, ny = air.shape[1:]
    widen(ext, air, xb, zb, xa, za)
    lo, hi = ZRIM, ZRIM + nz
    for x in range(nx):
        xe = x + RADIUS
        for c in range(3):
            load = field(ext, 1 + c)
            moved[c, x] = (
                wind[0, x] * d1(load, xe, lo, hi)
                + wind[1, x] * d2(load, xe, lo, hi)
                + wind[2, x] * d3(load(xe, lo, hi))
            )


def velocities(out, center, moved, medium, wide, nx, nz):
    lo, hi = ZRIM, ZRIM + nz
    load = plane(wide)
    for x in range(nx):
        xe = x + RADIUS
        slopes = (d1(load, xe, lo, hi), d2(load, xe, lo, hi), d3(load(xe, lo, hi)))
        out[0, x] = load(xe, lo, hi)
        for c in range(3):
            out[1 + c, x] = center[1 + c, x] - medium[1, x] * slopes[c] - moved[c, x]


def pack_air(out, xb, zb, xa, za):
    for rim, side in zip((xa, xb), sides("gx")):
        pack_x(rim, 0, out, side)
    for rim, side in zip((za, zb), sides("gz")):
        pack_z(rim, 0, out, side)


def injected_kernel(
    air, wind, medium, raw, moved, wxb, wzb, wxa, wza, pxb, pzb, pxa, pza, near, smap,
    out, oxb, ozb, oxa, oza, answer, spread, wide, wide_wind,
):
    nx, nz, ny = air.shape[1:]
    reach, _, slots = smap.shape
    low, high = by_side((pxa[0:HEAD, :], pxb[0:HEAD, :]), "gx")
    own = near[...]
    lists = [
        [table[3 * t + s:3 * t + s + 1] for t in range(3)]
        for table, s in ((low, 1), (own, 1), (low, 0), (own, 0), (high, 0), (own, 2), (high, 2))
    ]
    mul = functools.partial(
        lax.dot_general, dimension_numbers=(((1,), (1,)), ((), ())), preferred_element_type=F32
    )
    for da in range(3):
        for db in range(3):
            speed, cells = arrived(lists, da - 1, (1, 0, 2)[db], reach, slots)
            row_mask, third_mask = cell_masks(cells, nx * nz)
            columns = jnp.where(third_mask, 1.0, 0.0).astype(BF16)
            if da == 1 and db == 1:
                seen, rest = halves(air[0].reshape(nx * nz, ny))
                looked = jnp.dot(seen, columns, preferred_element_type=F32)
                looked = looked + jnp.dot(rest, columns, preferred_element_type=F32)
                answer[...] = jnp.sum(jnp.where(row_mask, looked, 0.0), axis=0, keepdims=True)
            block = mul(jnp.where(row_mask, speed, 0.0).astype(BF16), columns)
            spread[da * nx:(da + 1) * nx, db * nz:(db + 1) * nz] = block.reshape(nx, nz, ny)
    widen(wide_wind, wind, wxb, wzb, wxa, wza, first=air.shape[0])
    widen_pressure(wide, raw.at[0], pxb, pzb, pxa, pza)
    load = plane(spread)
    for x in range(nx + 2 * RADIUS):
        xs = x + nx - RADIUS
        if RADIUS <= x < RADIUS + nx:
            lo, hi = 0, nz + 2 * ZRIM
        else:
            lo, hi = ZRIM, ZRIM + nz
        slo, shi = lo + nz - ZRIM, hi + nz - ZRIM
        here = load(xs, slo, shi)
        turned = (
            wide_wind[0, x, lo:hi, :] * d1(load, xs, slo, shi)
            + wide_wind[1, x, lo:hi, :] * d2(load, xs, slo, shi)
            + wide_wind[2, x, lo:hi, :] * d3(here)
        )
        wide[x, lo:hi, :] = wide[x, lo:hi, :] + (here - turned)
    velocities(out, air, moved, medium, wide, nx, nz)
    pack_air(out, oxb, ozb, oxa, oza)
    for rim in (oxa, oxb):
        rim[0:HEAD, :] = put_rows((answer[...],))


def pressure_kernel(air, wind, medium, xb, zb, xa, za, answer, pressure, oxb, ozb, oxa, oza, ext):
    nx, nz, ny = air.shape[1:]
    widen(ext, air, xb, zb, xa, za)
    for x in range(nx):
        pressure[0, x] = pressure_rows(ext, wind, medium, x, nz)
    pack_pressure(pressure, (oxa, oxb), (oza, ozb))
    low, high = by_side((xa[0:1, :], xb[0:1, :]), "gx")
    for rim in (oxa, oxb):
        rim[0:HEAD, :] = put_rows((answer[...], low, high))
    for rim in (oza, ozb):
        rim[0:HEAD, :] = jnp.zeros((HEAD, LANES), F32)


def velocity_kernel(air, pressure, medium, moved, xb, zb, xa, za, out, *rest):
    nx, nz, ny = air.shape[1:]
    wide = rest[-1]
    widen_pressure(wide, pressure.at[0], xb, zb, xa, za)
    velocities(out, air, moved, medium, wide, nx, nz)
    if len(rest) > 1:
        pack_air(out, *rest[:-1])
        for rim in (rest[0], rest[2]):
            rim[0:HEAD, :] = jnp.zeros((HEAD, LANES), F32)


def volume_kernel(state, integral, jac, stiff, out, token, rot, sp):
    quants, basis, width = state.shape
    dims = stiff.shape[0]
    pad = sp.shape[0] // dims
    token[...] = jnp.zeros_like(token)
    sp[...] = jnp.zeros_like(sp)
    place = lax.broadcasted_iota(jnp.int32, (basis, basis), 0)
    other = lax.broadcasted_iota(jnp.int32, (basis, basis), 1)
    unit = jnp.where(place == other, 1.0, 0.0).astype(F32)
    for d in range(dims):
        sp[d * pad:d * pad + basis, 0:basis] = dot_exact(unit, stiff[d], (((1,), (1,)), ((), ())))
    rotate(rot, stacked_left(sp[...]), integral, quants, width)

    def emit(p, at, value):
        out[p, :, lanes(at)] = state[p, :, lanes(at)] + value[0:basis]

    jacobian_step(lambda p, q, d, cut: jac[p, q, d:d + 1, cut], rot, emit, quants, dims, width)


def flux_kernel(
    first, faces, base, traces, own, solvers, lift, neighbours, xb, zb, xa, za,
    out, token, tiles, flux, lp,
):
    token[...] = jnp.zeros_like(token)
    quants, basis, width = base.shape
    face_basis = lift.shape[0]
    skip = xa.shape[0] - sent_rows(quants, face_basis)
    for axis, base_tile, gots in (("gx", 0, (xa, xb)), ("gz", 2, (za, zb))):
        for got, side in zip(gots, sides(axis)):
            for q in range(quants):
                tiles[q, base_tile + side, 0:8, :] = got[skip + q * 8:skip + q * 8 + 8, :]
                at = skip + quants * 8 + q * 2
                tiles[q, base_tile + side, 8:face_basis, :] = got[at:at + 2, :]
                tiles[q, base_tile + side, face_basis:, :] = jnp.zeros((16 - face_basis, LANES), F32)
    for q in range(quants):
        tiles[q, 4] = -own[q] if q < 3 else own[q]
    lp[...] = jnp.zeros_like(lp)
    for f in range(faces):
        for j in range(face_basis):
            lp[f * 16 + j:f * 16 + j + 1, 0:basis] = lift[j, first + f:first + f + 1, :]
    unit = lax.broadcasted_iota(jnp.int32, (lp.shape[1], lp.shape[1]), 0) == lax.broadcasted_iota(
        jnp.int32, (lp.shape[1], lp.shape[1]), 1
    )
    lifted = dot_exact(jnp.where(unit, 1.0, 0.0).astype(F32), lp[...], (((1,), (1,)), ((), ())))
    lifted = stacked_left(lifted)
    local = traces.shape[2] // LANES
    halves_in = width // LANES

    def one(h, carry):
        at = h * LANES
        for f in range(faces):
            index = jnp.broadcast_to(neighbours[first + f:first + f + 1, lanes(at)], (16, LANES))
            acc = [None] * quants
            for q in range(quants):
                pool = [traces[q, :, s * LANES:(s + 1) * LANES] for s in range(local)]
                pool += [tiles[q, s] for s in range(5)]
                mine = traces[q, :, lanes((first + f) * width + at)]
                jump = take_slots(pool, index) - mine
                for p in range(quants):
                    term = solvers[p, q, first + f:first + f + 1, lanes(at)] * jump
                    acc[p] = term if acc[p] is None else acc[p] + term
            for p in range(quants):
                flux[f * 16:(f + 1) * 16, lanes(p * width + at)] = acc[p]
        return carry

    lax.fori_loop(0, halves_in, one, 0)
    for p in range(quants):
        cut = slice(p * width, (p + 1) * width)
        out[p] = base[p] + dot3(lifted, flux[:, cut])[0:basis]


def replies_kernel(base, solvers, lift, neighbours, smap, answer, rxb, rxa, out):
    quants, basis, width = base.shape
    face_basis, faces = lift.shape[:2]
    slots = smap.shape[2]
    low, high = by_side((rxa[0:HEAD, :], rxb[0:HEAD, :]), "gx")
    lane = lax.broadcasted_iota(jnp.int32, (1, LANES), 1)
    replies = jnp.zeros((1, LANES), F32)
    for r, row in enumerate((low[1:2], low[0:1], answer[...], high[0:1], high[2:3])):
        replies = jnp.where(lane // slots == r, row, replies)
    replies = jnp.broadcast_to(-2.0 * replies * flat_slots(smap)[2:3], (8, LANES))
    begin = faces * width + 4 * LANES
    square = lax.broadcasted_iota(jnp.int32, (basis, basis), 0) == lax.broadcasted_iota(
        jnp.int32, (basis, basis), 1
    )
    columns = []
    for f in range(faces):
        column = lift[0, f:f + 1, :]
        for j in range(1, face_basis):
            column = column + lift[j, f:f + 1, :]
        columns.append(jnp.sum(jnp.where(square, column, 0.0), axis=1, keepdims=True))
    for h in range(width // LANES):
        cut = slice(h * LANES, (h + 1) * LANES)
        spread = []
        for f in range(faces):
            index = jnp.broadcast_to(neighbours[f:f + 1, cut], (8, LANES))
            found = jnp.take_along_axis(replies, index % LANES, axis=1, mode="promise_in_bounds")
            spread.append(columns[f] * jnp.where(index >= begin, found, 0.0)[0:1])
        for p in range(quants):
            stress = solvers[p, 0, :, cut] + solvers[p, 1, :, cut] + solvers[p, 2, :, cut]
            total = base[p, :, cut]
            for f in range(faces):
                total = total + stress[f:f + 1] * spread[f]
            out[p, :, cut] = total


def sent_rows(quants, face_basis):
    return -(-quants * face_basis // 8) * 8


def shards(
    solid_state, jacobians, flux_solvers, stiffness, trace_matrix, lift_matrix,
    neighbours, send_faces, surface_map, surface_normals, air_state, wind_field, air_medium,
):
    quants, basis, width = solid_state.shape
    faces, face_basis = trace_matrix.shape[0], trace_matrix.shape[1]
    dims = stiffness.shape[0]
    nx, nz, ny = air_state.shape[1:]
    jacobians = jnp.transpose(jacobians, (1, 2, 0, 3))
    flux_solvers = jnp.transpose(flux_solvers, (1, 2, 0, 3))
    trace_matrix = jnp.transpose(trace_matrix, (1, 0, 2))
    lift_matrix = jnp.transpose(lift_matrix, (2, 0, 1))
    surface_map = jnp.transpose(surface_map, (1, 0, 2))
    surface_normals = jnp.transpose(surface_normals, (1, 0, 2))
    pad = -(-basis // 8) * 8
    pad_k = -(-basis // 16) * 16
    rim_z = (7, nx, RADIUS, ny)
    rim_x = (7, RADIUS, nz, ny)
    ext = (4, nx + 2 * RADIUS, nz + 2 * ZRIM, ny)
    wide = ext[1:]
    block = (1, nx, nz, ny)
    tile = (8, LANES)

    rims = exchange(
        *call(
            raw_rims_kernel, "raw_rims", [rim_x, rim_z, rim_x, rim_z], [air_state, wind_field],
        )
    )

    sent = (sent_rows(quants, face_basis), LANES)
    integral, traces, state = call(
        predict_kernel, "predict",
        [(pad_k, quants * width), (quants, 16, faces * width), solid_state.shape],
        [solid_state, jacobians, stiffness, trace_matrix],
        [(pad_k, quants * width), (dims * pad, quants * width), (dims * pad, pad_k), (faces * 16, pad_k)],
        flops=40_000_000,
    )
    own, row = call(
        own_list_kernel, "own_list", [(quants, 16, LANES), tile], [traces, surface_map, surface_normals],
        after=[rims[3]],
    )
    far = swap(row, "gx", 0, 2), swap(row, "gx", 1, 2)
    txa, txb, tza, tzb = call(
        outgoing_kernel, "outgoing", [sent, sent, sent, sent], [traces, send_faces],
        [(4, quants, 16, LANES)], flops=10_000_000, after=[row],
    )
    pressure_x = (HEAD + RADIUS * nz, ny)
    pressure_z = (HEAD + nx * ZRIM, ny)
    both_x = (pressure_x[0] + sent[0], LANES)
    both_z = (pressure_z[0] + sent[0], LANES)
    raw, zb, za = call(
        raw_pressure_kernel, "raw_pressure", [block, both_z, both_z],
        [air_state, wind_field, air_medium, *rims, tza, tzb, row, *far], [ext],
    )
    both_zb, both_za = swap(zb, "gz", 1), swap(za, "gz", 0)
    (moved,) = call(
        advection_kernel, "advection", [(3, nx, nz, ny)],
        [air_state, wind_field, *rims], [ext], flops=10_000_000, after=[za],
    )
    xb, xa, lists = call(
        merge_kernel, "merge", [both_x, both_x, (HEAD, LANES)], [raw, txa, txb, both_zb, both_za, row, *far]
    )
    both_xb, both_xa = swap(xb, "gx", 1), swap(xa, "gx", 0)
    both = both_xb, both_zb, both_xa, both_za
    volume, token = call(
        volume_kernel, "volume", [solid_state.shape, tile], [state, integral, jacobians, stiffness],
        [(dims * pad, quants * width), (dims * pad, pad_k)], flops=10_000_000, after=[lists],
    )

    rim_x = (HEAD + 4 * RADIUS * nz, ny)
    rim_z = (4, nx, RADIUS, ny)
    air, xb, zb, xa, za, answer = call(
        injected_kernel, "injected",
        [air_state.shape, rim_x, rim_z, rim_x, rim_z, (1, LANES)],
        [air_state, wind_field, air_medium, raw, moved, *rims, *both, lists, surface_map],
        [(3 * nx, 3 * nz, ny), wide, (3,) + wide], after=[token],
    )
    half = faces // 2
    solid = volume
    for substep in range(1, SUBSTEPS):
        rims = exchange(xb, zb, xa, za)
        solid, token = call(
            functools.partial(flux_kernel, (substep - 1) * half, half), "flux", [solid_state.shape, tile],
            [solid, traces, own, flux_solvers, lift_matrix, neighbours, *both],
            [(quants, 5, 16, LANES), (half * 16, quants * width), (half * 16, pad)], flops=20_000_000,
            after=[xa],
        )
        pressure, xb, zb, xa, za = call(
            pressure_kernel, "pressure", [block, pressure_x, pressure_z, pressure_x, pressure_z],
            [air, wind_field, air_medium, *rims, answer], [ext], after=[token],
        )
        rises = exchange(xb, zb, xa, za)
        if substep == 1:
            replies = [answer, rises[0], rises[2]]
        (moved,) = call(
            advection_kernel, "advection", [(3, nx, nz, ny)],
            [air, wind_field, *rims], [ext], flops=10_000_000, after=[xa],
        )
        last = substep == SUBSTEPS - 1
        if last:
            (solid,) = call(
                replies_kernel, "replies", [solid_state.shape],
                [solid, flux_solvers, lift_matrix, neighbours, surface_map, *replies], after=[moved],
            )
        outs = [air_state.shape] + ([] if last else [rim_x, rim_z, rim_x, rim_z])
        done = call(
            velocity_kernel, "velocity", outs, [air, pressure, air_medium, moved, *rises], [wide]
        )
        air = done[0]
        if not last:
            xb, zb, xa, za = done[1:]
    return (solid, air)


def solution(mesh):
    in_specs = (
        P(None, None, ("gx", "gz")),
        P(None, None, None, ("gx", "gz")),
        P(None, None, None, ("gx", "gz")),
        P(),
        P(),
        P(),
        P(None, ("gx", "gz")),
        P(None, ("gx", "gz")),
        P(None, None, ("gx", "gz")),
        P(None, None, ("gx", "gz")),
        P(None, "gx", "gz", None),
        P(None, "gx", "gz", None),
        P(None, "gx", "gz", None),
    )
    out_specs = (P(None, None, ("gx", "gz")), P(None, "gx", "gz", None))
    return jax.shard_map(shards, mesh=mesh, in_specs=in_specs, out_specs=out_specs, check_vma=False)
```

```python
import functools

import jax
import jax.numpy as jnp
from jax import lax
from jax.experimental import pallas as pl
from jax.experimental.pallas import tpu as pltpu
from jax.sharding import PartitionSpec as P

ORDERS = 4
RADIUS = 4
SUBSTEPS = 3
ZRIM = 8
LANES = 128
HEAD = 8
FACE_ROWS = 10
K = 32
TIME_STEP = 0.5
STENCIL_WEIGHTS = (0.8, -0.2, 4.0 / 105.0, -1.0 / 280.0)
F32 = jnp.float32
BF16 = jnp.bfloat16


def call(kernel, name, outs, ins, scratch=(), flops=1_000_000, after=()):
    count, skip = len(ins), len(after)
    nbytes = 4 * sum(x.size for x in ins) + 4 * sum(functools.reduce(lambda m, n: m * n, s, 1) for s in outs)

    def body(*refs):
        kernel(*refs[:count], *refs[count + skip:])

    return pl.pallas_call(
        body,
        out_shape=[jax.ShapeDtypeStruct(s, F32) for s in outs],
        in_specs=[pl.BlockSpec(memory_space=pltpu.VMEM) for _ in ins]
        + [pl.BlockSpec(memory_space=pl.ANY) for _ in after],
        out_specs=[pl.BlockSpec(memory_space=pltpu.VMEM) for _ in outs],
        scratch_shapes=[pltpu.VMEM(s, F32) for s in scratch],
        compiler_params=pltpu.CompilerParams(vmem_limit_bytes=8 * 1024 * 1024),
        cost_estimate=pl.CostEstimate(flops=flops, bytes_accessed=nbytes, transcendentals=0),
        name=name,
    )(*ins, *after)


def swap(values, axis, odd, by=1):
    count = lax.axis_size(axis)
    pairs = []
    for i in range(count - by):
        if i // by % 2 == odd:
            pairs += [(i, i + by), (i + by, i)]
    return lax.ppermute(values, axis, pairs)


def exchange(xb, zb, xa, za):
    return swap(xb, "gx", 1), swap(zb, "gz", 1), swap(xa, "gx", 0), swap(za, "gz", 0)


def sides(axis, by=1):
    parity = (lax.axis_index(axis) // by) & 1
    return 1 - parity, parity


def by_side(pair, axis, by=1):
    first = sides(axis, by)[0]
    return jnp.where(first == 0, pair[0], pair[1]), jnp.where(first == 1, pair[0], pair[1])


def halves(values):
    high = values.astype(BF16)
    return high, (values - high.astype(F32)).astype(BF16)


def stacked_left(matrix):
    spread = matrix + pltpu.roll(matrix, K, 1) + pltpu.roll(matrix, 2 * K, 1)
    high = spread.astype(BF16).astype(F32)
    lane = lax.broadcasted_iota(jnp.int32, spread.shape, 1)
    return jnp.where(lane < 2 * K, high, spread - high).astype(BF16)[:, 0:3 * K]


def dot3(left, right):
    high, low = halves(right)
    return jnp.dot(left, jnp.concatenate([high, low, high], axis=0), preferred_element_type=F32)


def dot_exact(left, right, dims=(((1,), (0,)), ((), ()))):
    return lax.dot_general(
        left, right, dims, precision=lax.Precision.HIGHEST, preferred_element_type=F32
    )


def flat_slots(table, spread):
    rows, fields, slots = table.shape
    lane = lax.broadcasted_iota(jnp.int32, (8, LANES), 1)
    for r in range(rows):
        spread[r, 0:fields, 0:slots] = table[r].astype(F32)
    flat = jnp.zeros((8, LANES), F32)
    for r in range(rows):
        got = jnp.take_along_axis(spread[r], lane % slots, axis=1, mode="promise_in_bounds")
        flat = jnp.where(lane // slots == r, got, flat)
    return flat


def pack_x(out, at, source, side):
    fields, nx, nz, ny = source.shape
    start = side * (nx - RADIUS)
    rows = fields * RADIUS * nz
    at = HEAD + at * RADIUS * nz
    out[at:at + rows, :] = source[:, pl.ds(start, RADIUS)].reshape(rows, ny)


def pack_z(out, at, source, side):
    fields, nz = source.shape[0], source.shape[2]
    out[at:at + fields] = jnp.where(side == 1, source[:, :, nz - RADIUS:, :], source[:, :, 0:RADIUS, :])


def widen(ext, center, xb, zb, xa, za, first=0):
    fields, nx, nz, ny = center.shape
    ext[:, RADIUS:RADIUS + nx, ZRIM:ZRIM + nz] = center[...]
    for got, side in zip((xa, xb), sides("gx")):
        place = pl.ds(side * (nx + RADIUS), RADIUS)
        if len(got.shape) == 4:
            rows = got[first:first + fields]
        else:
            rows = got[HEAD:HEAD + fields * RADIUS * nz, :].reshape(fields, RADIUS, nz, ny)
        ext[:, place, ZRIM:ZRIM + nz] = rows
    low, high = by_side([got[first:first + fields] for got in (za, zb)], "gz")
    ext[:, RADIUS:RADIUS + nx, ZRIM - RADIUS:ZRIM] = low
    ext[:, RADIUS:RADIUS + nx, ZRIM + nz:ZRIM + nz + RADIUS] = high


def d1(load, x, lo, hi):
    total = None
    for m, w in enumerate(STENCIL_WEIGHTS, 1):
        term = w * (load(x + m, lo, hi) - load(x - m, lo, hi))
        total = term if total is None else total + term
    return total


def d2(load, x, lo, hi):
    total = None
    for m, w in enumerate(STENCIL_WEIGHTS, 1):
        term = w * (load(x, lo + m, hi + m) - load(x, lo - m, hi - m))
        total = term if total is None else total + term
    return total


def d3(values):
    width = values.shape[1]
    lane = lax.broadcasted_iota(jnp.int32, (1, width), 1)
    total = None
    for m, w in enumerate(STENCIL_WEIGHTS, 1):
        ahead = jnp.where(lane < width - m, w, 0.0) * pltpu.roll(values, width - m, 1)
        behind = jnp.where(lane >= m, w, 0.0) * pltpu.roll(values, m, 1)
        term = ahead - behind
        total = term if total is None else total + term
    return total


def field(ref, c):
    return lambda x, lo, hi: ref[c, x, lo:hi, :]


def plane(ref):
    return lambda x, lo, hi: ref[x, lo:hi, :]


def arrived(table, strip, band, n_gx, n_gz, reach, slots):
    lane = lax.broadcasted_iota(jnp.int32, (1, LANES), 1)
    got = jnp.zeros((1, LANES), F32)
    inside = (strip >= 0) & (strip < n_gx) & (band >= 0) & (band < n_gz)
    for r in range(reach):
        source = strip - (r - reach // 2)
        valid = inside & (source >= 0) & (source < n_gx)
        row = table[pl.ds(jnp.where(valid, source * n_gz + band, 0), 1), :]
        here = ((lane & (LANES // 2 - 1)) // slots == r) & valid
        got = jnp.where(here, row, got)
    turned = pltpu.roll(got, LANES // 2, 1)
    speed = jnp.where(lane < LANES // 2, got, turned)
    high = speed.astype(BF16).astype(F32)
    return jnp.where(lane < LANES // 2, high, speed - high), jnp.where(lane < LANES // 2, turned, got)


def cell_masks(cells, rows):
    cells = cells.astype(jnp.int32)
    place = lax.broadcasted_iota(jnp.int32, (rows, LANES), 0)
    third = lax.broadcasted_iota(jnp.int32, (LANES, LANES), 0)
    return cells // LANES == place, cells % LANES == third


def raw_rims_kernel(air, wind, xb, zb, xa, za):
    fields, nx = air.shape[:2]
    for out, side in zip((xa, xb), sides("gx")):
        rows = pl.ds(side * (nx - RADIUS), RADIUS)
        out[0:fields] = air[:, rows]
        out[fields:] = wind[:, rows]
    for out, side in zip((za, zb), sides("gz")):
        pack_z(out, 0, air, side)
        pack_z(out, fields, wind, side)


def lanes(at):
    return pl.ds(at if isinstance(at, int) else pl.multiple_of(at, LANES), LANES)


def jacobian_step(load, rot, emit, quants, dims, width):
    rows = rot.shape[0] // dims

    def half(h, carry):
        at = h * LANES
        acc = [None] * quants
        for d in range(dims):
            for q in range(quants):
                turned = rot[d * rows:(d + 1) * rows, lanes(q * width + at)].reshape(rows // 8, 8, LANES)
                for p in range(quants):
                    term = load(p, q, d, lanes(at)) * turned
                    acc[p] = term if acc[p] is None else acc[p] + term
        for p in range(quants):
            emit(p, at, acc[p].reshape(rows, LANES))
        return carry

    lax.fori_loop(0, width // LANES, half, 0)


def rotate(rot, left, source, quants, width):
    for q in range(quants):
        cut = slice(q * width, (q + 1) * width)
        rot[:, cut] = dot3(left, source[:, cut])


def take_slots(tiles, index):
    low = index % LANES
    high = index // LANES
    got = None
    for s, tile in enumerate(tiles):
        picked = jnp.take_along_axis(tile, low, axis=1, mode="promise_in_bounds")
        got = picked if got is None else jnp.where(high == s, picked, got)
    return got


def predict_kernel(
    state, jac, stiff, trace,
    integral, traces, kept,
    cur, rot, sp, tp,
):
    quants, basis, width = state.shape
    pad = sp.shape[0] // stiff.shape[0]
    face_basis, faces = trace.shape[:2]
    dims = stiff.shape[0]
    sp[...] = jnp.zeros_like(sp)
    tp[...] = jnp.zeros_like(tp)
    cur[...] = jnp.zeros_like(cur)
    for d in range(dims):
        sp[d * pad:d * pad + basis, 0:basis] = stiff[d]
    for f in range(faces):
        for j in range(face_basis):
            tp[f * 16 + j:f * 16 + j + 1, 0:basis] = trace[j, f:f + 1, :]
    for q in range(quants):
        cur[0:basis, q * width:(q + 1) * width] = state[q]
    kept[...] = state[...]
    integral[...] = TIME_STEP * cur[...]
    left = stacked_left(sp[...])

    def degree(k, weight):
        weight = jnp.where(k == 1, TIME_STEP**2 / 2, jnp.where(k == 2, TIME_STEP**3 / 6, TIME_STEP**4 / 24))
        rotate(rot, left, cur, quants, width)

        def emit(p, at, value):
            cut = lanes(p * width + at)
            cur[0:pad, cut] = -value
            integral[0:pad, cut] = integral[0:pad, cut] - weight * value

        jacobian_step(lambda p, q, d, cut: jac[p, q, d:d + 1, cut], rot, emit, quants, dims, width)
        return weight

    lax.fori_loop(1, ORDERS, degree, F32(0))
    restrict = stacked_left(tp[...])
    for q in range(quants):
        cut = slice(q * width, (q + 1) * width)
        done = dot3(restrict, integral[:, cut])
        for f in range(faces):
            traces[q, :, f * width:(f + 1) * width] = done[f * 16:(f + 1) * 16]


def own_list_kernel(traces, smap, normals, own, rows, spread):
    quants, _, all_slots = traces.shape
    slots = flat_slots(smap, spread)
    wanted = jnp.broadcast_to(slots[0:1].astype(jnp.int32), (16, LANES))

    def gather(q, carry):
        own[q] = take_slots([traces[q, :, s * LANES:(s + 1) * LANES] for s in range(all_slots // LANES)], wanted)
        return carry

    lax.fori_loop(0, quants, gather, 0)
    normal = flat_slots(normals, spread)
    speed = jnp.zeros((1, LANES), F32)
    for c in range(3):
        mean = jnp.sum(own[6 + c, 0:FACE_ROWS, :], axis=0, keepdims=True) * (1.0 / FACE_ROWS)
        speed = speed + normal[c:c + 1] * mean
    lane = lax.broadcasted_iota(jnp.int32, (1, LANES), 1)
    cells = pltpu.roll(slots[1:2], LANES // 2, 1)
    rows[...] = jnp.broadcast_to(jnp.where(lane < LANES // 2, slots[2:3] * speed, cells), rows.shape)


def outgoing_kernel(traces, sends, xa, xb, za, zb, picked):
    quants, _, slots = traces.shape
    rows = sent_rows(quants, FACE_ROWS)
    wanted = [jnp.broadcast_to(sends[d:d + 1, :], (16, LANES)) for d in range(4)]

    def gather(q, carry):
        tiles = [traces[q, :, s * LANES:(s + 1) * LANES] for s in range(slots // LANES)]
        for d in range(4):
            picked[d, q] = take_slots(tiles, wanted[d])
        return carry

    lax.fori_loop(0, quants, gather, 0)
    rest = FACE_ROWS - 8
    for axis, base, outs in (("gx", 0, (xa, xb)), ("gz", 2, (za, zb))):
        for out, side in zip(outs, sides(axis)):
            for q in range(quants):
                out[q * 8:q * 8 + 8, :] = picked[base + side, q, 0:8, :]
                at = quants * 8 + q * rest
                out[at:at + rest, :] = picked[base + side, q, 8:FACE_ROWS, :]
            out[quants * FACE_ROWS:, :] = jnp.zeros((rows - quants * FACE_ROWS, LANES), F32)


def pressure_rows(ext, wind, medium, x, nz):
    lo, hi = ZRIM, ZRIM + nz
    xe = x + RADIUS
    pressure = field(ext, 0)
    here = pressure(xe, lo, hi)
    divergence = d1(field(ext, 1), xe, lo, hi) + d2(field(ext, 2), xe, lo, hi) + d3(ext[3, xe, lo:hi, :])
    moved = (
        wind[0, x] * d1(pressure, xe, lo, hi)
        + wind[1, x] * d2(pressure, xe, lo, hi)
        + wind[2, x] * d3(here)
    )
    return here - medium[0, x] * divergence - moved


def pack_pressure(center, xs, zs):
    nx, nz, ny = center.shape[1:]
    for out, side in zip(xs, sides("gx")):
        start = side * (nx - RADIUS)
        out[HEAD:HEAD + RADIUS * nz, :] = center[0, pl.ds(start, RADIUS)].reshape(RADIUS * nz, ny)
    for out, side in zip(zs, sides("gz")):
        start = pl.multiple_of(side * (nz - ZRIM), ZRIM)
        out[HEAD:HEAD + nx * ZRIM, :] = center[0, :, pl.ds(start, ZRIM), :].reshape(nx * ZRIM, ny)


def widen_pressure(ext, center, xb, zb, xa, za):
    nx, nz, ny = center.shape
    ext[RADIUS:RADIUS + nx, ZRIM:ZRIM + nz] = center[...]
    for got, side in zip((xa, xb), sides("gx")):
        ext[pl.ds(side * (nx + RADIUS), RADIUS), ZRIM:ZRIM + nz] = got[HEAD:HEAD + RADIUS * nz, :].reshape(RADIUS, nz, ny)
    for got, side in zip((za, zb), sides("gz")):
        start = pl.multiple_of(side * (nz + ZRIM), ZRIM)
        ext[RADIUS:RADIUS + nx, pl.ds(start, ZRIM)] = got[HEAD:HEAD + nx * ZRIM, :].reshape(nx, ZRIM, ny)


def raw_pressure_kernel(
    air, wind, medium, xb, zb, xa, za, txa, txb, tza, tzb, pressure, oxb, ozb, oxa, oza, ext
):
    nx, nz, ny = air.shape[1:]
    widen(ext, air, xb, zb, xa, za)
    for x in range(nx):
        pressure[0, x] = pressure_rows(ext, wind, medium, x, nz)
    pack_pressure(pressure, (oxa, oxb), (oza, ozb))
    for out, sent in zip((oxa, oxb, oza, ozb), (txa, txb, tza, tzb)):
        out[0:HEAD, :] = jnp.zeros((HEAD, LANES), F32)
        out[out.shape[0] - sent.shape[0]:, :] = sent[...]


def put_rows(rows):
    place = lax.broadcasted_iota(jnp.int32, (HEAD, LANES), 0)
    out = jnp.zeros((HEAD, LANES), F32)
    for at, row in enumerate(rows):
        out = jnp.where(place == at, row, out)
    return out


def advection_kernel(air, wind, xb, zb, xa, za, moved, ext):
    nx, nz, ny = air.shape[1:]
    widen(ext, air, xb, zb, xa, za)
    lo, hi = ZRIM, ZRIM + nz
    for x in range(nx):
        xe = x + RADIUS
        for c in range(3):
            load = field(ext, 1 + c)
            moved[c, x] = (
                wind[0, x] * d1(load, xe, lo, hi)
                + wind[1, x] * d2(load, xe, lo, hi)
                + wind[2, x] * d3(load(xe, lo, hi))
            )


def velocities(out, center, moved, medium, wide, nx, nz):
    lo, hi = ZRIM, ZRIM + nz
    load = plane(wide)
    for x in range(nx):
        xe = x + RADIUS
        slopes = (d1(load, xe, lo, hi), d2(load, xe, lo, hi), d3(load(xe, lo, hi)))
        out[0, x] = load(xe, lo, hi)
        for c in range(3):
            out[1 + c, x] = center[1 + c, x] - medium[1, x] * slopes[c] - moved[c, x]


def pack_air(out, xb, zb, xa, za):
    for rim, side in zip((xa, xb), sides("gx")):
        pack_x(rim, 0, out, side)
    for rim, side in zip((za, zb), sides("gz")):
        pack_z(rim, 0, out, side)


def injected_kernel(
    n_gx, n_gz, air, wind, medium, raw, moved, wxb, wzb, wxa, wza, pxb, pzb, pxa, pza, table, smap,
    out, oxb, ozb, oxa, oza, answer, spread, wide, wide_wind,
):
    nx, nz, ny = air.shape[1:]
    reach, _, slots = smap.shape
    strip, band = lax.axis_index("gx"), lax.axis_index("gz")
    mul = functools.partial(
        lax.dot_general, dimension_numbers=(((1,), (1,)), ((), ())), preferred_element_type=F32
    )
    for da in range(3):
        for db in range(3):
            speed, cells = arrived(table, strip + da - 1, band + db - 1, n_gx, n_gz, reach, slots)
            row_mask, third_mask = cell_masks(cells, nx * nz)
            columns = jnp.where(third_mask, 1.0, 0.0).astype(BF16)
            if da == 1 and db == 1:
                seen, rest = halves(air[0].reshape(nx * nz, ny))
                looked = jnp.dot(seen, columns, preferred_element_type=F32)
                looked = looked + jnp.dot(rest, columns, preferred_element_type=F32)
                answer[...] = jnp.sum(jnp.where(row_mask, looked, 0.0), axis=0, keepdims=True)
            block = mul(jnp.where(row_mask, speed, 0.0).astype(BF16), columns)
            spread[da * nx:(da + 1) * nx, db * nz:(db + 1) * nz] = block.reshape(nx, nz, ny)
    widen(wide_wind, wind, wxb, wzb, wxa, wza, first=air.shape[0])
    widen_pressure(wide, raw.at[0], pxb, pzb, pxa, pza)
    load = plane(spread)
    for x in range(nx + 2 * RADIUS):
        xs = x + nx - RADIUS
        if RADIUS <= x < RADIUS + nx:
            lo, hi = 0, nz + 2 * ZRIM
        else:
            lo, hi = ZRIM, ZRIM + nz
        slo, shi = lo + nz - ZRIM, hi + nz - ZRIM
        here = load(xs, slo, shi)
        turned = (
            wide_wind[0, x, lo:hi, :] * d1(load, xs, slo, shi)
            + wide_wind[1, x, lo:hi, :] * d2(load, xs, slo, shi)
            + wide_wind[2, x, lo:hi, :] * d3(here)
        )
        wide[x, lo:hi, :] = wide[x, lo:hi, :] + (here - turned)
    velocities(out, air, moved, medium, wide, nx, nz)
    pack_air(out, oxb, ozb, oxa, oza)
    for rim in (oxa, oxb):
        rim[0:HEAD, :] = put_rows((answer[...],))


def pressure_kernel(air, wind, medium, xb, zb, xa, za, answer, pressure, oxb, ozb, oxa, oza, ext):
    nx, nz, ny = air.shape[1:]
    widen(ext, air, xb, zb, xa, za)
    for x in range(nx):
        pressure[0, x] = pressure_rows(ext, wind, medium, x, nz)
    pack_pressure(pressure, (oxa, oxb), (oza, ozb))
    low, high = by_side((xa[0:1, :], xb[0:1, :]), "gx")
    for rim in (oxa, oxb):
        rim[0:HEAD, :] = put_rows((answer[...], low, high))
    for rim in (oza, ozb):
        rim[0:HEAD, :] = jnp.zeros((HEAD, LANES), F32)


def velocity_kernel(air, pressure, medium, moved, xb, zb, xa, za, out, *rest):
    nx, nz, ny = air.shape[1:]
    wide = rest[-1]
    widen_pressure(wide, pressure.at[0], xb, zb, xa, za)
    velocities(out, air, moved, medium, wide, nx, nz)
    if len(rest) > 1:
        pack_air(out, *rest[:-1])
        for rim in (rest[0], rest[2]):
            rim[0:HEAD, :] = jnp.zeros((HEAD, LANES), F32)


def volume_kernel(state, integral, jac, stiff, out, token, rot, sp):
    quants, basis, width = state.shape
    dims = stiff.shape[0]
    pad = sp.shape[0] // dims
    token[...] = jnp.zeros_like(token)
    sp[...] = jnp.zeros_like(sp)
    place = lax.broadcasted_iota(jnp.int32, (basis, basis), 0)
    other = lax.broadcasted_iota(jnp.int32, (basis, basis), 1)
    unit = jnp.where(place == other, 1.0, 0.0).astype(F32)
    for d in range(dims):
        sp[d * pad:d * pad + basis, 0:basis] = dot_exact(unit, stiff[d], (((1,), (1,)), ((), ())))
    rotate(rot, stacked_left(sp[...]), integral, quants, width)

    def emit(p, at, value):
        out[p, :, lanes(at)] = state[p, :, lanes(at)] + value[0:basis]

    jacobian_step(lambda p, q, d, cut: jac[p, q, d:d + 1, cut], rot, emit, quants, dims, width)


def flux_kernel(
    first, faces, base, traces, own, solvers, lift, neighbours, xb, zb, xa, za,
    out, token, tiles, flux, lp,
):
    token[...] = jnp.zeros_like(token)
    quants, basis, width = base.shape
    face_basis = lift.shape[0]
    skip = xa.shape[0] - sent_rows(quants, face_basis)
    for axis, base_tile, gots in (("gx", 0, (xa, xb)), ("gz", 2, (za, zb))):
        for got, side in zip(gots, sides(axis)):
            for q in range(quants):
                tiles[q, base_tile + side, 0:8, :] = got[skip + q * 8:skip + q * 8 + 8, :]
                at = skip + quants * 8 + q * 2
                tiles[q, base_tile + side, 8:face_basis, :] = got[at:at + 2, :]
                tiles[q, base_tile + side, face_basis:, :] = jnp.zeros((16 - face_basis, LANES), F32)
    for q in range(quants):
        tiles[q, 4] = -own[q] if q < 3 else own[q]
    lp[...] = jnp.zeros_like(lp)
    for f in range(faces):
        for j in range(face_basis):
            lp[f * 16 + j:f * 16 + j + 1, 0:basis] = lift[j, first + f:first + f + 1, :]
    unit = lax.broadcasted_iota(jnp.int32, (lp.shape[1], lp.shape[1]), 0) == lax.broadcasted_iota(
        jnp.int32, (lp.shape[1], lp.shape[1]), 1
    )
    lifted = stacked_left(dot_exact(jnp.where(unit, 1.0, 0.0).astype(F32), lp[...], (((1,), (1,)), ((), ()))))
    local = traces.shape[2] // LANES
    halves_in = width // LANES

    def one(h, carry):
        at = h * LANES
        for f in range(faces):
            index = jnp.broadcast_to(neighbours[first + f:first + f + 1, lanes(at)], (16, LANES))
            acc = [None] * quants
            for q in range(quants):
                pool = [traces[q, :, s * LANES:(s + 1) * LANES] for s in range(local)]
                pool += [tiles[q, s] for s in range(5)]
                mine = traces[q, :, lanes((first + f) * width + at)]
                jump = take_slots(pool, index) - mine
                for p in range(quants):
                    term = solvers[p, q, first + f:first + f + 1, lanes(at)] * jump
                    acc[p] = term if acc[p] is None else acc[p] + term
            for p in range(quants):
                flux[f * 16:(f + 1) * 16, lanes(p * width + at)] = acc[p]
        return carry

    lax.fori_loop(0, halves_in, one, 0)
    for p in range(quants):
        cut = slice(p * width, (p + 1) * width)
        out[p] = base[p] + dot3(lifted, flux[:, cut])[0:basis]


def replies_kernel(base, solvers, lift, neighbours, smap, answer, rxb, rxa, out, slot_spread):
    quants, basis, width = base.shape
    face_basis, faces = lift.shape[:2]
    slots = smap.shape[2]
    low, high = by_side((rxa[0:HEAD, :], rxb[0:HEAD, :]), "gx")
    lane = lax.broadcasted_iota(jnp.int32, (1, LANES), 1)
    replies = jnp.zeros((1, LANES), F32)
    for r, row in enumerate((low[1:2], low[0:1], answer[...], high[0:1], high[2:3])):
        replies = jnp.where(lane // slots == r, row, replies)
    replies = jnp.broadcast_to(-2.0 * replies * flat_slots(smap, slot_spread)[2:3], (8, LANES))
    begin = faces * width + 4 * LANES
    square = lax.broadcasted_iota(jnp.int32, (basis, basis), 0) == lax.broadcasted_iota(
        jnp.int32, (basis, basis), 1
    )
    columns = []
    for f in range(faces):
        column = lift[0, f:f + 1, :]
        for j in range(1, face_basis):
            column = column + lift[j, f:f + 1, :]
        columns.append(jnp.sum(jnp.where(square, column, 0.0), axis=1, keepdims=True))
    for h in range(width // LANES):
        cut = slice(h * LANES, (h + 1) * LANES)
        spread = []
        for f in range(faces):
            index = jnp.broadcast_to(neighbours[f:f + 1, cut], (8, LANES))
            found = jnp.take_along_axis(replies, index % LANES, axis=1, mode="promise_in_bounds")
            spread.append(columns[f] * jnp.where(index >= begin, found, 0.0)[0:1])
        for p in range(quants):
            stress = solvers[p, 0, :, cut] + solvers[p, 1, :, cut] + solvers[p, 2, :, cut]
            total = base[p, :, cut]
            for f in range(faces):
                total = total + stress[f:f + 1] * spread[f]
            out[p, :, cut] = total


def sent_rows(quants, face_basis):
    return -(-quants * face_basis // 8) * 8


def shards(
    solid_state, jacobians, flux_solvers, stiffness, trace_matrix, lift_matrix,
    neighbours, send_faces, surface_map, surface_normals, air_state, wind_field, air_medium,
):
    quants, basis, width = solid_state.shape
    faces, face_basis = trace_matrix.shape[0], trace_matrix.shape[1]
    dims = stiffness.shape[0]
    nx, nz, ny = air_state.shape[1:]
    n_gx, n_gz = lax.axis_size("gx"), lax.axis_size("gz")
    jacobians = jnp.transpose(jacobians, (1, 2, 0, 3))
    flux_solvers = jnp.transpose(flux_solvers, (1, 2, 0, 3))
    trace_matrix = jnp.transpose(trace_matrix, (1, 0, 2))
    lift_matrix = jnp.transpose(lift_matrix, (2, 0, 1))
    surface_map = jnp.transpose(surface_map, (1, 0, 2))
    surface_normals = jnp.transpose(surface_normals, (1, 0, 2))
    pad = -(-basis // 8) * 8
    rim_z = (7, nx, RADIUS, ny)
    rim_x = (7, RADIUS, nz, ny)
    ext = (4, nx + 2 * RADIUS, nz + 2 * ZRIM, ny)
    wide = ext[1:]
    block = (1, nx, nz, ny)
    tile = (8, LANES)

    rims = exchange(
        *call(
            raw_rims_kernel, "raw_rims", [rim_x, rim_z, rim_x, rim_z], [air_state, wind_field],
        )
    )

    sent = (sent_rows(quants, face_basis), LANES)
    integral, traces, state = call(
        predict_kernel, "predict",
        [(K, quants * width), (quants, 16, faces * width), solid_state.shape],
        [solid_state, jacobians, stiffness, trace_matrix],
        [(K, quants * width), (dims * pad, quants * width), (dims * pad, LANES), (faces * 16, LANES)],
        flops=40_000_000,
    )
    own, rows = call(
        own_list_kernel, "own_list", [(quants, 16, LANES), (n_gx * n_gz, LANES)],
        [traces, surface_map, surface_normals], [(surface_map.shape[0], 8, LANES)], after=[rims[3]],
    )
    lists = lax.all_to_all(rows, ("gx", "gz"), split_axis=0, concat_axis=0, tiled=True)
    sent_four = call(
        outgoing_kernel, "outgoing", [sent, sent, sent, sent], [traces, send_faces],
        [(4, quants, 16, LANES)], flops=10_000_000, after=[rows],
    )
    pressure_x = (HEAD + RADIUS * nz, ny)
    pressure_z = (HEAD + nx * ZRIM, ny)
    both_x = (pressure_x[0] + sent[0], LANES)
    both_z = (pressure_z[0] + sent[0], LANES)
    raw, xb, zb, xa, za = call(
        raw_pressure_kernel, "raw_pressure", [block, both_x, both_z, both_x, both_z],
        [air_state, wind_field, air_medium, *rims, *sent_four], [ext],
    )
    both = exchange(xb, zb, xa, za)
    (moved,) = call(
        advection_kernel, "advection", [(3, nx, nz, ny)],
        [air_state, wind_field, *rims], [ext], flops=10_000_000, after=[xa],
    )
    volume, token = call(
        volume_kernel, "volume", [solid_state.shape, tile], [state, integral, jacobians, stiffness],
        [(dims * pad, quants * width), (dims * pad, LANES)], flops=10_000_000, after=[xa],
    )

    rim_x = (HEAD + 4 * RADIUS * nz, ny)
    rim_z = (4, nx, RADIUS, ny)
    air, xb, zb, xa, za, answer = call(
        functools.partial(injected_kernel, n_gx, n_gz), "injected",
        [air_state.shape, rim_x, rim_z, rim_x, rim_z, (1, LANES)],
        [air_state, wind_field, air_medium, raw, moved, *rims, *both, lists, surface_map],
        [(3 * nx, 3 * nz, ny), wide, (3,) + wide], after=[token],
    )
    half = faces // 2
    solid = volume
    for substep in range(1, SUBSTEPS):
        rims = exchange(xb, zb, xa, za)
        solid, token = call(
            functools.partial(flux_kernel, (substep - 1) * half, half), "flux", [solid_state.shape, tile],
            [solid, traces, own, flux_solvers, lift_matrix, neighbours, *both],
            [(quants, 5, 16, LANES), (half * 16, quants * width), (LANES, pad)], flops=20_000_000,
            after=[xa],
        )
        pressure, xb, zb, xa, za = call(
            pressure_kernel, "pressure", [block, pressure_x, pressure_z, pressure_x, pressure_z],
            [air, wind_field, air_medium, *rims, answer], [ext], after=[token],
        )
        rises = exchange(xb, zb, xa, za)
        if substep == 1:
            replies = [answer, rises[0], rises[2]]
        (moved,) = call(
            advection_kernel, "advection", [(3, nx, nz, ny)],
            [air, wind_field, *rims], [ext], flops=10_000_000, after=[xa],
        )
        last = substep == SUBSTEPS - 1
        if last:
            (solid,) = call(
                replies_kernel, "replies", [solid_state.shape],
                [solid, flux_solvers, lift_matrix, neighbours, surface_map, *replies],
                [(surface_map.shape[0], 8, LANES)], after=[moved],
            )
        outs = [air_state.shape] + ([] if last else [rim_x, rim_z, rim_x, rim_z])
        done = call(
            velocity_kernel, "velocity", outs, [air, pressure, air_medium, moved, *rises], [wide]
        )
        air = done[0]
        if not last:
            xb, zb, xa, za = done[1:]
    return (solid, air)


def solution(mesh):
    in_specs = (
        P(None, None, ("gx", "gz")),
        P(None, None, None, ("gx", "gz")),
        P(None, None, None, ("gx", "gz")),
        P(),
        P(),
        P(),
        P(None, ("gx", "gz")),
        P(None, ("gx", "gz")),
        P(None, None, ("gx", "gz")),
        P(None, None, ("gx", "gz")),
        P(None, "gx", "gz", None),
        P(None, "gx", "gz", None),
        P(None, "gx", "gz", None),
    )
    out_specs = (P(None, None, ("gx", "gz")), P(None, "gx", "gz", None))
    return jax.shard_map(shards, mesh=mesh, in_specs=in_specs, out_specs=out_specs, check_vma=False)
```

```python
import functools

import jax
import jax.numpy as jnp
from jax import lax
from jax.experimental import pallas as pl
from jax.experimental.pallas import tpu as pltpu
from jax.sharding import PartitionSpec as P

ORDERS = 4
RADIUS = 4
SUBSTEPS = 3
ZRIM = 8
LANES = 128
HEAD = 8
FACE_ROWS = 10
K = 32
TIME_STEP = 0.5
STENCIL_WEIGHTS = (0.8, -0.2, 4.0 / 105.0, -1.0 / 280.0)
F32 = jnp.float32
BF16 = jnp.bfloat16


def call(kernel, name, outs, ins, scratch=(), flops=1_000_000, after=()):
    count, skip = len(ins), len(after)
    nbytes = 4 * sum(x.size for x in ins) + 4 * sum(functools.reduce(lambda m, n: m * n, s, 1) for s in outs)

    def body(*refs):
        kernel(*refs[:count], *refs[count + skip:])

    return pl.pallas_call(
        body,
        out_shape=[jax.ShapeDtypeStruct(s, F32) for s in outs],
        in_specs=[pl.BlockSpec(memory_space=pltpu.VMEM) for _ in ins]
        + [pl.BlockSpec(memory_space=pl.ANY) for _ in after],
        out_specs=[pl.BlockSpec(memory_space=pltpu.VMEM) for _ in outs],
        scratch_shapes=[pltpu.VMEM(s, F32) for s in scratch],
        compiler_params=pltpu.CompilerParams(vmem_limit_bytes=8 * 1024 * 1024),
        cost_estimate=pl.CostEstimate(flops=flops, bytes_accessed=nbytes, transcendentals=0),
        name=name,
    )(*ins, *after)


def swap(values, axis, odd, by=1):
    count = lax.axis_size(axis)
    pairs = []
    for i in range(count - by):
        if i // by % 2 == odd:
            pairs += [(i, i + by), (i + by, i)]
    return lax.ppermute(values, axis, pairs)


def exchange(xb, zb, xa, za):
    return swap(xb, "gx", 1), swap(zb, "gz", 1), swap(xa, "gx", 0), swap(za, "gz", 0)


def sides(axis, by=1):
    parity = (lax.axis_index(axis) // by) & 1
    return 1 - parity, parity


def by_side(pair, axis, by=1):
    first = sides(axis, by)[0]
    return jnp.where(first == 0, pair[0], pair[1]), jnp.where(first == 1, pair[0], pair[1])


def halves(values):
    high = values.astype(BF16)
    return high, (values - high.astype(F32)).astype(BF16)


def stacked_left(matrix):
    spread = matrix + pltpu.roll(matrix, K, 1) + pltpu.roll(matrix, 2 * K, 1)
    high = spread.astype(BF16).astype(F32)
    lane = lax.broadcasted_iota(jnp.int32, spread.shape, 1)
    return jnp.where(lane < 2 * K, high, spread - high).astype(BF16)[:, 0:3 * K]


def dot3(left, right):
    high, low = halves(right)
    return jnp.dot(left, jnp.concatenate([high, low, high], axis=0), preferred_element_type=F32)


def dot_exact(left, right, dims=(((1,), (0,)), ((), ()))):
    return lax.dot_general(
        left, right, dims, precision=lax.Precision.HIGHEST, preferred_element_type=F32
    )


def flat_slots(table, spread):
    rows, fields, slots = table.shape
    lane = lax.broadcasted_iota(jnp.int32, (8, LANES), 1)
    for r in range(rows):
        spread[r, 0:fields, 0:slots] = table[r].astype(F32)
    flat = jnp.zeros((8, LANES), F32)
    for r in range(rows):
        got = jnp.take_along_axis(spread[r], lane % slots, axis=1, mode="promise_in_bounds")
        flat = jnp.where(lane // slots == r, got, flat)
    return flat


def pack_x(out, at, source, side):
    fields, nx, nz, ny = source.shape
    start = side * (nx - RADIUS)
    rows = fields * RADIUS * nz
    at = HEAD + at * RADIUS * nz
    out[at:at + rows, :] = source[:, pl.ds(start, RADIUS)].reshape(rows, ny)


def pack_z(out, at, source, side):
    fields, nz = source.shape[0], source.shape[2]
    out[at:at + fields] = jnp.where(side == 1, source[:, :, nz - RADIUS:, :], source[:, :, 0:RADIUS, :])


def widen(ext, center, xb, zb, xa, za, first=0):
    fields, nx, nz, ny = center.shape
    ext[:, RADIUS:RADIUS + nx, ZRIM:ZRIM + nz] = center[...]
    for got, side in zip((xa, xb), sides("gx")):
        place = pl.ds(side * (nx + RADIUS), RADIUS)
        if len(got.shape) == 4:
            rows = got[first:first + fields]
        else:
            rows = got[HEAD:HEAD + fields * RADIUS * nz, :].reshape(fields, RADIUS, nz, ny)
        ext[:, place, ZRIM:ZRIM + nz] = rows
    low, high = by_side([got[first:first + fields] for got in (za, zb)], "gz")
    ext[:, RADIUS:RADIUS + nx, ZRIM - RADIUS:ZRIM] = low
    ext[:, RADIUS:RADIUS + nx, ZRIM + nz:ZRIM + nz + RADIUS] = high


def d1(load, x, lo, hi):
    total = None
    for m, w in enumerate(STENCIL_WEIGHTS, 1):
        term = w * (load(x + m, lo, hi) - load(x - m, lo, hi))
        total = term if total is None else total + term
    return total


def d2(load, x, lo, hi):
    total = None
    for m, w in enumerate(STENCIL_WEIGHTS, 1):
        term = w * (load(x, lo + m, hi + m) - load(x, lo - m, hi - m))
        total = term if total is None else total + term
    return total


def d3(values):
    width = values.shape[1]
    lane = lax.broadcasted_iota(jnp.int32, (1, width), 1)
    total = None
    for m, w in enumerate(STENCIL_WEIGHTS, 1):
        ahead = jnp.where(lane < width - m, w, 0.0) * pltpu.roll(values, width - m, 1)
        behind = jnp.where(lane >= m, w, 0.0) * pltpu.roll(values, m, 1)
        term = ahead - behind
        total = term if total is None else total + term
    return total


def field(ref, c):
    return lambda x, lo, hi: ref[c, x, lo:hi, :]


def plane(ref):
    return lambda x, lo, hi: ref[x, lo:hi, :]


def arrived(table, strip, band, n_gx, n_gz, reach, slots):
    lane = lax.broadcasted_iota(jnp.int32, (1, LANES), 1)
    got = jnp.zeros((1, LANES), F32)
    inside = (strip >= 0) & (strip < n_gx) & (band >= 0) & (band < n_gz)
    for r in range(reach):
        source = strip - (r - reach // 2)
        valid = inside & (source >= 0) & (source < n_gx)
        at = jnp.where(valid, source * n_gz + band, 0) * 8
        row = table[pl.ds(pl.multiple_of(at, 8), 8), :][0:1]
        here = ((lane & (LANES // 2 - 1)) // slots == r) & valid
        got = jnp.where(here, row, got)
    turned = pltpu.roll(got, LANES // 2, 1)
    speed = jnp.where(lane < LANES // 2, got, turned)
    high = speed.astype(BF16).astype(F32)
    return jnp.where(lane < LANES // 2, high, speed - high), jnp.where(lane < LANES // 2, turned, got)


def cell_masks(cells, rows):
    cells = cells.astype(jnp.int32)
    place = lax.broadcasted_iota(jnp.int32, (rows, LANES), 0)
    third = lax.broadcasted_iota(jnp.int32, (LANES, LANES), 0)
    return cells // LANES == place, cells % LANES == third


def raw_rims_kernel(air, wind, xb, zb, xa, za):
    fields, nx = air.shape[:2]
    for out, side in zip((xa, xb), sides("gx")):
        rows = pl.ds(side * (nx - RADIUS), RADIUS)
        out[0:fields] = air[:, rows]
        out[fields:] = wind[:, rows]
    for out, side in zip((za, zb), sides("gz")):
        pack_z(out, 0, air, side)
        pack_z(out, fields, wind, side)


def lanes(at):
    return pl.ds(at if isinstance(at, int) else pl.multiple_of(at, LANES), LANES)


def jacobian_step(load, rot, emit, quants, dims, width):
    rows = rot.shape[0] // dims

    def half(h, carry):
        at = h * LANES
        acc = [None] * quants
        for d in range(dims):
            for q in range(quants):
                turned = rot[d * rows:(d + 1) * rows, lanes(q * width + at)].reshape(rows // 8, 8, LANES)
                for p in range(quants):
                    term = load(p, q, d, lanes(at)) * turned
                    acc[p] = term if acc[p] is None else acc[p] + term
        for p in range(quants):
            emit(p, at, acc[p].reshape(rows, LANES))
        return carry

    lax.fori_loop(0, width // LANES, half, 0)


def rotate(rot, left, source, quants, width):
    for q in range(quants):
        cut = slice(q * width, (q + 1) * width)
        rot[:, cut] = dot3(left, source[:, cut])


def take_slots(tiles, index):
    low = index % LANES
    high = index // LANES
    got = None
    for s, tile in enumerate(tiles):
        picked = jnp.take_along_axis(tile, low, axis=1, mode="promise_in_bounds")
        got = picked if got is None else jnp.where(high == s, picked, got)
    return got


def predict_kernel(
    state, jac, stiff, trace,
    integral, traces, kept,
    cur, rot, sp, tp,
):
    quants, basis, width = state.shape
    pad = sp.shape[0] // stiff.shape[0]
    face_basis, faces = trace.shape[:2]
    dims = stiff.shape[0]
    sp[...] = jnp.zeros_like(sp)
    tp[...] = jnp.zeros_like(tp)
    cur[...] = jnp.zeros_like(cur)
    for d in range(dims):
        sp[d * pad:d * pad + basis, 0:basis] = stiff[d]
    for f in range(faces):
        for j in range(face_basis):
            tp[f * 16 + j:f * 16 + j + 1, 0:basis] = trace[j, f:f + 1, :]
    for q in range(quants):
        cur[0:basis, q * width:(q + 1) * width] = state[q]
    kept[...] = state[...]
    integral[...] = TIME_STEP * cur[...]
    left = stacked_left(sp[...])

    def degree(k, weight):
        weight = jnp.where(k == 1, TIME_STEP**2 / 2, jnp.where(k == 2, TIME_STEP**3 / 6, TIME_STEP**4 / 24))
        rotate(rot, left, cur, quants, width)

        def emit(p, at, value):
            cut = lanes(p * width + at)
            cur[0:pad, cut] = -value
            integral[0:pad, cut] = integral[0:pad, cut] - weight * value

        jacobian_step(lambda p, q, d, cut: jac[p, q, d:d + 1, cut], rot, emit, quants, dims, width)
        return weight

    lax.fori_loop(1, ORDERS, degree, F32(0))
    restrict = stacked_left(tp[...])
    for q in range(quants):
        cut = slice(q * width, (q + 1) * width)
        done = dot3(restrict, integral[:, cut])
        for f in range(faces):
            traces[q, :, f * width:(f + 1) * width] = done[f * 16:(f + 1) * 16]


def own_list_kernel(traces, smap, normals, own, rows, spread):
    quants, _, all_slots = traces.shape
    slots = flat_slots(smap, spread)
    wanted = jnp.broadcast_to(slots[0:1].astype(jnp.int32), (16, LANES))

    def gather(q, carry):
        own[q] = take_slots([traces[q, :, s * LANES:(s + 1) * LANES] for s in range(all_slots // LANES)], wanted)
        return carry

    lax.fori_loop(0, quants, gather, 0)
    normal = flat_slots(normals, spread)
    speed = jnp.zeros((1, LANES), F32)
    for c in range(3):
        mean = jnp.sum(own[6 + c, 0:FACE_ROWS, :], axis=0, keepdims=True) * (1.0 / FACE_ROWS)
        speed = speed + normal[c:c + 1] * mean
    lane = lax.broadcasted_iota(jnp.int32, (1, LANES), 1)
    cells = pltpu.roll(slots[1:2], LANES // 2, 1)
    rows[...] = jnp.broadcast_to(jnp.where(lane < LANES // 2, slots[2:3] * speed, cells), rows.shape)


def outgoing_kernel(traces, sends, xa, xb, za, zb, picked):
    quants, _, slots = traces.shape
    rows = sent_rows(quants, FACE_ROWS)
    wanted = [jnp.broadcast_to(sends[d:d + 1, :], (16, LANES)) for d in range(4)]

    def gather(q, carry):
        tiles = [traces[q, :, s * LANES:(s + 1) * LANES] for s in range(slots // LANES)]
        for d in range(4):
            picked[d, q] = take_slots(tiles, wanted[d])
        return carry

    lax.fori_loop(0, quants, gather, 0)
    rest = FACE_ROWS - 8
    for axis, base, outs in (("gx", 0, (xa, xb)), ("gz", 2, (za, zb))):
        for out, side in zip(outs, sides(axis)):
            for q in range(quants):
                out[q * 8:q * 8 + 8, :] = picked[base + side, q, 0:8, :]
                at = quants * 8 + q * rest
                out[at:at + rest, :] = picked[base + side, q, 8:FACE_ROWS, :]
            out[quants * FACE_ROWS:, :] = jnp.zeros((rows - quants * FACE_ROWS, LANES), F32)


def pressure_rows(ext, wind, medium, x, nz):
    lo, hi = ZRIM, ZRIM + nz
    xe = x + RADIUS
    pressure = field(ext, 0)
    here = pressure(xe, lo, hi)
    divergence = d1(field(ext, 1), xe, lo, hi) + d2(field(ext, 2), xe, lo, hi) + d3(ext[3, xe, lo:hi, :])
    moved = (
        wind[0, x] * d1(pressure, xe, lo, hi)
        + wind[1, x] * d2(pressure, xe, lo, hi)
        + wind[2, x] * d3(here)
    )
    return here - medium[0, x] * divergence - moved


def pack_pressure(center, xs, zs):
    nx, nz, ny = center.shape[1:]
    for out, side in zip(xs, sides("gx")):
        start = side * (nx - RADIUS)
        out[HEAD:HEAD + RADIUS * nz, :] = center[0, pl.ds(start, RADIUS)].reshape(RADIUS * nz, ny)
    for out, side in zip(zs, sides("gz")):
        start = pl.multiple_of(side * (nz - ZRIM), ZRIM)
        out[HEAD:HEAD + nx * ZRIM, :] = center[0, :, pl.ds(start, ZRIM), :].reshape(nx * ZRIM, ny)


def widen_pressure(ext, center, xb, zb, xa, za):
    nx, nz, ny = center.shape
    ext[RADIUS:RADIUS + nx, ZRIM:ZRIM + nz] = center[...]
    for got, side in zip((xa, xb), sides("gx")):
        ext[pl.ds(side * (nx + RADIUS), RADIUS), ZRIM:ZRIM + nz] = got[HEAD:HEAD + RADIUS * nz, :].reshape(RADIUS, nz, ny)
    for got, side in zip((za, zb), sides("gz")):
        start = pl.multiple_of(side * (nz + ZRIM), ZRIM)
        ext[RADIUS:RADIUS + nx, pl.ds(start, ZRIM)] = got[HEAD:HEAD + nx * ZRIM, :].reshape(nx, ZRIM, ny)


def raw_pressure_kernel(
    air, wind, medium, xb, zb, xa, za, txa, txb, tza, tzb, pressure, oxb, ozb, oxa, oza, ext
):
    nx, nz, ny = air.shape[1:]
    widen(ext, air, xb, zb, xa, za)
    for x in range(nx):
        pressure[0, x] = pressure_rows(ext, wind, medium, x, nz)
    pack_pressure(pressure, (oxa, oxb), (oza, ozb))
    for out, sent in zip((oxa, oxb, oza, ozb), (txa, txb, tza, tzb)):
        out[0:HEAD, :] = jnp.zeros((HEAD, LANES), F32)
        out[out.shape[0] - sent.shape[0]:, :] = sent[...]


def put_rows(rows):
    place = lax.broadcasted_iota(jnp.int32, (HEAD, LANES), 0)
    out = jnp.zeros((HEAD, LANES), F32)
    for at, row in enumerate(rows):
        out = jnp.where(place == at, row, out)
    return out


def advection_kernel(air, wind, xb, zb, xa, za, moved, ext):
    nx, nz, ny = air.shape[1:]
    widen(ext, air, xb, zb, xa, za)
    lo, hi = ZRIM, ZRIM + nz
    for x in range(nx):
        xe = x + RADIUS
        for c in range(3):
            load = field(ext, 1 + c)
            moved[c, x] = (
                wind[0, x] * d1(load, xe, lo, hi)
                + wind[1, x] * d2(load, xe, lo, hi)
                + wind[2, x] * d3(load(xe, lo, hi))
            )


def velocities(out, center, moved, medium, wide, nx, nz):
    lo, hi = ZRIM, ZRIM + nz
    load = plane(wide)
    for x in range(nx):
        xe = x + RADIUS
        slopes = (d1(load, xe, lo, hi), d2(load, xe, lo, hi), d3(load(xe, lo, hi)))
        out[0, x] = load(xe, lo, hi)
        for c in range(3):
            out[1 + c, x] = center[1 + c, x] - medium[1, x] * slopes[c] - moved[c, x]


def pack_air(out, xb, zb, xa, za):
    for rim, side in zip((xa, xb), sides("gx")):
        pack_x(rim, 0, out, side)
    for rim, side in zip((za, zb), sides("gz")):
        pack_z(rim, 0, out, side)


def injected_kernel(
    n_gx, n_gz, air, wind, medium, raw, moved, wxb, wzb, wxa, wza, pxb, pzb, pxa, pza, table, smap,
    out, oxb, ozb, oxa, oza, answer, spread, wide, wide_wind,
):
    nx, nz, ny = air.shape[1:]
    reach, _, slots = smap.shape
    strip, band = lax.axis_index("gx"), lax.axis_index("gz")
    mul = functools.partial(
        lax.dot_general, dimension_numbers=(((1,), (1,)), ((), ())), preferred_element_type=F32
    )
    for da in range(3):
        for db in range(3):
            speed, cells = arrived(table, strip + da - 1, band + db - 1, n_gx, n_gz, reach, slots)
            row_mask, third_mask = cell_masks(cells, nx * nz)
            columns = jnp.where(third_mask, 1.0, 0.0).astype(BF16)
            if da == 1 and db == 1:
                seen, rest = halves(air[0].reshape(nx * nz, ny))
                looked = jnp.dot(seen, columns, preferred_element_type=F32)
                looked = looked + jnp.dot(rest, columns, preferred_element_type=F32)
                answer[...] = jnp.sum(jnp.where(row_mask, looked, 0.0), axis=0, keepdims=True)
            block = mul(jnp.where(row_mask, speed, 0.0).astype(BF16), columns)
            spread[da * nx:(da + 1) * nx, db * nz:(db + 1) * nz] = block.reshape(nx, nz, ny)
    widen(wide_wind, wind, wxb, wzb, wxa, wza, first=air.shape[0])
    widen_pressure(wide, raw.at[0], pxb, pzb, pxa, pza)
    load = plane(spread)
    for x in range(nx + 2 * RADIUS):
        xs = x + nx - RADIUS
        if RADIUS <= x < RADIUS + nx:
            lo, hi = 0, nz + 2 * ZRIM
        else:
            lo, hi = ZRIM, ZRIM + nz
        slo, shi = lo + nz - ZRIM, hi + nz - ZRIM
        here = load(xs, slo, shi)
        turned = (
            wide_wind[0, x, lo:hi, :] * d1(load, xs, slo, shi)
            + wide_wind[1, x, lo:hi, :] * d2(load, xs, slo, shi)
            + wide_wind[2, x, lo:hi, :] * d3(here)
        )
        wide[x, lo:hi, :] = wide[x, lo:hi, :] + (here - turned)
    velocities(out, air, moved, medium, wide, nx, nz)
    pack_air(out, oxb, ozb, oxa, oza)
    for rim in (oxa, oxb):
        rim[0:HEAD, :] = put_rows((answer[...],))


def pressure_kernel(air, wind, medium, xb, zb, xa, za, answer, pressure, oxb, ozb, oxa, oza, ext):
    nx, nz, ny = air.shape[1:]
    widen(ext, air, xb, zb, xa, za)
    for x in range(nx):
        pressure[0, x] = pressure_rows(ext, wind, medium, x, nz)
    pack_pressure(pressure, (oxa, oxb), (oza, ozb))
    low, high = by_side((xa[0:1, :], xb[0:1, :]), "gx")
    for rim in (oxa, oxb):
        rim[0:HEAD, :] = put_rows((answer[...], low, high))
    for rim in (oza, ozb):
        rim[0:HEAD, :] = jnp.zeros((HEAD, LANES), F32)


def velocity_kernel(air, pressure, medium, moved, xb, zb, xa, za, out, *rest):
    nx, nz, ny = air.shape[1:]
    wide = rest[-1]
    widen_pressure(wide, pressure.at[0], xb, zb, xa, za)
    velocities(out, air, moved, medium, wide, nx, nz)
    if len(rest) > 1:
        pack_air(out, *rest[:-1])
        for rim in (rest[0], rest[2]):
            rim[0:HEAD, :] = jnp.zeros((HEAD, LANES), F32)


def volume_kernel(state, integral, jac, stiff, out, token, rot, sp):
    quants, basis, width = state.shape
    dims = stiff.shape[0]
    pad = sp.shape[0] // dims
    token[...] = jnp.zeros_like(token)
    sp[...] = jnp.zeros_like(sp)
    place = lax.broadcasted_iota(jnp.int32, (basis, basis), 0)
    other = lax.broadcasted_iota(jnp.int32, (basis, basis), 1)
    unit = jnp.where(place == other, 1.0, 0.0).astype(F32)
    for d in range(dims):
        sp[d * pad:d * pad + basis, 0:basis] = dot_exact(unit, stiff[d], (((1,), (1,)), ((), ())))
    rotate(rot, stacked_left(sp[...]), integral, quants, width)

    def emit(p, at, value):
        out[p, :, lanes(at)] = state[p, :, lanes(at)] + value[0:basis]

    jacobian_step(lambda p, q, d, cut: jac[p, q, d:d + 1, cut], rot, emit, quants, dims, width)


def flux_kernel(
    first, faces, base, traces, own, solvers, lift, neighbours, xb, zb, xa, za,
    out, token, tiles, flux, lp,
):
    token[...] = jnp.zeros_like(token)
    quants, basis, width = base.shape
    face_basis = lift.shape[0]
    skip = xa.shape[0] - sent_rows(quants, face_basis)
    for axis, base_tile, gots in (("gx", 0, (xa, xb)), ("gz", 2, (za, zb))):
        for got, side in zip(gots, sides(axis)):
            for q in range(quants):
                tiles[q, base_tile + side, 0:8, :] = got[skip + q * 8:skip + q * 8 + 8, :]
                at = skip + quants * 8 + q * 2
                tiles[q, base_tile + side, 8:face_basis, :] = got[at:at + 2, :]
                tiles[q, base_tile + side, face_basis:, :] = jnp.zeros((16 - face_basis, LANES), F32)
    for q in range(quants):
        tiles[q, 4] = -own[q] if q < 3 else own[q]
    lp[...] = jnp.zeros_like(lp)
    for f in range(faces):
        for j in range(face_basis):
            lp[f * 16 + j:f * 16 + j + 1, 0:basis] = lift[j, first + f:first + f + 1, :]
    unit = lax.broadcasted_iota(jnp.int32, (lp.shape[1], lp.shape[1]), 0) == lax.broadcasted_iota(
        jnp.int32, (lp.shape[1], lp.shape[1]), 1
    )
    lifted = stacked_left(dot_exact(jnp.where(unit, 1.0, 0.0).astype(F32), lp[...], (((1,), (1,)), ((), ()))))
    local = traces.shape[2] // LANES
    halves_in = width // LANES

    def one(h, carry):
        at = h * LANES
        for f in range(faces):
            index = jnp.broadcast_to(neighbours[first + f:first + f + 1, lanes(at)], (16, LANES))
            acc = [None] * quants
            for q in range(quants):
                pool = [traces[q, :, s * LANES:(s + 1) * LANES] for s in range(local)]
                pool += [tiles[q, s] for s in range(5)]
                mine = traces[q, :, lanes((first + f) * width + at)]
                jump = take_slots(pool, index) - mine
                for p in range(quants):
                    term = solvers[p, q, first + f:first + f + 1, lanes(at)] * jump
                    acc[p] = term if acc[p] is None else acc[p] + term
            for p in range(quants):
                flux[f * 16:(f + 1) * 16, lanes(p * width + at)] = acc[p]
        return carry

    lax.fori_loop(0, halves_in, one, 0)
    for p in range(quants):
        cut = slice(p * width, (p + 1) * width)
        out[p] = base[p] + dot3(lifted, flux[:, cut])[0:basis]


def replies_kernel(base, solvers, lift, neighbours, smap, answer, rxb, rxa, out, slot_spread):
    quants, basis, width = base.shape
    face_basis, faces = lift.shape[:2]
    slots = smap.shape[2]
    low, high = by_side((rxa[0:HEAD, :], rxb[0:HEAD, :]), "gx")
    lane = lax.broadcasted_iota(jnp.int32, (1, LANES), 1)
    replies = jnp.zeros((1, LANES), F32)
    for r, row in enumerate((low[1:2], low[0:1], answer[...], high[0:1], high[2:3])):
        replies = jnp.where(lane // slots == r, row, replies)
    replies = jnp.broadcast_to(-2.0 * replies * flat_slots(smap, slot_spread)[2:3], (8, LANES))
    begin = faces * width + 4 * LANES
    square = lax.broadcasted_iota(jnp.int32, (basis, basis), 0) == lax.broadcasted_iota(
        jnp.int32, (basis, basis), 1
    )
    columns = []
    for f in range(faces):
        column = lift[0, f:f + 1, :]
        for j in range(1, face_basis):
            column = column + lift[j, f:f + 1, :]
        columns.append(jnp.sum(jnp.where(square, column, 0.0), axis=1, keepdims=True))
    for h in range(width // LANES):
        cut = slice(h * LANES, (h + 1) * LANES)
        spread = []
        for f in range(faces):
            index = jnp.broadcast_to(neighbours[f:f + 1, cut], (8, LANES))
            found = jnp.take_along_axis(replies, index % LANES, axis=1, mode="promise_in_bounds")
            spread.append(columns[f] * jnp.where(index >= begin, found, 0.0)[0:1])
        for p in range(quants):
            stress = solvers[p, 0, :, cut] + solvers[p, 1, :, cut] + solvers[p, 2, :, cut]
            total = base[p, :, cut]
            for f in range(faces):
                total = total + stress[f:f + 1] * spread[f]
            out[p, :, cut] = total


def sent_rows(quants, face_basis):
    return -(-quants * face_basis // 8) * 8


def shards(
    solid_state, jacobians, flux_solvers, stiffness, trace_matrix, lift_matrix,
    neighbours, send_faces, surface_map, surface_normals, air_state, wind_field, air_medium,
):
    quants, basis, width = solid_state.shape
    faces, face_basis = trace_matrix.shape[0], trace_matrix.shape[1]
    dims = stiffness.shape[0]
    nx, nz, ny = air_state.shape[1:]
    n_gx, n_gz = lax.axis_size("gx"), lax.axis_size("gz")
    jacobians = jnp.transpose(jacobians, (1, 2, 0, 3))
    flux_solvers = jnp.transpose(flux_solvers, (1, 2, 0, 3))
    trace_matrix = jnp.transpose(trace_matrix, (1, 0, 2))
    lift_matrix = jnp.transpose(lift_matrix, (2, 0, 1))
    surface_map = jnp.transpose(surface_map, (1, 0, 2))
    surface_normals = jnp.transpose(surface_normals, (1, 0, 2))
    pad = -(-basis // 8) * 8
    rim_z = (7, nx, RADIUS, ny)
    rim_x = (7, RADIUS, nz, ny)
    ext = (4, nx + 2 * RADIUS, nz + 2 * ZRIM, ny)
    wide = ext[1:]
    block = (1, nx, nz, ny)
    tile = (8, LANES)

    rims = exchange(
        *call(
            raw_rims_kernel, "raw_rims", [rim_x, rim_z, rim_x, rim_z], [air_state, wind_field],
        )
    )

    sent = (sent_rows(quants, face_basis), LANES)
    integral, traces, state = call(
        predict_kernel, "predict",
        [(K, quants * width), (quants, 16, faces * width), solid_state.shape],
        [solid_state, jacobians, stiffness, trace_matrix],
        [(K, quants * width), (dims * pad, quants * width), (dims * pad, LANES), (faces * 16, LANES)],
        flops=40_000_000,
    )
    own, rows = call(
        own_list_kernel, "own_list", [(quants, 16, LANES), (n_gx * n_gz * 8, LANES)],
        [traces, surface_map, surface_normals], [(surface_map.shape[0], 8, LANES)], after=[rims[3]],
    )
    lists = lax.all_to_all(rows, ("gx", "gz"), split_axis=0, concat_axis=0, tiled=True)
    sent_four = call(
        outgoing_kernel, "outgoing", [sent, sent, sent, sent], [traces, send_faces],
        [(4, quants, 16, LANES)], flops=10_000_000, after=[rows],
    )
    (moved,) = call(
        advection_kernel, "advection", [(3, nx, nz, ny)],
        [air_state, wind_field, *rims], [ext], flops=10_000_000, after=[rows],
    )
    volume, token = call(
        volume_kernel, "volume", [solid_state.shape, tile], [state, integral, jacobians, stiffness],
        [(dims * pad, quants * width), (dims * pad, LANES)], flops=10_000_000, after=[rows],
    )
    pressure_x = (HEAD + RADIUS * nz, ny)
    pressure_z = (HEAD + nx * ZRIM, ny)
    both_x = (pressure_x[0] + sent[0], LANES)
    both_z = (pressure_z[0] + sent[0], LANES)
    raw, xb, zb, xa, za = call(
        raw_pressure_kernel, "raw_pressure", [block, both_x, both_z, both_x, both_z],
        [air_state, wind_field, air_medium, *rims, *sent_four], [ext], after=[moved, token],
    )
    both = exchange(xb, zb, xa, za)
    rim_x = (HEAD + 4 * RADIUS * nz, ny)
    rim_z = (4, nx, RADIUS, ny)
    air, xb, zb, xa, za, answer = call(
        functools.partial(injected_kernel, n_gx, n_gz), "injected",
        [air_state.shape, rim_x, rim_z, rim_x, rim_z, (1, LANES)],
        [air_state, wind_field, air_medium, raw, moved, *rims, *both, lists, surface_map],
        [(3 * nx, 3 * nz, ny), wide, (3,) + wide], after=[token],
    )
    half = faces // 2
    solid = volume
    for substep in range(1, SUBSTEPS):
        rims = exchange(xb, zb, xa, za)
        solid, token = call(
            functools.partial(flux_kernel, (substep - 1) * half, half), "flux", [solid_state.shape, tile],
            [solid, traces, own, flux_solvers, lift_matrix, neighbours, *both],
            [(quants, 5, 16, LANES), (half * 16, quants * width), (LANES, pad)], flops=20_000_000,
            after=[xa],
        )
        pressure, xb, zb, xa, za = call(
            pressure_kernel, "pressure", [block, pressure_x, pressure_z, pressure_x, pressure_z],
            [air, wind_field, air_medium, *rims, answer], [ext], after=[token],
        )
        rises = exchange(xb, zb, xa, za)
        if substep == 1:
            replies = [answer, rises[0], rises[2]]
        (moved,) = call(
            advection_kernel, "advection", [(3, nx, nz, ny)],
            [air, wind_field, *rims], [ext], flops=10_000_000, after=[xa],
        )
        last = substep == SUBSTEPS - 1
        if last:
            (solid,) = call(
                replies_kernel, "replies", [solid_state.shape],
                [solid, flux_solvers, lift_matrix, neighbours, surface_map, *replies],
                [(surface_map.shape[0], 8, LANES)], after=[moved],
            )
        outs = [air_state.shape] + ([] if last else [rim_x, rim_z, rim_x, rim_z])
        done = call(
            velocity_kernel, "velocity", outs, [air, pressure, air_medium, moved, *rises], [wide]
        )
        air = done[0]
        if not last:
            xb, zb, xa, za = done[1:]
    return (solid, air)


def solution(mesh):
    in_specs = (
        P(None, None, ("gx", "gz")),
        P(None, None, None, ("gx", "gz")),
        P(None, None, None, ("gx", "gz")),
        P(),
        P(),
        P(),
        P(None, ("gx", "gz")),
        P(None, ("gx", "gz")),
        P(None, None, ("gx", "gz")),
        P(None, None, ("gx", "gz")),
        P(None, "gx", "gz", None),
        P(None, "gx", "gz", None),
        P(None, "gx", "gz", None),
    )
    out_specs = (P(None, None, ("gx", "gz")), P(None, "gx", "gz", None))
    return jax.shard_map(shards, mesh=mesh, in_specs=in_specs, out_specs=out_specs, check_vma=False)
```

```python
import functools

import jax
import jax.numpy as jnp
from jax import lax
from jax.experimental import pallas as pl
from jax.experimental.pallas import tpu as pltpu
from jax.sharding import PartitionSpec as P

ORDERS = 4
RADIUS = 4
SUBSTEPS = 3
ZRIM = 8
LANES = 128
HEAD = 8
FACE_ROWS = 10
K = 32
TIME_STEP = 0.5
STENCIL_WEIGHTS = (0.8, -0.2, 4.0 / 105.0, -1.0 / 280.0)
F32 = jnp.float32
BF16 = jnp.bfloat16


def call(kernel, name, outs, ins, scratch=(), flops=1_000_000, after=()):
    count, skip = len(ins), len(after)
    nbytes = 4 * sum(x.size for x in ins) + 4 * sum(functools.reduce(lambda m, n: m * n, s, 1) for s in outs)

    def body(*refs):
        kernel(*refs[:count], *refs[count + skip:])

    return pl.pallas_call(
        body,
        out_shape=[jax.ShapeDtypeStruct(s, F32) for s in outs],
        in_specs=[pl.BlockSpec(memory_space=pltpu.VMEM) for _ in ins]
        + [pl.BlockSpec(memory_space=pl.ANY) for _ in after],
        out_specs=[pl.BlockSpec(memory_space=pltpu.VMEM) for _ in outs],
        scratch_shapes=[pltpu.VMEM(s, F32) for s in scratch],
        compiler_params=pltpu.CompilerParams(vmem_limit_bytes=8 * 1024 * 1024),
        cost_estimate=pl.CostEstimate(flops=flops, bytes_accessed=nbytes, transcendentals=0),
        name=name,
    )(*ins, *after)


def swap(values, axis, odd, by=1):
    count = lax.axis_size(axis)
    pairs = []
    for i in range(count - by):
        if i // by % 2 == odd:
            pairs += [(i, i + by), (i + by, i)]
    return lax.ppermute(values, axis, pairs)


def exchange(xb, zb, xa, za):
    return swap(xb, "gx", 1), swap(zb, "gz", 1), swap(xa, "gx", 0), swap(za, "gz", 0)


def sides(axis, by=1):
    parity = (lax.axis_index(axis) // by) & 1
    return 1 - parity, parity


def by_side(pair, axis, by=1):
    first = sides(axis, by)[0]
    return jnp.where(first == 0, pair[0], pair[1]), jnp.where(first == 1, pair[0], pair[1])


def halves(values):
    high = values.astype(BF16)
    return high, (values - high.astype(F32)).astype(BF16)


def stacked_left(matrix):
    spread = matrix + pltpu.roll(matrix, K, 1) + pltpu.roll(matrix, 2 * K, 1)
    high = spread.astype(BF16).astype(F32)
    lane = lax.broadcasted_iota(jnp.int32, spread.shape, 1)
    return jnp.where(lane < 2 * K, high, spread - high).astype(BF16)[:, 0:3 * K]


def dot3(left, right):
    high, low = halves(right)
    return jnp.dot(left, jnp.concatenate([high, low, high], axis=0), preferred_element_type=F32)


def dot_exact(left, right, dims=(((1,), (0,)), ((), ()))):
    return lax.dot_general(
        left, right, dims, precision=lax.Precision.HIGHEST, preferred_element_type=F32
    )


def flat_slots(table, spread):
    rows, fields, slots = table.shape
    lane = lax.broadcasted_iota(jnp.int32, (8, LANES), 1)
    for r in range(rows):
        spread[r, 0:fields, 0:slots] = table[r].astype(F32)
    flat = jnp.zeros((8, LANES), F32)
    for r in range(rows):
        got = jnp.take_along_axis(spread[r], lane % slots, axis=1, mode="promise_in_bounds")
        flat = jnp.where(lane // slots == r, got, flat)
    return flat


def pack_x(out, at, source, side):
    fields, nx, nz, ny = source.shape
    start = side * (nx - RADIUS)
    rows = fields * RADIUS * nz
    at = HEAD + at * RADIUS * nz
    out[at:at + rows, :] = source[:, pl.ds(start, RADIUS)].reshape(rows, ny)


def pack_z(out, at, source, side):
    fields, nz = source.shape[0], source.shape[2]
    out[at:at + fields] = jnp.where(side == 1, source[:, :, nz - RADIUS:, :], source[:, :, 0:RADIUS, :])


def widen(ext, center, xb, zb, xa, za, first=0):
    fields, nx, nz, ny = center.shape
    ext[:, RADIUS:RADIUS + nx, ZRIM:ZRIM + nz] = center[...]
    for got, side in zip((xa, xb), sides("gx")):
        place = pl.ds(side * (nx + RADIUS), RADIUS)
        if len(got.shape) == 4:
            rows = got[first:first + fields]
        else:
            rows = got[HEAD:HEAD + fields * RADIUS * nz, :].reshape(fields, RADIUS, nz, ny)
        ext[:, place, ZRIM:ZRIM + nz] = rows
    low, high = by_side([got[first:first + fields] for got in (za, zb)], "gz")
    ext[:, RADIUS:RADIUS + nx, ZRIM - RADIUS:ZRIM] = low
    ext[:, RADIUS:RADIUS + nx, ZRIM + nz:ZRIM + nz + RADIUS] = high


def d1(load, x, lo, hi):
    total = None
    for m, w in enumerate(STENCIL_WEIGHTS, 1):
        term = w * (load(x + m, lo, hi) - load(x - m, lo, hi))
        total = term if total is None else total + term
    return total


def d2(load, x, lo, hi):
    total = None
    for m, w in enumerate(STENCIL_WEIGHTS, 1):
        term = w * (load(x, lo + m, hi + m) - load(x, lo - m, hi - m))
        total = term if total is None else total + term
    return total


def d3(values):
    width = values.shape[1]
    lane = lax.broadcasted_iota(jnp.int32, (1, width), 1)
    total = None
    for m, w in enumerate(STENCIL_WEIGHTS, 1):
        ahead = jnp.where(lane < width - m, w, 0.0) * pltpu.roll(values, width - m, 1)
        behind = jnp.where(lane >= m, w, 0.0) * pltpu.roll(values, m, 1)
        term = ahead - behind
        total = term if total is None else total + term
    return total


def field(ref, c):
    return lambda x, lo, hi: ref[c, x, lo:hi, :]


def plane(ref):
    return lambda x, lo, hi: ref[x, lo:hi, :]


def arrived(table, strip, band, n_gx, n_gz, reach, slots):
    lane = lax.broadcasted_iota(jnp.int32, (1, LANES), 1)
    got = jnp.zeros((1, LANES), F32)
    inside = (strip >= 0) & (strip < n_gx) & (band >= 0) & (band < n_gz)
    for r in range(reach):
        source = strip - (r - reach // 2)
        valid = inside & (source >= 0) & (source < n_gx)
        at = jnp.where(valid, source * n_gz + band, 0) * 8
        row = table[pl.ds(pl.multiple_of(at, 8), 8), :][0:1]
        here = ((lane & (LANES // 2 - 1)) // slots == r) & valid
        got = jnp.where(here, row, got)
    turned = pltpu.roll(got, LANES // 2, 1)
    speed = jnp.where(lane < LANES // 2, got, turned)
    high = speed.astype(BF16).astype(F32)
    return jnp.where(lane < LANES // 2, high, speed - high), jnp.where(lane < LANES // 2, turned, got)


def cell_masks(cells, rows):
    cells = cells.astype(jnp.int32)
    place = lax.broadcasted_iota(jnp.int32, (rows, LANES), 0)
    third = lax.broadcasted_iota(jnp.int32, (LANES, LANES), 0)
    return cells // LANES == place, cells % LANES == third


def raw_rims_kernel(air, wind, xb, zb, xa, za):
    fields, nx = air.shape[:2]
    for out, side in zip((xa, xb), sides("gx")):
        rows = pl.ds(side * (nx - RADIUS), RADIUS)
        out[0:fields] = air[:, rows]
        out[fields:] = wind[:, rows]
    for out, side in zip((za, zb), sides("gz")):
        pack_z(out, 0, air, side)
        pack_z(out, fields, wind, side)


def lanes(at):
    return pl.ds(at if isinstance(at, int) else pl.multiple_of(at, LANES), LANES)


def jacobian_step(load, rot, emit, quants, dims, width):
    rows = rot.shape[0] // dims

    def half(h, carry):
        at = h * LANES
        acc = [None] * quants
        for d in range(dims):
            for q in range(quants):
                turned = rot[d * rows:(d + 1) * rows, lanes(q * width + at)].reshape(rows // 8, 8, LANES)
                for p in range(quants):
                    term = load(p, q, d, lanes(at)) * turned
                    acc[p] = term if acc[p] is None else acc[p] + term
        for p in range(quants):
            emit(p, at, acc[p].reshape(rows, LANES))
        return carry

    lax.fori_loop(0, width // LANES, half, 0)


def rotate(rot, left, source, quants, width):
    for q in range(quants):
        cut = slice(q * width, (q + 1) * width)
        rot[:, cut] = dot3(left, source[:, cut])


def take_slots(tiles, index):
    low = index % LANES
    high = index // LANES
    got = None
    for s, tile in enumerate(tiles):
        picked = jnp.take_along_axis(tile, low, axis=1, mode="promise_in_bounds")
        got = picked if got is None else jnp.where(high == s, picked, got)
    return got


def predict_kernel(
    state, jac, stiff, trace,
    integral, traces, kept,
    cur, rot, sp, tp,
):
    quants, basis, width = state.shape
    pad = sp.shape[0] // stiff.shape[0]
    face_basis, faces = trace.shape[:2]
    dims = stiff.shape[0]
    sp[...] = jnp.zeros_like(sp)
    tp[...] = jnp.zeros_like(tp)
    cur[...] = jnp.zeros_like(cur)
    for d in range(dims):
        sp[d * pad:d * pad + basis, 0:basis] = stiff[d]
    for f in range(faces):
        for j in range(face_basis):
            tp[f * 16 + j:f * 16 + j + 1, 0:basis] = trace[j, f:f + 1, :]
    for q in range(quants):
        cur[0:basis, q * width:(q + 1) * width] = state[q]
    kept[...] = state[...]
    integral[...] = TIME_STEP * cur[...]
    left = stacked_left(sp[...])

    def degree(k, weight):
        weight = jnp.where(k == 1, TIME_STEP**2 / 2, jnp.where(k == 2, TIME_STEP**3 / 6, TIME_STEP**4 / 24))
        rotate(rot, left, cur, quants, width)

        def emit(p, at, value):
            cut = lanes(p * width + at)
            cur[0:pad, cut] = -value
            integral[0:pad, cut] = integral[0:pad, cut] - weight * value

        jacobian_step(lambda p, q, d, cut: jac[p, q, d:d + 1, cut], rot, emit, quants, dims, width)
        return weight

    lax.fori_loop(1, ORDERS, degree, F32(0))
    restrict = stacked_left(tp[...])
    for q in range(quants):
        cut = slice(q * width, (q + 1) * width)
        done = dot3(restrict, integral[:, cut])
        for f in range(faces):
            traces[q, :, f * width:(f + 1) * width] = done[f * 16:(f + 1) * 16]


def own_list_kernel(traces, smap, normals, own, rows, spread):
    quants, _, all_slots = traces.shape
    slots = flat_slots(smap, spread)
    wanted = jnp.broadcast_to(slots[0:1].astype(jnp.int32), (16, LANES))

    def gather(q, carry):
        own[q] = take_slots([traces[q, :, s * LANES:(s + 1) * LANES] for s in range(all_slots // LANES)], wanted)
        return carry

    lax.fori_loop(0, quants, gather, 0)
    normal = flat_slots(normals, spread)
    speed = jnp.zeros((1, LANES), F32)
    for c in range(3):
        mean = jnp.sum(own[6 + c, 0:FACE_ROWS, :], axis=0, keepdims=True) * (1.0 / FACE_ROWS)
        speed = speed + normal[c:c + 1] * mean
    lane = lax.broadcasted_iota(jnp.int32, (1, LANES), 1)
    cells = pltpu.roll(slots[1:2], LANES // 2, 1)
    rows[...] = jnp.broadcast_to(jnp.where(lane < LANES // 2, slots[2:3] * speed, cells), rows.shape)


def outgoing_kernel(traces, sends, xa, xb, za, zb, picked):
    quants, _, slots = traces.shape
    rows = sent_rows(quants, FACE_ROWS)
    wanted = [jnp.broadcast_to(sends[d:d + 1, :], (16, LANES)) for d in range(4)]

    def gather(q, carry):
        tiles = [traces[q, :, s * LANES:(s + 1) * LANES] for s in range(slots // LANES)]
        for d in range(4):
            picked[d, q] = take_slots(tiles, wanted[d])
        return carry

    lax.fori_loop(0, quants, gather, 0)
    rest = FACE_ROWS - 8
    for axis, base, outs in (("gx", 0, (xa, xb)), ("gz", 2, (za, zb))):
        for out, side in zip(outs, sides(axis)):
            for q in range(quants):
                out[q * 8:q * 8 + 8, :] = picked[base + side, q, 0:8, :]
                at = quants * 8 + q * rest
                out[at:at + rest, :] = picked[base + side, q, 8:FACE_ROWS, :]
            out[quants * FACE_ROWS:, :] = jnp.zeros((rows - quants * FACE_ROWS, LANES), F32)


def pressure_rows(ext, wind, medium, x, nz):
    lo, hi = ZRIM, ZRIM + nz
    xe = x + RADIUS
    pressure = field(ext, 0)
    here = pressure(xe, lo, hi)
    divergence = d1(field(ext, 1), xe, lo, hi) + d2(field(ext, 2), xe, lo, hi) + d3(ext[3, xe, lo:hi, :])
    moved = (
        wind[0, x] * d1(pressure, xe, lo, hi)
        + wind[1, x] * d2(pressure, xe, lo, hi)
        + wind[2, x] * d3(here)
    )
    return here - medium[0, x] * divergence - moved


def pack_pressure(center, xs, zs):
    nx, nz, ny = center.shape[1:]
    for out, side in zip(xs, sides("gx")):
        start = side * (nx - RADIUS)
        out[HEAD:HEAD + RADIUS * nz, :] = center[0, pl.ds(start, RADIUS)].reshape(RADIUS * nz, ny)
    for out, side in zip(zs, sides("gz")):
        start = pl.multiple_of(side * (nz - ZRIM), ZRIM)
        out[HEAD:HEAD + nx * ZRIM, :] = center[0, :, pl.ds(start, ZRIM), :].reshape(nx * ZRIM, ny)


def widen_pressure(ext, center, xb, zb, xa, za):
    nx, nz, ny = center.shape
    ext[RADIUS:RADIUS + nx, ZRIM:ZRIM + nz] = center[...]
    for got, side in zip((xa, xb), sides("gx")):
        ext[pl.ds(side * (nx + RADIUS), RADIUS), ZRIM:ZRIM + nz] = got[HEAD:HEAD + RADIUS * nz, :].reshape(RADIUS, nz, ny)
    for got, side in zip((za, zb), sides("gz")):
        start = pl.multiple_of(side * (nz + ZRIM), ZRIM)
        ext[RADIUS:RADIUS + nx, pl.ds(start, ZRIM)] = got[HEAD:HEAD + nx * ZRIM, :].reshape(nx, ZRIM, ny)


def raw_pressure_kernel(
    air, wind, medium, xb, zb, xa, za, txa, txb, tza, tzb, pressure, oxb, ozb, oxa, oza, ext
):
    nx, nz, ny = air.shape[1:]
    widen(ext, air, xb, zb, xa, za)
    for x in range(nx):
        pressure[0, x] = pressure_rows(ext, wind, medium, x, nz)
    pack_pressure(pressure, (oxa, oxb), (oza, ozb))
    for out, sent in zip((oxa, oxb, oza, ozb), (txa, txb, tza, tzb)):
        out[0:HEAD, :] = jnp.zeros((HEAD, LANES), F32)
        out[out.shape[0] - sent.shape[0]:, :] = sent[...]


def put_rows(rows):
    place = lax.broadcasted_iota(jnp.int32, (HEAD, LANES), 0)
    out = jnp.zeros((HEAD, LANES), F32)
    for at, row in enumerate(rows):
        out = jnp.where(place == at, row, out)
    return out


def advection_kernel(air, wind, xb, zb, xa, za, moved, ext):
    nx, nz, ny = air.shape[1:]
    widen(ext, air, xb, zb, xa, za)
    lo, hi = ZRIM, ZRIM + nz
    for x in range(nx):
        xe = x + RADIUS
        for c in range(3):
            load = field(ext, 1 + c)
            moved[c, x] = (
                wind[0, x] * d1(load, xe, lo, hi)
                + wind[1, x] * d2(load, xe, lo, hi)
                + wind[2, x] * d3(load(xe, lo, hi))
            )


def velocities(out, center, moved, medium, wide, nx, nz):
    lo, hi = ZRIM, ZRIM + nz
    load = plane(wide)
    for x in range(nx):
        xe = x + RADIUS
        slopes = (d1(load, xe, lo, hi), d2(load, xe, lo, hi), d3(load(xe, lo, hi)))
        out[0, x] = load(xe, lo, hi)
        for c in range(3):
            out[1 + c, x] = center[1 + c, x] - medium[1, x] * slopes[c] - moved[c, x]


def pack_air(out, xb, zb, xa, za):
    for rim, side in zip((xa, xb), sides("gx")):
        pack_x(rim, 0, out, side)
    for rim, side in zip((za, zb), sides("gz")):
        pack_z(rim, 0, out, side)


def injected_kernel(
    n_gx, n_gz, air, wind, medium, raw, moved, wxb, wzb, wxa, wza, pxb, pzb, pxa, pza, table, smap,
    out, oxb, ozb, oxa, oza, answer, spread, wide, wide_wind,
):
    nx, nz, ny = air.shape[1:]
    reach, _, slots = smap.shape
    strip, band = lax.axis_index("gx"), lax.axis_index("gz")
    mul = functools.partial(
        lax.dot_general, dimension_numbers=(((1,), (1,)), ((), ())), preferred_element_type=F32
    )
    for da in range(3):
        for db in range(3):
            speed, cells = arrived(table, strip + da - 1, band + db - 1, n_gx, n_gz, reach, slots)
            row_mask, third_mask = cell_masks(cells, nx * nz)
            columns = jnp.where(third_mask, 1.0, 0.0).astype(BF16)
            if da == 1 and db == 1:
                seen, rest = halves(air[0].reshape(nx * nz, ny))
                looked = jnp.dot(seen, columns, preferred_element_type=F32)
                looked = looked + jnp.dot(rest, columns, preferred_element_type=F32)
                answer[...] = jnp.sum(jnp.where(row_mask, looked, 0.0), axis=0, keepdims=True)
            block = mul(jnp.where(row_mask, speed, 0.0).astype(BF16), columns)
            spread[da * nx:(da + 1) * nx, db * nz:(db + 1) * nz] = block.reshape(nx, nz, ny)
    widen(wide_wind, wind, wxb, wzb, wxa, wza, first=air.shape[0])
    widen_pressure(wide, raw.at[0], pxb, pzb, pxa, pza)
    load = plane(spread)
    for x in range(nx + 2 * RADIUS):
        xs = x + nx - RADIUS
        if RADIUS <= x < RADIUS + nx:
            lo, hi = 0, nz + 2 * ZRIM
        else:
            lo, hi = ZRIM, ZRIM + nz
        slo, shi = lo + nz - ZRIM, hi + nz - ZRIM
        here = load(xs, slo, shi)
        turned = (
            wide_wind[0, x, lo:hi, :] * d1(load, xs, slo, shi)
            + wide_wind[1, x, lo:hi, :] * d2(load, xs, slo, shi)
            + wide_wind[2, x, lo:hi, :] * d3(here)
        )
        wide[x, lo:hi, :] = wide[x, lo:hi, :] + (here - turned)
    velocities(out, air, moved, medium, wide, nx, nz)
    pack_air(out, oxb, ozb, oxa, oza)
    for rim in (oxa, oxb):
        rim[0:HEAD, :] = put_rows((answer[...],))


def pressure_kernel(air, wind, medium, xb, zb, xa, za, answer, pressure, oxb, ozb, oxa, oza, ext):
    nx, nz, ny = air.shape[1:]
    widen(ext, air, xb, zb, xa, za)
    for x in range(nx):
        pressure[0, x] = pressure_rows(ext, wind, medium, x, nz)
    pack_pressure(pressure, (oxa, oxb), (oza, ozb))
    low, high = by_side((xa[0:1, :], xb[0:1, :]), "gx")
    for rim in (oxa, oxb):
        rim[0:HEAD, :] = put_rows((answer[...], low, high))
    for rim in (oza, ozb):
        rim[0:HEAD, :] = jnp.zeros((HEAD, LANES), F32)


def velocity_kernel(air, pressure, medium, moved, xb, zb, xa, za, out, *rest):
    nx, nz, ny = air.shape[1:]
    wide = rest[-1]
    widen_pressure(wide, pressure.at[0], xb, zb, xa, za)
    velocities(out, air, moved, medium, wide, nx, nz)
    if len(rest) > 1:
        pack_air(out, *rest[:-1])
        for rim in (rest[0], rest[2]):
            rim[0:HEAD, :] = jnp.zeros((HEAD, LANES), F32)


def volume_kernel(state, integral, jac, stiff, out, token, rot, sp):
    quants, basis, width = state.shape
    dims = stiff.shape[0]
    pad = sp.shape[0] // dims
    token[...] = jnp.zeros_like(token)
    sp[...] = jnp.zeros_like(sp)
    place = lax.broadcasted_iota(jnp.int32, (basis, basis), 0)
    other = lax.broadcasted_iota(jnp.int32, (basis, basis), 1)
    unit = jnp.where(place == other, 1.0, 0.0).astype(F32)
    for d in range(dims):
        sp[d * pad:d * pad + basis, 0:basis] = dot_exact(unit, stiff[d], (((1,), (1,)), ((), ())))
    rotate(rot, stacked_left(sp[...]), integral, quants, width)

    def emit(p, at, value):
        out[p, :, lanes(at)] = state[p, :, lanes(at)] + value[0:basis]

    jacobian_step(lambda p, q, d, cut: jac[p, q, d:d + 1, cut], rot, emit, quants, dims, width)


def flux_kernel(
    first, faces, base, traces, own, solvers, lift, neighbours, xb, zb, xa, za,
    out, token, tiles, flux, lp,
):
    token[...] = jnp.zeros_like(token)
    quants, basis, width = base.shape
    face_basis = lift.shape[0]
    skip = xa.shape[0] - sent_rows(quants, face_basis)
    for axis, base_tile, gots in (("gx", 0, (xa, xb)), ("gz", 2, (za, zb))):
        for got, side in zip(gots, sides(axis)):
            for q in range(quants):
                tiles[q, base_tile + side, 0:8, :] = got[skip + q * 8:skip + q * 8 + 8, :]
                at = skip + quants * 8 + q * 2
                tiles[q, base_tile + side, 8:face_basis, :] = got[at:at + 2, :]
                tiles[q, base_tile + side, face_basis:, :] = jnp.zeros((16 - face_basis, LANES), F32)
    for q in range(quants):
        tiles[q, 4] = -own[q] if q < 3 else own[q]
    lp[...] = jnp.zeros_like(lp)
    for f in range(faces):
        for j in range(face_basis):
            lp[f * 16 + j:f * 16 + j + 1, 0:basis] = lift[j, first + f:first + f + 1, :]
    unit = lax.broadcasted_iota(jnp.int32, (lp.shape[1], lp.shape[1]), 0) == lax.broadcasted_iota(
        jnp.int32, (lp.shape[1], lp.shape[1]), 1
    )
    lifted = stacked_left(dot_exact(jnp.where(unit, 1.0, 0.0).astype(F32), lp[...], (((1,), (1,)), ((), ()))))
    local = traces.shape[2] // LANES
    halves_in = width // LANES

    def one(h, carry):
        at = h * LANES
        for f in range(faces):
            index = jnp.broadcast_to(neighbours[first + f:first + f + 1, lanes(at)], (16, LANES))
            acc = [None] * quants
            for q in range(quants):
                pool = [traces[q, :, s * LANES:(s + 1) * LANES] for s in range(local)]
                pool += [tiles[q, s] for s in range(5)]
                mine = traces[q, :, lanes((first + f) * width + at)]
                jump = take_slots(pool, index) - mine
                for p in range(quants):
                    term = solvers[p, q, first + f:first + f + 1, lanes(at)] * jump
                    acc[p] = term if acc[p] is None else acc[p] + term
            for p in range(quants):
                flux[f * 16:(f + 1) * 16, lanes(p * width + at)] = acc[p]
        return carry

    lax.fori_loop(0, halves_in, one, 0)
    for p in range(quants):
        cut = slice(p * width, (p + 1) * width)
        out[p] = base[p] + dot3(lifted, flux[:, cut])[0:basis]


def replies_kernel(base, solvers, lift, neighbours, smap, answer, rxb, rxa, out, slot_spread):
    quants, basis, width = base.shape
    face_basis, faces = lift.shape[:2]
    slots = smap.shape[2]
    low, high = by_side((rxa[0:HEAD, :], rxb[0:HEAD, :]), "gx")
    lane = lax.broadcasted_iota(jnp.int32, (1, LANES), 1)
    replies = jnp.zeros((1, LANES), F32)
    for r, row in enumerate((low[1:2], low[0:1], answer[...], high[0:1], high[2:3])):
        replies = jnp.where(lane // slots == r, row, replies)
    replies = jnp.broadcast_to(-2.0 * replies * flat_slots(smap, slot_spread)[2:3], (8, LANES))
    begin = faces * width + 4 * LANES
    square = lax.broadcasted_iota(jnp.int32, (basis, basis), 0) == lax.broadcasted_iota(
        jnp.int32, (basis, basis), 1
    )
    columns = []
    for f in range(faces):
        column = lift[0, f:f + 1, :]
        for j in range(1, face_basis):
            column = column + lift[j, f:f + 1, :]
        columns.append(jnp.sum(jnp.where(square, column, 0.0), axis=1, keepdims=True))
    for h in range(width // LANES):
        cut = slice(h * LANES, (h + 1) * LANES)
        spread = []
        for f in range(faces):
            index = jnp.broadcast_to(neighbours[f:f + 1, cut], (8, LANES))
            found = jnp.take_along_axis(replies, index % LANES, axis=1, mode="promise_in_bounds")
            spread.append(columns[f] * jnp.where(index >= begin, found, 0.0)[0:1])
        for p in range(quants):
            stress = solvers[p, 0, :, cut] + solvers[p, 1, :, cut] + solvers[p, 2, :, cut]
            total = base[p, :, cut]
            for f in range(faces):
                total = total + stress[f:f + 1] * spread[f]
            out[p, :, cut] = total


def sent_rows(quants, face_basis):
    return -(-quants * face_basis // 8) * 8


def shards(
    solid_state, jacobians, flux_solvers, stiffness, trace_matrix, lift_matrix,
    neighbours, send_faces, surface_map, surface_normals, air_state, wind_field, air_medium,
):
    quants, basis, width = solid_state.shape
    faces, face_basis = trace_matrix.shape[0], trace_matrix.shape[1]
    dims = stiffness.shape[0]
    nx, nz, ny = air_state.shape[1:]
    n_gx, n_gz = lax.axis_size("gx"), lax.axis_size("gz")
    jacobians = jnp.transpose(jacobians, (1, 2, 0, 3))
    flux_solvers = jnp.transpose(flux_solvers, (1, 2, 0, 3))
    trace_matrix = jnp.transpose(trace_matrix, (1, 0, 2))
    lift_matrix = jnp.transpose(lift_matrix, (2, 0, 1))
    surface_map = jnp.transpose(surface_map, (1, 0, 2))
    surface_normals = jnp.transpose(surface_normals, (1, 0, 2))
    pad = -(-basis // 8) * 8
    rim_z = (7, nx, RADIUS, ny)
    rim_x = (7, RADIUS, nz, ny)
    ext = (4, nx + 2 * RADIUS, nz + 2 * ZRIM, ny)
    wide = ext[1:]
    block = (1, nx, nz, ny)
    tile = (8, LANES)

    rims = exchange(
        *call(
            raw_rims_kernel, "raw_rims", [rim_x, rim_z, rim_x, rim_z], [air_state, wind_field],
        )
    )

    sent = (sent_rows(quants, face_basis), LANES)
    integral, traces, state = call(
        predict_kernel, "predict",
        [(K, quants * width), (quants, 16, faces * width), solid_state.shape],
        [solid_state, jacobians, stiffness, trace_matrix],
        [(K, quants * width), (dims * pad, quants * width), (dims * pad, LANES), (faces * 16, LANES)],
        flops=40_000_000,
    )
    own, rows = call(
        own_list_kernel, "own_list", [(quants, 16, LANES), (n_gx * n_gz * 8, LANES)],
        [traces, surface_map, surface_normals], [(surface_map.shape[0], 8, LANES)],
    )
    lists = lax.all_to_all(rows, ("gx", "gz"), split_axis=0, concat_axis=0, tiled=True)
    sent_four = call(
        outgoing_kernel, "outgoing", [sent, sent, sent, sent], [traces, send_faces],
        [(4, quants, 16, LANES)], flops=10_000_000, after=[rows],
    )
    (moved,) = call(
        advection_kernel, "advection", [(3, nx, nz, ny)],
        [air_state, wind_field, *rims], [ext], flops=10_000_000, after=[rows],
    )
    pressure_x = (HEAD + RADIUS * nz, ny)
    pressure_z = (HEAD + nx * ZRIM, ny)
    both_x = (pressure_x[0] + sent[0], LANES)
    both_z = (pressure_z[0] + sent[0], LANES)
    raw, xb, zb, xa, za = call(
        raw_pressure_kernel, "raw_pressure", [block, both_x, both_z, both_x, both_z],
        [air_state, wind_field, air_medium, *rims, *sent_four], [ext], after=[moved],
    )
    both = exchange(xb, zb, xa, za)
    rim_x = (HEAD + 4 * RADIUS * nz, ny)
    rim_z = (4, nx, RADIUS, ny)
    air, xb, zb, xa, za, answer = call(
        functools.partial(injected_kernel, n_gx, n_gz), "injected",
        [air_state.shape, rim_x, rim_z, rim_x, rim_z, (1, LANES)],
        [air_state, wind_field, air_medium, raw, moved, *rims, *both, lists, surface_map],
        [(3 * nx, 3 * nz, ny), wide, (3,) + wide],
    )
    half = faces // 2
    solid = state
    for substep in range(1, SUBSTEPS):
        rims = exchange(xb, zb, xa, za)
        solid, token = call(
            functools.partial(flux_kernel, (substep - 1) * half, half), "flux", [solid_state.shape, tile],
            [solid, traces, own, flux_solvers, lift_matrix, neighbours, *both],
            [(quants, 5, 16, LANES), (half * 16, quants * width), (LANES, pad)], flops=20_000_000,
            after=[xa],
        )
        pressure, xb, zb, xa, za = call(
            pressure_kernel, "pressure", [block, pressure_x, pressure_z, pressure_x, pressure_z],
            [air, wind_field, air_medium, *rims, answer], [ext], after=[token],
        )
        rises = exchange(xb, zb, xa, za)
        if substep == 1:
            replies = [answer, rises[0], rises[2]]
        (moved,) = call(
            advection_kernel, "advection", [(3, nx, nz, ny)],
            [air, wind_field, *rims], [ext], flops=10_000_000, after=[xa],
        )
        last = substep == SUBSTEPS - 1
        if not last:
            solid, token = call(
                volume_kernel, "volume", [solid_state.shape, tile], [solid, integral, jacobians, stiffness],
                [(dims * pad, quants * width), (dims * pad, LANES)], flops=10_000_000, after=[moved],
            )
        else:
            (solid,) = call(
                replies_kernel, "replies", [solid_state.shape],
                [solid, flux_solvers, lift_matrix, neighbours, surface_map, *replies],
                [(surface_map.shape[0], 8, LANES)], after=[moved],
            )
        outs = [air_state.shape] + ([] if last else [rim_x, rim_z, rim_x, rim_z])
        done = call(
            velocity_kernel, "velocity", outs, [air, pressure, air_medium, moved, *rises], [wide],
            after=[token],
        )
        air = done[0]
        if not last:
            xb, zb, xa, za = done[1:]
    return (solid, air)


def solution(mesh):
    in_specs = (
        P(None, None, ("gx", "gz")),
        P(None, None, None, ("gx", "gz")),
        P(None, None, None, ("gx", "gz")),
        P(),
        P(),
        P(),
        P(None, ("gx", "gz")),
        P(None, ("gx", "gz")),
        P(None, None, ("gx", "gz")),
        P(None, None, ("gx", "gz")),
        P(None, "gx", "gz", None),
        P(None, "gx", "gz", None),
        P(None, "gx", "gz", None),
    )
    out_specs = (P(None, None, ("gx", "gz")), P(None, "gx", "gz", None))
    return jax.shard_map(shards, mesh=mesh, in_specs=in_specs, out_specs=out_specs, check_vma=False)
```

```python
import functools

import jax
import jax.numpy as jnp
from jax import lax
from jax.experimental import pallas as pl
from jax.experimental.pallas import tpu as pltpu
from jax.sharding import PartitionSpec as P

ORDERS = 4
RADIUS = 4
SUBSTEPS = 3
ZRIM = 8
LANES = 128
HEAD = 8
FACE_ROWS = 10
K = 32
TIME_STEP = 0.5
STENCIL_WEIGHTS = (0.8, -0.2, 4.0 / 105.0, -1.0 / 280.0)
F32 = jnp.float32
BF16 = jnp.bfloat16


def call(kernel, name, outs, ins, scratch=(), flops=1_000_000, after=()):
    count, skip = len(ins), len(after)
    nbytes = 4 * sum(x.size for x in ins) + 4 * sum(functools.reduce(lambda m, n: m * n, s, 1) for s in outs)

    def body(*refs):
        kernel(*refs[:count], *refs[count + skip:])

    return pl.pallas_call(
        body,
        out_shape=[jax.ShapeDtypeStruct(s, F32) for s in outs],
        in_specs=[pl.BlockSpec(memory_space=pltpu.VMEM) for _ in ins]
        + [pl.BlockSpec(memory_space=pl.ANY) for _ in after],
        out_specs=[pl.BlockSpec(memory_space=pltpu.VMEM) for _ in outs],
        scratch_shapes=[pltpu.VMEM(s, F32) for s in scratch],
        compiler_params=pltpu.CompilerParams(vmem_limit_bytes=8 * 1024 * 1024),
        cost_estimate=pl.CostEstimate(flops=flops, bytes_accessed=nbytes, transcendentals=0),
        name=name,
    )(*ins, *after)


def swap(values, axis, odd, by=1):
    count = lax.axis_size(axis)
    pairs = []
    for i in range(count - by):
        if i // by % 2 == odd:
            pairs += [(i, i + by), (i + by, i)]
    return lax.ppermute(values, axis, pairs)


def exchange(xb, zb, xa, za):
    return swap(xb, "gx", 1), swap(zb, "gz", 1), swap(xa, "gx", 0), swap(za, "gz", 0)


def sides(axis, by=1):
    parity = (lax.axis_index(axis) // by) & 1
    return 1 - parity, parity


def by_side(pair, axis, by=1):
    first = sides(axis, by)[0]
    return jnp.where(first == 0, pair[0], pair[1]), jnp.where(first == 1, pair[0], pair[1])


def halves(values):
    high = values.astype(BF16)
    return high, (values - high.astype(F32)).astype(BF16)


def stacked_left(matrix):
    spread = matrix + pltpu.roll(matrix, K, 1) + pltpu.roll(matrix, 2 * K, 1)
    high = spread.astype(BF16).astype(F32)
    lane = lax.broadcasted_iota(jnp.int32, spread.shape, 1)
    return jnp.where(lane < 2 * K, high, spread - high).astype(BF16)[:, 0:3 * K]


def dot3(left, right):
    high, low = halves(right)
    return jnp.dot(left, jnp.concatenate([high, low, high], axis=0), preferred_element_type=F32)


def dot_exact(left, right, dims=(((1,), (0,)), ((), ()))):
    return lax.dot_general(
        left, right, dims, precision=lax.Precision.HIGHEST, preferred_element_type=F32
    )


def flat_slots(table, spread):
    rows, fields, slots = table.shape
    lane = lax.broadcasted_iota(jnp.int32, (8, LANES), 1)
    for r in range(rows):
        spread[r, 0:fields, 0:slots] = table[r].astype(F32)
    flat = jnp.zeros((8, LANES), F32)
    for r in range(rows):
        got = jnp.take_along_axis(spread[r], lane % slots, axis=1, mode="promise_in_bounds")
        flat = jnp.where(lane // slots == r, got, flat)
    return flat


def pack_x(out, at, source, side):
    fields, nx, nz, ny = source.shape
    start = side * (nx - RADIUS)
    rows = fields * RADIUS * nz
    at = HEAD + at * RADIUS * nz
    out[at:at + rows, :] = source[:, pl.ds(start, RADIUS)].reshape(rows, ny)


def pack_z(out, at, source, side):
    fields, nz = source.shape[0], source.shape[2]
    out[at:at + fields] = jnp.where(side == 1, source[:, :, nz - RADIUS:, :], source[:, :, 0:RADIUS, :])


def widen(ext, center, xb, zb, xa, za, first=0):
    fields, nx, nz, ny = center.shape
    ext[:, RADIUS:RADIUS + nx, ZRIM:ZRIM + nz] = center[...]
    for got, side in zip((xa, xb), sides("gx")):
        place = pl.ds(side * (nx + RADIUS), RADIUS)
        if len(got.shape) == 4:
            rows = got[first:first + fields]
        else:
            rows = got[HEAD:HEAD + fields * RADIUS * nz, :].reshape(fields, RADIUS, nz, ny)
        ext[:, place, ZRIM:ZRIM + nz] = rows
    low, high = by_side([got[first:first + fields] for got in (za, zb)], "gz")
    ext[:, RADIUS:RADIUS + nx, ZRIM - RADIUS:ZRIM] = low
    ext[:, RADIUS:RADIUS + nx, ZRIM + nz:ZRIM + nz + RADIUS] = high


def d1(load, x, lo, hi):
    total = None
    for m, w in enumerate(STENCIL_WEIGHTS, 1):
        term = w * (load(x + m, lo, hi) - load(x - m, lo, hi))
        total = term if total is None else total + term
    return total


def d2(load, x, lo, hi):
    total = None
    for m, w in enumerate(STENCIL_WEIGHTS, 1):
        term = w * (load(x, lo + m, hi + m) - load(x, lo - m, hi - m))
        total = term if total is None else total + term
    return total


def d3(values):
    width = values.shape[1]
    lane = lax.broadcasted_iota(jnp.int32, (1, width), 1)
    total = None
    for m, w in enumerate(STENCIL_WEIGHTS, 1):
        ahead = jnp.where(lane < width - m, w, 0.0) * pltpu.roll(values, width - m, 1)
        behind = jnp.where(lane >= m, w, 0.0) * pltpu.roll(values, m, 1)
        term = ahead - behind
        total = term if total is None else total + term
    return total


def field(ref, c):
    return lambda x, lo, hi: ref[c, x, lo:hi, :]


def plane(ref):
    return lambda x, lo, hi: ref[x, lo:hi, :]


def arrived(table, strip, band, n_gx, n_gz, reach, slots):
    lane = lax.broadcasted_iota(jnp.int32, (1, LANES), 1)
    got = jnp.zeros((1, LANES), F32)
    inside = (strip >= 0) & (strip < n_gx) & (band >= 0) & (band < n_gz)
    for r in range(reach):
        source = strip - (r - reach // 2)
        valid = inside & (source >= 0) & (source < n_gx)
        at = jnp.where(valid, source * n_gz + band, 0) * 8
        row = table[pl.ds(pl.multiple_of(at, 8), 8), :][0:1]
        here = ((lane & (LANES // 2 - 1)) // slots == r) & valid
        got = jnp.where(here, row, got)
    turned = pltpu.roll(got, LANES // 2, 1)
    speed = jnp.where(lane < LANES // 2, got, turned)
    high = speed.astype(BF16).astype(F32)
    return jnp.where(lane < LANES // 2, high, speed - high), jnp.where(lane < LANES // 2, turned, got)


def cell_masks(cells, rows):
    cells = cells.astype(jnp.int32)
    place = lax.broadcasted_iota(jnp.int32, (rows, LANES), 0)
    third = lax.broadcasted_iota(jnp.int32, (LANES, LANES), 0)
    return cells // LANES == place, cells % LANES == third


def raw_rims_kernel(air, wind, xb, zb, xa, za):
    fields, nx = air.shape[:2]
    for out, side in zip((xa, xb), sides("gx")):
        rows = pl.ds(side * (nx - RADIUS), RADIUS)
        out[0:fields] = air[:, rows]
        out[fields:] = wind[:, rows]
    for out, side in zip((za, zb), sides("gz")):
        pack_z(out, 0, air, side)
        pack_z(out, fields, wind, side)


def lanes(at):
    return pl.ds(at if isinstance(at, int) else pl.multiple_of(at, LANES), LANES)


def jacobian_step(load, rot, emit, quants, dims, width):
    rows = rot.shape[0] // dims

    def half(h, carry):
        at = h * LANES
        acc = [None] * quants
        for d in range(dims):
            for q in range(quants):
                turned = rot[d * rows:(d + 1) * rows, lanes(q * width + at)].reshape(rows // 8, 8, LANES)
                for p in range(quants):
                    term = load(p, q, d, lanes(at)) * turned
                    acc[p] = term if acc[p] is None else acc[p] + term
        for p in range(quants):
            emit(p, at, acc[p].reshape(rows, LANES))
        return carry

    lax.fori_loop(0, width // LANES, half, 0)


def rotate(rot, left, source, quants, width):
    for q in range(quants):
        cut = slice(q * width, (q + 1) * width)
        rot[:, cut] = dot3(left, source[:, cut])


def take_slots(tiles, index):
    low = index % LANES
    high = index // LANES
    got = None
    for s, tile in enumerate(tiles):
        picked = jnp.take_along_axis(tile, low, axis=1, mode="promise_in_bounds")
        got = picked if got is None else jnp.where(high == s, picked, got)
    return got


def predict_kernel(
    state, jac, stiff, trace,
    integral, traces, kept,
    cur, rot, sp, tp,
):
    quants, basis, width = state.shape
    pad = sp.shape[0] // stiff.shape[0]
    face_basis, faces = trace.shape[:2]
    dims = stiff.shape[0]
    sp[...] = jnp.zeros_like(sp)
    tp[...] = jnp.zeros_like(tp)
    cur[...] = jnp.zeros_like(cur)
    for d in range(dims):
        sp[d * pad:d * pad + basis, 0:basis] = stiff[d]
    for f in range(faces):
        for j in range(face_basis):
            tp[f * 16 + j:f * 16 + j + 1, 0:basis] = trace[j, f:f + 1, :]
    for q in range(quants):
        cur[0:basis, q * width:(q + 1) * width] = state[q]
    kept[...] = state[...]
    integral[...] = TIME_STEP * cur[...]
    left = stacked_left(sp[...])

    def degree(k, weight):
        weight = jnp.where(k == 1, TIME_STEP**2 / 2, jnp.where(k == 2, TIME_STEP**3 / 6, TIME_STEP**4 / 24))
        rotate(rot, left, cur, quants, width)

        def emit(p, at, value):
            cut = lanes(p * width + at)
            cur[0:pad, cut] = -value
            integral[0:pad, cut] = integral[0:pad, cut] - weight * value

        jacobian_step(lambda p, q, d, cut: jac[p, q, d:d + 1, cut], rot, emit, quants, dims, width)
        return weight

    lax.fori_loop(1, ORDERS, degree, F32(0))
    restrict = stacked_left(tp[...])
    for q in range(quants):
        cut = slice(q * width, (q + 1) * width)
        done = dot3(restrict, integral[:, cut])
        for f in range(faces):
            traces[q, :, f * width:(f + 1) * width] = done[f * 16:(f + 1) * 16]


def own_list_kernel(traces, smap, normals, own, rows, spread):
    quants, _, all_slots = traces.shape
    slots = flat_slots(smap, spread)
    wanted = jnp.broadcast_to(slots[0:1].astype(jnp.int32), (16, LANES))

    def gather(q, carry):
        own[q] = take_slots([traces[q, :, s * LANES:(s + 1) * LANES] for s in range(all_slots // LANES)], wanted)
        return carry

    lax.fori_loop(0, quants, gather, 0)
    normal = flat_slots(normals, spread)
    speed = jnp.zeros((1, LANES), F32)
    for c in range(3):
        mean = jnp.sum(own[6 + c, 0:FACE_ROWS, :], axis=0, keepdims=True) * (1.0 / FACE_ROWS)
        speed = speed + normal[c:c + 1] * mean
    lane = lax.broadcasted_iota(jnp.int32, (1, LANES), 1)
    cells = pltpu.roll(slots[1:2], LANES // 2, 1)
    rows[...] = jnp.broadcast_to(jnp.where(lane < LANES // 2, slots[2:3] * speed, cells), rows.shape)


def outgoing_kernel(traces, sends, xa, xb, za, zb, picked):
    quants, _, slots = traces.shape
    rows = sent_rows(quants, FACE_ROWS)
    wanted = [jnp.broadcast_to(sends[d:d + 1, :], (16, LANES)) for d in range(4)]

    def gather(q, carry):
        tiles = [traces[q, :, s * LANES:(s + 1) * LANES] for s in range(slots // LANES)]
        for d in range(4):
            picked[d, q] = take_slots(tiles, wanted[d])
        return carry

    lax.fori_loop(0, quants, gather, 0)
    rest = FACE_ROWS - 8
    for axis, base, outs in (("gx", 0, (xa, xb)), ("gz", 2, (za, zb))):
        for out, side in zip(outs, sides(axis)):
            for q in range(quants):
                out[q * 8:q * 8 + 8, :] = picked[base + side, q, 0:8, :]
                at = quants * 8 + q * rest
                out[at:at + rest, :] = picked[base + side, q, 8:FACE_ROWS, :]
            out[quants * FACE_ROWS:, :] = jnp.zeros((rows - quants * FACE_ROWS, LANES), F32)


def pressure_rows(ext, wind, medium, x, nz):
    lo, hi = ZRIM, ZRIM + nz
    xe = x + RADIUS
    pressure = field(ext, 0)
    here = pressure(xe, lo, hi)
    divergence = d1(field(ext, 1), xe, lo, hi) + d2(field(ext, 2), xe, lo, hi) + d3(ext[3, xe, lo:hi, :])
    moved = (
        wind[0, x] * d1(pressure, xe, lo, hi)
        + wind[1, x] * d2(pressure, xe, lo, hi)
        + wind[2, x] * d3(here)
    )
    return here - medium[0, x] * divergence - moved


def pack_pressure(center, xs, zs):
    nx, nz, ny = center.shape[1:]
    for out, side in zip(xs, sides("gx")):
        start = side * (nx - RADIUS)
        out[HEAD:HEAD + RADIUS * nz, :] = center[0, pl.ds(start, RADIUS)].reshape(RADIUS * nz, ny)
    for out, side in zip(zs, sides("gz")):
        start = pl.multiple_of(side * (nz - ZRIM), ZRIM)
        out[HEAD:HEAD + nx * ZRIM, :] = center[0, :, pl.ds(start, ZRIM), :].reshape(nx * ZRIM, ny)


def widen_pressure(ext, center, xb, zb, xa, za):
    nx, nz, ny = center.shape
    ext[RADIUS:RADIUS + nx, ZRIM:ZRIM + nz] = center[...]
    for got, side in zip((xa, xb), sides("gx")):
        ext[pl.ds(side * (nx + RADIUS), RADIUS), ZRIM:ZRIM + nz] = got[HEAD:HEAD + RADIUS * nz, :].reshape(RADIUS, nz, ny)
    for got, side in zip((za, zb), sides("gz")):
        start = pl.multiple_of(side * (nz + ZRIM), ZRIM)
        ext[RADIUS:RADIUS + nx, pl.ds(start, ZRIM)] = got[HEAD:HEAD + nx * ZRIM, :].reshape(nx, ZRIM, ny)


def raw_pressure_kernel(
    air, wind, medium, xb, zb, xa, za, txa, txb, tza, tzb, pressure, oxb, ozb, oxa, oza, ext
):
    nx, nz, ny = air.shape[1:]
    widen(ext, air, xb, zb, xa, za)
    for x in range(nx):
        pressure[0, x] = pressure_rows(ext, wind, medium, x, nz)
    pack_pressure(pressure, (oxa, oxb), (oza, ozb))
    for out, sent in zip((oxa, oxb, oza, ozb), (txa, txb, tza, tzb)):
        out[0:HEAD, :] = jnp.zeros((HEAD, LANES), F32)
        out[out.shape[0] - sent.shape[0]:, :] = sent[...]


def put_rows(rows):
    place = lax.broadcasted_iota(jnp.int32, (HEAD, LANES), 0)
    out = jnp.zeros((HEAD, LANES), F32)
    for at, row in enumerate(rows):
        out = jnp.where(place == at, row, out)
    return out


def advection_kernel(air, wind, xb, zb, xa, za, moved, ext):
    nx, nz, ny = air.shape[1:]
    widen(ext, air, xb, zb, xa, za)
    lo, hi = ZRIM, ZRIM + nz
    for x in range(nx):
        xe = x + RADIUS
        for c in range(3):
            load = field(ext, 1 + c)
            moved[c, x] = (
                wind[0, x] * d1(load, xe, lo, hi)
                + wind[1, x] * d2(load, xe, lo, hi)
                + wind[2, x] * d3(load(xe, lo, hi))
            )


def velocities(out, center, moved, medium, wide, nx, nz):
    lo, hi = ZRIM, ZRIM + nz
    load = plane(wide)
    for x in range(nx):
        xe = x + RADIUS
        slopes = (d1(load, xe, lo, hi), d2(load, xe, lo, hi), d3(load(xe, lo, hi)))
        out[0, x] = load(xe, lo, hi)
        for c in range(3):
            out[1 + c, x] = center[1 + c, x] - medium[1, x] * slopes[c] - moved[c, x]


def pack_air(out, xb, zb, xa, za):
    for rim, side in zip((xa, xb), sides("gx")):
        pack_x(rim, 0, out, side)
    for rim, side in zip((za, zb), sides("gz")):
        pack_z(rim, 0, out, side)


def injected_kernel(
    n_gx, n_gz, air, wind, medium, raw, moved, wxb, wzb, wxa, wza, pxb, pzb, pxa, pza, table, smap,
    out, oxb, ozb, oxa, oza, answer, spread, wide, wide_wind,
):
    nx, nz, ny = air.shape[1:]
    reach, _, slots = smap.shape
    strip, band = lax.axis_index("gx"), lax.axis_index("gz")
    mul = functools.partial(
        lax.dot_general, dimension_numbers=(((1,), (1,)), ((), ())), preferred_element_type=F32
    )
    for da in range(3):
        for db in range(3):
            speed, cells = arrived(table, strip + da - 1, band + db - 1, n_gx, n_gz, reach, slots)
            row_mask, third_mask = cell_masks(cells, nx * nz)
            columns = jnp.where(third_mask, 1.0, 0.0).astype(BF16)
            if da == 1 and db == 1:
                seen, rest = halves(air[0].reshape(nx * nz, ny))
                looked = jnp.dot(seen, columns, preferred_element_type=F32)
                looked = looked + jnp.dot(rest, columns, preferred_element_type=F32)
                answer[...] = jnp.sum(jnp.where(row_mask, looked, 0.0), axis=0, keepdims=True)
            block = mul(jnp.where(row_mask, speed, 0.0).astype(BF16), columns)
            spread[da * nx:(da + 1) * nx, db * nz:(db + 1) * nz] = block.reshape(nx, nz, ny)
    widen(wide_wind, wind, wxb, wzb, wxa, wza, first=air.shape[0])
    widen_pressure(wide, raw.at[0], pxb, pzb, pxa, pza)
    load = plane(spread)
    for x in range(nx + 2 * RADIUS):
        xs = x + nx - RADIUS
        if RADIUS <= x < RADIUS + nx:
            lo, hi = 0, nz + 2 * ZRIM
        else:
            lo, hi = ZRIM, ZRIM + nz
        slo, shi = lo + nz - ZRIM, hi + nz - ZRIM
        here = load(xs, slo, shi)
        turned = (
            wide_wind[0, x, lo:hi, :] * d1(load, xs, slo, shi)
            + wide_wind[1, x, lo:hi, :] * d2(load, xs, slo, shi)
            + wide_wind[2, x, lo:hi, :] * d3(here)
        )
        wide[x, lo:hi, :] = wide[x, lo:hi, :] + (here - turned)
    velocities(out, air, moved, medium, wide, nx, nz)
    pack_air(out, oxb, ozb, oxa, oza)
    for rim in (oxa, oxb):
        rim[0:HEAD, :] = put_rows((answer[...],))


def pressure_kernel(air, wind, medium, xb, zb, xa, za, answer, pressure, oxb, ozb, oxa, oza, ext):
    nx, nz, ny = air.shape[1:]
    widen(ext, air, xb, zb, xa, za)
    for x in range(nx):
        pressure[0, x] = pressure_rows(ext, wind, medium, x, nz)
    pack_pressure(pressure, (oxa, oxb), (oza, ozb))
    low, high = by_side((xa[0:1, :], xb[0:1, :]), "gx")
    for rim in (oxa, oxb):
        rim[0:HEAD, :] = put_rows((answer[...], low, high))
    for rim in (oza, ozb):
        rim[0:HEAD, :] = jnp.zeros((HEAD, LANES), F32)


def velocity_kernel(air, pressure, medium, moved, xb, zb, xa, za, out, *rest):
    nx, nz, ny = air.shape[1:]
    wide = rest[-1]
    widen_pressure(wide, pressure.at[0], xb, zb, xa, za)
    velocities(out, air, moved, medium, wide, nx, nz)
    if len(rest) > 1:
        pack_air(out, *rest[:-1])
        for rim in (rest[0], rest[2]):
            rim[0:HEAD, :] = jnp.zeros((HEAD, LANES), F32)


def volume_kernel(state, integral, jac, stiff, out, token, rot, sp):
    quants, basis, width = state.shape
    dims = stiff.shape[0]
    pad = sp.shape[0] // dims
    token[...] = jnp.zeros_like(token)
    sp[...] = jnp.zeros_like(sp)
    place = lax.broadcasted_iota(jnp.int32, (basis, basis), 0)
    other = lax.broadcasted_iota(jnp.int32, (basis, basis), 1)
    unit = jnp.where(place == other, 1.0, 0.0).astype(F32)
    for d in range(dims):
        sp[d * pad:d * pad + basis, 0:basis] = dot_exact(unit, stiff[d], (((1,), (1,)), ((), ())))
    rotate(rot, stacked_left(sp[...]), integral, quants, width)

    def emit(p, at, value):
        out[p, :, lanes(at)] = state[p, :, lanes(at)] + value[0:basis]

    jacobian_step(lambda p, q, d, cut: jac[p, q, d:d + 1, cut], rot, emit, quants, dims, width)


def flux_kernel(
    first, faces, base, traces, own, solvers, lift, neighbours, xb, zb, xa, za,
    out, token, tiles, flux, lp,
):
    token[...] = jnp.zeros_like(token)
    quants, basis, width = base.shape
    face_basis = lift.shape[0]
    skip = xa.shape[0] - sent_rows(quants, face_basis)
    for axis, base_tile, gots in (("gx", 0, (xa, xb)), ("gz", 2, (za, zb))):
        for got, side in zip(gots, sides(axis)):
            for q in range(quants):
                tiles[q, base_tile + side, 0:8, :] = got[skip + q * 8:skip + q * 8 + 8, :]
                at = skip + quants * 8 + q * 2
                tiles[q, base_tile + side, 8:face_basis, :] = got[at:at + 2, :]
                tiles[q, base_tile + side, face_basis:, :] = jnp.zeros((16 - face_basis, LANES), F32)
    for q in range(quants):
        tiles[q, 4] = -own[q] if q < 3 else own[q]
    lp[...] = jnp.zeros_like(lp)
    for f in range(faces):
        for j in range(face_basis):
            lp[f * 16 + j:f * 16 + j + 1, 0:basis] = lift[j, first + f:first + f + 1, :]
    unit = lax.broadcasted_iota(jnp.int32, (lp.shape[1], lp.shape[1]), 0) == lax.broadcasted_iota(
        jnp.int32, (lp.shape[1], lp.shape[1]), 1
    )
    lifted = stacked_left(dot_exact(jnp.where(unit, 1.0, 0.0).astype(F32), lp[...], (((1,), (1,)), ((), ()))))
    local = traces.shape[2] // LANES
    halves_in = width // LANES

    def one(h, carry):
        at = h * LANES
        for f in range(faces):
            index = jnp.broadcast_to(neighbours[first + f:first + f + 1, lanes(at)], (16, LANES))
            acc = [None] * quants
            for q in range(quants):
                pool = [traces[q, :, s * LANES:(s + 1) * LANES] for s in range(local)]
                pool += [tiles[q, s] for s in range(5)]
                mine = traces[q, :, lanes((first + f) * width + at)]
                jump = take_slots(pool, index) - mine
                for p in range(quants):
                    term = solvers[p, q, first + f:first + f + 1, lanes(at)] * jump
                    acc[p] = term if acc[p] is None else acc[p] + term
            for p in range(quants):
                flux[f * 16:(f + 1) * 16, lanes(p * width + at)] = acc[p]
        return carry

    lax.fori_loop(0, halves_in, one, 0)
    for p in range(quants):
        cut = slice(p * width, (p + 1) * width)
        out[p] = base[p] + dot3(lifted, flux[:, cut])[0:basis]


def replies_kernel(base, solvers, lift, neighbours, smap, answer, rxb, rxa, out, slot_spread):
    quants, basis, width = base.shape
    face_basis, faces = lift.shape[:2]
    slots = smap.shape[2]
    low, high = by_side((rxa[0:HEAD, :], rxb[0:HEAD, :]), "gx")
    lane = lax.broadcasted_iota(jnp.int32, (1, LANES), 1)
    replies = jnp.zeros((1, LANES), F32)
    for r, row in enumerate((low[1:2], low[0:1], answer[...], high[0:1], high[2:3])):
        replies = jnp.where(lane // slots == r, row, replies)
    replies = jnp.broadcast_to(-2.0 * replies * flat_slots(smap, slot_spread)[2:3], (8, LANES))
    begin = faces * width + 4 * LANES
    square = lax.broadcasted_iota(jnp.int32, (basis, basis), 0) == lax.broadcasted_iota(
        jnp.int32, (basis, basis), 1
    )
    columns = []
    for f in range(faces):
        column = lift[0, f:f + 1, :]
        for j in range(1, face_basis):
            column = column + lift[j, f:f + 1, :]
        columns.append(jnp.sum(jnp.where(square, column, 0.0), axis=1, keepdims=True))
    for h in range(width // LANES):
        cut = slice(h * LANES, (h + 1) * LANES)
        spread = []
        for f in range(faces):
            index = jnp.broadcast_to(neighbours[f:f + 1, cut], (8, LANES))
            found = jnp.take_along_axis(replies, index % LANES, axis=1, mode="promise_in_bounds")
            spread.append(columns[f] * jnp.where(index >= begin, found, 0.0)[0:1])
        for p in range(quants):
            stress = solvers[p, 0, :, cut] + solvers[p, 1, :, cut] + solvers[p, 2, :, cut]
            total = base[p, :, cut]
            for f in range(faces):
                total = total + stress[f:f + 1] * spread[f]
            out[p, :, cut] = total


def sent_rows(quants, face_basis):
    return -(-quants * face_basis // 8) * 8


def shards(
    solid_state, jacobians, flux_solvers, stiffness, trace_matrix, lift_matrix,
    neighbours, send_faces, surface_map, surface_normals, air_state, wind_field, air_medium,
):
    quants, basis, width = solid_state.shape
    faces, face_basis = trace_matrix.shape[0], trace_matrix.shape[1]
    dims = stiffness.shape[0]
    nx, nz, ny = air_state.shape[1:]
    n_gx, n_gz = lax.axis_size("gx"), lax.axis_size("gz")
    jacobians = jnp.transpose(jacobians, (1, 2, 0, 3))
    flux_solvers = jnp.transpose(flux_solvers, (1, 2, 0, 3))
    trace_matrix = jnp.transpose(trace_matrix, (1, 0, 2))
    lift_matrix = jnp.transpose(lift_matrix, (2, 0, 1))
    surface_map = jnp.transpose(surface_map, (1, 0, 2))
    surface_normals = jnp.transpose(surface_normals, (1, 0, 2))
    pad = -(-basis // 8) * 8
    rim_z = (7, nx, RADIUS, ny)
    rim_x = (7, RADIUS, nz, ny)
    ext = (4, nx + 2 * RADIUS, nz + 2 * ZRIM, ny)
    wide = ext[1:]
    block = (1, nx, nz, ny)
    tile = (8, LANES)

    rims = exchange(
        *call(
            raw_rims_kernel, "raw_rims", [rim_x, rim_z, rim_x, rim_z], [air_state, wind_field],
        )
    )

    sent = (sent_rows(quants, face_basis), LANES)
    integral, traces, state = call(
        predict_kernel, "predict",
        [(K, quants * width), (quants, 16, faces * width), solid_state.shape],
        [solid_state, jacobians, stiffness, trace_matrix],
        [(K, quants * width), (dims * pad, quants * width), (dims * pad, LANES), (faces * 16, LANES)],
        flops=40_000_000,
    )
    own, rows = call(
        own_list_kernel, "own_list", [(quants, 16, LANES), (n_gx * n_gz * 8, LANES)],
        [traces, surface_map, surface_normals], [(surface_map.shape[0], 8, LANES)],
        after=[rims[1], rims[3]],
    )
    lists = lax.all_to_all(rows, ("gx", "gz"), split_axis=0, concat_axis=0, tiled=True)
    sent_four = call(
        outgoing_kernel, "outgoing", [sent, sent, sent, sent], [traces, send_faces],
        [(4, quants, 16, LANES)], flops=10_000_000, after=[rows],
    )
    (moved,) = call(
        advection_kernel, "advection", [(3, nx, nz, ny)],
        [air_state, wind_field, *rims], [ext], flops=10_000_000, after=[rows],
    )
    pressure_x = (HEAD + RADIUS * nz, ny)
    pressure_z = (HEAD + nx * ZRIM, ny)
    both_x = (pressure_x[0] + sent[0], LANES)
    both_z = (pressure_z[0] + sent[0], LANES)
    raw, xb, zb, xa, za = call(
        raw_pressure_kernel, "raw_pressure", [block, both_x, both_z, both_x, both_z],
        [air_state, wind_field, air_medium, *rims, *sent_four], [ext], after=[moved],
    )
    both = exchange(xb, zb, xa, za)
    rim_x = (HEAD + 4 * RADIUS * nz, ny)
    rim_z = (4, nx, RADIUS, ny)
    air, xb, zb, xa, za, answer = call(
        functools.partial(injected_kernel, n_gx, n_gz), "injected",
        [air_state.shape, rim_x, rim_z, rim_x, rim_z, (1, LANES)],
        [air_state, wind_field, air_medium, raw, moved, *rims, *both, lists, surface_map],
        [(3 * nx, 3 * nz, ny), wide, (3,) + wide],
    )
    half = faces // 2
    solid = state
    for substep in range(1, SUBSTEPS):
        rims = exchange(xb, zb, xa, za)
        solid, token = call(
            functools.partial(flux_kernel, (substep - 1) * half, half), "flux", [solid_state.shape, tile],
            [solid, traces, own, flux_solvers, lift_matrix, neighbours, *both],
            [(quants, 5, 16, LANES), (half * 16, quants * width), (LANES, pad)], flops=20_000_000,
            after=[xa],
        )
        pressure, xb, zb, xa, za = call(
            pressure_kernel, "pressure", [block, pressure_x, pressure_z, pressure_x, pressure_z],
            [air, wind_field, air_medium, *rims, answer], [ext], after=[token],
        )
        rises = exchange(xb, zb, xa, za)
        if substep == 1:
            replies = [answer, rises[0], rises[2]]
        (moved,) = call(
            advection_kernel, "advection", [(3, nx, nz, ny)],
            [air, wind_field, *rims], [ext], flops=10_000_000, after=[xa],
        )
        last = substep == SUBSTEPS - 1
        if not last:
            solid, token = call(
                volume_kernel, "volume", [solid_state.shape, tile], [solid, integral, jacobians, stiffness],
                [(dims * pad, quants * width), (dims * pad, LANES)], flops=10_000_000, after=[moved],
            )
        else:
            (solid,) = call(
                replies_kernel, "replies", [solid_state.shape],
                [solid, flux_solvers, lift_matrix, neighbours, surface_map, *replies],
                [(surface_map.shape[0], 8, LANES)], after=[moved],
            )
        outs = [air_state.shape] + ([] if last else [rim_x, rim_z, rim_x, rim_z])
        done = call(
            velocity_kernel, "velocity", outs, [air, pressure, air_medium, moved, *rises], [wide],
            after=[token],
        )
        air = done[0]
        if not last:
            xb, zb, xa, za = done[1:]
    return (solid, air)


def solution(mesh):
    in_specs = (
        P(None, None, ("gx", "gz")),
        P(None, None, None, ("gx", "gz")),
        P(None, None, None, ("gx", "gz")),
        P(),
        P(),
        P(),
        P(None, ("gx", "gz")),
        P(None, ("gx", "gz")),
        P(None, None, ("gx", "gz")),
        P(None, None, ("gx", "gz")),
        P(None, "gx", "gz", None),
        P(None, "gx", "gz", None),
        P(None, "gx", "gz", None),
    )
    out_specs = (P(None, None, ("gx", "gz")), P(None, "gx", "gz", None))
    return jax.shard_map(shards, mesh=mesh, in_specs=in_specs, out_specs=out_specs, check_vma=False)
```

```python
import functools

import jax
import jax.numpy as jnp
from jax import lax
from jax.experimental import pallas as pl
from jax.experimental.pallas import tpu as pltpu
from jax.sharding import PartitionSpec as P

ORDERS = 4
RADIUS = 4
SUBSTEPS = 3
ZRIM = 8
LANES = 128
HEAD = 8
FACE_ROWS = 10
K = 32
TIME_STEP = 0.5
STENCIL_WEIGHTS = (0.8, -0.2, 4.0 / 105.0, -1.0 / 280.0)
F32 = jnp.float32
BF16 = jnp.bfloat16


def call(kernel, name, outs, ins, scratch=(), flops=1_000_000, after=()):
    count, skip = len(ins), len(after)
    nbytes = 4 * sum(x.size for x in ins) + 4 * sum(functools.reduce(lambda m, n: m * n, s, 1) for s in outs)

    def body(*refs):
        kernel(*refs[:count], *refs[count + skip:])

    return pl.pallas_call(
        body,
        out_shape=[jax.ShapeDtypeStruct(s, F32) for s in outs],
        in_specs=[pl.BlockSpec(memory_space=pltpu.VMEM) for _ in ins]
        + [pl.BlockSpec(memory_space=pl.ANY) for _ in after],
        out_specs=[pl.BlockSpec(memory_space=pltpu.VMEM) for _ in outs],
        scratch_shapes=[pltpu.VMEM(s, F32) for s in scratch],
        compiler_params=pltpu.CompilerParams(vmem_limit_bytes=8 * 1024 * 1024),
        cost_estimate=pl.CostEstimate(flops=flops, bytes_accessed=nbytes, transcendentals=0),
        name=name,
    )(*ins, *after)


def swap(values, axis, odd, by=1):
    count = lax.axis_size(axis)
    pairs = []
    for i in range(count - by):
        if i // by % 2 == odd:
            pairs += [(i, i + by), (i + by, i)]
    return lax.ppermute(values, axis, pairs)


def exchange(xb, zb, xa, za):
    return swap(xb, "gx", 1), swap(zb, "gz", 1), swap(xa, "gx", 0), swap(za, "gz", 0)


def sides(axis, by=1):
    parity = (lax.axis_index(axis) // by) & 1
    return 1 - parity, parity


def by_side(pair, axis, by=1):
    first = sides(axis, by)[0]
    return jnp.where(first == 0, pair[0], pair[1]), jnp.where(first == 1, pair[0], pair[1])


def halves(values):
    high = values.astype(BF16)
    return high, (values - high.astype(F32)).astype(BF16)


def stacked_left(matrix):
    spread = matrix + pltpu.roll(matrix, K, 1) + pltpu.roll(matrix, 2 * K, 1)
    high = spread.astype(BF16).astype(F32)
    lane = lax.broadcasted_iota(jnp.int32, spread.shape, 1)
    return jnp.where(lane < 2 * K, high, spread - high).astype(BF16)[:, 0:3 * K]


def dot3(left, right):
    high, low = halves(right)
    return jnp.dot(left, jnp.concatenate([high, low, high], axis=0), preferred_element_type=F32)


def dot_exact(left, right, dims=(((1,), (0,)), ((), ()))):
    return lax.dot_general(
        left, right, dims, precision=lax.Precision.HIGHEST, preferred_element_type=F32
    )


def flat_slots(table, spread):
    rows, fields, slots = table.shape
    lane = lax.broadcasted_iota(jnp.int32, (8, LANES), 1)
    for r in range(rows):
        spread[r, 0:fields, 0:slots] = table[r].astype(F32)
    flat = jnp.zeros((8, LANES), F32)
    for r in range(rows):
        got = jnp.take_along_axis(spread[r], lane % slots, axis=1, mode="promise_in_bounds")
        flat = jnp.where(lane // slots == r, got, flat)
    return flat


def pack_x(out, at, source, side):
    fields, nx, nz, ny = source.shape
    start = side * (nx - RADIUS)
    rows = fields * RADIUS * nz
    at = HEAD + at * RADIUS * nz
    out[at:at + rows, :] = source[:, pl.ds(start, RADIUS)].reshape(rows, ny)


def pack_z(out, at, source, side):
    fields, nz = source.shape[0], source.shape[2]
    out[at:at + fields] = jnp.where(side == 1, source[:, :, nz - RADIUS:, :], source[:, :, 0:RADIUS, :])


def widen(ext, center, xb, zb, xa, za, first=0):
    fields, nx, nz, ny = center.shape
    ext[:, RADIUS:RADIUS + nx, ZRIM:ZRIM + nz] = center[...]
    for got, side in zip((xa, xb), sides("gx")):
        place = pl.ds(side * (nx + RADIUS), RADIUS)
        if len(got.shape) == 4:
            rows = got[first:first + fields]
        else:
            rows = got[HEAD:HEAD + fields * RADIUS * nz, :].reshape(fields, RADIUS, nz, ny)
        ext[:, place, ZRIM:ZRIM + nz] = rows
    low, high = by_side([got[first:first + fields] for got in (za, zb)], "gz")
    ext[:, RADIUS:RADIUS + nx, ZRIM - RADIUS:ZRIM] = low
    ext[:, RADIUS:RADIUS + nx, ZRIM + nz:ZRIM + nz + RADIUS] = high


def d1(load, x, lo, hi):
    total = None
    for m, w in enumerate(STENCIL_WEIGHTS, 1):
        term = w * (load(x + m, lo, hi) - load(x - m, lo, hi))
        total = term if total is None else total + term
    return total


def d2(load, x, lo, hi):
    total = None
    for m, w in enumerate(STENCIL_WEIGHTS, 1):
        term = w * (load(x, lo + m, hi + m) - load(x, lo - m, hi - m))
        total = term if total is None else total + term
    return total


def d3(values):
    width = values.shape[1]
    lane = lax.broadcasted_iota(jnp.int32, (1, width), 1)
    total = None
    for m, w in enumerate(STENCIL_WEIGHTS, 1):
        ahead = jnp.where(lane < width - m, w, 0.0) * pltpu.roll(values, width - m, 1)
        behind = jnp.where(lane >= m, w, 0.0) * pltpu.roll(values, m, 1)
        term = ahead - behind
        total = term if total is None else total + term
    return total


def field(ref, c):
    return lambda x, lo, hi: ref[c, x, lo:hi, :]


def plane(ref):
    return lambda x, lo, hi: ref[x, lo:hi, :]


def arrived(table, strip, band, n_gx, n_gz, reach, slots):
    lane = lax.broadcasted_iota(jnp.int32, (1, LANES), 1)
    got = jnp.zeros((1, LANES), F32)
    inside = (strip >= 0) & (strip < n_gx) & (band >= 0) & (band < n_gz)
    for r in range(reach):
        source = strip - (r - reach // 2)
        valid = inside & (source >= 0) & (source < n_gx)
        at = jnp.where(valid, source * n_gz + band, 0) * 8
        row = table[pl.ds(pl.multiple_of(at, 8), 8), :][0:1]
        here = ((lane & (LANES // 2 - 1)) // slots == r) & valid
        got = jnp.where(here, row, got)
    turned = pltpu.roll(got, LANES // 2, 1)
    speed = jnp.where(lane < LANES // 2, got, turned)
    high = speed.astype(BF16).astype(F32)
    return jnp.where(lane < LANES // 2, high, speed - high), jnp.where(lane < LANES // 2, turned, got)


def cell_masks(cells, rows):
    cells = cells.astype(jnp.int32)
    place = lax.broadcasted_iota(jnp.int32, (rows, LANES), 0)
    third = lax.broadcasted_iota(jnp.int32, (LANES, LANES), 0)
    return cells // LANES == place, cells % LANES == third


def raw_rims_kernel(air, wind, xb, zb, xa, za):
    fields, nx = air.shape[:2]
    for out, side in zip((xa, xb), sides("gx")):
        rows = pl.ds(side * (nx - RADIUS), RADIUS)
        out[0:fields] = air[:, rows]
        out[fields:] = wind[:, rows]
    for out, side in zip((za, zb), sides("gz")):
        pack_z(out, 0, air, side)
        pack_z(out, fields, wind, side)


def lanes(at):
    return pl.ds(at if isinstance(at, int) else pl.multiple_of(at, LANES), LANES)


def jacobian_step(load, rot, emit, quants, dims, width):
    rows = rot.shape[0] // dims

    def half(h, carry):
        at = h * LANES
        acc = [None] * quants
        for d in range(dims):
            for q in range(quants):
                turned = rot[d * rows:(d + 1) * rows, lanes(q * width + at)].reshape(rows // 8, 8, LANES)
                for p in range(quants):
                    term = load(p, q, d, lanes(at)) * turned
                    acc[p] = term if acc[p] is None else acc[p] + term
        for p in range(quants):
            emit(p, at, acc[p].reshape(rows, LANES))
        return carry

    lax.fori_loop(0, width // LANES, half, 0)


def rotate(rot, left, source, quants, width):
    for q in range(quants):
        cut = slice(q * width, (q + 1) * width)
        rot[:, cut] = dot3(left, source[:, cut])


def take_slots(tiles, index):
    low = index % LANES
    high = index // LANES
    got = None
    for s, tile in enumerate(tiles):
        picked = jnp.take_along_axis(tile, low, axis=1, mode="promise_in_bounds")
        got = picked if got is None else jnp.where(high == s, picked, got)
    return got


def predict_kernel(
    state, jac, stiff, trace,
    integral, traces, kept,
    cur, rot, sp, tp,
):
    quants, basis, width = state.shape
    pad = sp.shape[0] // stiff.shape[0]
    face_basis, faces = trace.shape[:2]
    dims = stiff.shape[0]
    sp[...] = jnp.zeros_like(sp)
    tp[...] = jnp.zeros_like(tp)
    cur[...] = jnp.zeros_like(cur)
    for d in range(dims):
        sp[d * pad:d * pad + basis, 0:basis] = stiff[d]
    for f in range(faces):
        for j in range(face_basis):
            tp[f * 16 + j:f * 16 + j + 1, 0:basis] = trace[j, f:f + 1, :]
    for q in range(quants):
        cur[0:basis, q * width:(q + 1) * width] = state[q]
    kept[...] = state[...]
    integral[...] = TIME_STEP * cur[...]
    left = stacked_left(sp[...])

    def degree(k, weight):
        weight = jnp.where(k == 1, TIME_STEP**2 / 2, jnp.where(k == 2, TIME_STEP**3 / 6, TIME_STEP**4 / 24))
        rotate(rot, left, cur, quants, width)

        def emit(p, at, value):
            cut = lanes(p * width + at)
            cur[0:pad, cut] = -value
            integral[0:pad, cut] = integral[0:pad, cut] - weight * value

        jacobian_step(lambda p, q, d, cut: jac[p, q, d:d + 1, cut], rot, emit, quants, dims, width)
        return weight

    lax.fori_loop(1, ORDERS, degree, F32(0))
    restrict = stacked_left(tp[...])
    for q in range(quants):
        cut = slice(q * width, (q + 1) * width)
        done = dot3(restrict, integral[:, cut])
        for f in range(faces):
            traces[q, :, f * width:(f + 1) * width] = done[f * 16:(f + 1) * 16]


def own_list_kernel(traces, smap, normals, own, rows, spread):
    quants, _, all_slots = traces.shape
    slots = flat_slots(smap, spread)
    wanted = jnp.broadcast_to(slots[0:1].astype(jnp.int32), (16, LANES))

    def gather(q, carry):
        own[q] = take_slots([traces[q, :, s * LANES:(s + 1) * LANES] for s in range(all_slots // LANES)], wanted)
        return carry

    lax.fori_loop(0, quants, gather, 0)
    normal = flat_slots(normals, spread)
    speed = jnp.zeros((1, LANES), F32)
    for c in range(3):
        mean = jnp.sum(own[6 + c, 0:FACE_ROWS, :], axis=0, keepdims=True) * (1.0 / FACE_ROWS)
        speed = speed + normal[c:c + 1] * mean
    lane = lax.broadcasted_iota(jnp.int32, (1, LANES), 1)
    cells = pltpu.roll(slots[1:2], LANES // 2, 1)
    rows[...] = jnp.broadcast_to(jnp.where(lane < LANES // 2, slots[2:3] * speed, cells), rows.shape)


def outgoing_kernel(traces, sends, xa, xb, za, zb, picked):
    quants, _, slots = traces.shape
    rows = sent_rows(quants, FACE_ROWS)
    wanted = [jnp.broadcast_to(sends[d:d + 1, :], (16, LANES)) for d in range(4)]

    def gather(q, carry):
        tiles = [traces[q, :, s * LANES:(s + 1) * LANES] for s in range(slots // LANES)]
        for d in range(4):
            picked[d, q] = take_slots(tiles, wanted[d])
        return carry

    lax.fori_loop(0, quants, gather, 0)
    rest = FACE_ROWS - 8
    for axis, base, outs in (("gx", 0, (xa, xb)), ("gz", 2, (za, zb))):
        for out, side in zip(outs, sides(axis)):
            for q in range(quants):
                out[q * 8:q * 8 + 8, :] = picked[base + side, q, 0:8, :]
                at = quants * 8 + q * rest
                out[at:at + rest, :] = picked[base + side, q, 8:FACE_ROWS, :]
            out[quants * FACE_ROWS:, :] = jnp.zeros((rows - quants * FACE_ROWS, LANES), F32)


def pressure_rows(ext, wind, medium, x, nz):
    lo, hi = ZRIM, ZRIM + nz
    xe = x + RADIUS
    pressure = field(ext, 0)
    here = pressure(xe, lo, hi)
    divergence = d1(field(ext, 1), xe, lo, hi) + d2(field(ext, 2), xe, lo, hi) + d3(ext[3, xe, lo:hi, :])
    moved = (
        wind[0, x] * d1(pressure, xe, lo, hi)
        + wind[1, x] * d2(pressure, xe, lo, hi)
        + wind[2, x] * d3(here)
    )
    return here - medium[0, x] * divergence - moved


def pack_pressure(center, xs, zs):
    nx, nz, ny = center.shape[1:]
    for out, side in zip(xs, sides("gx")):
        start = side * (nx - RADIUS)
        out[HEAD:HEAD + RADIUS * nz, :] = center[0, pl.ds(start, RADIUS)].reshape(RADIUS * nz, ny)
    for out, side in zip(zs, sides("gz")):
        start = pl.multiple_of(side * (nz - ZRIM), ZRIM)
        out[HEAD:HEAD + nx * ZRIM, :] = center[0, :, pl.ds(start, ZRIM), :].reshape(nx * ZRIM, ny)


def widen_pressure(ext, center, xb, zb, xa, za):
    nx, nz, ny = ext.shape[0] - 2 * RADIUS, ext.shape[1] - 2 * ZRIM, ext.shape[2]
    if center is not None:
        ext[RADIUS:RADIUS + nx, ZRIM:ZRIM + nz] = center[...]
    for got, side in zip((xa, xb), sides("gx")):
        ext[pl.ds(side * (nx + RADIUS), RADIUS), ZRIM:ZRIM + nz] = got[HEAD:HEAD + RADIUS * nz, :].reshape(RADIUS, nz, ny)
    for got, side in zip((za, zb), sides("gz")):
        start = pl.multiple_of(side * (nz + ZRIM), ZRIM)
        ext[RADIUS:RADIUS + nx, pl.ds(start, ZRIM)] = got[HEAD:HEAD + nx * ZRIM, :].reshape(nx, ZRIM, ny)


def raw_pressure_kernel(
    air, wind, medium, xb, zb, xa, za, txa, txb, tza, tzb, oxb, ozb, oxa, oza, ext, pressure
):
    nx, nz, ny = air.shape[1:]
    widen(ext, air, xb, zb, xa, za)
    for x in range(nx):
        pressure[0, x] = pressure_rows(ext, wind, medium, x, nz)
    pack_pressure(pressure, (oxa, oxb), (oza, ozb))
    for out, sent in zip((oxa, oxb, oza, ozb), (txa, txb, tza, tzb)):
        out[0:HEAD, :] = jnp.zeros((HEAD, LANES), F32)
        out[out.shape[0] - sent.shape[0]:, :] = sent[...]


def put_rows(rows):
    place = lax.broadcasted_iota(jnp.int32, (HEAD, LANES), 0)
    out = jnp.zeros((HEAD, LANES), F32)
    for at, row in enumerate(rows):
        out = jnp.where(place == at, row, out)
    return out


def advection_kernel(air, wind, xb, zb, xa, za, moved, ext):
    nx, nz, ny = air.shape[1:]
    widen(ext, air, xb, zb, xa, za)
    lo, hi = ZRIM, ZRIM + nz
    for x in range(nx):
        xe = x + RADIUS
        for c in range(3):
            load = field(ext, 1 + c)
            moved[c, x] = (
                wind[0, x] * d1(load, xe, lo, hi)
                + wind[1, x] * d2(load, xe, lo, hi)
                + wind[2, x] * d3(load(xe, lo, hi))
            )


def velocities(out, center, moved, medium, wide, nx, nz):
    lo, hi = ZRIM, ZRIM + nz
    load = plane(wide)
    for x in range(nx):
        xe = x + RADIUS
        slopes = (d1(load, xe, lo, hi), d2(load, xe, lo, hi), d3(load(xe, lo, hi)))
        out[0, x] = load(xe, lo, hi)
        for c in range(3):
            out[1 + c, x] = center[1 + c, x] - medium[1, x] * slopes[c] - moved[c, x]


def pack_air(out, xb, zb, xa, za):
    for rim, side in zip((xa, xb), sides("gx")):
        pack_x(rim, 0, out, side)
    for rim, side in zip((za, zb), sides("gz")):
        pack_z(rim, 0, out, side)


def injected_kernel(
    n_gx, n_gz, air, wind, medium, rxb, rxa, moved, wxb, wzb, wxa, wza, pxb, pzb, pxa, pza, table, smap,
    out, oxb, ozb, oxa, oza, answer, spread, wide, wide_wind,
):
    nx, nz, ny = air.shape[1:]
    reach, _, slots = smap.shape
    strip, band = lax.axis_index("gx"), lax.axis_index("gz")
    mul = functools.partial(
        lax.dot_general, dimension_numbers=(((1,), (1,)), ((), ())), preferred_element_type=F32
    )
    for da in range(3):
        for db in range(3):
            speed, cells = arrived(table, strip + da - 1, band + db - 1, n_gx, n_gz, reach, slots)
            row_mask, third_mask = cell_masks(cells, nx * nz)
            columns = jnp.where(third_mask, 1.0, 0.0).astype(BF16)
            if da == 1 and db == 1:
                seen, rest = halves(air[0].reshape(nx * nz, ny))
                looked = jnp.dot(seen, columns, preferred_element_type=F32)
                looked = looked + jnp.dot(rest, columns, preferred_element_type=F32)
                answer[...] = jnp.sum(jnp.where(row_mask, looked, 0.0), axis=0, keepdims=True)
            block = mul(jnp.where(row_mask, speed, 0.0).astype(BF16), columns)
            spread[da * nx:(da + 1) * nx, db * nz:(db + 1) * nz] = block.reshape(nx, nz, ny)
    widen(wide_wind, wind, wxb, wzb, wxa, wza, first=air.shape[0])
    widen_pressure(wide, None, pxb, pzb, pxa, pza)
    for got, side in zip((rxa, rxb), sides("gx")):
        rows = got[HEAD:HEAD + RADIUS * nz, :].reshape(RADIUS, nz, ny)
        wide[pl.ds(RADIUS + side * (nx - RADIUS), RADIUS), ZRIM:ZRIM + nz] = rows
    load = plane(spread)
    for x in range(nx + 2 * RADIUS):
        xs = x + nx - RADIUS
        if RADIUS <= x < RADIUS + nx:
            lo, hi = 0, nz + 2 * ZRIM
        else:
            lo, hi = ZRIM, ZRIM + nz
        slo, shi = lo + nz - ZRIM, hi + nz - ZRIM
        here = load(xs, slo, shi)
        turned = (
            wide_wind[0, x, lo:hi, :] * d1(load, xs, slo, shi)
            + wide_wind[1, x, lo:hi, :] * d2(load, xs, slo, shi)
            + wide_wind[2, x, lo:hi, :] * d3(here)
        )
        wide[x, lo:hi, :] = wide[x, lo:hi, :] + (here - turned)
    velocities(out, air, moved, medium, wide, nx, nz)
    pack_air(out, oxb, ozb, oxa, oza)
    for rim in (oxa, oxb):
        rim[0:HEAD, :] = put_rows((answer[...],))


def pressure_kernel(air, wind, medium, xb, zb, xa, za, answer, pressure, oxb, ozb, oxa, oza, ext):
    nx, nz, ny = air.shape[1:]
    widen(ext, air, xb, zb, xa, za)
    for x in range(nx):
        pressure[0, x] = pressure_rows(ext, wind, medium, x, nz)
    pack_pressure(pressure, (oxa, oxb), (oza, ozb))
    low, high = by_side((xa[0:1, :], xb[0:1, :]), "gx")
    for rim in (oxa, oxb):
        rim[0:HEAD, :] = put_rows((answer[...], low, high))
    for rim in (oza, ozb):
        rim[0:HEAD, :] = jnp.zeros((HEAD, LANES), F32)


def velocity_kernel(air, pressure, medium, moved, xb, zb, xa, za, out, *rest):
    nx, nz, ny = air.shape[1:]
    wide = rest[-1]
    widen_pressure(wide, pressure.at[0], xb, zb, xa, za)
    velocities(out, air, moved, medium, wide, nx, nz)
    if len(rest) > 1:
        pack_air(out, *rest[:-1])
        for rim in (rest[0], rest[2]):
            rim[0:HEAD, :] = jnp.zeros((HEAD, LANES), F32)


def volume_kernel(state, integral, jac, stiff, out, token, rot, sp):
    quants, basis, width = state.shape
    dims = stiff.shape[0]
    pad = sp.shape[0] // dims
    token[...] = jnp.zeros_like(token)
    sp[...] = jnp.zeros_like(sp)
    place = lax.broadcasted_iota(jnp.int32, (basis, basis), 0)
    other = lax.broadcasted_iota(jnp.int32, (basis, basis), 1)
    unit = jnp.where(place == other, 1.0, 0.0).astype(F32)
    for d in range(dims):
        sp[d * pad:d * pad + basis, 0:basis] = dot_exact(unit, stiff[d], (((1,), (1,)), ((), ())))
    rotate(rot, stacked_left(sp[...]), integral, quants, width)

    def emit(p, at, value):
        out[p, :, lanes(at)] = state[p, :, lanes(at)] + value[0:basis]

    jacobian_step(lambda p, q, d, cut: jac[p, q, d:d + 1, cut], rot, emit, quants, dims, width)


def flux_kernel(
    first, faces, base, traces, own, solvers, lift, neighbours, xb, zb, xa, za,
    out, token, tiles, flux, lp,
):
    token[...] = jnp.zeros_like(token)
    quants, basis, width = base.shape
    face_basis = lift.shape[0]
    skip = xa.shape[0] - sent_rows(quants, face_basis)
    for axis, base_tile, gots in (("gx", 0, (xa, xb)), ("gz", 2, (za, zb))):
        for got, side in zip(gots, sides(axis)):
            for q in range(quants):
                tiles[q, base_tile + side, 0:8, :] = got[skip + q * 8:skip + q * 8 + 8, :]
                at = skip + quants * 8 + q * 2
                tiles[q, base_tile + side, 8:face_basis, :] = got[at:at + 2, :]
                tiles[q, base_tile + side, face_basis:, :] = jnp.zeros((16 - face_basis, LANES), F32)
    for q in range(quants):
        tiles[q, 4] = -own[q] if q < 3 else own[q]
    lp[...] = jnp.zeros_like(lp)
    for f in range(faces):
        for j in range(face_basis):
            lp[f * 16 + j:f * 16 + j + 1, 0:basis] = lift[j, first + f:first + f + 1, :]
    unit = lax.broadcasted_iota(jnp.int32, (lp.shape[1], lp.shape[1]), 0) == lax.broadcasted_iota(
        jnp.int32, (lp.shape[1], lp.shape[1]), 1
    )
    lifted = stacked_left(dot_exact(jnp.where(unit, 1.0, 0.0).astype(F32), lp[...], (((1,), (1,)), ((), ()))))
    local = traces.shape[2] // LANES
    halves_in = width // LANES

    def one(h, carry):
        at = h * LANES
        for f in range(faces):
            index = jnp.broadcast_to(neighbours[first + f:first + f + 1, lanes(at)], (16, LANES))
            acc = [None] * quants
            for q in range(quants):
                pool = [traces[q, :, s * LANES:(s + 1) * LANES] for s in range(local)]
                pool += [tiles[q, s] for s in range(5)]
                mine = traces[q, :, lanes((first + f) * width + at)]
                jump = take_slots(pool, index) - mine
                for p in range(quants):
                    term = solvers[p, q, first + f:first + f + 1, lanes(at)] * jump
                    acc[p] = term if acc[p] is None else acc[p] + term
            for p in range(quants):
                flux[f * 16:(f + 1) * 16, lanes(p * width + at)] = acc[p]
        return carry

    lax.fori_loop(0, halves_in, one, 0)
    for p in range(quants):
        cut = slice(p * width, (p + 1) * width)
        out[p] = base[p] + dot3(lifted, flux[:, cut])[0:basis]


def replies_kernel(base, solvers, lift, neighbours, smap, answer, rxb, rxa, out, slot_spread):
    quants, basis, width = base.shape
    face_basis, faces = lift.shape[:2]
    slots = smap.shape[2]
    low, high = by_side((rxa[0:HEAD, :], rxb[0:HEAD, :]), "gx")
    lane = lax.broadcasted_iota(jnp.int32, (1, LANES), 1)
    replies = jnp.zeros((1, LANES), F32)
    for r, row in enumerate((low[1:2], low[0:1], answer[...], high[0:1], high[2:3])):
        replies = jnp.where(lane // slots == r, row, replies)
    replies = jnp.broadcast_to(-2.0 * replies * flat_slots(smap, slot_spread)[2:3], (8, LANES))
    begin = faces * width + 4 * LANES
    square = lax.broadcasted_iota(jnp.int32, (basis, basis), 0) == lax.broadcasted_iota(
        jnp.int32, (basis, basis), 1
    )
    columns = []
    for f in range(faces):
        column = lift[0, f:f + 1, :]
        for j in range(1, face_basis):
            column = column + lift[j, f:f + 1, :]
        columns.append(jnp.sum(jnp.where(square, column, 0.0), axis=1, keepdims=True))
    for h in range(width // LANES):
        cut = slice(h * LANES, (h + 1) * LANES)
        spread = []
        for f in range(faces):
            index = jnp.broadcast_to(neighbours[f:f + 1, cut], (8, LANES))
            found = jnp.take_along_axis(replies, index % LANES, axis=1, mode="promise_in_bounds")
            spread.append(columns[f] * jnp.where(index >= begin, found, 0.0)[0:1])
        for p in range(quants):
            stress = solvers[p, 0, :, cut] + solvers[p, 1, :, cut] + solvers[p, 2, :, cut]
            total = base[p, :, cut]
            for f in range(faces):
                total = total + stress[f:f + 1] * spread[f]
            out[p, :, cut] = total


def sent_rows(quants, face_basis):
    return -(-quants * face_basis // 8) * 8


def shards(
    solid_state, jacobians, flux_solvers, stiffness, trace_matrix, lift_matrix,
    neighbours, send_faces, surface_map, surface_normals, air_state, wind_field, air_medium,
):
    quants, basis, width = solid_state.shape
    faces, face_basis = trace_matrix.shape[0], trace_matrix.shape[1]
    dims = stiffness.shape[0]
    nx, nz, ny = air_state.shape[1:]
    n_gx, n_gz = lax.axis_size("gx"), lax.axis_size("gz")
    jacobians = jnp.transpose(jacobians, (1, 2, 0, 3))
    flux_solvers = jnp.transpose(flux_solvers, (1, 2, 0, 3))
    trace_matrix = jnp.transpose(trace_matrix, (1, 0, 2))
    lift_matrix = jnp.transpose(lift_matrix, (2, 0, 1))
    surface_map = jnp.transpose(surface_map, (1, 0, 2))
    surface_normals = jnp.transpose(surface_normals, (1, 0, 2))
    pad = -(-basis // 8) * 8
    rim_z = (7, nx, RADIUS, ny)
    rim_x = (7, RADIUS, nz, ny)
    ext = (4, nx + 2 * RADIUS, nz + 2 * ZRIM, ny)
    wide = ext[1:]
    block = (1, nx, nz, ny)
    tile = (8, LANES)

    rims = exchange(
        *call(
            raw_rims_kernel, "raw_rims", [rim_x, rim_z, rim_x, rim_z], [air_state, wind_field],
        )
    )

    sent = (sent_rows(quants, face_basis), LANES)
    integral, traces, state = call(
        predict_kernel, "predict",
        [(K, quants * width), (quants, 16, faces * width), solid_state.shape],
        [solid_state, jacobians, stiffness, trace_matrix],
        [(K, quants * width), (dims * pad, quants * width), (dims * pad, LANES), (faces * 16, LANES)],
        flops=40_000_000,
    )
    own, rows = call(
        own_list_kernel, "own_list", [(quants, 16, LANES), (n_gx * n_gz * 8, LANES)],
        [traces, surface_map, surface_normals], [(surface_map.shape[0], 8, LANES)],
        after=[rims[1], rims[3]],
    )
    lists = lax.all_to_all(rows, ("gx", "gz"), split_axis=0, concat_axis=0, tiled=True)
    sent_four = call(
        outgoing_kernel, "outgoing", [sent, sent, sent, sent], [traces, send_faces],
        [(4, quants, 16, LANES)], flops=10_000_000, after=[rows],
    )
    (moved,) = call(
        advection_kernel, "advection", [(3, nx, nz, ny)],
        [air_state, wind_field, *rims], [ext], flops=10_000_000, after=[rows],
    )
    pressure_x = (HEAD + RADIUS * nz, ny)
    pressure_z = (HEAD + nx * ZRIM, ny)
    both_x = (pressure_x[0] + sent[0], LANES)
    both_z = (pressure_z[0] + sent[0], LANES)
    raw_xb, zb, raw_xa, za = call(
        raw_pressure_kernel, "raw_pressure", [both_x, both_z, both_x, both_z],
        [air_state, wind_field, air_medium, *rims, *sent_four], [ext, block], after=[moved],
    )
    both = exchange(raw_xb, zb, raw_xa, za)
    rim_x = (HEAD + 4 * RADIUS * nz, ny)
    rim_z = (4, nx, RADIUS, ny)
    air, xb, zb, xa, za, answer = call(
        functools.partial(injected_kernel, n_gx, n_gz), "injected",
        [air_state.shape, rim_x, rim_z, rim_x, rim_z, (1, LANES)],
        [air_state, wind_field, air_medium, raw_xb, raw_xa, moved, *rims, *both, lists, surface_map],
        [(3 * nx, 3 * nz, ny), wide, (3,) + wide],
    )
    half = faces // 2
    solid = state
    for substep in range(1, SUBSTEPS):
        rims = exchange(xb, zb, xa, za)
        solid, token = call(
            functools.partial(flux_kernel, (substep - 1) * half, half), "flux", [solid_state.shape, tile],
            [solid, traces, own, flux_solvers, lift_matrix, neighbours, *both],
            [(quants, 5, 16, LANES), (half * 16, quants * width), (LANES, pad)], flops=20_000_000,
            after=[xa],
        )
        pressure, xb, zb, xa, za = call(
            pressure_kernel, "pressure", [block, pressure_x, pressure_z, pressure_x, pressure_z],
            [air, wind_field, air_medium, *rims, answer], [ext], after=[token],
        )
        rises = exchange(xb, zb, xa, za)
        if substep == 1:
            replies = [answer, rises[0], rises[2]]
        (moved,) = call(
            advection_kernel, "advection", [(3, nx, nz, ny)],
            [air, wind_field, *rims], [ext], flops=10_000_000, after=[xa],
        )
        last = substep == SUBSTEPS - 1
        if not last:
            solid, token = call(
                volume_kernel, "volume", [solid_state.shape, tile], [solid, integral, jacobians, stiffness],
                [(dims * pad, quants * width), (dims * pad, LANES)], flops=10_000_000, after=[moved],
            )
        else:
            (solid,) = call(
                replies_kernel, "replies", [solid_state.shape],
                [solid, flux_solvers, lift_matrix, neighbours, surface_map, *replies],
                [(surface_map.shape[0], 8, LANES)], after=[moved],
            )
        outs = [air_state.shape] + ([] if last else [rim_x, rim_z, rim_x, rim_z])
        done = call(
            velocity_kernel, "velocity", outs, [air, pressure, air_medium, moved, *rises], [wide],
            after=[token],
        )
        air = done[0]
        if not last:
            xb, zb, xa, za = done[1:]
    return (solid, air)


def solution(mesh):
    in_specs = (
        P(None, None, ("gx", "gz")),
        P(None, None, None, ("gx", "gz")),
        P(None, None, None, ("gx", "gz")),
        P(),
        P(),
        P(),
        P(None, ("gx", "gz")),
        P(None, ("gx", "gz")),
        P(None, None, ("gx", "gz")),
        P(None, None, ("gx", "gz")),
        P(None, "gx", "gz", None),
        P(None, "gx", "gz", None),
        P(None, "gx", "gz", None),
    )
    out_specs = (P(None, None, ("gx", "gz")), P(None, "gx", "gz", None))
    return jax.shard_map(shards, mesh=mesh, in_specs=in_specs, out_specs=out_specs, check_vma=False)
```

```python
import functools

import jax
import jax.numpy as jnp
from jax import lax
from jax.experimental import pallas as pl
from jax.experimental.pallas import tpu as pltpu
from jax.sharding import PartitionSpec as P

ORDERS = 4
RADIUS = 4
SUBSTEPS = 3
ZRIM = 8
LANES = 128
HEAD = 8
FACE_ROWS = 10
K = 32
TIME_STEP = 0.5
STENCIL_WEIGHTS = (0.8, -0.2, 4.0 / 105.0, -1.0 / 280.0)
F32 = jnp.float32
BF16 = jnp.bfloat16


def call(kernel, name, outs, ins, scratch=(), flops=1_000_000, after=()):
    count, skip = len(ins), len(after)
    nbytes = 4 * sum(x.size for x in ins) + 4 * sum(functools.reduce(lambda m, n: m * n, s, 1) for s in outs)

    def body(*refs):
        kernel(*refs[:count], *refs[count + skip:])

    return pl.pallas_call(
        body,
        out_shape=[jax.ShapeDtypeStruct(s, F32) for s in outs],
        in_specs=[pl.BlockSpec(memory_space=pltpu.VMEM) for _ in ins]
        + [pl.BlockSpec(memory_space=pl.ANY) for _ in after],
        out_specs=[pl.BlockSpec(memory_space=pltpu.VMEM) for _ in outs],
        scratch_shapes=[pltpu.VMEM(s, F32) for s in scratch],
        compiler_params=pltpu.CompilerParams(vmem_limit_bytes=8 * 1024 * 1024),
        cost_estimate=pl.CostEstimate(flops=flops, bytes_accessed=nbytes, transcendentals=0),
        name=name,
    )(*ins, *after)


def swap(values, axis, odd, by=1):
    count = lax.axis_size(axis)
    pairs = []
    for i in range(count - by):
        if i // by % 2 == odd:
            pairs += [(i, i + by), (i + by, i)]
    return lax.ppermute(values, axis, pairs)


def exchange(xb, zb, xa, za):
    return swap(xb, "gx", 1), swap(zb, "gz", 1), swap(xa, "gx", 0), swap(za, "gz", 0)


def sides(axis, by=1):
    parity = (lax.axis_index(axis) // by) & 1
    return 1 - parity, parity


def by_side(pair, axis, by=1):
    first = sides(axis, by)[0]
    return jnp.where(first == 0, pair[0], pair[1]), jnp.where(first == 1, pair[0], pair[1])


def halves(values):
    high = values.astype(BF16)
    return high, (values - high.astype(F32)).astype(BF16)


def stacked_left(matrix):
    spread = matrix + pltpu.roll(matrix, K, 1) + pltpu.roll(matrix, 2 * K, 1)
    high = spread.astype(BF16).astype(F32)
    lane = lax.broadcasted_iota(jnp.int32, spread.shape, 1)
    return jnp.where(lane < 2 * K, high, spread - high).astype(BF16)[:, 0:3 * K]


def dot3(left, right):
    high, low = halves(right)
    return jnp.dot(left, jnp.concatenate([high, low, high], axis=0), preferred_element_type=F32)


def dot_exact(left, right, dims=(((1,), (0,)), ((), ()))):
    return lax.dot_general(
        left, right, dims, precision=lax.Precision.HIGHEST, preferred_element_type=F32
    )


def flat_slots(table, spread):
    rows, fields, slots = table.shape
    lane = lax.broadcasted_iota(jnp.int32, (8, LANES), 1)
    for r in range(rows):
        spread[r, 0:fields, 0:slots] = table[r].astype(F32)
    flat = jnp.zeros((8, LANES), F32)
    for r in range(rows):
        got = jnp.take_along_axis(spread[r], lane % slots, axis=1, mode="promise_in_bounds")
        flat = jnp.where(lane // slots == r, got, flat)
    return flat


def pack_x(out, at, source, side):
    fields, nx, nz, ny = source.shape
    start = side * (nx - RADIUS)
    rows = fields * RADIUS * nz
    at = HEAD + at * RADIUS * nz
    out[at:at + rows, :] = source[:, pl.ds(start, RADIUS)].reshape(rows, ny)


def pack_z(out, at, source, side):
    fields, nz = source.shape[0], source.shape[2]
    out[at:at + fields] = jnp.where(side == 1, source[:, :, nz - RADIUS:, :], source[:, :, 0:RADIUS, :])


def widen(ext, center, xb, zb, xa, za, first=0):
    fields, nx, nz, ny = center.shape
    ext[:, RADIUS:RADIUS + nx, ZRIM:ZRIM + nz] = center[...]
    for got, side in zip((xa, xb), sides("gx")):
        place = pl.ds(side * (nx + RADIUS), RADIUS)
        if len(got.shape) == 4:
            rows = got[first:first + fields]
        else:
            rows = got[HEAD:HEAD + fields * RADIUS * nz, :].reshape(fields, RADIUS, nz, ny)
        ext[:, place, ZRIM:ZRIM + nz] = rows
    low, high = by_side([got[first:first + fields] for got in (za, zb)], "gz")
    ext[:, RADIUS:RADIUS + nx, ZRIM - RADIUS:ZRIM] = low
    ext[:, RADIUS:RADIUS + nx, ZRIM + nz:ZRIM + nz + RADIUS] = high


def d1(load, x, lo, hi):
    total = None
    for m, w in enumerate(STENCIL_WEIGHTS, 1):
        term = w * (load(x + m, lo, hi) - load(x - m, lo, hi))
        total = term if total is None else total + term
    return total


def d2(load, x, lo, hi):
    total = None
    for m, w in enumerate(STENCIL_WEIGHTS, 1):
        term = w * (load(x, lo + m, hi + m) - load(x, lo - m, hi - m))
        total = term if total is None else total + term
    return total


def d3(values):
    width = values.shape[1]
    lane = lax.broadcasted_iota(jnp.int32, (1, width), 1)
    total = None
    for m, w in enumerate(STENCIL_WEIGHTS, 1):
        ahead = jnp.where(lane < width - m, w, 0.0) * pltpu.roll(values, width - m, 1)
        behind = jnp.where(lane >= m, w, 0.0) * pltpu.roll(values, m, 1)
        term = ahead - behind
        total = term if total is None else total + term
    return total


def field(ref, c):
    return lambda x, lo, hi: ref[c, x, lo:hi, :]


def plane(ref):
    return lambda x, lo, hi: ref[x, lo:hi, :]


def arrived(table, strip, band, n_gx, n_gz, reach, slots):
    lane = lax.broadcasted_iota(jnp.int32, (1, LANES), 1)
    got = jnp.zeros((1, LANES), F32)
    inside = (strip >= 0) & (strip < n_gx) & (band >= 0) & (band < n_gz)
    for r in range(reach):
        source = strip - (r - reach // 2)
        valid = inside & (source >= 0) & (source < n_gx)
        at = jnp.where(valid, source * n_gz + band, 0) * 8
        row = table[pl.ds(pl.multiple_of(at, 8), 8), :][0:1]
        here = ((lane & (LANES // 2 - 1)) // slots == r) & valid
        got = jnp.where(here, row, got)
    turned = pltpu.roll(got, LANES // 2, 1)
    speed = jnp.where(lane < LANES // 2, got, turned)
    high = speed.astype(BF16).astype(F32)
    return jnp.where(lane < LANES // 2, high, speed - high), jnp.where(lane < LANES // 2, turned, got)


def cell_masks(cells, rows):
    cells = cells.astype(jnp.int32)
    place = lax.broadcasted_iota(jnp.int32, (rows, LANES), 0)
    third = lax.broadcasted_iota(jnp.int32, (LANES, LANES), 0)
    return cells // LANES == place, cells % LANES == third


def raw_rims_kernel(air, wind, xb, zb, xa, za):
    fields, nx = air.shape[:2]
    for out, side in zip((xa, xb), sides("gx")):
        rows = pl.ds(side * (nx - RADIUS), RADIUS)
        out[0:fields] = air[:, rows]
        out[fields:] = wind[:, rows]
    for out, side in zip((za, zb), sides("gz")):
        pack_z(out, 0, air, side)
        pack_z(out, fields, wind, side)


def lanes(at):
    return pl.ds(at if isinstance(at, int) else pl.multiple_of(at, LANES), LANES)


def jacobian_step(load, rot, emit, quants, dims, width):
    rows = rot.shape[0] // dims

    def half(h, carry):
        at = h * LANES
        acc = [None] * quants
        for d in range(dims):
            for q in range(quants):
                turned = rot[d * rows:(d + 1) * rows, lanes(q * width + at)].reshape(rows // 8, 8, LANES)
                for p in range(quants):
                    term = load(p, q, d, lanes(at)) * turned
                    acc[p] = term if acc[p] is None else acc[p] + term
        for p in range(quants):
            emit(p, at, acc[p].reshape(rows, LANES))
        return carry

    lax.fori_loop(0, width // LANES, half, 0)


def rotate(rot, left, source, quants, width):
    for q in range(quants):
        cut = slice(q * width, (q + 1) * width)
        rot[:, cut] = dot3(left, source[:, cut])


def take_slots(tiles, index):
    low = index % LANES
    high = index // LANES
    got = None
    for s, tile in enumerate(tiles):
        picked = jnp.take_along_axis(tile, low, axis=1, mode="promise_in_bounds")
        got = picked if got is None else jnp.where(high == s, picked, got)
    return got


def predict_kernel(
    state, jac, stiff, trace,
    integral, traces, kept,
    cur, rot, sp, tp,
):
    quants, basis, width = state.shape
    pad = sp.shape[0] // stiff.shape[0]
    face_basis, faces = trace.shape[:2]
    dims = stiff.shape[0]
    sp[...] = jnp.zeros_like(sp)
    tp[...] = jnp.zeros_like(tp)
    cur[...] = jnp.zeros_like(cur)
    for d in range(dims):
        sp[d * pad:d * pad + basis, 0:basis] = stiff[d]
    for f in range(faces):
        for j in range(face_basis):
            tp[f * 16 + j:f * 16 + j + 1, 0:basis] = trace[j, f:f + 1, :]
    for q in range(quants):
        cur[0:basis, q * width:(q + 1) * width] = state[q]
    kept[...] = state[...]
    integral[...] = TIME_STEP * cur[...]
    left = stacked_left(sp[...])

    def degree(k, weight):
        weight = jnp.where(k == 1, TIME_STEP**2 / 2, jnp.where(k == 2, TIME_STEP**3 / 6, TIME_STEP**4 / 24))
        rotate(rot, left, cur, quants, width)

        def emit(p, at, value):
            cut = lanes(p * width + at)
            cur[0:pad, cut] = -value
            integral[0:pad, cut] = integral[0:pad, cut] - weight * value

        jacobian_step(lambda p, q, d, cut: jac[p, q, d:d + 1, cut], rot, emit, quants, dims, width)
        return weight

    lax.fori_loop(1, ORDERS, degree, F32(0))
    restrict = stacked_left(tp[...])
    for q in range(quants):
        cut = slice(q * width, (q + 1) * width)
        done = dot3(restrict, integral[:, cut])
        for f in range(faces):
            traces[q, :, f * width:(f + 1) * width] = done[f * 16:(f + 1) * 16]


def own_list_kernel(traces, smap, normals, own, rows, spread):
    quants, _, all_slots = traces.shape
    slots = flat_slots(smap, spread)
    wanted = jnp.broadcast_to(slots[0:1].astype(jnp.int32), (16, LANES))

    def gather(q, carry):
        own[q] = take_slots([traces[q, :, s * LANES:(s + 1) * LANES] for s in range(all_slots // LANES)], wanted)
        return carry

    lax.fori_loop(0, quants, gather, 0)
    normal = flat_slots(normals, spread)
    speed = jnp.zeros((1, LANES), F32)
    for c in range(3):
        mean = jnp.sum(own[6 + c, 0:FACE_ROWS, :], axis=0, keepdims=True) * (1.0 / FACE_ROWS)
        speed = speed + normal[c:c + 1] * mean
    lane = lax.broadcasted_iota(jnp.int32, (1, LANES), 1)
    cells = pltpu.roll(slots[1:2], LANES // 2, 1)
    rows[...] = jnp.broadcast_to(jnp.where(lane < LANES // 2, slots[2:3] * speed, cells), rows.shape)


def outgoing_kernel(traces, sends, xa, xb, za, zb, picked):
    quants, _, slots = traces.shape
    rows = sent_rows(quants, FACE_ROWS)
    wanted = [jnp.broadcast_to(sends[d:d + 1, :], (16, LANES)) for d in range(4)]

    def gather(q, carry):
        tiles = [traces[q, :, s * LANES:(s + 1) * LANES] for s in range(slots // LANES)]
        for d in range(4):
            picked[d, q] = take_slots(tiles, wanted[d])
        return carry

    lax.fori_loop(0, quants, gather, 0)
    rest = FACE_ROWS - 8
    for axis, base, outs in (("gx", 0, (xa, xb)), ("gz", 2, (za, zb))):
        for out, side in zip(outs, sides(axis)):
            for q in range(quants):
                out[q * 8:q * 8 + 8, :] = picked[base + side, q, 0:8, :]
                at = quants * 8 + q * rest
                out[at:at + rest, :] = picked[base + side, q, 8:FACE_ROWS, :]
            out[quants * FACE_ROWS:, :] = jnp.zeros((rows - quants * FACE_ROWS, LANES), F32)


def pressure_rows(ext, wind, medium, x, nz):
    lo, hi = ZRIM, ZRIM + nz
    xe = x + RADIUS
    pressure = field(ext, 0)
    here = pressure(xe, lo, hi)
    divergence = d1(field(ext, 1), xe, lo, hi) + d2(field(ext, 2), xe, lo, hi) + d3(ext[3, xe, lo:hi, :])
    moved = (
        wind[0, x] * d1(pressure, xe, lo, hi)
        + wind[1, x] * d2(pressure, xe, lo, hi)
        + wind[2, x] * d3(here)
    )
    return here - medium[0, x] * divergence - moved


def pack_pressure(center, xs, zs):
    nx, nz, ny = center.shape[1:]
    for out, side in zip(xs, sides("gx")):
        start = side * (nx - RADIUS)
        out[HEAD:HEAD + RADIUS * nz, :] = center[0, pl.ds(start, RADIUS)].reshape(RADIUS * nz, ny)
    for out, side in zip(zs, sides("gz")):
        start = pl.multiple_of(side * (nz - ZRIM), ZRIM)
        out[HEAD:HEAD + nx * ZRIM, :] = center[0, :, pl.ds(start, ZRIM), :].reshape(nx * ZRIM, ny)


def widen_pressure(ext, center, xb, zb, xa, za):
    nx, nz, ny = ext.shape[0] - 2 * RADIUS, ext.shape[1] - 2 * ZRIM, ext.shape[2]
    if center is not None:
        ext[RADIUS:RADIUS + nx, ZRIM:ZRIM + nz] = center[...]
    for got, side in zip((xa, xb), sides("gx")):
        ext[pl.ds(side * (nx + RADIUS), RADIUS), ZRIM:ZRIM + nz] = got[HEAD:HEAD + RADIUS * nz, :].reshape(RADIUS, nz, ny)
    for got, side in zip((za, zb), sides("gz")):
        start = pl.multiple_of(side * (nz + ZRIM), ZRIM)
        ext[RADIUS:RADIUS + nx, pl.ds(start, ZRIM)] = got[HEAD:HEAD + nx * ZRIM, :].reshape(nx, ZRIM, ny)


def raw_pressure_kernel(
    air, wind, medium, xb, zb, xa, za, txa, txb, tza, tzb, oxb, ozb, oxa, oza, ext, pressure
):
    nx, nz, ny = air.shape[1:]
    widen(ext, air, xb, zb, xa, za)
    for x in range(nx):
        pressure[0, x] = pressure_rows(ext, wind, medium, x, nz)
    pack_pressure(pressure, (oxa, oxb), (oza, ozb))
    for out, sent in zip((oxa, oxb, oza, ozb), (txa, txb, tza, tzb)):
        out[0:HEAD, :] = jnp.zeros((HEAD, LANES), F32)
        out[out.shape[0] - sent.shape[0]:, :] = sent[...]


def put_rows(rows):
    place = lax.broadcasted_iota(jnp.int32, (HEAD, LANES), 0)
    out = jnp.zeros((HEAD, LANES), F32)
    for at, row in enumerate(rows):
        out = jnp.where(place == at, row, out)
    return out


def advection_kernel(air, wind, xb, zb, xa, za, moved, ext):
    nx, nz, ny = air.shape[1:]
    widen(ext, air, xb, zb, xa, za)
    lo, hi = ZRIM, ZRIM + nz
    for x in range(nx):
        xe = x + RADIUS
        for c in range(3):
            load = field(ext, 1 + c)
            moved[c, x] = (
                wind[0, x] * d1(load, xe, lo, hi)
                + wind[1, x] * d2(load, xe, lo, hi)
                + wind[2, x] * d3(load(xe, lo, hi))
            )


def velocities(out, center, moved, medium, wide, nx, nz):
    lo, hi = ZRIM, ZRIM + nz
    load = plane(wide)
    for x in range(nx):
        xe = x + RADIUS
        slopes = (d1(load, xe, lo, hi), d2(load, xe, lo, hi), d3(load(xe, lo, hi)))
        out[0, x] = load(xe, lo, hi)
        for c in range(3):
            out[1 + c, x] = center[1 + c, x] - medium[1, x] * slopes[c] - moved[c, x]


def pack_air(out, xb, zb, xa, za):
    for rim, side in zip((xa, xb), sides("gx")):
        pack_x(rim, 0, out, side)
    for rim, side in zip((za, zb), sides("gz")):
        pack_z(rim, 0, out, side)


def injected_kernel(
    n_gx, n_gz, air, wind, medium, moved, wxb, wzb, wxa, wza, pxb, pzb, pxa, pza, table, smap,
    out, oxb, ozb, oxa, oza, answer, spread, wide, wide_wind, ext,
):
    nx, nz, ny = air.shape[1:]
    reach, _, slots = smap.shape
    strip, band = lax.axis_index("gx"), lax.axis_index("gz")
    mul = functools.partial(
        lax.dot_general, dimension_numbers=(((1,), (1,)), ((), ())), preferred_element_type=F32
    )
    for da in range(3):
        for db in range(3):
            speed, cells = arrived(table, strip + da - 1, band + db - 1, n_gx, n_gz, reach, slots)
            row_mask, third_mask = cell_masks(cells, nx * nz)
            columns = jnp.where(third_mask, 1.0, 0.0).astype(BF16)
            if da == 1 and db == 1:
                seen, rest = halves(air[0].reshape(nx * nz, ny))
                looked = jnp.dot(seen, columns, preferred_element_type=F32)
                looked = looked + jnp.dot(rest, columns, preferred_element_type=F32)
                answer[...] = jnp.sum(jnp.where(row_mask, looked, 0.0), axis=0, keepdims=True)
            block = mul(jnp.where(row_mask, speed, 0.0).astype(BF16), columns)
            spread[da * nx:(da + 1) * nx, db * nz:(db + 1) * nz] = block.reshape(nx, nz, ny)
    widen(wide_wind, wind, wxb, wzb, wxa, wza, first=air.shape[0])
    widen_pressure(wide, None, pxb, pzb, pxa, pza)
    widen(ext, air, wxb, wzb, wxa, wza)
    for x in range(nx):
        wide[RADIUS + x, ZRIM:ZRIM + nz] = pressure_rows(ext, wind, medium, x, nz)
    load = plane(spread)
    for x in range(nx + 2 * RADIUS):
        xs = x + nx - RADIUS
        if RADIUS <= x < RADIUS + nx:
            lo, hi = 0, nz + 2 * ZRIM
        else:
            lo, hi = ZRIM, ZRIM + nz
        slo, shi = lo + nz - ZRIM, hi + nz - ZRIM
        here = load(xs, slo, shi)
        turned = (
            wide_wind[0, x, lo:hi, :] * d1(load, xs, slo, shi)
            + wide_wind[1, x, lo:hi, :] * d2(load, xs, slo, shi)
            + wide_wind[2, x, lo:hi, :] * d3(here)
        )
        wide[x, lo:hi, :] = wide[x, lo:hi, :] + (here - turned)
    velocities(out, air, moved, medium, wide, nx, nz)
    pack_air(out, oxb, ozb, oxa, oza)
    for rim in (oxa, oxb):
        rim[0:HEAD, :] = put_rows((answer[...],))


def pressure_kernel(air, wind, medium, xb, zb, xa, za, answer, pressure, oxb, ozb, oxa, oza, ext):
    nx, nz, ny = air.shape[1:]
    widen(ext, air, xb, zb, xa, za)
    for x in range(nx):
        pressure[0, x] = pressure_rows(ext, wind, medium, x, nz)
    pack_pressure(pressure, (oxa, oxb), (oza, ozb))
    low, high = by_side((xa[0:1, :], xb[0:1, :]), "gx")
    for rim in (oxa, oxb):
        rim[0:HEAD, :] = put_rows((answer[...], low, high))
    for rim in (oza, ozb):
        rim[0:HEAD, :] = jnp.zeros((HEAD, LANES), F32)


def velocity_kernel(air, pressure, medium, moved, xb, zb, xa, za, out, *rest):
    nx, nz, ny = air.shape[1:]
    wide = rest[-1]
    widen_pressure(wide, pressure.at[0], xb, zb, xa, za)
    velocities(out, air, moved, medium, wide, nx, nz)
    if len(rest) > 1:
        pack_air(out, *rest[:-1])
        for rim in (rest[0], rest[2]):
            rim[0:HEAD, :] = jnp.zeros((HEAD, LANES), F32)


def volume_kernel(state, integral, jac, stiff, out, token, rot, sp):
    quants, basis, width = state.shape
    dims = stiff.shape[0]
    pad = sp.shape[0] // dims
    token[...] = jnp.zeros_like(token)
    sp[...] = jnp.zeros_like(sp)
    place = lax.broadcasted_iota(jnp.int32, (basis, basis), 0)
    other = lax.broadcasted_iota(jnp.int32, (basis, basis), 1)
    unit = jnp.where(place == other, 1.0, 0.0).astype(F32)
    for d in range(dims):
        sp[d * pad:d * pad + basis, 0:basis] = dot_exact(unit, stiff[d], (((1,), (1,)), ((), ())))
    rotate(rot, stacked_left(sp[...]), integral, quants, width)

    def emit(p, at, value):
        out[p, :, lanes(at)] = state[p, :, lanes(at)] + value[0:basis]

    jacobian_step(lambda p, q, d, cut: jac[p, q, d:d + 1, cut], rot, emit, quants, dims, width)


def flux_kernel(
    first, faces, base, traces, own, solvers, lift, neighbours, xb, zb, xa, za,
    out, token, tiles, flux, lp,
):
    token[...] = jnp.zeros_like(token)
    quants, basis, width = base.shape
    face_basis = lift.shape[0]
    skip = xa.shape[0] - sent_rows(quants, face_basis)
    for axis, base_tile, gots in (("gx", 0, (xa, xb)), ("gz", 2, (za, zb))):
        for got, side in zip(gots, sides(axis)):
            for q in range(quants):
                tiles[q, base_tile + side, 0:8, :] = got[skip + q * 8:skip + q * 8 + 8, :]
                at = skip + quants * 8 + q * 2
                tiles[q, base_tile + side, 8:face_basis, :] = got[at:at + 2, :]
                tiles[q, base_tile + side, face_basis:, :] = jnp.zeros((16 - face_basis, LANES), F32)
    for q in range(quants):
        tiles[q, 4] = -own[q] if q < 3 else own[q]
    lp[...] = jnp.zeros_like(lp)
    for f in range(faces):
        for j in range(face_basis):
            lp[f * 16 + j:f * 16 + j + 1, 0:basis] = lift[j, first + f:first + f + 1, :]
    unit = lax.broadcasted_iota(jnp.int32, (lp.shape[1], lp.shape[1]), 0) == lax.broadcasted_iota(
        jnp.int32, (lp.shape[1], lp.shape[1]), 1
    )
    lifted = stacked_left(dot_exact(jnp.where(unit, 1.0, 0.0).astype(F32), lp[...], (((1,), (1,)), ((), ()))))
    local = traces.shape[2] // LANES
    halves_in = width // LANES

    def one(h, carry):
        at = h * LANES
        for f in range(faces):
            index = jnp.broadcast_to(neighbours[first + f:first + f + 1, lanes(at)], (16, LANES))
            acc = [None] * quants
            for q in range(quants):
                pool = [traces[q, :, s * LANES:(s + 1) * LANES] for s in range(local)]
                pool += [tiles[q, s] for s in range(5)]
                mine = traces[q, :, lanes((first + f) * width + at)]
                jump = take_slots(pool, index) - mine
                for p in range(quants):
                    term = solvers[p, q, first + f:first + f + 1, lanes(at)] * jump
                    acc[p] = term if acc[p] is None else acc[p] + term
            for p in range(quants):
                flux[f * 16:(f + 1) * 16, lanes(p * width + at)] = acc[p]
        return carry

    lax.fori_loop(0, halves_in, one, 0)
    for p in range(quants):
        cut = slice(p * width, (p + 1) * width)
        out[p] = base[p] + dot3(lifted, flux[:, cut])[0:basis]


def replies_kernel(base, solvers, lift, neighbours, smap, answer, rxb, rxa, out, slot_spread):
    quants, basis, width = base.shape
    face_basis, faces = lift.shape[:2]
    slots = smap.shape[2]
    low, high = by_side((rxa[0:HEAD, :], rxb[0:HEAD, :]), "gx")
    lane = lax.broadcasted_iota(jnp.int32, (1, LANES), 1)
    replies = jnp.zeros((1, LANES), F32)
    for r, row in enumerate((low[1:2], low[0:1], answer[...], high[0:1], high[2:3])):
        replies = jnp.where(lane // slots == r, row, replies)
    replies = jnp.broadcast_to(-2.0 * replies * flat_slots(smap, slot_spread)[2:3], (8, LANES))
    begin = faces * width + 4 * LANES
    square = lax.broadcasted_iota(jnp.int32, (basis, basis), 0) == lax.broadcasted_iota(
        jnp.int32, (basis, basis), 1
    )
    columns = []
    for f in range(faces):
        column = lift[0, f:f + 1, :]
        for j in range(1, face_basis):
            column = column + lift[j, f:f + 1, :]
        columns.append(jnp.sum(jnp.where(square, column, 0.0), axis=1, keepdims=True))
    for h in range(width // LANES):
        cut = slice(h * LANES, (h + 1) * LANES)
        spread = []
        for f in range(faces):
            index = jnp.broadcast_to(neighbours[f:f + 1, cut], (8, LANES))
            found = jnp.take_along_axis(replies, index % LANES, axis=1, mode="promise_in_bounds")
            spread.append(columns[f] * jnp.where(index >= begin, found, 0.0)[0:1])
        for p in range(quants):
            stress = solvers[p, 0, :, cut] + solvers[p, 1, :, cut] + solvers[p, 2, :, cut]
            total = base[p, :, cut]
            for f in range(faces):
                total = total + stress[f:f + 1] * spread[f]
            out[p, :, cut] = total


def sent_rows(quants, face_basis):
    return -(-quants * face_basis // 8) * 8


def shards(
    solid_state, jacobians, flux_solvers, stiffness, trace_matrix, lift_matrix,
    neighbours, send_faces, surface_map, surface_normals, air_state, wind_field, air_medium,
):
    quants, basis, width = solid_state.shape
    faces, face_basis = trace_matrix.shape[0], trace_matrix.shape[1]
    dims = stiffness.shape[0]
    nx, nz, ny = air_state.shape[1:]
    n_gx, n_gz = lax.axis_size("gx"), lax.axis_size("gz")
    jacobians = jnp.transpose(jacobians, (1, 2, 0, 3))
    flux_solvers = jnp.transpose(flux_solvers, (1, 2, 0, 3))
    trace_matrix = jnp.transpose(trace_matrix, (1, 0, 2))
    lift_matrix = jnp.transpose(lift_matrix, (2, 0, 1))
    surface_map = jnp.transpose(surface_map, (1, 0, 2))
    surface_normals = jnp.transpose(surface_normals, (1, 0, 2))
    pad = -(-basis // 8) * 8
    rim_z = (7, nx, RADIUS, ny)
    rim_x = (7, RADIUS, nz, ny)
    ext = (4, nx + 2 * RADIUS, nz + 2 * ZRIM, ny)
    wide = ext[1:]
    block = (1, nx, nz, ny)
    tile = (8, LANES)

    rims = exchange(
        *call(
            raw_rims_kernel, "raw_rims", [rim_x, rim_z, rim_x, rim_z], [air_state, wind_field],
        )
    )

    sent = (sent_rows(quants, face_basis), LANES)
    integral, traces, state = call(
        predict_kernel, "predict",
        [(K, quants * width), (quants, 16, faces * width), solid_state.shape],
        [solid_state, jacobians, stiffness, trace_matrix],
        [(K, quants * width), (dims * pad, quants * width), (dims * pad, LANES), (faces * 16, LANES)],
        flops=40_000_000,
    )
    own, rows = call(
        own_list_kernel, "own_list", [(quants, 16, LANES), (n_gx * n_gz * 8, LANES)],
        [traces, surface_map, surface_normals], [(surface_map.shape[0], 8, LANES)],
        after=[rims[1], rims[3]],
    )
    lists = lax.all_to_all(rows, ("gx", "gz"), split_axis=0, concat_axis=0, tiled=True)
    sent_four = call(
        outgoing_kernel, "outgoing", [sent, sent, sent, sent], [traces, send_faces],
        [(4, quants, 16, LANES)], flops=10_000_000, after=[rows],
    )
    (moved,) = call(
        advection_kernel, "advection", [(3, nx, nz, ny)],
        [air_state, wind_field, *rims], [ext], flops=10_000_000, after=[rows],
    )
    pressure_x = (HEAD + RADIUS * nz, ny)
    pressure_z = (HEAD + nx * ZRIM, ny)
    both_x = (pressure_x[0] + sent[0], LANES)
    both_z = (pressure_z[0] + sent[0], LANES)
    xb, zb, xa, za = call(
        raw_pressure_kernel, "raw_pressure", [both_x, both_z, both_x, both_z],
        [air_state, wind_field, air_medium, *rims, *sent_four], [ext, block], after=[moved],
    )
    both = exchange(xb, zb, xa, za)
    rim_x = (HEAD + 4 * RADIUS * nz, ny)
    rim_z = (4, nx, RADIUS, ny)
    air, xb, zb, xa, za, answer = call(
        functools.partial(injected_kernel, n_gx, n_gz), "injected",
        [air_state.shape, rim_x, rim_z, rim_x, rim_z, (1, LANES)],
        [air_state, wind_field, air_medium, moved, *rims, *both, lists, surface_map],
        [(3 * nx, 3 * nz, ny), wide, (3,) + wide, ext],
    )
    half = faces // 2
    solid = state
    for substep in range(1, SUBSTEPS):
        rims = exchange(xb, zb, xa, za)
        solid, token = call(
            functools.partial(flux_kernel, (substep - 1) * half, half), "flux", [solid_state.shape, tile],
            [solid, traces, own, flux_solvers, lift_matrix, neighbours, *both],
            [(quants, 5, 16, LANES), (half * 16, quants * width), (LANES, pad)], flops=20_000_000,
            after=[xa],
        )
        pressure, xb, zb, xa, za = call(
            pressure_kernel, "pressure", [block, pressure_x, pressure_z, pressure_x, pressure_z],
            [air, wind_field, air_medium, *rims, answer], [ext], after=[token],
        )
        rises = exchange(xb, zb, xa, za)
        if substep == 1:
            replies = [answer, rises[0], rises[2]]
        (moved,) = call(
            advection_kernel, "advection", [(3, nx, nz, ny)],
            [air, wind_field, *rims], [ext], flops=10_000_000, after=[xa],
        )
        last = substep == SUBSTEPS - 1
        if not last:
            solid, token = call(
                volume_kernel, "volume", [solid_state.shape, tile], [solid, integral, jacobians, stiffness],
                [(dims * pad, quants * width), (dims * pad, LANES)], flops=10_000_000, after=[moved],
            )
        else:
            (solid,) = call(
                replies_kernel, "replies", [solid_state.shape],
                [solid, flux_solvers, lift_matrix, neighbours, surface_map, *replies],
                [(surface_map.shape[0], 8, LANES)], after=[moved],
            )
        outs = [air_state.shape] + ([] if last else [rim_x, rim_z, rim_x, rim_z])
        done = call(
            velocity_kernel, "velocity", outs, [air, pressure, air_medium, moved, *rises], [wide],
            after=[token],
        )
        air = done[0]
        if not last:
            xb, zb, xa, za = done[1:]
    return (solid, air)


def solution(mesh):
    in_specs = (
        P(None, None, ("gx", "gz")),
        P(None, None, None, ("gx", "gz")),
        P(None, None, None, ("gx", "gz")),
        P(),
        P(),
        P(),
        P(None, ("gx", "gz")),
        P(None, ("gx", "gz")),
        P(None, None, ("gx", "gz")),
        P(None, None, ("gx", "gz")),
        P(None, "gx", "gz", None),
        P(None, "gx", "gz", None),
        P(None, "gx", "gz", None),
    )
    out_specs = (P(None, None, ("gx", "gz")), P(None, "gx", "gz", None))
    return jax.shard_map(shards, mesh=mesh, in_specs=in_specs, out_specs=out_specs, check_vma=False)
```

```python
import functools

import jax
import jax.numpy as jnp
from jax import lax
from jax.experimental import pallas as pl
from jax.experimental.pallas import tpu as pltpu
from jax.sharding import PartitionSpec as P

ORDERS = 4
RADIUS = 4
SUBSTEPS = 3
ZRIM = 8
LANES = 128
HEAD = 8
FACE_ROWS = 10
K = 32
TIME_STEP = 0.5
STENCIL_WEIGHTS = (0.8, -0.2, 4.0 / 105.0, -1.0 / 280.0)
F32 = jnp.float32
BF16 = jnp.bfloat16


def call(kernel, name, outs, ins, scratch=(), flops=1_000_000, after=()):
    count, skip = len(ins), len(after)
    nbytes = 4 * sum(x.size for x in ins) + 4 * sum(functools.reduce(lambda m, n: m * n, s, 1) for s in outs)

    def body(*refs):
        kernel(*refs[:count], *refs[count + skip:])

    return pl.pallas_call(
        body,
        out_shape=[jax.ShapeDtypeStruct(s, F32) for s in outs],
        in_specs=[pl.BlockSpec(memory_space=pltpu.VMEM) for _ in ins]
        + [pl.BlockSpec(memory_space=pl.ANY) for _ in after],
        out_specs=[pl.BlockSpec(memory_space=pltpu.VMEM) for _ in outs],
        scratch_shapes=[pltpu.VMEM(s, F32) for s in scratch],
        compiler_params=pltpu.CompilerParams(vmem_limit_bytes=8 * 1024 * 1024),
        cost_estimate=pl.CostEstimate(flops=flops, bytes_accessed=nbytes, transcendentals=0),
        name=name,
    )(*ins, *after)


def swap(values, axis, odd, by=1):
    count = lax.axis_size(axis)
    pairs = []
    for i in range(count - by):
        if i // by % 2 == odd:
            pairs += [(i, i + by), (i + by, i)]
    return lax.ppermute(values, axis, pairs)


def exchange(xb, zb, xa, za):
    return swap(xb, "gx", 1), swap(zb, "gz", 1), swap(xa, "gx", 0), swap(za, "gz", 0)


def sides(axis, by=1):
    parity = (lax.axis_index(axis) // by) & 1
    return 1 - parity, parity


def by_side(pair, axis, by=1):
    first = sides(axis, by)[0]
    return jnp.where(first == 0, pair[0], pair[1]), jnp.where(first == 1, pair[0], pair[1])


def halves(values):
    high = values.astype(BF16)
    return high, (values - high.astype(F32)).astype(BF16)


def stacked_left(matrix):
    spread = matrix + pltpu.roll(matrix, K, 1) + pltpu.roll(matrix, 2 * K, 1)
    high = spread.astype(BF16).astype(F32)
    lane = lax.broadcasted_iota(jnp.int32, spread.shape, 1)
    return jnp.where(lane < 2 * K, high, spread - high).astype(BF16)[:, 0:3 * K]


def dot3(left, right):
    high, low = halves(right)
    return jnp.dot(left, jnp.concatenate([high, low, high], axis=0), preferred_element_type=F32)


def dot_exact(left, right, dims=(((1,), (0,)), ((), ()))):
    return lax.dot_general(
        left, right, dims, precision=lax.Precision.HIGHEST, preferred_element_type=F32
    )


def flat_slots(table, spread):
    rows, fields, slots = table.shape
    lane = lax.broadcasted_iota(jnp.int32, (8, LANES), 1)
    for r in range(rows):
        spread[r, 0:fields, 0:slots] = table[r].astype(F32)
    flat = jnp.zeros((8, LANES), F32)
    for r in range(rows):
        got = jnp.take_along_axis(spread[r], lane % slots, axis=1, mode="promise_in_bounds")
        flat = jnp.where(lane // slots == r, got, flat)
    return flat


def pack_x(out, at, source, side):
    fields, nx, nz, ny = source.shape
    start = side * (nx - RADIUS)
    rows = fields * RADIUS * nz
    at = HEAD + at * RADIUS * nz
    out[at:at + rows, :] = source[:, pl.ds(start, RADIUS)].reshape(rows, ny)


def pack_z(out, at, source, side):
    fields, nz = source.shape[0], source.shape[2]
    out[at:at + fields] = jnp.where(side == 1, source[:, :, nz - RADIUS:, :], source[:, :, 0:RADIUS, :])


def widen(ext, center, xb, zb, xa, za, first=0):
    fields, nx, nz, ny = center.shape
    ext[:, RADIUS:RADIUS + nx, ZRIM:ZRIM + nz] = center[...]
    for got, side in zip((xa, xb), sides("gx")):
        place = pl.ds(side * (nx + RADIUS), RADIUS)
        if len(got.shape) == 4:
            rows = got[first:first + fields]
        else:
            rows = got[HEAD:HEAD + fields * RADIUS * nz, :].reshape(fields, RADIUS, nz, ny)
        ext[:, place, ZRIM:ZRIM + nz] = rows
    low, high = by_side([got[first:first + fields] for got in (za, zb)], "gz")
    ext[:, RADIUS:RADIUS + nx, ZRIM - RADIUS:ZRIM] = low
    ext[:, RADIUS:RADIUS + nx, ZRIM + nz:ZRIM + nz + RADIUS] = high


def d1(load, x, lo, hi):
    total = None
    for m, w in enumerate(STENCIL_WEIGHTS, 1):
        term = w * (load(x + m, lo, hi) - load(x - m, lo, hi))
        total = term if total is None else total + term
    return total


def d2(load, x, lo, hi):
    total = None
    for m, w in enumerate(STENCIL_WEIGHTS, 1):
        term = w * (load(x, lo + m, hi + m) - load(x, lo - m, hi - m))
        total = term if total is None else total + term
    return total


def d3(values):
    width = values.shape[1]
    lane = lax.broadcasted_iota(jnp.int32, (1, width), 1)
    total = None
    for m, w in enumerate(STENCIL_WEIGHTS, 1):
        ahead = jnp.where(lane < width - m, w, 0.0) * pltpu.roll(values, width - m, 1)
        behind = jnp.where(lane >= m, w, 0.0) * pltpu.roll(values, m, 1)
        term = ahead - behind
        total = term if total is None else total + term
    return total


def field(ref, c):
    return lambda x, lo, hi: ref[c, x, lo:hi, :]


def plane(ref):
    return lambda x, lo, hi: ref[x, lo:hi, :]


def arrived(table, strip, band, n_gx, n_gz, reach, slots):
    lane = lax.broadcasted_iota(jnp.int32, (1, LANES), 1)
    got = jnp.zeros((1, LANES), F32)
    inside = (strip >= 0) & (strip < n_gx) & (band >= 0) & (band < n_gz)
    for r in range(reach):
        source = strip - (r - reach // 2)
        valid = inside & (source >= 0) & (source < n_gx)
        at = jnp.where(valid, source * n_gz + band, 0) * 8
        row = table[pl.ds(pl.multiple_of(at, 8), 8), :][0:1]
        here = ((lane & (LANES // 2 - 1)) // slots == r) & valid
        got = jnp.where(here, row, got)
    turned = pltpu.roll(got, LANES // 2, 1)
    speed = jnp.where(lane < LANES // 2, got, turned)
    high = speed.astype(BF16).astype(F32)
    return jnp.where(lane < LANES // 2, high, speed - high), jnp.where(lane < LANES // 2, turned, got)


def cell_masks(cells, rows):
    cells = cells.astype(jnp.int32)
    place = lax.broadcasted_iota(jnp.int32, (rows, LANES), 0)
    third = lax.broadcasted_iota(jnp.int32, (LANES, LANES), 0)
    return cells // LANES == place, cells % LANES == third


def raw_rims_kernel(air, wind, xb, zb, xa, za):
    fields, nx = air.shape[:2]
    for out, side in zip((xa, xb), sides("gx")):
        rows = pl.ds(side * (nx - RADIUS), RADIUS)
        out[0:fields] = air[:, rows]
        out[fields:] = wind[:, rows]
    for out, side in zip((za, zb), sides("gz")):
        pack_z(out, 0, air, side)
        pack_z(out, fields, wind, side)


def lanes(at):
    return pl.ds(at if isinstance(at, int) else pl.multiple_of(at, LANES), LANES)


def jacobian_step(load, rot, emit, quants, dims, width):
    rows = rot.shape[0] // dims

    def half(h, carry):
        at = h * LANES
        acc = [None] * quants
        for d in range(dims):
            for q in range(quants):
                turned = rot[d * rows:(d + 1) * rows, lanes(q * width + at)].reshape(rows // 8, 8, LANES)
                for p in range(quants):
                    term = load(p, q, d, lanes(at)) * turned
                    acc[p] = term if acc[p] is None else acc[p] + term
        for p in range(quants):
            emit(p, at, acc[p].reshape(rows, LANES))
        return carry

    lax.fori_loop(0, width // LANES, half, 0)


def rotate(rot, left, source, quants, width):
    for q in range(quants):
        cut = slice(q * width, (q + 1) * width)
        rot[:, cut] = dot3(left, source[:, cut])


def take_slots(tiles, index):
    low = index % LANES
    high = index // LANES
    got = None
    for s, tile in enumerate(tiles):
        picked = jnp.take_along_axis(tile, low, axis=1, mode="promise_in_bounds")
        got = picked if got is None else jnp.where(high == s, picked, got)
    return got


def predict_kernel(
    state, jac, stiff, trace,
    integral, traces, kept,
    cur, rot, sp, tp,
):
    quants, basis, width = state.shape
    pad = sp.shape[0] // stiff.shape[0]
    face_basis, faces = trace.shape[:2]
    dims = stiff.shape[0]
    sp[...] = jnp.zeros_like(sp)
    tp[...] = jnp.zeros_like(tp)
    cur[...] = jnp.zeros_like(cur)
    for d in range(dims):
        sp[d * pad:d * pad + basis, 0:basis] = stiff[d]
    for f in range(faces):
        for j in range(face_basis):
            tp[f * 16 + j:f * 16 + j + 1, 0:basis] = trace[j, f:f + 1, :]
    for q in range(quants):
        cur[0:basis, q * width:(q + 1) * width] = state[q]
    kept[...] = state[...]
    integral[...] = TIME_STEP * cur[...]
    left = stacked_left(sp[...])

    def degree(k, weight):
        weight = jnp.where(k == 1, TIME_STEP**2 / 2, jnp.where(k == 2, TIME_STEP**3 / 6, TIME_STEP**4 / 24))
        rotate(rot, left, cur, quants, width)

        def emit(p, at, value):
            cut = lanes(p * width + at)
            cur[0:pad, cut] = -value
            integral[0:pad, cut] = integral[0:pad, cut] - weight * value

        jacobian_step(lambda p, q, d, cut: jac[p, q, d:d + 1, cut], rot, emit, quants, dims, width)
        return weight

    lax.fori_loop(1, ORDERS, degree, F32(0))
    restrict = stacked_left(tp[...])
    for q in range(quants):
        cut = slice(q * width, (q + 1) * width)
        done = dot3(restrict, integral[:, cut])
        for f in range(faces):
            traces[q, :, f * width:(f + 1) * width] = done[f * 16:(f + 1) * 16]


def own_list_kernel(traces, smap, normals, rows, spread, own):
    all_slots = traces.shape[2]
    slots = flat_slots(smap, spread)
    wanted = jnp.broadcast_to(slots[0:1].astype(jnp.int32), (16, LANES))

    def gather(q, carry):
        own[q] = take_slots([traces[6 + q, :, s * LANES:(s + 1) * LANES] for s in range(all_slots // LANES)], wanted)
        return carry

    lax.fori_loop(0, 3, gather, 0)
    normal = flat_slots(normals, spread)
    speed = jnp.zeros((1, LANES), F32)
    for c in range(3):
        mean = jnp.sum(own[c, 0:FACE_ROWS, :], axis=0, keepdims=True) * (1.0 / FACE_ROWS)
        speed = speed + normal[c:c + 1] * mean
    lane = lax.broadcasted_iota(jnp.int32, (1, LANES), 1)
    cells = pltpu.roll(slots[1:2], LANES // 2, 1)
    rows[...] = jnp.broadcast_to(jnp.where(lane < LANES // 2, slots[2:3] * speed, cells), rows.shape)


def own_traces_kernel(traces, smap, own, spread):
    quants, _, all_slots = traces.shape
    wanted = jnp.broadcast_to(flat_slots(smap, spread)[0:1].astype(jnp.int32), (16, LANES))

    def gather(q, carry):
        own[q] = take_slots([traces[q, :, s * LANES:(s + 1) * LANES] for s in range(all_slots // LANES)], wanted)
        return carry

    lax.fori_loop(0, quants, gather, 0)


def outgoing_kernel(traces, sends, xa, xb, za, zb, picked):
    quants, _, slots = traces.shape
    rows = sent_rows(quants, FACE_ROWS)
    wanted = [jnp.broadcast_to(sends[d:d + 1, :], (16, LANES)) for d in range(4)]

    def gather(q, carry):
        tiles = [traces[q, :, s * LANES:(s + 1) * LANES] for s in range(slots // LANES)]
        for d in range(4):
            picked[d, q] = take_slots(tiles, wanted[d])
        return carry

    lax.fori_loop(0, quants, gather, 0)
    rest = FACE_ROWS - 8
    for axis, base, outs in (("gx", 0, (xa, xb)), ("gz", 2, (za, zb))):
        for out, side in zip(outs, sides(axis)):
            for q in range(quants):
                out[q * 8:q * 8 + 8, :] = picked[base + side, q, 0:8, :]
                at = quants * 8 + q * rest
                out[at:at + rest, :] = picked[base + side, q, 8:FACE_ROWS, :]
            out[quants * FACE_ROWS:, :] = jnp.zeros((rows - quants * FACE_ROWS, LANES), F32)


def pressure_rows(ext, wind, medium, x, nz):
    lo, hi = ZRIM, ZRIM + nz
    xe = x + RADIUS
    pressure = field(ext, 0)
    here = pressure(xe, lo, hi)
    divergence = d1(field(ext, 1), xe, lo, hi) + d2(field(ext, 2), xe, lo, hi) + d3(ext[3, xe, lo:hi, :])
    moved = (
        wind[0, x] * d1(pressure, xe, lo, hi)
        + wind[1, x] * d2(pressure, xe, lo, hi)
        + wind[2, x] * d3(here)
    )
    return here - medium[0, x] * divergence - moved


def pack_pressure(center, xs, zs):
    nx, nz, ny = center.shape[1:]
    for out, side in zip(xs, sides("gx")):
        start = side * (nx - RADIUS)
        out[HEAD:HEAD + RADIUS * nz, :] = center[0, pl.ds(start, RADIUS)].reshape(RADIUS * nz, ny)
    for out, side in zip(zs, sides("gz")):
        start = pl.multiple_of(side * (nz - ZRIM), ZRIM)
        out[HEAD:HEAD + nx * ZRIM, :] = center[0, :, pl.ds(start, ZRIM), :].reshape(nx * ZRIM, ny)


def widen_pressure(ext, center, xb, zb, xa, za):
    nx, nz, ny = ext.shape[0] - 2 * RADIUS, ext.shape[1] - 2 * ZRIM, ext.shape[2]
    if center is not None:
        ext[RADIUS:RADIUS + nx, ZRIM:ZRIM + nz] = center[...]
    for got, side in zip((xa, xb), sides("gx")):
        ext[pl.ds(side * (nx + RADIUS), RADIUS), ZRIM:ZRIM + nz] = got[HEAD:HEAD + RADIUS * nz, :].reshape(RADIUS, nz, ny)
    for got, side in zip((za, zb), sides("gz")):
        start = pl.multiple_of(side * (nz + ZRIM), ZRIM)
        ext[RADIUS:RADIUS + nx, pl.ds(start, ZRIM)] = got[HEAD:HEAD + nx * ZRIM, :].reshape(nx, ZRIM, ny)


def raw_pressure_kernel(
    air, wind, medium, xb, zb, xa, za, txa, txb, tza, tzb, oxb, ozb, oxa, oza, ext, pressure
):
    nx, nz, ny = air.shape[1:]
    widen(ext, air, xb, zb, xa, za)
    for x in range(nx):
        pressure[0, x] = pressure_rows(ext, wind, medium, x, nz)
    pack_pressure(pressure, (oxa, oxb), (oza, ozb))
    for out, sent in zip((oxa, oxb, oza, ozb), (txa, txb, tza, tzb)):
        out[0:HEAD, :] = jnp.zeros((HEAD, LANES), F32)
        out[out.shape[0] - sent.shape[0]:, :] = sent[...]


def put_rows(rows):
    place = lax.broadcasted_iota(jnp.int32, (HEAD, LANES), 0)
    out = jnp.zeros((HEAD, LANES), F32)
    for at, row in enumerate(rows):
        out = jnp.where(place == at, row, out)
    return out


def advection_kernel(air, wind, xb, zb, xa, za, moved, ext):
    nx, nz, ny = air.shape[1:]
    widen(ext, air, xb, zb, xa, za)
    lo, hi = ZRIM, ZRIM + nz
    for x in range(nx):
        xe = x + RADIUS
        for c in range(3):
            load = field(ext, 1 + c)
            moved[c, x] = (
                wind[0, x] * d1(load, xe, lo, hi)
                + wind[1, x] * d2(load, xe, lo, hi)
                + wind[2, x] * d3(load(xe, lo, hi))
            )


def velocities(out, center, moved, medium, wide, nx, nz):
    lo, hi = ZRIM, ZRIM + nz
    load = plane(wide)
    for x in range(nx):
        xe = x + RADIUS
        slopes = (d1(load, xe, lo, hi), d2(load, xe, lo, hi), d3(load(xe, lo, hi)))
        out[0, x] = load(xe, lo, hi)
        for c in range(3):
            out[1 + c, x] = center[1 + c, x] - medium[1, x] * slopes[c] - moved[c, x]


def pack_air(out, xb, zb, xa, za):
    for rim, side in zip((xa, xb), sides("gx")):
        pack_x(rim, 0, out, side)
    for rim, side in zip((za, zb), sides("gz")):
        pack_z(rim, 0, out, side)


def injected_kernel(
    n_gx, n_gz, air, wind, medium, moved, wxb, wzb, wxa, wza, pxb, pzb, pxa, pza, table, smap,
    out, oxb, ozb, oxa, oza, answer, spread, wide, wide_wind, ext,
):
    nx, nz, ny = air.shape[1:]
    reach, _, slots = smap.shape
    strip, band = lax.axis_index("gx"), lax.axis_index("gz")
    mul = functools.partial(
        lax.dot_general, dimension_numbers=(((1,), (1,)), ((), ())), preferred_element_type=F32
    )
    for da in range(3):
        for db in range(3):
            speed, cells = arrived(table, strip + da - 1, band + db - 1, n_gx, n_gz, reach, slots)
            row_mask, third_mask = cell_masks(cells, nx * nz)
            columns = jnp.where(third_mask, 1.0, 0.0).astype(BF16)
            if da == 1 and db == 1:
                seen, rest = halves(air[0].reshape(nx * nz, ny))
                looked = jnp.dot(seen, columns, preferred_element_type=F32)
                looked = looked + jnp.dot(rest, columns, preferred_element_type=F32)
                answer[...] = jnp.sum(jnp.where(row_mask, looked, 0.0), axis=0, keepdims=True)
            block = mul(jnp.where(row_mask, speed, 0.0).astype(BF16), columns)
            spread[da * nx:(da + 1) * nx, db * nz:(db + 1) * nz] = block.reshape(nx, nz, ny)
    widen(wide_wind, wind, wxb, wzb, wxa, wza, first=air.shape[0])
    widen_pressure(wide, None, pxb, pzb, pxa, pza)
    widen(ext, air, wxb, wzb, wxa, wza)
    for x in range(nx):
        wide[RADIUS + x, ZRIM:ZRIM + nz] = pressure_rows(ext, wind, medium, x, nz)
    load = plane(spread)
    for x in range(nx + 2 * RADIUS):
        xs = x + nx - RADIUS
        if RADIUS <= x < RADIUS + nx:
            lo, hi = 0, nz + 2 * ZRIM
        else:
            lo, hi = ZRIM, ZRIM + nz
        slo, shi = lo + nz - ZRIM, hi + nz - ZRIM
        here = load(xs, slo, shi)
        turned = (
            wide_wind[0, x, lo:hi, :] * d1(load, xs, slo, shi)
            + wide_wind[1, x, lo:hi, :] * d2(load, xs, slo, shi)
            + wide_wind[2, x, lo:hi, :] * d3(here)
        )
        wide[x, lo:hi, :] = wide[x, lo:hi, :] + (here - turned)
    velocities(out, air, moved, medium, wide, nx, nz)
    pack_air(out, oxb, ozb, oxa, oza)
    for rim in (oxa, oxb):
        rim[0:HEAD, :] = put_rows((answer[...],))


def pressure_kernel(air, wind, medium, xb, zb, xa, za, answer, pressure, oxb, ozb, oxa, oza, ext):
    nx, nz, ny = air.shape[1:]
    widen(ext, air, xb, zb, xa, za)
    for x in range(nx):
        pressure[0, x] = pressure_rows(ext, wind, medium, x, nz)
    pack_pressure(pressure, (oxa, oxb), (oza, ozb))
    low, high = by_side((xa[0:1, :], xb[0:1, :]), "gx")
    for rim in (oxa, oxb):
        rim[0:HEAD, :] = put_rows((answer[...], low, high))
    for rim in (oza, ozb):
        rim[0:HEAD, :] = jnp.zeros((HEAD, LANES), F32)


def velocity_kernel(air, pressure, medium, moved, xb, zb, xa, za, out, *rest):
    nx, nz, ny = air.shape[1:]
    wide = rest[-1]
    widen_pressure(wide, pressure.at[0], xb, zb, xa, za)
    velocities(out, air, moved, medium, wide, nx, nz)
    if len(rest) > 1:
        pack_air(out, *rest[:-1])
        for rim in (rest[0], rest[2]):
            rim[0:HEAD, :] = jnp.zeros((HEAD, LANES), F32)


def volume_kernel(state, integral, jac, stiff, out, token, rot, sp):
    quants, basis, width = state.shape
    dims = stiff.shape[0]
    pad = sp.shape[0] // dims
    token[...] = jnp.zeros_like(token)
    sp[...] = jnp.zeros_like(sp)
    place = lax.broadcasted_iota(jnp.int32, (basis, basis), 0)
    other = lax.broadcasted_iota(jnp.int32, (basis, basis), 1)
    unit = jnp.where(place == other, 1.0, 0.0).astype(F32)
    for d in range(dims):
        sp[d * pad:d * pad + basis, 0:basis] = dot_exact(unit, stiff[d], (((1,), (1,)), ((), ())))
    rotate(rot, stacked_left(sp[...]), integral, quants, width)

    def emit(p, at, value):
        out[p, :, lanes(at)] = state[p, :, lanes(at)] + value[0:basis]

    jacobian_step(lambda p, q, d, cut: jac[p, q, d:d + 1, cut], rot, emit, quants, dims, width)


def flux_kernel(
    first, faces, base, traces, own, solvers, lift, neighbours, xb, zb, xa, za,
    out, token, tiles, flux, lp,
):
    token[...] = jnp.zeros_like(token)
    quants, basis, width = base.shape
    face_basis = lift.shape[0]
    skip = xa.shape[0] - sent_rows(quants, face_basis)
    for axis, base_tile, gots in (("gx", 0, (xa, xb)), ("gz", 2, (za, zb))):
        for got, side in zip(gots, sides(axis)):
            for q in range(quants):
                tiles[q, base_tile + side, 0:8, :] = got[skip + q * 8:skip + q * 8 + 8, :]
                at = skip + quants * 8 + q * 2
                tiles[q, base_tile + side, 8:face_basis, :] = got[at:at + 2, :]
                tiles[q, base_tile + side, face_basis:, :] = jnp.zeros((16 - face_basis, LANES), F32)
    for q in range(quants):
        tiles[q, 4] = -own[q] if q < 3 else own[q]
    lp[...] = jnp.zeros_like(lp)
    for f in range(faces):
        for j in range(face_basis):
            lp[f * 16 + j:f * 16 + j + 1, 0:basis] = lift[j, first + f:first + f + 1, :]
    unit = lax.broadcasted_iota(jnp.int32, (lp.shape[1], lp.shape[1]), 0) == lax.broadcasted_iota(
        jnp.int32, (lp.shape[1], lp.shape[1]), 1
    )
    lifted = stacked_left(dot_exact(jnp.where(unit, 1.0, 0.0).astype(F32), lp[...], (((1,), (1,)), ((), ()))))
    local = traces.shape[2] // LANES
    halves_in = width // LANES

    def one(h, carry):
        at = h * LANES
        for f in range(faces):
            index = jnp.broadcast_to(neighbours[first + f:first + f + 1, lanes(at)], (16, LANES))
            acc = [None] * quants
            for q in range(quants):
                pool = [traces[q, :, s * LANES:(s + 1) * LANES] for s in range(local)]
                pool += [tiles[q, s] for s in range(5)]
                mine = traces[q, :, lanes((first + f) * width + at)]
                jump = take_slots(pool, index) - mine
                for p in range(quants):
                    term = solvers[p, q, first + f:first + f + 1, lanes(at)] * jump
                    acc[p] = term if acc[p] is None else acc[p] + term
            for p in range(quants):
                flux[f * 16:(f + 1) * 16, lanes(p * width + at)] = acc[p]
        return carry

    lax.fori_loop(0, halves_in, one, 0)
    for p in range(quants):
        cut = slice(p * width, (p + 1) * width)
        out[p] = base[p] + dot3(lifted, flux[:, cut])[0:basis]


def replies_kernel(base, solvers, lift, neighbours, smap, answer, rxb, rxa, out, slot_spread):
    quants, basis, width = base.shape
    face_basis, faces = lift.shape[:2]
    slots = smap.shape[2]
    low, high = by_side((rxa[0:HEAD, :], rxb[0:HEAD, :]), "gx")
    lane = lax.broadcasted_iota(jnp.int32, (1, LANES), 1)
    replies = jnp.zeros((1, LANES), F32)
    for r, row in enumerate((low[1:2], low[0:1], answer[...], high[0:1], high[2:3])):
        replies = jnp.where(lane // slots == r, row, replies)
    replies = jnp.broadcast_to(-2.0 * replies * flat_slots(smap, slot_spread)[2:3], (8, LANES))
    begin = faces * width + 4 * LANES
    square = lax.broadcasted_iota(jnp.int32, (basis, basis), 0) == lax.broadcasted_iota(
        jnp.int32, (basis, basis), 1
    )
    columns = []
    for f in range(faces):
        column = lift[0, f:f + 1, :]
        for j in range(1, face_basis):
            column = column + lift[j, f:f + 1, :]
        columns.append(jnp.sum(jnp.where(square, column, 0.0), axis=1, keepdims=True))
    for h in range(width // LANES):
        cut = slice(h * LANES, (h + 1) * LANES)
        spread = []
        for f in range(faces):
            index = jnp.broadcast_to(neighbours[f:f + 1, cut], (8, LANES))
            found = jnp.take_along_axis(replies, index % LANES, axis=1, mode="promise_in_bounds")
            spread.append(columns[f] * jnp.where(index >= begin, found, 0.0)[0:1])
        for p in range(quants):
            stress = solvers[p, 0, :, cut] + solvers[p, 1, :, cut] + solvers[p, 2, :, cut]
            total = base[p, :, cut]
            for f in range(faces):
                total = total + stress[f:f + 1] * spread[f]
            out[p, :, cut] = total


def sent_rows(quants, face_basis):
    return -(-quants * face_basis // 8) * 8


def shards(
    solid_state, jacobians, flux_solvers, stiffness, trace_matrix, lift_matrix,
    neighbours, send_faces, surface_map, surface_normals, air_state, wind_field, air_medium,
):
    quants, basis, width = solid_state.shape
    faces, face_basis = trace_matrix.shape[0], trace_matrix.shape[1]
    dims = stiffness.shape[0]
    nx, nz, ny = air_state.shape[1:]
    n_gx, n_gz = lax.axis_size("gx"), lax.axis_size("gz")
    jacobians = jnp.transpose(jacobians, (1, 2, 0, 3))
    flux_solvers = jnp.transpose(flux_solvers, (1, 2, 0, 3))
    trace_matrix = jnp.transpose(trace_matrix, (1, 0, 2))
    lift_matrix = jnp.transpose(lift_matrix, (2, 0, 1))
    surface_map = jnp.transpose(surface_map, (1, 0, 2))
    surface_normals = jnp.transpose(surface_normals, (1, 0, 2))
    pad = -(-basis // 8) * 8
    rim_z = (7, nx, RADIUS, ny)
    rim_x = (7, RADIUS, nz, ny)
    ext = (4, nx + 2 * RADIUS, nz + 2 * ZRIM, ny)
    wide = ext[1:]
    block = (1, nx, nz, ny)
    tile = (8, LANES)

    rims = exchange(
        *call(
            raw_rims_kernel, "raw_rims", [rim_x, rim_z, rim_x, rim_z], [air_state, wind_field],
        )
    )

    sent = (sent_rows(quants, face_basis), LANES)
    integral, traces, state = call(
        predict_kernel, "predict",
        [(K, quants * width), (quants, 16, faces * width), solid_state.shape],
        [solid_state, jacobians, stiffness, trace_matrix],
        [(K, quants * width), (dims * pad, quants * width), (dims * pad, LANES), (faces * 16, LANES)],
        flops=40_000_000,
    )
    (rows,) = call(
        own_list_kernel, "own_list", [(n_gx * n_gz * 8, LANES)],
        [traces, surface_map, surface_normals], [(surface_map.shape[0], 8, LANES), (3, 16, LANES)],
        after=[rims[1], rims[3]],
    )
    lists = lax.all_to_all(rows, ("gx", "gz"), split_axis=0, concat_axis=0, tiled=True)
    sent_four = call(
        outgoing_kernel, "outgoing", [sent, sent, sent, sent], [traces, send_faces],
        [(4, quants, 16, LANES)], flops=10_000_000, after=[rows],
    )
    pressure_x = (HEAD + RADIUS * nz, ny)
    pressure_z = (HEAD + nx * ZRIM, ny)
    both_x = (pressure_x[0] + sent[0], LANES)
    both_z = (pressure_z[0] + sent[0], LANES)
    xb, zb, xa, za = call(
        raw_pressure_kernel, "raw_pressure", [both_x, both_z, both_x, both_z],
        [air_state, wind_field, air_medium, *rims, *sent_four], [ext, block],
    )
    both = exchange(xb, zb, xa, za)
    (moved,) = call(
        advection_kernel, "advection", [(3, nx, nz, ny)],
        [air_state, wind_field, *rims], [ext], flops=10_000_000, after=[xa],
    )
    (own,) = call(
        own_traces_kernel, "own_traces", [(quants, 16, LANES)], [traces, surface_map],
        [(surface_map.shape[0], 8, LANES)], after=[xa],
    )

    rim_x = (HEAD + 4 * RADIUS * nz, ny)
    rim_z = (4, nx, RADIUS, ny)
    air, xb, zb, xa, za, answer = call(
        functools.partial(injected_kernel, n_gx, n_gz), "injected",
        [air_state.shape, rim_x, rim_z, rim_x, rim_z, (1, LANES)],
        [air_state, wind_field, air_medium, moved, *rims, *both, lists, surface_map],
        [(3 * nx, 3 * nz, ny), wide, (3,) + wide, ext], after=[own],
    )
    half = faces // 2
    solid = state
    for substep in range(1, SUBSTEPS):
        rims = exchange(xb, zb, xa, za)
        solid, token = call(
            functools.partial(flux_kernel, (substep - 1) * half, half), "flux", [solid_state.shape, tile],
            [solid, traces, own, flux_solvers, lift_matrix, neighbours, *both],
            [(quants, 5, 16, LANES), (half * 16, quants * width), (LANES, pad)], flops=20_000_000,
            after=[xa],
        )
        pressure, xb, zb, xa, za = call(
            pressure_kernel, "pressure", [block, pressure_x, pressure_z, pressure_x, pressure_z],
            [air, wind_field, air_medium, *rims, answer], [ext], after=[token],
        )
        rises = exchange(xb, zb, xa, za)
        if substep == 1:
            replies = [answer, rises[0], rises[2]]
        (moved,) = call(
            advection_kernel, "advection", [(3, nx, nz, ny)],
            [air, wind_field, *rims], [ext], flops=10_000_000, after=[xa],
        )
        last = substep == SUBSTEPS - 1
        if not last:
            solid, token = call(
                volume_kernel, "volume", [solid_state.shape, tile], [solid, integral, jacobians, stiffness],
                [(dims * pad, quants * width), (dims * pad, LANES)], flops=10_000_000, after=[moved],
            )
        else:
            (solid,) = call(
                replies_kernel, "replies", [solid_state.shape],
                [solid, flux_solvers, lift_matrix, neighbours, surface_map, *replies],
                [(surface_map.shape[0], 8, LANES)], after=[moved],
            )
        outs = [air_state.shape] + ([] if last else [rim_x, rim_z, rim_x, rim_z])
        done = call(
            velocity_kernel, "velocity", outs, [air, pressure, air_medium, moved, *rises], [wide],
            after=[token],
        )
        air = done[0]
        if not last:
            xb, zb, xa, za = done[1:]
    return (solid, air)


def solution(mesh):
    in_specs = (
        P(None, None, ("gx", "gz")),
        P(None, None, None, ("gx", "gz")),
        P(None, None, None, ("gx", "gz")),
        P(),
        P(),
        P(),
        P(None, ("gx", "gz")),
        P(None, ("gx", "gz")),
        P(None, None, ("gx", "gz")),
        P(None, None, ("gx", "gz")),
        P(None, "gx", "gz", None),
        P(None, "gx", "gz", None),
        P(None, "gx", "gz", None),
    )
    out_specs = (P(None, None, ("gx", "gz")), P(None, "gx", "gz", None))
    return jax.shard_map(shards, mesh=mesh, in_specs=in_specs, out_specs=out_specs, check_vma=False)
```
